32 devices in a mesh: seq: 4 (over y, x), fsdp: 8 (over z, core).
Axes of the slice: x: 2, y: 2, z: 4, core: 2. Of those that a mesh axis runs over, the one named last changes fastest.
Arguments:
- tokens: bfloat16 [16, 1024, 2048], P('fsdp', 'seq'), may hold values from -6 to 6
- cotangent: bfloat16 [16, 1024, 2048], P('fsdp', 'seq'), may hold values from -6 to 6
- w_qkv: bfloat16 [2048, 6144], P('fsdp'), may hold values from -0.125 to 0.125
- qv_bias: float32 [2, 2048], replicated, may hold values from -3 to 3
- w_out: bfloat16 [2048, 2048], P('fsdp'), may hold values from -0.375 to 0.375
- out_bias: float32 [2048], replicated, may hold values from -3 to 3
- ln1_gain: float32 [2048], replicated, may hold values from 0.25 to 1.75
- ln1_shift: float32 [2048], replicated, may hold values from -2 to 2
- ln2_gain: float32 [2048], replicated, may hold values from 0.25 to 1.75
- ln2_shift: float32 [2048], replicated, may hold values from -2 to 2
- w_up: bfloat16 [2048, 8192], P('fsdp'), may hold values from -0.125 to 0.125
- up_bias: float32 [8192], replicated, may hold values from -3 to 3
- w_down: bfloat16 [8192, 2048], P(None, 'fsdp'), may hold values from -0.0625 to 0.0625
- down_bias: float32 [2048], replicated, may hold values from -3 to 3
Outputs:
- result: bfloat16 [16, 1024, 2048], P('fsdp', 'seq')
- grad_tokens: bfloat16 [16, 1024, 2048], P('fsdp', 'seq')
- grad_w_qkv: float32 [2048, 6144], P(('seq', 'fsdp'))
- grad_qv_bias: float32 [2, 2048], replicated
- grad_w_out: float32 [2048, 2048], P(('seq', 'fsdp'))
- grad_out_bias: float32 [2048], replicated
- grad_ln1_gain: float32 [2048], replicated
- grad_ln1_shift: float32 [2048], replicated
- grad_ln2_gain: float32 [2048], replicated
- grad_ln2_shift: float32 [2048], replicated
- grad_w_up: float32 [2048, 8192], P(('seq', 'fsdp'))
- grad_up_bias: float32 [8192], replicated
- grad_w_down: float32 [8192, 2048], P(None, ('seq', 'fsdp'))
- grad_down_bias: float32 [2048], replicated
The draws below stay inside these ranges and needn't reach their ends.
All inputs are finite; a program needn't handle non-finite values.
Results may differ from the reference program's by a relative error of at most 0.012.
Values may be sent and summed in bfloat16 or wider, within the bound.
A program may use at most 768 MiB of HBM per device.

```python
import math
import jax
import jax.numpy as jnp
from jax import lax

D = 2048
HEADS = 32
HEAD_DIM = 64
FF = 8192
LENGTH = 1024
BLOCK = 256
SEQS = 2
SEQUENCES = 16
N_FSDP = 8


def block_levels(stream_key, dims, cuts, smallest, high):
    level, own = 1.0, jax.random.fold_in(stream_key, 6)
    for dim, shards_of in cuts:
        draws = jnp.exp(jax.random.uniform(jax.random.fold_in(own, dim), (shards_of,), jnp.float32, smallest / len(cuts), high / len(cuts)))
        level = level * jnp.repeat(draws, dims[dim] // shards_of).reshape([-1 if axis == dim else 1 for axis in range(len(dims))])
    return level


def normal_values(rng, extent, scale, most, split=(), kind=jnp.bfloat16):
    level = block_levels(rng, extent, split, -0.22, 0.18) if split else 1.0
    entries = jax.random.normal(rng, extent, jnp.float32) * scale * level
    return jnp.minimum(jnp.maximum(entries, -most), most).astype(kind)


def setup_inputs(seed: int = 0) -> dict:
    key_list = jax.random.split(jax.random.key(seed), 15)
    tokens = normal_values(key_list[0], (SEQUENCES, LENGTH, D), 1.0, 6.0, ((0, 8), (1, 4)))
    cotangent = normal_values(key_list[1], (SEQUENCES, LENGTH, D), 1.0, 6.0, ((0, 8), (1, 4)))
    w_qkv = normal_values(key_list[2], (D, 3 * D), D ** -0.5, 0.125, ((0, 8),))
    qv_bias = normal_values(key_list[3], (2, D), 0.5, 3.0, (), jnp.float32)
    w_out = normal_values(key_list[4], (D, D), (D // 8) ** -0.5, 0.375, ((0, 8),))
    out_bias = normal_values(key_list[5], (D,), 0.5, 3.0, (), jnp.float32)
    ln1_gain = jnp.clip(1.0 + 0.15 * jax.random.normal(key_list[6], (D,), jnp.float32), 0.25, 1.75)
    ln1_shift = normal_values(key_list[7], (D,), 0.3, 2.0, (), jnp.float32)
    ln2_gain = jnp.clip(1.0 + 0.15 * jax.random.normal(key_list[8], (D,), jnp.float32), 0.25, 1.75)
    ln2_shift = normal_values(key_list[9], (D,), 0.3, 2.0, (), jnp.float32)
    w_up = normal_values(key_list[10], (D, FF), D ** -0.5, 0.125, ((0, 8),))
    up_bias = normal_values(key_list[11], (FF,), 0.5, 3.0, (), jnp.float32)
    w_down = normal_values(key_list[12], (FF, D), FF ** -0.5, 0.0625, ((1, 8),))
    down_bias = normal_values(key_list[13], (D,), 0.5, 3.0, (), jnp.float32)
    return dict(tokens=tokens, cotangent=cotangent, w_qkv=w_qkv, qv_bias=qv_bias, w_out=w_out, out_bias=out_bias, ln1_gain=ln1_gain, ln1_shift=ln1_shift, ln2_gain=ln2_gain, ln2_shift=ln2_shift, w_up=w_up, up_bias=up_bias, w_down=w_down, down_bias=down_bias)


@jax.custom_vjp
def low(v):
    return lax.optimization_barrier(v.astype(jnp.bfloat16)).astype(jnp.float32)

@jax.custom_vjp
def low_back(v):
    return v

def low_keep(v):
    return (low(v), None)

def low_pass(kept, grad):
    return (grad,)

def back_keep(v):
    return (v, None)

def back_low(kept, grad):
    return (low(grad),)
low.defvjp(low_keep, low_pass)
low_back.defvjp(back_keep, back_low)

def layer_norm(token_rows, gain_vec, shift_vec):
    average = lax.optimization_barrier(jnp.mean(token_rows, axis=-1, keepdims=True))
    centred = token_rows - average
    spread = lax.optimization_barrier(jnp.mean(centred * centred, axis=-1, keepdims=True))
    return centred * lax.rsqrt(spread + 1e-05) * gain_vec + shift_vec

def product(left_side, right_side):
    return jnp.dot(left_side, right_side, precision=lax.Precision.HIGHEST, preferred_element_type=jnp.float32)

def attend(pieces):
    queries, key_rows, values = pieces
    position = jnp.arange(LENGTH, dtype=jnp.int32)
    distance = jnp.abs(position[:, None] - position[None, :]).astype(jnp.float32)
    allowed = position[None, :] // BLOCK <= position[:, None] // BLOCK
    slopes = 2.0 ** (-8.0 * jnp.arange(1, HEADS + 1, dtype=jnp.int32).astype(jnp.float32) / HEADS)
    scores = jnp.einsum('qhd,khd->hqk', queries, key_rows, precision=lax.Precision.HIGHEST) * HEAD_DIM ** (-0.5)
    scores = scores - slopes[:, None, None] * distance[None]
    scores = jnp.where(allowed[None], scores, -1e+30)
    scores = low_back(scores)
    highest = lax.optimization_barrier(jnp.max(scores, axis=-1, keepdims=True))
    weights = jnp.exp(scores - highest)
    probs = low(weights / lax.optimization_barrier(jnp.sum(weights, axis=-1, keepdims=True)))
    return jnp.einsum('hqk,khd->qhd', probs, values, precision=lax.Precision.HIGHEST)

def forward(x_group, w_qkv, qv_bias, w_out, out_bias, ln1_gain, ln1_shift, ln2_gain, ln2_shift, w_up, up_bias, w_down, down_bias):
    members = x_group.shape[0]
    token_rows = x_group.reshape(-1, D)
    normed = low(layer_norm(token_rows, ln1_gain, ln1_shift))
    bias_row = jnp.concatenate([qv_bias[0], jnp.zeros_like(qv_bias[0]), qv_bias[1]])
    projected = low(low_back(product(normed, w_qkv) + bias_row))
    projected = projected.reshape(members, LENGTH, 3, HEADS, HEAD_DIM)
    mixed = lax.map(jax.checkpoint(attend), (projected[:, :, 0], projected[:, :, 1], projected[:, :, 2]))
    mixed = low(low_back(mixed.reshape(-1, D)))
    branch = low_back(product(mixed, w_out) + out_bias)
    middle = token_rows + branch
    second = low(layer_norm(middle, ln2_gain, ln2_shift))
    hidden = low_back(product(second, w_up) + up_bias)
    active = low(jax.nn.gelu(hidden, approximate=False))
    outcome = middle + (product(active, w_down) + down_bias)
    return outcome.reshape(x_group.shape)

def reference(tokens, cotangent, w_qkv, qv_bias, w_out, out_bias, ln1_gain, ln1_shift, ln2_gain, ln2_shift, w_up, up_bias, w_down, down_bias):
    overall = SEQS * N_FSDP
    members = math.gcd(overall, max(1, 4096 // LENGTH))
    params = tuple((param.astype(jnp.float32) for param in (w_qkv, qv_bias, w_out, out_bias, ln1_gain, ln1_shift, ln2_gain, ln2_shift, w_up, up_bias, w_down, down_bias)))
    inputs = tokens.astype(jnp.float32).reshape(overall // members, members, LENGTH, D)
    upstream = cotangent.astype(jnp.float32).reshape(overall // members, members, LENGTH, D)

    def advance(sums, pair):
        x_group, c_group = pair
        outcome, pullback = jax.vjp(forward, x_group, *params)
        gradients = pullback(c_group)
        sums = tuple((total_sum + piece for total_sum, piece in zip(sums, gradients[1:])))
        return (sums, (outcome.astype(jnp.bfloat16), gradients[0].astype(jnp.bfloat16)))
    zeros = tuple((jnp.zeros_like(param) for param in params))
    sums, (outcomes, input_grads) = lax.scan(advance, zeros, (inputs, upstream))
    result = outcomes.reshape(overall, LENGTH, D)
    grad_tokens = input_grads.reshape(overall, LENGTH, D)
    return (result, grad_tokens, sums[0], sums[1], sums[2], sums[3], sums[4], sums[5], sums[6], sums[7], sums[8], sums[9], sums[10], sums[11])
```

```python
from functools import partial

import jax
import jax.numpy as jnp
from jax import lax
from jax.experimental import pallas as pl
from jax.experimental.pallas import tpu as pltpu
from jax.sharding import PartitionSpec as P

HEADS = 32
HEAD_DIM = 64
BLOCK = 256
PAIR = 2 * HEAD_DIM


def layer_norm(token_rows, gain_vec, shift_vec):
    average = jnp.mean(token_rows, axis=-1, keepdims=True)
    centred = token_rows - average
    spread = jnp.mean(centred * centred, axis=-1, keepdims=True)
    return centred * lax.rsqrt(spread + 1e-05) * gain_vec + shift_vec


def exact_gelu(values):
    return jax.nn.gelu(values, approximate=False)


def contract(left_side, right_side):
    return lax.dot_general(
        left_side, right_side, (((1,), (0,)), ((), ())), preferred_element_type=jnp.float32
    )


def contract_last(left_side, right_side):
    return lax.dot_general(
        left_side, right_side, (((1,), (1,)), ((), ())), preferred_element_type=jnp.float32
    )


def contract_first(left_side, right_side):
    return lax.dot_general(
        left_side, right_side, (((0,), (0,)), ((), ())), preferred_element_type=jnp.float32
    )


def attend_forward_kernel(mask_ref, slope_ref, qkv_ref, mixed_ref, lse_ref, *, blocks):
    pair = pl.program_id(0)
    mask = mask_ref[0]
    lane = lax.broadcasted_iota(jnp.int32, (BLOCK, PAIR), 1)
    row = lax.broadcasted_iota(jnp.int32, (BLOCK, BLOCK), 0)
    column = lax.broadcasted_iota(jnp.int32, (BLOCK, BLOCK), 1)
    gap = (row - column).astype(jnp.float32)

    def rows(block):
        return pl.ds(pl.multiple_of((block ^ mask) * BLOCK, BLOCK), BLOCK)

    for i in range(blocks):
        q_pair = qkv_ref[rows(i), 0:PAIR]
        outs, lses = [], []
        for head in range(2):
            slope = slope_ref[pair * 2 + head]
            mine = (lane >= head * HEAD_DIM) & (lane < (head + 1) * HEAD_DIM)
            q = jnp.where(mine, q_pair, jnp.zeros_like(q_pair)) * jnp.bfloat16(HEAD_DIM**-0.5)
            parts, highest = [], None
            for j in range(i + 1):
                scores = contract_last(q, qkv_ref[rows(j), PAIR : 2 * PAIR])
                distance = jnp.abs(gap) if i == j else gap + float(BLOCK * (i - j))
                scores = scores - slope * distance
                parts.append(scores)
                top = jnp.max(scores, axis=-1, keepdims=True)
                highest = top if highest is None else jnp.maximum(highest, top)
            total, out = None, None
            for j in range(i + 1):
                weights = jnp.exp(parts[j] - highest)
                part = jnp.sum(weights, axis=-1, keepdims=True)
                mixed = contract(weights.astype(jnp.bfloat16), qkv_ref[rows(j), 2 * PAIR : 3 * PAIR])
                total = part if total is None else total + part
                out = mixed if out is None else out + mixed
            outs.append(out / total)
            lses.append(highest + jnp.log(total))
        first = lane < HEAD_DIM
        mixed_ref[rows(i), :] = jnp.where(first, outs[0], outs[1]).astype(mixed_ref.dtype)
        lse_ref[rows(i), :] = jnp.where(first, lses[0], lses[1])


def attend_backward_kernel(
    mask_ref, slope_ref, qkv_ref, lse_ref, mixed_ref, grad_ref, out_ref, dq_ref, dk_ref, dv_ref, *, blocks
):
    pair = pl.program_id(0)
    mask = mask_ref[0]
    lane = lax.broadcasted_iota(jnp.int32, (BLOCK, PAIR), 1)
    key = lax.broadcasted_iota(jnp.int32, (BLOCK, BLOCK), 0)
    query = lax.broadcasted_iota(jnp.int32, (BLOCK, BLOCK), 1)
    gap = (query - key).astype(jnp.float32)

    def rows(block):
        return pl.ds(pl.multiple_of((block ^ mask) * BLOCK, BLOCK), BLOCK)

    for i in range(blocks):
        q_pair = qkv_ref[rows(i), 0:PAIR]
        up_pair = grad_ref[rows(i), :]
        inner_all = (up_pair.astype(jnp.float32) * mixed_ref[rows(i), :].astype(jnp.float32)).T
        lse_all = lse_ref[rows(i), :].T
        dq = None
        for head in range(2):
            slope = slope_ref[pair * 2 + head]
            mine = (lane >= head * HEAD_DIM) & (lane < (head + 1) * HEAD_DIM)
            zero = jnp.zeros_like(q_pair)
            q = jnp.where(mine, q_pair, zero) * jnp.bfloat16(HEAD_DIM**-0.5)
            up = jnp.where(mine, up_pair, zero)
            inner = jnp.sum(inner_all[head * HEAD_DIM : (head + 1) * HEAD_DIM], axis=0, keepdims=True)
            lse = lse_all[head * HEAD_DIM : head * HEAD_DIM + 1]
            for j in range(i + 1):
                k_pair = qkv_ref[rows(j), PAIR : 2 * PAIR]
                distance = jnp.abs(gap) if i == j else gap + float(BLOCK * (i - j))
                probs = jnp.exp(contract_last(k_pair, q) - slope * distance - lse)
                prob_grad = contract_last(qkv_ref[rows(j), 2 * PAIR : 3 * PAIR], up)
                score_grad = (probs * (prob_grad - inner)).astype(jnp.bfloat16)
                dv = contract(probs.astype(jnp.bfloat16), up)
                dk = contract(score_grad, q)
                part = contract_first(score_grad, jnp.where(mine, k_pair, zero))
                dq = part if dq is None else dq + part
                if i == j and head == 0:
                    dv_ref[j] = dv
                    dk_ref[j] = dk
                else:
                    dv_ref[j] += dv
                    dk_ref[j] += dk
        dq_ref[i] = dq
    for i in range(blocks):
        out_ref[rows(i), 0:PAIR] = (dq_ref[i] * HEAD_DIM**-0.5).astype(out_ref.dtype)
        out_ref[rows(i), PAIR : 2 * PAIR] = dk_ref[i].astype(out_ref.dtype)
        out_ref[rows(i), 2 * PAIR : 3 * PAIR] = dv_ref[i].astype(out_ref.dtype)


def attend_forward(mask, slopes, qkv):
    length, width = qkv.shape
    pairs, blocks = width // (3 * PAIR), length // BLOCK
    scored = pairs * blocks * (blocks + 1) * BLOCK * BLOCK
    return pl.pallas_call(
        partial(attend_forward_kernel, blocks=blocks),
        grid_spec=pltpu.PrefetchScalarGridSpec(
            num_scalar_prefetch=2,
            grid=(pairs,),
            in_specs=[pl.BlockSpec((length, 3 * PAIR), lambda p, *_: (0, p))],
            out_specs=[pl.BlockSpec((length, PAIR), lambda p, *_: (0, p))] * 2,
        ),
        out_shape=[
            jax.ShapeDtypeStruct((length, pairs * PAIR), jnp.bfloat16),
            jax.ShapeDtypeStruct((length, pairs * PAIR), jnp.float32),
        ],
        compiler_params=pltpu.CompilerParams(vmem_limit_bytes=40 * 2**20),
        cost_estimate=pl.CostEstimate(
            flops=scored * 2 * 512, bytes_accessed=length * pairs * PAIR * 12, transcendentals=scored
        ),
        name="attend_forward",
    )(mask, slopes, qkv)


def attend_backward(mask, slopes, qkv, lse, mixed, grad):
    length, width = qkv.shape
    pairs, blocks = width // (3 * PAIR), length // BLOCK
    scored = pairs * blocks * (blocks + 1) * BLOCK * BLOCK
    narrow = pl.BlockSpec((length, PAIR), lambda p, *_: (0, p))
    wide = pl.BlockSpec((length, 3 * PAIR), lambda p, *_: (0, p))
    return pl.pallas_call(
        partial(attend_backward_kernel, blocks=blocks),
        grid_spec=pltpu.PrefetchScalarGridSpec(
            num_scalar_prefetch=2,
            grid=(pairs,),
            in_specs=[wide, narrow, narrow, narrow],
            out_specs=wide,
            scratch_shapes=[pltpu.VMEM((blocks, BLOCK, PAIR), jnp.float32)] * 3,
        ),
        out_shape=jax.ShapeDtypeStruct((length, width), jnp.bfloat16),
        compiler_params=pltpu.CompilerParams(vmem_limit_bytes=40 * 2**20),
        cost_estimate=pl.CostEstimate(
            flops=scored * 2 * 1280, bytes_accessed=length * pairs * PAIR * 20, transcendentals=scored
        ),
        name="attend_backward",
    )(mask, slopes, qkv, lse, mixed, grad)


def swap(values, bit):
    return lax.ppermute(values, "seq", [(i, i ^ bit) for i in range(4)])


def by_index(parts, me):
    odd, upper = (me & 1) == 1, (me & 2) == 2
    a, b, c, d = parts
    a, b, c, d = (
        jnp.where(odd, b, a),
        jnp.where(odd, a, b),
        jnp.where(odd, d, c),
        jnp.where(odd, c, d),
    )
    return [jnp.where(upper, c, a), jnp.where(upper, d, b), jnp.where(upper, a, c), jnp.where(upper, b, d)]


def gather_rows(rows):
    if lax.axis_size("seq") != 4:
        return lax.all_gather(rows, "seq", axis=0, tiled=True)
    half = rows.shape[0] // 2
    first, second = swap(rows, 1), swap(rows, 2)
    return jnp.concatenate([rows, first, second, swap(second[:half], 1), swap(first[half:], 2)], axis=0)


def scatter_rows(slots):
    groups = lax.axis_size("seq")
    if groups != 4:
        return lax.psum_scatter(slots, "seq", scatter_dimension=0, tiled=True).astype(jnp.float32)
    rows = slots.shape[0] // groups
    half = rows // 2
    own, first, second, far = (slots[j * rows : (j + 1) * rows].astype(jnp.float32) for j in range(4))
    low_far = far.astype(slots.dtype)
    top, bottom = swap(low_far[:half], 1), swap(low_far[half:], 2)
    first = jnp.concatenate([first[:half], first[half:] + bottom.astype(jnp.float32)], axis=0)
    second = jnp.concatenate([second[:half] + top.astype(jnp.float32), second[half:]], axis=0)
    from_first, from_second = swap(first.astype(slots.dtype), 1), swap(second.astype(slots.dtype), 2)
    return own + from_first.astype(jnp.float32) + from_second.astype(jnp.float32)


def heads_to_rows(slots, me):
    groups = lax.axis_size("seq")
    rows = slots.shape[0] // groups
    parts = slots.reshape(groups, rows, slots.shape[1])
    if groups != 4:
        swapped = lax.all_to_all(parts, "seq", split_axis=0, concat_axis=0, tiled=True)
        return jnp.swapaxes(swapped, 0, 1).reshape(rows, -1)
    return jnp.concatenate(by_index([parts[0]] + [swap(parts[j], j) for j in (1, 2, 3)], me), axis=1)


def rows_to_heads(rows, me):
    groups = lax.axis_size("seq")
    slab = rows.shape[1] // groups
    parts = [rows[:, j * slab : (j + 1) * slab] for j in range(groups)]
    if groups != 4:
        swapped = lax.all_to_all(jnp.stack(parts), "seq", split_axis=0, concat_axis=0, tiled=True)
        return swapped.reshape(-1, slab)
    parts = by_index(parts, me)
    return jnp.concatenate([parts[0]] + [swap(parts[j], j) for j in (1, 2, 3)], axis=0)


def scatter_slab(partial_sums, me):
    groups, shards = lax.axis_size("seq"), lax.axis_size("fsdp")
    width = partial_sums.shape[1]
    parts = partial_sums.astype(jnp.bfloat16).reshape(groups, shards, -1, width)
    parts = jnp.swapaxes(parts, 0, 1).reshape(-1, width)
    summed = lax.psum_scatter(parts, "fsdp", scatter_dimension=0, tiled=True).reshape(groups, -1, width)
    slabs = lax.all_to_all(summed, "seq", split_axis=0, concat_axis=0, tiled=True)
    return jnp.swapaxes(slabs, 0, 1).astype(jnp.float32)


def local(
    tokens,
    cotangent,
    w_qkv,
    qv_bias,
    w_out,
    out_bias,
    ln1_gain,
    ln1_shift,
    ln2_gain,
    ln2_shift,
    w_up,
    up_bias,
    w_down,
    down_bias,
):
    seq_count, local_len, model_width = tokens.shape
    groups = lax.axis_size("seq")
    me = lax.axis_index("seq")
    heads_here = HEADS // groups
    slab = heads_here * HEAD_DIM
    pairs = slab // PAIR
    hidden_width = w_up.shape[1]
    hidden_slab = hidden_width // groups
    shard = w_qkv.shape[0]
    sequences = range(seq_count)
    mask = jnp.reshape(me if groups == 4 else jnp.zeros_like(me), (1,)).astype(jnp.int32)
    head_index = me * heads_here + jnp.arange(1, heads_here + 1, dtype=jnp.int32)
    slopes = 2.0 ** (-8.0 * head_index.astype(jnp.float32) / HEADS)

    def head_columns(values):
        split = values.reshape(-1, 3, groups, pairs, PAIR)
        mine = lax.dynamic_index_in_dim(split, me, axis=2, keepdims=False)
        return jnp.swapaxes(mine, 1, 2).reshape(values.shape[0], -1)

    qkv_slab = lax.all_gather(head_columns(w_qkv), "fsdp", axis=0, tiled=True)
    full_out = lax.all_gather(w_out, "fsdp", axis=0, tiled=True)
    up_slab = lax.all_gather(
        lax.dynamic_slice_in_dim(w_up, me * hidden_slab, hidden_slab, axis=1), "fsdp", axis=0, tiled=True
    )
    down_slab = lax.all_gather(
        lax.dynamic_slice_in_dim(w_down, me * hidden_slab, hidden_slab, axis=0), "fsdp", axis=1, tiled=True
    )
    qkv_bias = head_columns(
        jnp.concatenate([qv_bias[0], jnp.zeros_like(qv_bias[0]), qv_bias[1]])[None]
    )
    up_bias_slab = lax.dynamic_slice_in_dim(up_bias, me * hidden_slab, hidden_slab, axis=0)

    x = [tokens[b].astype(jnp.float32) for b in sequences]
    dz = [cotangent[b].astype(jnp.float32) for b in sequences]
    first_norm = [jax.vjp(layer_norm, x[b], ln1_gain, ln1_shift) for b in sequences]
    normed = [gather_rows(first_norm[b][0].astype(jnp.bfloat16)) for b in sequences]
    qkv = [(contract(normed[b], qkv_slab) + qkv_bias).astype(jnp.bfloat16) for b in sequences]
    attended = [attend_forward(mask, slopes, qkv[b]) for b in sequences]
    mixed_rows = [heads_to_rows(attended[b][0], me) for b in sequences]
    middle = [x[b] + (contract(mixed_rows[b], full_out) + out_bias) for b in sequences]
    second_norm = [jax.vjp(layer_norm, middle[b], ln2_gain, ln2_shift) for b in sequences]
    second = [gather_rows(second_norm[b][0].astype(jnp.bfloat16)) for b in sequences]
    upstream = [gather_rows(cotangent[b]) for b in sequences]
    hidden = [contract(second[b], up_slab) + up_bias_slab for b in sequences]
    gelu = [jax.vjp(exact_gelu, hidden[b]) for b in sequences]
    active = [gelu[b][0].astype(jnp.bfloat16) for b in sequences]
    hidden_grad = [
        gelu[b][1](contract_last(upstream[b], down_slab))[0].astype(jnp.bfloat16) for b in sequences
    ]
    second_grad = [
        scatter_rows(contract_last(hidden_grad[b], up_slab).astype(jnp.bfloat16)) for b in sequences
    ]
    outcome = [scatter_rows(contract(active[b], down_slab).astype(jnp.bfloat16)) for b in sequences]
    result = jnp.stack([(middle[b] + (outcome[b] + down_bias)).astype(jnp.bfloat16) for b in sequences])

    second_back = [second_norm[b][1](second_grad[b]) for b in sequences]
    middle_grad = [dz[b] + second_back[b][0] for b in sequences]
    branch_grad = [middle_grad[b].astype(jnp.bfloat16) for b in sequences]
    mixed_grad = [
        rows_to_heads(contract_last(branch_grad[b], full_out).astype(jnp.bfloat16), me) for b in sequences
    ]
    qkv_grad = [
        attend_backward(mask, slopes, qkv[b], attended[b][1], attended[b][0], mixed_grad[b]) for b in sequences
    ]
    normed_grad = [
        scatter_rows(contract_last(qkv_grad[b], qkv_slab).astype(jnp.bfloat16)) for b in sequences
    ]
    first_back = [first_norm[b][1](normed_grad[b]) for b in sequences]
    grad_tokens = jnp.stack([(middle_grad[b] + first_back[b][0]).astype(jnp.bfloat16) for b in sequences])

    def outer(left_parts, right_parts):
        return contract_first(jnp.concatenate(left_parts, axis=0), jnp.concatenate(right_parts, axis=0))

    grad_w_up = scatter_slab(outer(second, hidden_grad), me).reshape(-1, hidden_width)
    grad_w_down = scatter_slab(outer(upstream, active), me).reshape(-1, hidden_width).T
    grad_w_out = lax.psum_scatter(
        outer(mixed_rows, branch_grad).astype(jnp.bfloat16), ("seq", "fsdp"), scatter_dimension=0, tiled=True
    ).astype(jnp.float32)
    grad_w_qkv = scatter_slab(outer(normed, qkv_grad), me).reshape(-1, groups, pairs, 3, PAIR)
    grad_w_qkv = jnp.transpose(grad_w_qkv, (0, 3, 1, 2, 4)).reshape(-1, 3 * model_width)

    def column_sum(parts):
        return sum(jnp.sum(part.astype(jnp.float32), axis=0) for part in parts)

    hidden_sum = lax.dynamic_update_slice_in_dim(
        jnp.zeros((hidden_width,), jnp.float32), column_sum(hidden_grad), me * hidden_slab, axis=0
    )
    qkv_sum = jnp.transpose(column_sum(qkv_grad).reshape(pairs, 3, PAIR), (1, 0, 2)).reshape(3, slab)
    qv_sum = lax.dynamic_update_slice_in_dim(
        jnp.zeros((2, model_width), jnp.float32), qkv_sum[0::2], me * slab, axis=1
    )
    early = lax.psum(
        (
            column_sum(branch_grad),
            sum(part[1] for part in second_back),
            sum(part[2] for part in second_back),
            hidden_sum,
            column_sum(dz),
        ),
        ("seq", "fsdp"),
    )
    late = lax.psum(
        (qv_sum, sum(part[1] for part in first_back), sum(part[2] for part in first_back)), ("seq", "fsdp")
    )
    return (
        result,
        grad_tokens,
        grad_w_qkv,
        late[0],
        grad_w_out,
        early[0],
        late[1],
        late[2],
        early[1],
        early[2],
        grad_w_up,
        early[3],
        grad_w_down,
        early[4],
    )


def solution(mesh):
    return jax.shard_map(
        local,
        mesh=mesh,
        in_specs=(
            P("fsdp", "seq", None),
            P("fsdp", "seq", None),
            P("fsdp", None),
            P(),
            P("fsdp", None),
            P(),
            P(),
            P(),
            P(),
            P(),
            P("fsdp", None),
            P(),
            P(None, "fsdp"),
            P(),
        ),
        out_specs=(
            P("fsdp", "seq", None),
            P("fsdp", "seq", None),
            P(("seq", "fsdp"), None),
            P(),
            P(("seq", "fsdp"), None),
            P(),
            P(),
            P(),
            P(),
            P(),
            P(("seq", "fsdp"), None),
            P(),
            P(None, ("seq", "fsdp")),
            P(),
        ),
        check_vma=False,
    )
```

```python
from functools import partial

import jax
import jax.numpy as jnp
from jax import lax
from jax.experimental import pallas as pl
from jax.experimental.pallas import tpu as pltpu
from jax.sharding import PartitionSpec as P

HEADS = 32
HEAD_DIM = 64
BLOCK = 256
PAIR = 2 * HEAD_DIM


def layer_norm(token_rows, gain_vec, shift_vec):
    average = jnp.mean(token_rows, axis=-1, keepdims=True)
    centred = token_rows - average
    spread = jnp.mean(centred * centred, axis=-1, keepdims=True)
    return centred * lax.rsqrt(spread + 1e-05) * gain_vec + shift_vec


def exact_gelu(values):
    return jax.nn.gelu(values, approximate=False)


def contract(left_side, right_side):
    return lax.dot_general(
        left_side, right_side, (((1,), (0,)), ((), ())), preferred_element_type=jnp.float32
    )


def contract_last(left_side, right_side):
    return lax.dot_general(
        left_side, right_side, (((1,), (1,)), ((), ())), preferred_element_type=jnp.float32
    )


def contract_first(left_side, right_side):
    return lax.dot_general(
        left_side, right_side, (((0,), (0,)), ((), ())), preferred_element_type=jnp.float32
    )


def row_pieces(mask, sequence, block, seqs, local):
    per = BLOCK // local
    return [
        pl.ds(pl.multiple_of((((block * per + r) ^ mask) * seqs + sequence) * local, local), local)
        for r in range(per)
    ]


def load_rows(ref, pieces, columns):
    parts = [ref[piece, columns] for piece in pieces]
    return parts[0] if len(parts) == 1 else jnp.concatenate(parts, axis=0)


def store_rows(ref, pieces, columns, values):
    local = values.shape[0] // len(pieces)
    for r, piece in enumerate(pieces):
        ref[piece, columns] = values[r * local : (r + 1) * local]


Q_COLUMNS, K_COLUMNS, V_COLUMNS = (slice(t * PAIR, (t + 1) * PAIR) for t in range(3))


def attend_forward_kernel(mask_ref, slope_ref, qkv_ref, mixed_ref, lse_ref, *, blocks, seqs, local):
    pair, sequence = pl.program_id(0), pl.program_id(1)
    mask = mask_ref[0]
    lane = lax.broadcasted_iota(jnp.int32, (BLOCK, PAIR), 1)
    row = lax.broadcasted_iota(jnp.int32, (BLOCK, BLOCK), 0)
    column = lax.broadcasted_iota(jnp.int32, (BLOCK, BLOCK), 1)
    gap = (row - column).astype(jnp.float32)
    pieces = [row_pieces(mask, sequence, block, seqs, local) for block in range(blocks)]

    for i in range(blocks):
        q_pair = load_rows(qkv_ref, pieces[i], Q_COLUMNS)
        outs, lses = [], []
        for head in range(2):
            slope = slope_ref[pair * 2 + head]
            mine = (lane >= head * HEAD_DIM) & (lane < (head + 1) * HEAD_DIM)
            q = jnp.where(mine, q_pair, jnp.zeros_like(q_pair)) * jnp.bfloat16(HEAD_DIM**-0.5)
            parts, highest = [], None
            for j in range(i + 1):
                scores = contract_last(q, load_rows(qkv_ref, pieces[j], K_COLUMNS))
                distance = jnp.abs(gap) if i == j else gap + float(BLOCK * (i - j))
                scores = scores - slope * distance
                parts.append(scores)
                top = jnp.max(scores, axis=-1, keepdims=True)
                highest = top if highest is None else jnp.maximum(highest, top)
            total, out = None, None
            for j in range(i + 1):
                weights = jnp.exp(parts[j] - highest)
                part = jnp.sum(weights, axis=-1, keepdims=True)
                mixed = contract(weights.astype(jnp.bfloat16), load_rows(qkv_ref, pieces[j], V_COLUMNS))
                total = part if total is None else total + part
                out = mixed if out is None else out + mixed
            outs.append(out / total)
            lses.append(highest + jnp.log(total))
        first = lane < HEAD_DIM
        everything = slice(0, PAIR)
        store_rows(
            mixed_ref, pieces[i], everything, jnp.where(first, outs[0], outs[1]).astype(mixed_ref.dtype)
        )
        store_rows(lse_ref, pieces[i], everything, jnp.where(first, lses[0], lses[1]))


def attend_backward_kernel(
    mask_ref, slope_ref, qkv_ref, lse_ref, mixed_ref, grad_ref, *rest, blocks, seqs, local, start
):
    out_ref, dq_ref, dk_ref, dv_ref = rest[-4:]
    pair, sequence = pl.program_id(0) + start, pl.program_id(1)
    mask = mask_ref[0]
    lane = lax.broadcasted_iota(jnp.int32, (BLOCK, PAIR), 1)
    key = lax.broadcasted_iota(jnp.int32, (BLOCK, BLOCK), 0)
    query = lax.broadcasted_iota(jnp.int32, (BLOCK, BLOCK), 1)
    gap = (query - key).astype(jnp.float32)
    pieces = [row_pieces(mask, sequence, block, seqs, local) for block in range(blocks)]
    everything = slice(0, PAIR)

    for i in range(blocks):
        q_pair = load_rows(qkv_ref, pieces[i], Q_COLUMNS)
        up_pair = load_rows(grad_ref, pieces[i], everything)
        mixed_pair = load_rows(mixed_ref, pieces[i], everything)
        inner_all = (up_pair.astype(jnp.float32) * mixed_pair.astype(jnp.float32)).T
        lse_all = load_rows(lse_ref, pieces[i], everything).T
        dq = None
        for head in range(2):
            slope = slope_ref[pair * 2 + head]
            mine = (lane >= head * HEAD_DIM) & (lane < (head + 1) * HEAD_DIM)
            zero = jnp.zeros_like(q_pair)
            q = jnp.where(mine, q_pair, zero) * jnp.bfloat16(HEAD_DIM**-0.5)
            up = jnp.where(mine, up_pair, zero)
            inner = jnp.sum(inner_all[head * HEAD_DIM : (head + 1) * HEAD_DIM], axis=0, keepdims=True)
            lse = lse_all[head * HEAD_DIM : head * HEAD_DIM + 1]
            for j in range(i + 1):
                k_pair = load_rows(qkv_ref, pieces[j], K_COLUMNS)
                distance = jnp.abs(gap) if i == j else gap + float(BLOCK * (i - j))
                probs = jnp.exp(contract_last(k_pair, q) - slope * distance - lse)
                prob_grad = contract_last(load_rows(qkv_ref, pieces[j], V_COLUMNS), up)
                score_grad = (probs * (prob_grad - inner)).astype(jnp.bfloat16)
                dv = contract(probs.astype(jnp.bfloat16), up)
                dk = contract(score_grad, q)
                part = contract_first(score_grad, jnp.where(mine, k_pair, zero))
                dq = part if dq is None else dq + part
                if i == j and head == 0:
                    dv_ref[j] = dv
                    dk_ref[j] = dk
                else:
                    dv_ref[j] += dv
                    dk_ref[j] += dk
        dq_ref[i] = dq
    for i in range(blocks):
        store_rows(out_ref, pieces[i], Q_COLUMNS, (dq_ref[i] * HEAD_DIM**-0.5).astype(out_ref.dtype))
        store_rows(out_ref, pieces[i], K_COLUMNS, dk_ref[i].astype(out_ref.dtype))
        store_rows(out_ref, pieces[i], V_COLUMNS, dv_ref[i].astype(out_ref.dtype))


def attend_forward(mask, slopes, qkv, seqs, local):
    rows, width = qkv.shape
    pairs, blocks = width // (3 * PAIR), rows // seqs // BLOCK
    scored = pairs * seqs * blocks * (blocks + 1) * BLOCK * BLOCK
    return pl.pallas_call(
        partial(attend_forward_kernel, blocks=blocks, seqs=seqs, local=local),
        grid_spec=pltpu.PrefetchScalarGridSpec(
            num_scalar_prefetch=2,
            grid=(pairs, seqs),
            in_specs=[pl.BlockSpec((rows, 3 * PAIR), lambda p, *_: (0, p))],
            out_specs=[pl.BlockSpec((rows, PAIR), lambda p, *_: (0, p))] * 2,
        ),
        out_shape=[
            jax.ShapeDtypeStruct((rows, pairs * PAIR), jnp.bfloat16),
            jax.ShapeDtypeStruct((rows, pairs * PAIR), jnp.float32),
        ],
        compiler_params=pltpu.CompilerParams(vmem_limit_bytes=40 * 2**20),
        cost_estimate=pl.CostEstimate(
            flops=scored * 2 * 512, bytes_accessed=rows * pairs * PAIR * 12, transcendentals=scored
        ),
        name="attend_forward",
    )(mask, slopes, qkv)


def attend_backward(mask, slopes, qkv, lse, mixed, grad, seqs, local, start, stop, begun=None):
    rows, width = qkv.shape
    blocks = rows // seqs // BLOCK
    scored = (stop - start) * seqs * blocks * (blocks + 1) * BLOCK * BLOCK
    narrow = pl.BlockSpec((rows, PAIR), lambda p, *_: (0, p + start))
    wide = pl.BlockSpec((rows, 3 * PAIR), lambda p, *_: (0, p + start))
    earlier = [] if begun is None else [begun]
    return pl.pallas_call(
        partial(attend_backward_kernel, blocks=blocks, seqs=seqs, local=local, start=start),
        grid_spec=pltpu.PrefetchScalarGridSpec(
            num_scalar_prefetch=2,
            grid=(stop - start, seqs),
            in_specs=[wide, narrow, narrow, narrow] + [pl.BlockSpec(memory_space=pl.ANY)] * len(earlier),
            out_specs=wide,
            scratch_shapes=[pltpu.VMEM((blocks, BLOCK, PAIR), jnp.float32)] * 3,
        ),
        out_shape=jax.ShapeDtypeStruct((rows, width), jnp.bfloat16),
        input_output_aliases={6: 0} if earlier else {},
        compiler_params=pltpu.CompilerParams(vmem_limit_bytes=40 * 2**20),
        cost_estimate=pl.CostEstimate(
            flops=scored * 2 * 1280,
            bytes_accessed=rows * (stop - start) * PAIR * 20,
            transcendentals=scored,
        ),
        name="attend_backward",
    )(mask, slopes, qkv, lse, mixed, grad, *earlier)


def swap(values, bit):
    return lax.ppermute(values, "seq", [(i, i ^ bit) for i in range(4)])


def by_index(parts, me):
    if len(parts) != 4:
        return parts
    odd, upper = (me & 1) == 1, (me & 2) == 2
    a, b, c, d = parts
    a, b, c, d = (
        jnp.where(odd, b, a),
        jnp.where(odd, a, b),
        jnp.where(odd, d, c),
        jnp.where(odd, c, d),
    )
    return [jnp.where(upper, c, a), jnp.where(upper, d, b), jnp.where(upper, a, c), jnp.where(upper, b, d)]


def gather(rows):
    if lax.axis_size("seq") != 4:
        return [lax.all_gather(rows, "seq", axis=0, tiled=True)]
    half = rows.shape[0] // 2
    first, second = swap(rows, 1), swap(rows, 2)
    return [rows, first, second, swap(second[:half], 1), swap(first[half:], 2)]


def near(slots):
    far, first, second, own = slots
    half = far.shape[0] // 2
    top, bottom = swap(far[:half], 1), swap(far[half:], 2)
    wide = jnp.float32
    low_first = (first[half:].astype(wide) + bottom.astype(wide)).astype(first.dtype)
    low_second = (second[:half].astype(wide) + top.astype(wide)).astype(first.dtype)
    first = jnp.concatenate([first[:half], low_first], axis=0)
    second = jnp.concatenate([low_second, second[half:]], axis=0)
    return first, second, own


def close(first, second, own):
    wide = jnp.float32
    return own.astype(wide) + swap(first, 1).astype(wide) + swap(second, 2).astype(wide)


def exchange(slots):
    if lax.axis_size("seq") != 4:
        return list(lax.all_to_all(jnp.stack(slots), "seq", split_axis=0, concat_axis=0, tiled=True))
    return [slots[0]] + [swap(slots[j], j) for j in (1, 2, 3)]


def total(values):
    for axis in ("fsdp", "seq"):
        count, bit = lax.axis_size(axis), 1
        while bit < count:
            other = [(i, i ^ bit) for i in range(count)]
            values = values + lax.ppermute(values, axis, other)
            bit *= 2
    return values


def scatter_slab(partial_sums, me):
    groups, shards = lax.axis_size("seq"), lax.axis_size("fsdp")
    width = partial_sums.shape[1]
    parts = jnp.swapaxes(partial_sums.reshape(groups, shards, -1, width), 0, 1).reshape(-1, width)
    summed = lax.psum_scatter(parts, "fsdp", scatter_dimension=0, tiled=True).reshape(groups, -1, width)
    slabs = exchange(by_index([summed[j] for j in range(groups)], me))
    return jnp.stack(by_index(slabs, me), axis=1).astype(jnp.float32)


def gate(values, *before):
    return lax.optimization_barrier((values, *before))[0]


class Order:
    def __init__(self):
        self.pending = []

    def after(self, *values):
        self.pending += values

    def __call__(self, operation, first, *others):
        if self.pending:
            first = gate(first, *self.pending)
        made = operation(first, *others)
        self.pending = [jax.tree.leaves(made)[0]]
        return made


def local(
    tokens,
    cotangent,
    w_qkv,
    qv_bias,
    w_out,
    out_bias,
    ln1_gain,
    ln1_shift,
    ln2_gain,
    ln2_shift,
    w_up,
    up_bias,
    w_down,
    down_bias,
):
    seq_count, local_len, model_width = tokens.shape
    groups, shards = lax.axis_size("seq"), lax.axis_size("fsdp")
    me = lax.axis_index("seq")
    square = groups == 4
    heads_here = HEADS // groups
    slab = heads_here * HEAD_DIM
    pairs = slab // PAIR
    hidden_width = w_up.shape[1]
    hidden_slab = hidden_width // groups
    rows_here = seq_count * local_len
    low, wide = jnp.bfloat16, jnp.float32
    mask = jnp.reshape(me if square else jnp.zeros_like(me), (1,)).astype(jnp.int32)
    head_index = me * heads_here + jnp.arange(1, heads_here + 1, dtype=jnp.int32)
    slopes = 2.0 ** (-8.0 * head_index.astype(wide) / HEADS)

    def head_columns(values):
        split = values.reshape(-1, 3, groups, pairs, PAIR)
        mine = lax.dynamic_index_in_dim(split, me, axis=2, keepdims=False)
        return jnp.swapaxes(mine, 1, 2).reshape(values.shape[0], -1)

    def own_slab(values, axis):
        width = values.shape[axis] // groups
        return lax.dynamic_slice_in_dim(values, me * width, width, axis=axis)

    qkv_slab = lax.all_gather(head_columns(w_qkv), "fsdp", axis=0, tiled=True)
    out_columns = lax.all_gather(gate(own_slab(w_out, 1), qkv_slab), "fsdp", axis=0, tiled=True)
    up_slab = lax.all_gather(own_slab(w_up, 1), "fsdp", axis=0, tiled=True)
    down_slab = lax.all_gather(own_slab(w_down, 0), "fsdp", axis=1, tiled=True)
    qkv_bias = head_columns(jnp.concatenate([qv_bias[0], jnp.zeros_like(qv_bias[0]), qv_bias[1]])[None])
    up_bias_slab = own_slab(up_bias, 0)

    def whole(parts):
        return parts[0] if len(parts) == 1 else jnp.concatenate(parts, axis=0)

    def by_slots(product, rows, order):
        if not square:
            return order(product, rows)
        cut = [rows[j * rows_here : (j + 1) * rows_here] for j in range(4)]
        return [order(product, cut[j]) for j in (3, 1, 2, 0)]

    def sum_over_seq(slots):
        if not square:
            return lax.psum_scatter(slots, "seq", scatter_dimension=0, tiled=True).astype(wide)
        return close(*slots)

    order = Order()
    x = tokens.reshape(rows_here, model_width).astype(wide)
    dz_low = cotangent.reshape(rows_here, model_width)
    dz = dz_low.astype(wide)
    first_norm, first_back = jax.vjp(layer_norm, x, ln1_gain, ln1_shift)
    normed = whole(gather(first_norm.astype(low)))
    qkv = order(lambda rows: (contract(rows, qkv_slab) + qkv_bias).astype(low), normed)
    out_parts = gather(out_columns) if square else None
    attended, log_totals = order(lambda rows: attend_forward(mask, slopes, rows, seq_count, local_len), qkv)
    mixed_slots = exchange([attended[j * rows_here : (j + 1) * rows_here] for j in range(groups)])
    mixed_rows = jnp.concatenate(by_index(mixed_slots, me), axis=1)
    mixed_slots = jnp.concatenate(mixed_slots, axis=1)
    if square:
        out_parts = by_index(out_parts[:3] + [whole(out_parts[3:])], me)
        full_out = jnp.concatenate(out_parts, axis=1)
    else:
        full_out = lax.all_gather(out_columns, "seq", axis=1, tiled=True)
    middle = x + (order(lambda rows: contract(rows, full_out), mixed_rows) + out_bias)
    second_norm, second_back = jax.vjp(layer_norm, middle, ln2_gain, ln2_shift)
    second = whole(gather(second_norm.astype(low)))
    upstream = whole(gather(gate(dz_low, second)))
    hidden = order(lambda rows: contract(rows, up_slab) + up_bias_slab, second)

    def bend(values):
        made, back = jax.vjp(exact_gelu, values)
        return made.astype(low), back(jnp.ones_like(values))[0]

    active, slope = order(bend, hidden)
    order.after(upstream)
    down_sum = order(lambda left: contract_first(left, active).astype(low), upstream)
    hidden_grad = order(lambda rows: (contract_last(rows, down_slab) * slope).astype(low), upstream)
    second_parts = by_slots(lambda rows: contract_last(rows, up_slab).astype(low), hidden_grad, order)
    if square:
        second_parts = near(second_parts)
        order.after(*second_parts)
    up_sum = order(lambda left: contract_first(left, hidden_grad).astype(low), second)
    outcome = by_slots(lambda rows: contract(rows, down_slab).astype(low), active, order)
    second_grad = sum_over_seq(second_parts)
    middle_part, ln2_gain_grad, ln2_shift_grad = second_back(second_grad)
    middle_grad = dz + middle_part
    branch_grad = middle_grad.astype(low)
    mixed_grad = order(lambda rows: contract_last(rows, full_out).astype(low), branch_grad)
    mixed_grad = whole(
        exchange(by_index([mixed_grad[:, j * slab : (j + 1) * slab] for j in range(groups)], me))
    )
    out_sum = order(lambda left: contract_first(left, branch_grad).astype(low), mixed_slots)
    if square:
        outcome = near([gate(outcome[0], mixed_grad)] + outcome[1:])
    order.after(mixed_grad)
    attention = (mask, slopes, qkv, log_totals, attended)
    begun = order(lambda rows: attend_backward(*attention, rows, seq_count, local_len, 0, pairs // 2), mixed_grad)
    if square:
        order.after(*outcome)
    qkv_grad = order(
        lambda rows: attend_backward(*attention, rows, seq_count, local_len, pairs // 2, pairs, begun), mixed_grad
    )
    normed_parts = by_slots(lambda rows: contract_last(rows, qkv_slab).astype(low), qkv_grad, order)
    outcome = sum_over_seq(outcome)
    if square:
        normed_parts = near(normed_parts)
        order.after(*normed_parts)
    qkv_sum = order(lambda left: contract_first(left, qkv_grad).astype(low), normed)
    normed_grad = sum_over_seq(normed_parts)
    result = (middle + (outcome + down_bias)).astype(low).reshape(tokens.shape)
    input_part, ln1_gain_grad, ln1_shift_grad = first_back(normed_grad)
    grad_tokens = (middle_grad + input_part).astype(low).reshape(tokens.shape)

    grad_w_down = scatter_slab(down_sum, me).reshape(-1, hidden_width).T
    grad_w_up = scatter_slab(up_sum, me).reshape(-1, hidden_width)
    if square:
        out_slots = [out_sum[j * slab : (j + 1) * slab] for j in (3, 1, 2, 0)]
        out_sum = close(*near([gate(out_slots[0], normed_grad)] + out_slots[1:])).astype(low)
    else:
        out_sum = lax.psum_scatter(out_sum, "seq", scatter_dimension=0, tiled=True)
    grad_w_out = lax.psum_scatter(out_sum, "fsdp", scatter_dimension=0, tiled=True).astype(wide)
    grad_w_qkv = scatter_slab(qkv_sum, me).reshape(-1, groups, pairs, 3, PAIR)
    grad_w_qkv = jnp.transpose(grad_w_qkv, (0, 3, 1, 2, 4)).reshape(-1, 3 * model_width)

    def column_sum(values):
        return jnp.sum(values.astype(wide), axis=0)

    hidden_sum = lax.dynamic_update_slice_in_dim(
        jnp.zeros((hidden_width,), wide), column_sum(hidden_grad), me * hidden_slab, axis=0
    )
    head_sum = jnp.transpose(column_sum(qkv_grad).reshape(pairs, 3, PAIR), (1, 0, 2)).reshape(3, slab)
    qv_sum = lax.dynamic_update_slice_in_dim(
        jnp.zeros((2, model_width), wide), head_sum[0::2], me * slab, axis=1
    )
    early = [column_sum(branch_grad), ln2_gain_grad, ln2_shift_grad, hidden_sum, column_sum(dz)]
    early = total(jnp.concatenate(early).reshape(-1, PAIR)).reshape(-1)
    late = [qv_sum.reshape(-1), ln1_gain_grad, ln1_shift_grad]
    late = total(jnp.concatenate(late).reshape(-1, PAIR)).reshape(-1)

    def cut(values, at, count):
        return values[at * model_width : (at + count) * model_width]

    ratio = hidden_width // model_width
    return (
        result,
        grad_tokens,
        grad_w_qkv,
        cut(late, 0, 2).reshape(2, model_width),
        grad_w_out,
        cut(early, 0, 1),
        cut(late, 2, 1),
        cut(late, 3, 1),
        cut(early, 1, 1),
        cut(early, 2, 1),
        grad_w_up,
        cut(early, 3, ratio),
        grad_w_down,
        cut(early, 3 + ratio, 1),
    )


def solution(mesh):
    return jax.shard_map(
        local,
        mesh=mesh,
        in_specs=(
            P("fsdp", "seq", None),
            P("fsdp", "seq", None),
            P("fsdp", None),
            P(),
            P("fsdp", None),
            P(),
            P(),
            P(),
            P(),
            P(),
            P("fsdp", None),
            P(),
            P(None, "fsdp"),
            P(),
        ),
        out_specs=(
            P("fsdp", "seq", None),
            P("fsdp", "seq", None),
            P(("seq", "fsdp"), None),
            P(),
            P(("seq", "fsdp"), None),
            P(),
            P(),
            P(),
            P(),
            P(),
            P(("seq", "fsdp"), None),
            P(),
            P(None, ("seq", "fsdp")),
            P(),
        ),
        check_vma=False,
    )
```

```python
from functools import partial

import jax
import jax.numpy as jnp
from jax import lax
from jax.experimental import pallas as pl
from jax.experimental.pallas import tpu as pltpu
from jax.sharding import PartitionSpec as P

HEADS = 32
HEAD_DIM = 64
BLOCK = 256
PAIR = 2 * HEAD_DIM


def layer_norm(token_rows, gain_vec, shift_vec):
    average = jnp.mean(token_rows, axis=-1, keepdims=True)
    centred = token_rows - average
    spread = jnp.mean(centred * centred, axis=-1, keepdims=True)
    return centred * lax.rsqrt(spread + 1e-05) * gain_vec + shift_vec


def exact_gelu(values):
    return jax.nn.gelu(values, approximate=False)


def contract(left_side, right_side):
    return lax.dot_general(
        left_side, right_side, (((1,), (0,)), ((), ())), preferred_element_type=jnp.float32
    )


def contract_last(left_side, right_side):
    return lax.dot_general(
        left_side, right_side, (((1,), (1,)), ((), ())), preferred_element_type=jnp.float32
    )


def contract_first(left_side, right_side):
    return lax.dot_general(
        left_side, right_side, (((0,), (0,)), ((), ())), preferred_element_type=jnp.float32
    )


def row_pieces(mask, sequence, block, seqs, local):
    per = BLOCK // local
    return [
        pl.ds(pl.multiple_of((((block * per + r) ^ mask) * seqs + sequence) * local, local), local)
        for r in range(per)
    ]


def load_rows(ref, pieces, columns):
    parts = [ref[piece, columns] for piece in pieces]
    return parts[0] if len(parts) == 1 else jnp.concatenate(parts, axis=0)


def store_rows(ref, pieces, columns, values):
    local = values.shape[0] // len(pieces)
    for r, piece in enumerate(pieces):
        ref[piece, columns] = values[r * local : (r + 1) * local]


Q_COLUMNS, K_COLUMNS, V_COLUMNS = (slice(t * PAIR, (t + 1) * PAIR) for t in range(3))


def attend_forward_kernel(mask_ref, slope_ref, qkv_ref, mixed_ref, lse_ref, *, blocks, seqs, local):
    pair, sequence = pl.program_id(0), pl.program_id(1)
    mask = mask_ref[0]
    lane = lax.broadcasted_iota(jnp.int32, (BLOCK, PAIR), 1)
    row = lax.broadcasted_iota(jnp.int32, (BLOCK, BLOCK), 0)
    column = lax.broadcasted_iota(jnp.int32, (BLOCK, BLOCK), 1)
    gap = (row - column).astype(jnp.float32)
    pieces = [row_pieces(mask, sequence, block, seqs, local) for block in range(blocks)]

    for i in range(blocks):
        q_pair = load_rows(qkv_ref, pieces[i], Q_COLUMNS)
        outs, lses = [], []
        for head in range(2):
            slope = slope_ref[pair * 2 + head]
            mine = (lane >= head * HEAD_DIM) & (lane < (head + 1) * HEAD_DIM)
            q = jnp.where(mine, q_pair, jnp.zeros_like(q_pair)) * jnp.bfloat16(HEAD_DIM**-0.5)
            parts, highest = [], None
            for j in range(i + 1):
                scores = contract_last(q, load_rows(qkv_ref, pieces[j], K_COLUMNS))
                distance = jnp.abs(gap) if i == j else gap + float(BLOCK * (i - j))
                scores = scores - slope * distance
                parts.append(scores)
                top = jnp.max(scores, axis=-1, keepdims=True)
                highest = top if highest is None else jnp.maximum(highest, top)
            total, out = None, None
            for j in range(i + 1):
                weights = jnp.exp(parts[j] - highest)
                part = jnp.sum(weights, axis=-1, keepdims=True)
                mixed = contract(weights.astype(jnp.bfloat16), load_rows(qkv_ref, pieces[j], V_COLUMNS))
                total = part if total is None else total + part
                out = mixed if out is None else out + mixed
            outs.append(out / total)
            lses.append(highest + jnp.log(total))
        first = lane < HEAD_DIM
        everything = slice(0, PAIR)
        store_rows(
            mixed_ref, pieces[i], everything, jnp.where(first, outs[0], outs[1]).astype(mixed_ref.dtype)
        )
        store_rows(lse_ref, pieces[i], everything, jnp.where(first, lses[0], lses[1]))


def attend_backward_kernel(
    mask_ref, slope_ref, qkv_ref, lse_ref, mixed_ref, grad_ref, *rest, blocks, seqs, local, start
):
    out_ref, dq_ref, dk_ref, dv_ref = rest[-4:]
    pair, sequence = pl.program_id(0) + start, pl.program_id(1)
    mask = mask_ref[0]
    lane = lax.broadcasted_iota(jnp.int32, (BLOCK, PAIR), 1)
    key = lax.broadcasted_iota(jnp.int32, (BLOCK, BLOCK), 0)
    query = lax.broadcasted_iota(jnp.int32, (BLOCK, BLOCK), 1)
    gap = (query - key).astype(jnp.float32)
    pieces = [row_pieces(mask, sequence, block, seqs, local) for block in range(blocks)]
    everything = slice(0, PAIR)

    for i in range(blocks):
        q_pair = load_rows(qkv_ref, pieces[i], Q_COLUMNS)
        up_pair = load_rows(grad_ref, pieces[i], everything)
        mixed_pair = load_rows(mixed_ref, pieces[i], everything)
        inner_all = (up_pair.astype(jnp.float32) * mixed_pair.astype(jnp.float32)).T
        lse_all = load_rows(lse_ref, pieces[i], everything).T
        dq = None
        for head in range(2):
            slope = slope_ref[pair * 2 + head]
            mine = (lane >= head * HEAD_DIM) & (lane < (head + 1) * HEAD_DIM)
            zero = jnp.zeros_like(q_pair)
            q = jnp.where(mine, q_pair, zero) * jnp.bfloat16(HEAD_DIM**-0.5)
            up = jnp.where(mine, up_pair, zero)
            inner = jnp.sum(inner_all[head * HEAD_DIM : (head + 1) * HEAD_DIM], axis=0, keepdims=True)
            lse = lse_all[head * HEAD_DIM : head * HEAD_DIM + 1]
            for j in range(i + 1):
                k_pair = load_rows(qkv_ref, pieces[j], K_COLUMNS)
                distance = jnp.abs(gap) if i == j else gap + float(BLOCK * (i - j))
                probs = jnp.exp(contract_last(k_pair, q) - slope * distance - lse)
                prob_grad = contract_last(load_rows(qkv_ref, pieces[j], V_COLUMNS), up)
                score_grad = (probs * (prob_grad - inner)).astype(jnp.bfloat16)
                dv = contract(probs.astype(jnp.bfloat16), up)
                dk = contract(score_grad, q)
                part = contract_first(score_grad, jnp.where(mine, k_pair, zero))
                dq = part if dq is None else dq + part
                if i == j and head == 0:
                    dv_ref[j] = dv
                    dk_ref[j] = dk
                else:
                    dv_ref[j] += dv
                    dk_ref[j] += dk
        dq_ref[i] = dq
    for i in range(blocks):
        store_rows(out_ref, pieces[i], Q_COLUMNS, (dq_ref[i] * HEAD_DIM**-0.5).astype(out_ref.dtype))
        store_rows(out_ref, pieces[i], K_COLUMNS, dk_ref[i].astype(out_ref.dtype))
        store_rows(out_ref, pieces[i], V_COLUMNS, dv_ref[i].astype(out_ref.dtype))


def attend_forward(mask, slopes, qkv, seqs, local):
    rows, width = qkv.shape
    pairs, blocks = width // (3 * PAIR), rows // seqs // BLOCK
    scored = pairs * seqs * blocks * (blocks + 1) * BLOCK * BLOCK
    return pl.pallas_call(
        partial(attend_forward_kernel, blocks=blocks, seqs=seqs, local=local),
        grid_spec=pltpu.PrefetchScalarGridSpec(
            num_scalar_prefetch=2,
            grid=(pairs, seqs),
            in_specs=[pl.BlockSpec((rows, 3 * PAIR), lambda p, *_: (0, p))],
            out_specs=[pl.BlockSpec((rows, PAIR), lambda p, *_: (0, p))] * 2,
        ),
        out_shape=[
            jax.ShapeDtypeStruct((rows, pairs * PAIR), jnp.bfloat16),
            jax.ShapeDtypeStruct((rows, pairs * PAIR), jnp.float32),
        ],
        compiler_params=pltpu.CompilerParams(vmem_limit_bytes=40 * 2**20),
        cost_estimate=pl.CostEstimate(
            flops=scored * 2 * 512, bytes_accessed=rows * pairs * PAIR * 12, transcendentals=scored
        ),
        name="attend_forward",
    )(mask, slopes, qkv)


def attend_backward(mask, slopes, qkv, lse, mixed, grad, seqs, local, start, stop, begun=None):
    rows, width = qkv.shape
    blocks = rows // seqs // BLOCK
    scored = (stop - start) * seqs * blocks * (blocks + 1) * BLOCK * BLOCK
    narrow = pl.BlockSpec((rows, PAIR), lambda p, *_: (0, p + start))
    wide = pl.BlockSpec((rows, 3 * PAIR), lambda p, *_: (0, p + start))
    earlier = [] if begun is None else [begun]
    return pl.pallas_call(
        partial(attend_backward_kernel, blocks=blocks, seqs=seqs, local=local, start=start),
        grid_spec=pltpu.PrefetchScalarGridSpec(
            num_scalar_prefetch=2,
            grid=(stop - start, seqs),
            in_specs=[wide, narrow, narrow, narrow] + [pl.BlockSpec(memory_space=pl.ANY)] * len(earlier),
            out_specs=wide,
            scratch_shapes=[pltpu.VMEM((blocks, BLOCK, PAIR), jnp.float32)] * 3,
        ),
        out_shape=jax.ShapeDtypeStruct((rows, width), jnp.bfloat16),
        input_output_aliases={6: 0} if earlier else {},
        compiler_params=pltpu.CompilerParams(vmem_limit_bytes=40 * 2**20),
        cost_estimate=pl.CostEstimate(
            flops=scored * 2 * 1280,
            bytes_accessed=rows * (stop - start) * PAIR * 20,
            transcendentals=scored,
        ),
        name="attend_backward",
    )(mask, slopes, qkv, lse, mixed, grad, *earlier)


def swap(values, bit):
    return lax.ppermute(values, "seq", [(i, i ^ bit) for i in range(4)])


def by_index(parts, me):
    if len(parts) != 4:
        return parts
    odd, upper = (me & 1) == 1, (me & 2) == 2
    a, b, c, d = parts
    a, b, c, d = (
        jnp.where(odd, b, a),
        jnp.where(odd, a, b),
        jnp.where(odd, d, c),
        jnp.where(odd, c, d),
    )
    return [jnp.where(upper, c, a), jnp.where(upper, d, b), jnp.where(upper, a, c), jnp.where(upper, b, d)]


def exchange(slots):
    if lax.axis_size("seq") != 4:
        return list(lax.all_to_all(jnp.stack(slots), "seq", split_axis=0, concat_axis=0, tiled=True))
    return [slots[0]] + [swap(slots[j], j) for j in (1, 2, 3)]


def gate(values, *before):
    return lax.optimization_barrier((values, *before))[0]


class Order:
    def __init__(self):
        self.pending = []

    def after(self, *values):
        self.pending += values

    def __call__(self, operation, *operands):
        if self.pending:
            count = len(operands)
            operands = lax.optimization_barrier((*operands, *self.pending))[:count]
        made = operation(*operands)
        self.pending = [jax.tree.leaves(made)[0]]
        return made

    def gather(self, rows):
        if lax.axis_size("seq") != 4:
            return lax.all_gather(rows, "seq", axis=0, tiled=True), None
        return rows, (swap(rows, 1), swap(rows, 2))

    def pass_on(self, begun):
        rows, came = begun
        if came is None:
            return rows
        half = rows.shape[0] // 2
        top, bottom = self(lambda first, second: (second[:half], first[half:]), *came)
        return [rows, *came, swap(top, 1), swap(bottom, 2)]

    def scatter(self, product, rows, axis=0):
        if lax.axis_size("seq") != 4:
            return lax.psum_scatter(self(product, rows), "seq", scatter_dimension=0, tiled=True), None
        count = rows.shape[axis] // 4
        cut = [lax.slice_in_dim(rows, j * count, (j + 1) * count, axis=axis) for j in range(4)]
        far = self(product, cut[3])
        half = far.shape[0] // 2
        top, bottom = swap(far[:half], 1), swap(far[half:], 2)
        return cut, (self(product, cut[1]), self(product, cut[2]), top, bottom)

    def add_far(self, begun, product):
        cut, parts = begun
        if parts is None:
            return begun
        half = parts[0].shape[0] // 2
        wide = jnp.float32

        def add(first, second, top, bottom):
            first_low = (first[half:].astype(wide) + bottom.astype(wide)).astype(first.dtype)
            second_low = (second[:half].astype(wide) + top.astype(wide)).astype(first.dtype)
            return (
                jnp.concatenate([first[:half], first_low], axis=0),
                jnp.concatenate([second_low, second[half:]], axis=0),
            )

        first, second = self(add, *parts)
        came = swap(first, 1), swap(second, 2)
        return self(product, cut[0]), came


class Total:
    def __init__(self, values):
        self.values = values
        self.steps = [
            (axis, 1 << bit) for axis in ("fsdp", "seq") for bit in range(lax.axis_size(axis).bit_length() - 1)
        ]
        self.send()

    def send(self):
        self.came = None
        if self.steps:
            axis, bit = self.steps.pop(0)
            other = [(i, i ^ bit) for i in range(lax.axis_size(axis))]
            self.came = lax.ppermute(self.values, axis, other)

    def step(self, order=None):
        if self.came is not None:
            add = lambda own, other: own + other
            self.values = (order or (lambda operation, *operands: operation(*operands)))(add, self.values, self.came)
            self.send()

    def done(self):
        while self.came is not None:
            self.step()
        return self.values.reshape(-1)


def summed(own, came):
    wide = jnp.float32
    return own.astype(wide) if came is None else own.astype(wide) + came[0].astype(wide) + came[1].astype(wide)


def whole(parts):
    return jnp.concatenate(parts, axis=0) if isinstance(parts, list) else parts


def local(
    tokens,
    cotangent,
    w_qkv,
    qv_bias,
    w_out,
    out_bias,
    ln1_gain,
    ln1_shift,
    ln2_gain,
    ln2_shift,
    w_up,
    up_bias,
    w_down,
    down_bias,
):
    seq_count, local_len, model_width = tokens.shape
    groups, shards = lax.axis_size("seq"), lax.axis_size("fsdp")
    me = lax.axis_index("seq")
    square = groups == 4
    heads_here = HEADS // groups
    slab = heads_here * HEAD_DIM
    pairs = slab // PAIR
    hidden_width = w_up.shape[1]
    hidden_slab = hidden_width // groups
    rows_here = seq_count * local_len
    low, wide = jnp.bfloat16, jnp.float32
    mask = jnp.reshape(me if square else jnp.zeros_like(me), (1,)).astype(jnp.int32)
    head_index = me * heads_here + jnp.arange(1, heads_here + 1, dtype=jnp.int32)
    slopes = 2.0 ** (-8.0 * head_index.astype(wide) / HEADS)

    def head_columns(values):
        split = values.reshape(-1, 3, groups, pairs, PAIR)
        mine = lax.dynamic_index_in_dim(split, me, axis=2, keepdims=False)
        return jnp.swapaxes(mine, 1, 2).reshape(values.shape[0], -1)

    def own_slab(values, axis):
        width = values.shape[axis] // groups
        return lax.dynamic_slice_in_dim(values, me * width, width, axis=axis)

    order = Order()
    x_low = tokens.reshape(rows_here, model_width)
    x = x_low.astype(wide)
    dz_low = cotangent.reshape(rows_here, model_width)
    dz = dz_low.astype(wide)
    qkv_slab = lax.all_gather(head_columns(w_qkv), "fsdp", axis=0, tiled=True)
    qkv_bias = head_columns(jnp.concatenate([qv_bias[0], jnp.zeros_like(qv_bias[0]), qv_bias[1]])[None])
    up_bias_slab = own_slab(up_bias, 0)

    first_norm, first_back = jax.vjp(layer_norm, x, ln1_gain, ln1_shift)
    normed = order.gather(order(lambda values: values.astype(low), first_norm))
    normed = order.pass_on(normed)
    full_out = lax.all_gather(gate(w_out, *normed[1:3]), "fsdp", axis=0, tiled=True)
    up_slab = lax.all_gather(own_slab(w_up, 1), "fsdp", axis=0, tiled=True)
    down_slab = lax.all_gather(own_slab(w_down, 0), "fsdp", axis=1, tiled=True)
    normed = whole(normed)
    upstream = order.gather(gate(dz_low, normed))
    qkv = order(lambda rows: (contract(rows, qkv_slab) + qkv_bias).astype(low), normed)
    attended, log_totals = order(lambda rows: attend_forward(mask, slopes, rows, seq_count, local_len), qkv)
    mixed_slots = exchange([attended[j * rows_here : (j + 1) * rows_here] for j in range(groups)])
    upstream = order.pass_on(upstream)
    mixed_rows = jnp.concatenate(by_index(mixed_slots, me), axis=1)
    mixed_slots = jnp.concatenate(mixed_slots, axis=1)

    def pair_swap(values):
        return lax.ppermute(values, "fsdp", [(i, i ^ 1) for i in range(shards)])

    parity = lax.axis_index("fsdp") & 1
    out_rows = model_width // (groups * shards)
    halves = mixed_slots.reshape(rows_here, -1, 2, out_rows)
    mine, theirs = (
        lax.dynamic_index_in_dim(halves, index, axis=2, keepdims=False).reshape(rows_here, -1)
        for index in (parity, 1 - parity)
    )
    mixed_half = jnp.concatenate([mine, pair_swap(theirs)], axis=0)
    middle = order(lambda rows: x + (contract(rows, full_out) + out_bias), mixed_rows)
    second_norm, second_back = jax.vjp(layer_norm, middle, ln2_gain, ln2_shift)
    second = order.gather(order(lambda values: values.astype(low), second_norm))
    second = whole(order.pass_on(second))
    hidden = order(lambda rows: contract(rows, up_slab) + up_bias_slab, second)

    def bend(values):
        made, back = jax.vjp(exact_gelu, values)
        return made.astype(low), back(jnp.ones_like(values))[0]

    active, slope = order(bend, hidden)
    upstream = whole(upstream)

    def slab_sum(left, right):
        made = order(lambda rows: contract_first(rows, right).astype(low), left)
        width = made.shape[1]
        made = jnp.swapaxes(made.reshape(groups, shards, -1, width), 0, 1).reshape(-1, width)
        return lax.psum_scatter(made, "fsdp", scatter_dimension=0, tiled=True)

    def slabs_of_rows(values):
        values = values.reshape(groups, -1, values.shape[1])
        slabs = lax.all_to_all(values, "seq", split_axis=0, concat_axis=0, tiled=True)
        return jnp.swapaxes(slabs, 0, 1).astype(wide)

    down_sum = slab_sum(upstream, active)

    hidden_grad = order(lambda rows: (contract_last(rows, down_slab) * slope).astype(low), upstream)

    def to_second(rows):
        return contract_last(rows, up_slab).astype(low)

    second_grad = order.add_far(order.scatter(to_second, hidden_grad), to_second)
    up_sum = slab_sum(second, hidden_grad)

    def to_result(rows):
        return contract(rows, down_slab).astype(low)

    outcome = order.scatter(to_result, active)

    def to_middle(own, came):
        middle_part, gain_grad, shift_grad = second_back(summed(own, came))
        middle_grad = dz + middle_part
        return middle_grad.astype(low), middle_grad, gain_grad, shift_grad

    branch_grad, middle_grad, ln2_gain_grad, ln2_shift_grad = order(
        lambda own, *came: to_middle(own, came or None), second_grad[0], *(second_grad[1] or ())
    )
    def column_sum(values):
        return jnp.sum(values.astype(wide), axis=0)

    hidden_sum = lax.dynamic_update_slice_in_dim(
        jnp.zeros((hidden_width,), wide), column_sum(hidden_grad), me * hidden_slab, axis=0
    )
    early = [column_sum(branch_grad), ln2_gain_grad, ln2_shift_grad, hidden_sum, column_sum(dz)]
    early = jnp.concatenate(early).reshape(-1, PAIR)
    mixed_grad = order(lambda rows: contract_last(rows, full_out).astype(low), branch_grad)
    mixed_grad = exchange(by_index([mixed_grad[:, j * slab : (j + 1) * slab] for j in range(groups)], me))
    branch_pair = jnp.concatenate([branch_grad, pair_swap(branch_grad)], axis=0)

    def to_out(columns):
        return contract_first(columns, branch_pair).astype(low)

    out_begun = order.scatter(to_out, mixed_half, axis=1)
    mixed_grad = jnp.concatenate(mixed_grad, axis=0)
    order.after(down_sum)
    attention = (mask, slopes, qkv, log_totals, attended)
    out_begun = order.add_far(out_begun, to_out)
    begun = order(lambda rows: attend_backward(*attention, rows, seq_count, local_len, 0, pairs // 2), mixed_grad)
    early = Total(gate(early, begun))
    out_sum = order(
        lambda own, *came: summed(own, came or None).astype(low), out_begun[0], *(out_begun[1] or ())
    ).reshape(-1, 1, out_rows, model_width)
    zero = jnp.zeros_like(out_sum)
    out_sum = jnp.concatenate(
        [jnp.where(parity == 0, out_sum, zero), jnp.where(parity == 1, out_sum, zero)], axis=1
    ).reshape(-1, model_width)
    grad_w_out = lax.psum_scatter(out_sum, "fsdp", scatter_dimension=0, tiled=True).astype(wide)
    outcome = order.add_far(outcome, to_result)
    early.step(order)
    qkv_grad = order(
        lambda rows: attend_backward(*attention, rows, seq_count, local_len, pairs // 2, pairs, begun), mixed_grad
    )

    def to_normed(rows):
        return contract_last(rows, qkv_slab).astype(low)

    early.step(order)
    normed_grad = order.scatter(to_normed, qkv_grad)
    early.step(order)
    normed_grad = order.add_far(normed_grad, to_normed)
    early.step(order)
    order.after(up_sum)
    qkv_sum = slab_sum(normed, qkv_grad)
    early.step(order)
    result = order(
        lambda own, *came: (middle + (summed(own, came or None) + down_bias)).astype(low),
        outcome[0],
        *(outcome[1] or ()),
    ).reshape(tokens.shape)

    def to_input(own, came):
        input_part, gain_grad, shift_grad = first_back(summed(own, came))
        return (middle_grad + input_part).astype(low), gain_grad, shift_grad

    grad_tokens, ln1_gain_grad, ln1_shift_grad = order(
        lambda own, *came: to_input(own, came or None), normed_grad[0], *(normed_grad[1] or ())
    )
    grad_tokens = grad_tokens.reshape(tokens.shape)
    grad_w_down = slabs_of_rows(down_sum).reshape(-1, hidden_width).T
    grad_w_up = slabs_of_rows(up_sum).reshape(-1, hidden_width)
    grad_w_qkv = slabs_of_rows(qkv_sum).reshape(-1, groups, pairs, 3, PAIR)
    grad_w_qkv = jnp.transpose(grad_w_qkv, (0, 3, 1, 2, 4)).reshape(-1, 3 * model_width)

    head_sum = jnp.transpose(column_sum(qkv_grad).reshape(pairs, 3, PAIR), (1, 0, 2)).reshape(3, slab)
    qv_sum = lax.dynamic_update_slice_in_dim(
        jnp.zeros((2, model_width), wide), head_sum[0::2], me * slab, axis=1
    )
    late = [qv_sum.reshape(-1), ln1_gain_grad, ln1_shift_grad]
    late = Total(jnp.concatenate(late).reshape(-1, PAIR)).done()
    early = early.done()

    def cut(values, at, count):
        return values[at * model_width : (at + count) * model_width]

    ratio = hidden_width // model_width
    return (
        result,
        grad_tokens,
        grad_w_qkv,
        cut(late, 0, 2).reshape(2, model_width),
        grad_w_out,
        cut(early, 0, 1),
        cut(late, 2, 1),
        cut(late, 3, 1),
        cut(early, 1, 1),
        cut(early, 2, 1),
        grad_w_up,
        cut(early, 3, ratio),
        grad_w_down,
        cut(early, 3 + ratio, 1),
    )


def solution(mesh):
    return jax.shard_map(
        local,
        mesh=mesh,
        in_specs=(
            P("fsdp", "seq", None),
            P("fsdp", "seq", None),
            P("fsdp", None),
            P(),
            P("fsdp", None),
            P(),
            P(),
            P(),
            P(),
            P(),
            P("fsdp", None),
            P(),
            P(None, "fsdp"),
            P(),
        ),
        out_specs=(
            P("fsdp", "seq", None),
            P("fsdp", "seq", None),
            P(("seq", "fsdp"), None),
            P(),
            P(("seq", "fsdp"), None),
            P(),
            P(),
            P(),
            P(),
            P(),
            P(("seq", "fsdp"), None),
            P(),
            P(None, ("seq", "fsdp")),
            P(),
        ),
        check_vma=False,
    )
```

```python
import math
from functools import partial

import jax
import jax.numpy as jnp
from jax import lax
from jax.experimental import pallas as pl
from jax.experimental.pallas import tpu as pltpu
from jax.sharding import PartitionSpec as P

HEADS = 32
HEAD_DIM = 64
BLOCK = 256
PAIR = 2 * HEAD_DIM


def layer_norm(token_rows, gain_vec, shift_vec):
    average = jnp.mean(token_rows, axis=-1, keepdims=True)
    centred = token_rows - average
    spread = jnp.mean(centred * centred, axis=-1, keepdims=True)
    return centred * lax.rsqrt(spread + 1e-05) * gain_vec + shift_vec


def contract(left_side, right_side):
    return lax.dot_general(
        left_side, right_side, (((1,), (0,)), ((), ())), preferred_element_type=jnp.float32
    )


def contract_last(left_side, right_side):
    return lax.dot_general(
        left_side, right_side, (((1,), (1,)), ((), ())), preferred_element_type=jnp.float32
    )


def contract_first(left_side, right_side):
    return lax.dot_general(
        left_side, right_side, (((0,), (0,)), ((), ())), preferred_element_type=jnp.float32
    )


def row_pieces(mask, sequence, block, seqs, local):
    per = BLOCK // local
    return [
        pl.ds(pl.multiple_of((((block * per + r) ^ mask) * seqs + sequence) * local, local), local)
        for r in range(per)
    ]


def load_rows(ref, pieces, columns):
    parts = [ref[piece, columns] for piece in pieces]
    return parts[0] if len(parts) == 1 else jnp.concatenate(parts, axis=0)


def store_rows(ref, pieces, columns, values):
    local = values.shape[0] // len(pieces)
    for r, piece in enumerate(pieces):
        ref[piece, columns] = values[r * local : (r + 1) * local]


Q_COLUMNS, K_COLUMNS, V_COLUMNS = (slice(t * PAIR, (t + 1) * PAIR) for t in range(3))


def attend_forward_kernel(mask_ref, slope_ref, qkv_ref, mixed_ref, lse_ref, *, blocks, seqs, local):
    pair, sequence = pl.program_id(0), pl.program_id(1)
    mask = mask_ref[0]
    lane = lax.broadcasted_iota(jnp.int32, (BLOCK, PAIR), 1)
    row = lax.broadcasted_iota(jnp.int32, (BLOCK, BLOCK), 0)
    column = lax.broadcasted_iota(jnp.int32, (BLOCK, BLOCK), 1)
    gap = (row - column).astype(jnp.float32)
    pieces = [row_pieces(mask, sequence, block, seqs, local) for block in range(blocks)]

    for i in range(blocks):
        q_pair = load_rows(qkv_ref, pieces[i], Q_COLUMNS)
        outs, lses = [], []
        for head in range(2):
            slope = slope_ref[pair * 2 + head]
            mine = (lane >= head * HEAD_DIM) & (lane < (head + 1) * HEAD_DIM)
            q = jnp.where(mine, q_pair, jnp.zeros_like(q_pair)) * jnp.bfloat16(HEAD_DIM**-0.5)
            parts, highest = [], None
            for j in range(i + 1):
                scores = contract_last(q, load_rows(qkv_ref, pieces[j], K_COLUMNS))
                distance = jnp.abs(gap) if i == j else gap + float(BLOCK * (i - j))
                scores = scores - slope * distance
                parts.append(scores)
                top = jnp.max(scores, axis=-1, keepdims=True)
                highest = top if highest is None else jnp.maximum(highest, top)
            total, out = None, None
            for j in range(i + 1):
                weights = jnp.exp(parts[j] - highest)
                part = jnp.sum(weights, axis=-1, keepdims=True)
                mixed = contract(weights.astype(jnp.bfloat16), load_rows(qkv_ref, pieces[j], V_COLUMNS))
                total = part if total is None else total + part
                out = mixed if out is None else out + mixed
            outs.append(out / total)
            lses.append(highest + jnp.log(total))
        first = lane < HEAD_DIM
        everything = slice(0, PAIR)
        store_rows(
            mixed_ref, pieces[i], everything, jnp.where(first, outs[0], outs[1]).astype(mixed_ref.dtype)
        )
        store_rows(lse_ref, pieces[i], everything, jnp.where(first, lses[0], lses[1]))


def attend_backward_kernel(
    mask_ref, slope_ref, qkv_ref, lse_ref, mixed_ref, grad_ref, *rest, blocks, seqs, local, start
):
    out_ref, dq_ref, dk_ref, dv_ref = rest[-4:]
    pair, sequence = pl.program_id(0) + start, pl.program_id(1)
    mask = mask_ref[0]
    lane = lax.broadcasted_iota(jnp.int32, (BLOCK, PAIR), 1)
    key = lax.broadcasted_iota(jnp.int32, (BLOCK, BLOCK), 0)
    query = lax.broadcasted_iota(jnp.int32, (BLOCK, BLOCK), 1)
    gap = (query - key).astype(jnp.float32)
    pieces = [row_pieces(mask, sequence, block, seqs, local) for block in range(blocks)]
    everything = slice(0, PAIR)

    for i in range(blocks):
        q_pair = load_rows(qkv_ref, pieces[i], Q_COLUMNS)
        up_pair = load_rows(grad_ref, pieces[i], everything)
        mixed_pair = load_rows(mixed_ref, pieces[i], everything)
        inner_all = (up_pair.astype(jnp.float32) * mixed_pair.astype(jnp.float32)).T
        lse_all = load_rows(lse_ref, pieces[i], everything).T
        dq = None
        for head in range(2):
            slope = slope_ref[pair * 2 + head]
            mine = (lane >= head * HEAD_DIM) & (lane < (head + 1) * HEAD_DIM)
            zero = jnp.zeros_like(q_pair)
            q = jnp.where(mine, q_pair, zero) * jnp.bfloat16(HEAD_DIM**-0.5)
            up = jnp.where(mine, up_pair, zero)
            inner = jnp.sum(inner_all[head * HEAD_DIM : (head + 1) * HEAD_DIM], axis=0, keepdims=True)
            lse = lse_all[head * HEAD_DIM : head * HEAD_DIM + 1]
            for j in range(i + 1):
                k_pair = load_rows(qkv_ref, pieces[j], K_COLUMNS)
                distance = jnp.abs(gap) if i == j else gap + float(BLOCK * (i - j))
                probs = jnp.exp(contract_last(k_pair, q) - slope * distance - lse)
                prob_grad = contract_last(load_rows(qkv_ref, pieces[j], V_COLUMNS), up)
                score_grad = (probs * (prob_grad - inner)).astype(jnp.bfloat16)
                dv = contract(probs.astype(jnp.bfloat16), up)
                dk = contract(score_grad, q)
                part = contract_first(score_grad, jnp.where(mine, k_pair, zero))
                dq = part if dq is None else dq + part
                if i == j and head == 0:
                    dv_ref[j] = dv
                    dk_ref[j] = dk
                else:
                    dv_ref[j] += dv
                    dk_ref[j] += dk
        dq_ref[i] = dq
    for i in range(blocks):
        store_rows(out_ref, pieces[i], Q_COLUMNS, (dq_ref[i] * HEAD_DIM**-0.5).astype(out_ref.dtype))
        store_rows(out_ref, pieces[i], K_COLUMNS, dk_ref[i].astype(out_ref.dtype))
        store_rows(out_ref, pieces[i], V_COLUMNS, dv_ref[i].astype(out_ref.dtype))


def attend_forward(mask, slopes, qkv, seqs, local):
    rows, width = qkv.shape
    pairs, blocks = width // (3 * PAIR), rows // seqs // BLOCK
    scored = pairs * seqs * blocks * (blocks + 1) * BLOCK * BLOCK
    return pl.pallas_call(
        partial(attend_forward_kernel, blocks=blocks, seqs=seqs, local=local),
        grid_spec=pltpu.PrefetchScalarGridSpec(
            num_scalar_prefetch=2,
            grid=(pairs, seqs),
            in_specs=[pl.BlockSpec((rows, 3 * PAIR), lambda p, *_: (0, p))],
            out_specs=[pl.BlockSpec((rows, PAIR), lambda p, *_: (0, p))] * 2,
        ),
        out_shape=[
            jax.ShapeDtypeStruct((rows, pairs * PAIR), jnp.bfloat16),
            jax.ShapeDtypeStruct((rows, pairs * PAIR), jnp.float32),
        ],
        compiler_params=pltpu.CompilerParams(vmem_limit_bytes=40 * 2**20),
        cost_estimate=pl.CostEstimate(
            flops=scored * 2 * 512, bytes_accessed=rows * pairs * PAIR * 12, transcendentals=scored
        ),
        name="attend_forward",
    )(mask, slopes, qkv)


def attend_backward(mask, slopes, qkv, lse, mixed, grad, seqs, local, start, stop, begun=None):
    rows, width = qkv.shape
    blocks = rows // seqs // BLOCK
    scored = (stop - start) * seqs * blocks * (blocks + 1) * BLOCK * BLOCK
    narrow = pl.BlockSpec((rows, PAIR), lambda p, *_: (0, p + start))
    wide = pl.BlockSpec((rows, 3 * PAIR), lambda p, *_: (0, p + start))
    earlier = [] if begun is None else [begun]
    return pl.pallas_call(
        partial(attend_backward_kernel, blocks=blocks, seqs=seqs, local=local, start=start),
        grid_spec=pltpu.PrefetchScalarGridSpec(
            num_scalar_prefetch=2,
            grid=(stop - start, seqs),
            in_specs=[wide, narrow, narrow, narrow] + [pl.BlockSpec(memory_space=pl.ANY)] * len(earlier),
            out_specs=wide,
            scratch_shapes=[pltpu.VMEM((blocks, BLOCK, PAIR), jnp.float32)] * 3,
        ),
        out_shape=jax.ShapeDtypeStruct((rows, width), jnp.bfloat16),
        input_output_aliases={6: 0} if earlier else {},
        compiler_params=pltpu.CompilerParams(vmem_limit_bytes=40 * 2**20),
        cost_estimate=pl.CostEstimate(
            flops=scored * 2 * 1280,
            bytes_accessed=rows * (stop - start) * PAIR * 20,
            transcendentals=scored,
        ),
        name="attend_backward",
    )(mask, slopes, qkv, lse, mixed, grad, *earlier)


def up_kernel(rows_ref, weight_ref, bias_ref, active_ref, slope_ref, *, chunk):
    rows = rows_ref[...]
    for at in range(0, weight_ref.shape[1], chunk):
        columns = slice(at, at + chunk)
        hidden = contract(rows, weight_ref[:, columns]) + bias_ref[:, columns]
        below = 0.5 + 0.5 * lax.erf(hidden * 2**-0.5)
        active_ref[:, columns] = (hidden * below).astype(active_ref.dtype)
        slope_ref[:, columns] = below + hidden * ((2 * math.pi) ** -0.5 * jnp.exp(-0.5 * hidden * hidden))


def hidden_grad_kernel(rows_ref, weight_ref, slope_ref, grad_ref, sum_ref, *, chunk):
    rows = rows_ref[...]
    starting = pl.program_id(0) == 0
    for at in range(0, weight_ref.shape[0], chunk):
        columns = slice(at, at + chunk)
        grad = contract_last(rows, weight_ref[columns, :]) * slope_ref[:, columns]
        grad = grad.astype(grad_ref.dtype)
        grad_ref[:, columns] = grad
        part = jnp.sum(grad.astype(jnp.float32), axis=0, keepdims=True)
        sum_ref[:, columns] = jnp.where(starting, part, sum_ref[:, columns] + part)


TILE = 512


def up_and_bend(rows, weight, bias):
    count, depth = rows.shape
    width = weight.shape[1]
    tile = pl.BlockSpec((TILE, width), lambda i: (i, 0))
    return pl.pallas_call(
        partial(up_kernel, chunk=TILE),
        grid=(count // TILE,),
        in_specs=[
            pl.BlockSpec((TILE, depth), lambda i: (i, 0)),
            pl.BlockSpec((depth, width), lambda i: (0, 0)),
            pl.BlockSpec((1, width), lambda i: (0, 0)),
        ],
        out_specs=[tile, tile],
        out_shape=[
            jax.ShapeDtypeStruct((count, width), jnp.bfloat16),
            jax.ShapeDtypeStruct((count, width), jnp.float32),
        ],
        compiler_params=pltpu.CompilerParams(vmem_limit_bytes=48 * 2**20),
        cost_estimate=pl.CostEstimate(
            flops=count * depth * width * 4,
            bytes_accessed=2 * count * depth + 2 * depth * width + 6 * count * width,
            transcendentals=2 * count * width,
        ),
        name="up_and_bend",
    )(rows, weight, bias)


def hidden_gradient(rows, weight, slope):
    count, depth = rows.shape
    width = weight.shape[0]
    tile = pl.BlockSpec((TILE, width), lambda i: (i, 0))
    line = pl.BlockSpec((1, width), lambda i: (0, 0))
    return pl.pallas_call(
        partial(hidden_grad_kernel, chunk=TILE),
        grid=(count // TILE,),
        in_specs=[
            pl.BlockSpec((TILE, depth), lambda i: (i, 0)),
            pl.BlockSpec((width, depth), lambda i: (0, 0)),
            tile,
        ],
        out_specs=[tile, line],
        out_shape=[
            jax.ShapeDtypeStruct((count, width), jnp.bfloat16),
            jax.ShapeDtypeStruct((1, width), jnp.float32),
        ],
        compiler_params=pltpu.CompilerParams(vmem_limit_bytes=48 * 2**20),
        cost_estimate=pl.CostEstimate(
            flops=count * depth * width * 3,
            bytes_accessed=2 * count * depth + 2 * depth * width + 6 * count * width,
            transcendentals=0,
        ),
        name="hidden_gradient",
    )(rows, weight, slope)


def swap(values, bit):
    return lax.ppermute(values, "seq", [(i, i ^ bit) for i in range(4)])


def by_index(parts, me):
    if len(parts) != 4:
        return parts
    odd, upper = (me & 1) == 1, (me & 2) == 2
    a, b, c, d = parts
    a, b, c, d = (
        jnp.where(odd, b, a),
        jnp.where(odd, a, b),
        jnp.where(odd, d, c),
        jnp.where(odd, c, d),
    )
    return [jnp.where(upper, c, a), jnp.where(upper, d, b), jnp.where(upper, a, c), jnp.where(upper, b, d)]


def exchange(slots):
    if lax.axis_size("seq") != 4:
        return list(lax.all_to_all(jnp.stack(slots), "seq", split_axis=0, concat_axis=0, tiled=True))
    return [slots[0]] + [swap(slots[j], j) for j in (1, 2, 3)]


def gate(values, *before):
    return lax.optimization_barrier((values, *before))[0]


class Order:
    def __init__(self):
        self.pending = []

    def after(self, *values):
        self.pending += values

    def __call__(self, operation, *operands):
        if self.pending:
            count = len(operands)
            operands = lax.optimization_barrier((*operands, *self.pending))[:count]
        made = operation(*operands)
        self.pending = jax.tree.leaves(made)
        return made

    def gather(self, rows):
        if lax.axis_size("seq") != 4:
            return lax.all_gather(jnp.concatenate(rows, axis=0), "seq", axis=0, tiled=True), None
        top, bottom = rows
        return rows, (swap(bottom, 1), swap(top, 2), swap(top, 1), swap(bottom, 2))

    def pass_on(self, begun):
        rows, came = begun
        if came is None:
            return rows
        first_bottom, second_top, first_top, second_bottom = came
        self.after(*came)
        far = [swap(second_top, 1), swap(first_bottom, 2)]
        return [*rows, first_top, first_bottom, second_top, second_bottom, *far]

    def scatter(self, product, rows, axis=0):
        if lax.axis_size("seq") != 4:
            return lax.psum_scatter(self(product, rows), "seq", scatter_dimension=0, tiled=True), None
        count = rows.shape[axis] // 4

        def far_half(values):
            made = product(lax.slice_in_dim(values, 3 * count, 4 * count, axis=axis))
            half = made.shape[0] // 2
            return made[:half], made[half:]

        top, bottom = self(far_half, rows)
        top, bottom = swap(top, 1), swap(bottom, 2)
        rest = self(lambda values: product(lax.slice_in_dim(values, 0, 3 * count, axis=axis)), rows)
        return rest, (top, bottom)

    def add_far(self, begun):
        rest, parts = begun
        if parts is None:
            return begun
        wide = jnp.float32

        def add(rest, top, bottom):
            half = top.shape[0]
            count = 2 * half
            first, second = rest[count : 2 * count], rest[2 * count :]
            first_low = (first[half:].astype(wide) + bottom.astype(wide)).astype(rest.dtype)
            second_low = (second[:half].astype(wide) + top.astype(wide)).astype(rest.dtype)
            return (
                jnp.concatenate([first[:half], first_low], axis=0),
                jnp.concatenate([second_low, second[half:]], axis=0),
            )

        first, second = self(add, rest, *parts)
        return rest, (swap(first, 1), swap(second, 2))


def summed(rest, came):
    wide = jnp.float32
    if came is None:
        return rest.astype(wide)
    own = rest[: came[0].shape[0]]
    return own.astype(wide) + came[0].astype(wide) + came[1].astype(wide)


def whole(parts):
    return jnp.concatenate(parts, axis=0) if isinstance(parts, list) else parts


class Total:
    def __init__(self, values):
        self.values = values
        self.steps = [
            (axis, 1 << bit) for axis in ("fsdp", "seq") for bit in range(lax.axis_size(axis).bit_length() - 1)
        ]
        self.send()

    def send(self):
        self.came = None
        if self.steps:
            axis, bit = self.steps.pop(0)
            other = [(i, i ^ bit) for i in range(lax.axis_size(axis))]
            self.came = lax.ppermute(self.values, axis, other)

    def step(self, order=None):
        if self.came is not None:
            add = lambda own, other: own + other
            self.values = (order or (lambda operation, *operands: operation(*operands)))(add, self.values, self.came)
            self.send()

    def done(self):
        while self.came is not None:
            self.step()
        return self.values.reshape(-1)


def local(
    tokens,
    cotangent,
    w_qkv,
    qv_bias,
    w_out,
    out_bias,
    ln1_gain,
    ln1_shift,
    ln2_gain,
    ln2_shift,
    w_up,
    up_bias,
    w_down,
    down_bias,
):
    seq_count, local_len, model_width = tokens.shape
    groups, shards = lax.axis_size("seq"), lax.axis_size("fsdp")
    me = lax.axis_index("seq")
    square = groups == 4
    heads_here = HEADS // groups
    slab = heads_here * HEAD_DIM
    pairs = slab // PAIR
    hidden_width = w_up.shape[1]
    hidden_slab = hidden_width // groups
    rows_here = seq_count * local_len
    low, wide = jnp.bfloat16, jnp.float32
    mask = jnp.reshape(me if square else jnp.zeros_like(me), (1,)).astype(jnp.int32)
    head_index = me * heads_here + jnp.arange(1, heads_here + 1, dtype=jnp.int32)
    slopes = 2.0 ** (-8.0 * head_index.astype(wide) / HEADS)

    def head_columns(values):
        split = values.reshape(-1, 3, groups, pairs, PAIR)
        mine = lax.dynamic_index_in_dim(split, me, axis=2, keepdims=False)
        return jnp.swapaxes(mine, 1, 2).reshape(values.shape[0], -1)

    def own_slab(values, axis):
        width = values.shape[axis] // groups
        return lax.dynamic_slice_in_dim(values, me * width, width, axis=axis)

    order = Order()
    x_low = tokens.reshape(rows_here, model_width)
    x = x_low.astype(wide)
    dz_low = cotangent.reshape(rows_here, model_width)
    dz = dz_low.astype(wide)
    qkv_slab = lax.all_gather(head_columns(w_qkv), "fsdp", axis=0, tiled=True)
    qkv_bias = head_columns(jnp.concatenate([qv_bias[0], jnp.zeros_like(qv_bias[0]), qv_bias[1]])[None])
    up_bias_slab = own_slab(up_bias, 0)

    first_norm, first_back = jax.vjp(layer_norm, x, ln1_gain, ln1_shift)
    half = rows_here // 2

    def halves_of(values):
        return values[:half].astype(low), values[half:].astype(low)

    normed = order.gather(order(halves_of, first_norm))
    normed = order.pass_on(normed)
    full_out = lax.all_gather(w_out, "fsdp", axis=0, tiled=True)
    up_slab = lax.all_gather(own_slab(w_up, 1), "fsdp", axis=0, tiled=True)
    down_slab = lax.all_gather(own_slab(w_down, 0), "fsdp", axis=1, tiled=True)
    normed = whole(normed)
    upstream = order.gather(halves_of(gate(dz_low, normed)))
    qkv = order(lambda rows: (contract(rows, qkv_slab) + qkv_bias).astype(low), normed)
    attended, log_totals = order(lambda rows: attend_forward(mask, slopes, rows, seq_count, local_len), qkv)
    mixed_slots = exchange([attended[j * rows_here : (j + 1) * rows_here] for j in range(groups)])
    upstream = order.pass_on(upstream)
    mixed_rows = jnp.concatenate(by_index(mixed_slots, me), axis=1)
    mixed_slots = jnp.concatenate(mixed_slots, axis=1)

    def pair_swap(values):
        return lax.ppermute(values, "fsdp", [(i, i ^ 1) for i in range(shards)])

    parity = lax.axis_index("fsdp") & 1
    out_rows = model_width // (groups * shards)
    halves = mixed_slots.reshape(rows_here, -1, 2, out_rows)
    mine, theirs = (
        lax.dynamic_index_in_dim(halves, index, axis=2, keepdims=False).reshape(rows_here, -1)
        for index in (parity, 1 - parity)
    )
    mixed_half = jnp.concatenate([mine, pair_swap(theirs)], axis=0)
    middle = order(lambda rows: x + (contract(rows, full_out) + out_bias), mixed_rows)
    second_norm, second_back = jax.vjp(layer_norm, middle, ln2_gain, ln2_shift)
    second = order.gather(order(halves_of, second_norm))
    second = whole(order.pass_on(second))
    active, slope = order(lambda rows: up_and_bend(rows, up_slab, up_bias_slab[None]), second)
    upstream = whole(upstream)

    def slab_sum(left, right):
        made = order(lambda rows: contract_first(rows, right).astype(low), left)
        width = made.shape[1]
        made = jnp.swapaxes(made.reshape(groups, shards, -1, width), 0, 1).reshape(-1, width)
        return lax.psum_scatter(made, "fsdp", scatter_dimension=0, tiled=True)

    def slabs_of_rows(values):
        values = values.reshape(groups, -1, values.shape[1])
        slabs = lax.all_to_all(values, "seq", split_axis=0, concat_axis=0, tiled=True)
        return jnp.swapaxes(slabs, 0, 1).astype(wide)

    down_sum = slab_sum(upstream, active)

    hidden_grad, hidden_sum = order(lambda rows: hidden_gradient(rows, down_slab, slope), upstream)

    def to_second(rows):
        return contract_last(rows, up_slab).astype(low)

    second_grad = order.add_far(order.scatter(to_second, hidden_grad))
    up_sum = slab_sum(second, hidden_grad)

    def to_result(rows):
        return contract(rows, down_slab).astype(low)

    outcome = order.scatter(to_result, active)

    def to_middle(own, came):
        middle_part, gain_grad, shift_grad = second_back(summed(own, came))
        middle_grad = dz + middle_part
        return middle_grad.astype(low), middle_grad, gain_grad, shift_grad

    branch_grad, middle_grad, ln2_gain_grad, ln2_shift_grad = order(
        lambda own, *came: to_middle(own, came or None), second_grad[0], *(second_grad[1] or ())
    )
    def column_sum(values):
        return jnp.sum(values.astype(wide), axis=0)

    hidden_sum = lax.dynamic_update_slice_in_dim(
        jnp.zeros((hidden_width,), wide), hidden_sum[0], me * hidden_slab, axis=0
    )
    early = [column_sum(branch_grad), ln2_gain_grad, ln2_shift_grad, hidden_sum, column_sum(dz)]
    early = jnp.concatenate(early).reshape(-1, PAIR)
    mixed_grad = order(lambda rows: contract_last(rows, full_out).astype(low), branch_grad)
    mixed_grad = exchange(by_index([mixed_grad[:, j * slab : (j + 1) * slab] for j in range(groups)], me))
    branch_pair = jnp.concatenate([branch_grad, pair_swap(branch_grad)], axis=0)

    def to_out(columns):
        return contract_first(columns, branch_pair).astype(low)

    out_begun = order.scatter(to_out, mixed_half, axis=1)
    mixed_grad = jnp.concatenate(mixed_grad, axis=0)
    order.after(down_sum)
    attention = (mask, slopes, qkv, log_totals, attended)
    begun = order(lambda rows: attend_backward(*attention, rows, seq_count, local_len, 0, pairs // 2), mixed_grad)
    early = Total(gate(early, begun))
    outcome = order.add_far(outcome)
    out_begun = order.add_far(out_begun)
    early.step(order)
    qkv_grad = order(
        lambda rows: attend_backward(*attention, rows, seq_count, local_len, pairs // 2, pairs, begun), mixed_grad
    )

    out_sum = order(
        lambda own, *came: summed(own, came or None).astype(low), out_begun[0], *(out_begun[1] or ())
    ).reshape(-1, 1, out_rows, model_width)
    zero = jnp.zeros_like(out_sum)
    out_sum = jnp.concatenate(
        [jnp.where(parity == 0, out_sum, zero), jnp.where(parity == 1, out_sum, zero)], axis=1
    ).reshape(-1, model_width)
    grad_w_out = lax.psum_scatter(out_sum, "fsdp", scatter_dimension=0, tiled=True).astype(wide)

    def to_normed(rows):
        return contract_last(rows, qkv_slab).astype(low)

    early.step(order)
    normed_grad = order.scatter(to_normed, qkv_grad)
    early.step(order)
    normed_grad = order.add_far(normed_grad)
    early.step(order)
    order.after(up_sum)
    qkv_sum = slab_sum(normed, qkv_grad)
    early.step(order)
    result = order(
        lambda own, *came: (middle + (summed(own, came or None) + down_bias)).astype(low),
        outcome[0],
        *(outcome[1] or ()),
    ).reshape(tokens.shape)

    def to_input(own, came):
        input_part, gain_grad, shift_grad = first_back(summed(own, came))
        return (middle_grad + input_part).astype(low), gain_grad, shift_grad

    grad_tokens, ln1_gain_grad, ln1_shift_grad = order(
        lambda own, *came: to_input(own, came or None), normed_grad[0], *(normed_grad[1] or ())
    )
    grad_tokens = grad_tokens.reshape(tokens.shape)
    grad_w_down = slabs_of_rows(down_sum).reshape(-1, hidden_width).T
    grad_w_up = slabs_of_rows(up_sum).reshape(-1, hidden_width)
    grad_w_qkv = slabs_of_rows(qkv_sum).reshape(-1, groups, pairs, 3, PAIR)
    grad_w_qkv = jnp.transpose(grad_w_qkv, (0, 3, 1, 2, 4)).reshape(-1, 3 * model_width)

    head_sum = jnp.transpose(column_sum(qkv_grad).reshape(pairs, 3, PAIR), (1, 0, 2)).reshape(3, slab)
    qv_sum = lax.dynamic_update_slice_in_dim(
        jnp.zeros((2, model_width), wide), head_sum[0::2], me * slab, axis=1
    )
    late = [qv_sum.reshape(-1), ln1_gain_grad, ln1_shift_grad]
    late = Total(jnp.concatenate(late).reshape(-1, PAIR)).done()
    early = early.done()

    def cut(values, at, count):
        return values[at * model_width : (at + count) * model_width]

    ratio = hidden_width // model_width
    return (
        result,
        grad_tokens,
        grad_w_qkv,
        cut(late, 0, 2).reshape(2, model_width),
        grad_w_out,
        cut(early, 0, 1),
        cut(late, 2, 1),
        cut(late, 3, 1),
        cut(early, 1, 1),
        cut(early, 2, 1),
        grad_w_up,
        cut(early, 3, ratio),
        grad_w_down,
        cut(early, 3 + ratio, 1),
    )


def solution(mesh):
    return jax.shard_map(
        local,
        mesh=mesh,
        in_specs=(
            P("fsdp", "seq", None),
            P("fsdp", "seq", None),
            P("fsdp", None),
            P(),
            P("fsdp", None),
            P(),
            P(),
            P(),
            P(),
            P(),
            P("fsdp", None),
            P(),
            P(None, "fsdp"),
            P(),
        ),
        out_specs=(
            P("fsdp", "seq", None),
            P("fsdp", "seq", None),
            P(("seq", "fsdp"), None),
            P(),
            P(("seq", "fsdp"), None),
            P(),
            P(),
            P(),
            P(),
            P(),
            P(("seq", "fsdp"), None),
            P(),
            P(None, ("seq", "fsdp")),
            P(),
        ),
        check_vma=False,
    )
```

```python
import math
from functools import partial

import jax
import jax.numpy as jnp
from jax import lax
from jax.experimental import pallas as pl
from jax.experimental.pallas import tpu as pltpu
from jax.sharding import PartitionSpec as P

HEADS = 32
HEAD_DIM = 64
BLOCK = 256
PAIR = 2 * HEAD_DIM


def layer_norm(token_rows, gain_vec, shift_vec):
    average = jnp.mean(token_rows, axis=-1, keepdims=True)
    centred = token_rows - average
    spread = jnp.mean(centred * centred, axis=-1, keepdims=True)
    return centred * lax.rsqrt(spread + 1e-05) * gain_vec + shift_vec


def contract(left_side, right_side):
    return lax.dot_general(
        left_side, right_side, (((1,), (0,)), ((), ())), preferred_element_type=jnp.float32
    )


def contract_last(left_side, right_side):
    return lax.dot_general(
        left_side, right_side, (((1,), (1,)), ((), ())), preferred_element_type=jnp.float32
    )


def contract_first(left_side, right_side):
    return lax.dot_general(
        left_side, right_side, (((0,), (0,)), ((), ())), preferred_element_type=jnp.float32
    )


def row_pieces(mask, sequence, block, seqs, local):
    per = BLOCK // local
    return [
        pl.ds(pl.multiple_of((((block * per + r) ^ mask) * seqs + sequence) * local, local), local)
        for r in range(per)
    ]


def load_rows(ref, pieces, columns):
    parts = [ref[piece, columns] for piece in pieces]
    return parts[0] if len(parts) == 1 else jnp.concatenate(parts, axis=0)


def store_rows(ref, pieces, columns, values):
    local = values.shape[0] // len(pieces)
    for r, piece in enumerate(pieces):
        ref[piece, columns] = values[r * local : (r + 1) * local]


Q_COLUMNS, K_COLUMNS, V_COLUMNS = (slice(t * PAIR, (t + 1) * PAIR) for t in range(3))


def attend_forward_kernel(mask_ref, slope_ref, qkv_ref, mixed_ref, lse_ref, *, blocks, seqs, local):
    pair, sequence = pl.program_id(0), pl.program_id(1)
    mask = mask_ref[0]
    lane = lax.broadcasted_iota(jnp.int32, (BLOCK, PAIR), 1)
    row = lax.broadcasted_iota(jnp.int32, (BLOCK, BLOCK), 0)
    column = lax.broadcasted_iota(jnp.int32, (BLOCK, BLOCK), 1)
    gap = (row - column).astype(jnp.float32)
    pieces = [row_pieces(mask, sequence, block, seqs, local) for block in range(blocks)]

    for i in range(blocks):
        q_pair = load_rows(qkv_ref, pieces[i], Q_COLUMNS)
        outs, lses = [], []
        for head in range(2):
            slope = slope_ref[pair * 2 + head]
            mine = (lane >= head * HEAD_DIM) & (lane < (head + 1) * HEAD_DIM)
            q = jnp.where(mine, q_pair, jnp.zeros_like(q_pair)) * jnp.bfloat16(HEAD_DIM**-0.5)
            parts, highest = [], None
            for j in range(i + 1):
                scores = contract_last(q, load_rows(qkv_ref, pieces[j], K_COLUMNS))
                distance = jnp.abs(gap) if i == j else gap + float(BLOCK * (i - j))
                scores = scores - slope * distance
                parts.append(scores)
                top = jnp.max(scores, axis=-1, keepdims=True)
                highest = top if highest is None else jnp.maximum(highest, top)
            total, out = None, None
            for j in range(i + 1):
                weights = jnp.exp(parts[j] - highest)
                part = jnp.sum(weights, axis=-1, keepdims=True)
                mixed = contract(weights.astype(jnp.bfloat16), load_rows(qkv_ref, pieces[j], V_COLUMNS))
                total = part if total is None else total + part
                out = mixed if out is None else out + mixed
            outs.append(out / total)
            lses.append(highest + jnp.log(total))
        first = lane < HEAD_DIM
        everything = slice(0, PAIR)
        store_rows(
            mixed_ref, pieces[i], everything, jnp.where(first, outs[0], outs[1]).astype(mixed_ref.dtype)
        )
        store_rows(lse_ref, pieces[i], everything, jnp.where(first, lses[0], lses[1]))


def attend_backward_kernel(
    mask_ref, slope_ref, qkv_ref, lse_ref, mixed_ref, grad_ref, *rest, blocks, seqs, local, start
):
    out_ref, dq_ref, dk_ref, dv_ref = rest[-4:]
    pair, sequence = pl.program_id(0) + start, pl.program_id(1)
    mask = mask_ref[0]
    lane = lax.broadcasted_iota(jnp.int32, (BLOCK, PAIR), 1)
    key = lax.broadcasted_iota(jnp.int32, (BLOCK, BLOCK), 0)
    query = lax.broadcasted_iota(jnp.int32, (BLOCK, BLOCK), 1)
    gap = (query - key).astype(jnp.float32)
    pieces = [row_pieces(mask, sequence, block, seqs, local) for block in range(blocks)]
    everything = slice(0, PAIR)

    for i in range(blocks):
        q_pair = load_rows(qkv_ref, pieces[i], Q_COLUMNS)
        up_pair = load_rows(grad_ref, pieces[i], everything)
        mixed_pair = load_rows(mixed_ref, pieces[i], everything)
        inner_all = (up_pair.astype(jnp.float32) * mixed_pair.astype(jnp.float32)).T
        lse_all = load_rows(lse_ref, pieces[i], everything).T
        dq = None
        for head in range(2):
            slope = slope_ref[pair * 2 + head]
            mine = (lane >= head * HEAD_DIM) & (lane < (head + 1) * HEAD_DIM)
            zero = jnp.zeros_like(q_pair)
            q = jnp.where(mine, q_pair, zero) * jnp.bfloat16(HEAD_DIM**-0.5)
            up = jnp.where(mine, up_pair, zero)
            inner = jnp.sum(inner_all[head * HEAD_DIM : (head + 1) * HEAD_DIM], axis=0, keepdims=True)
            lse = lse_all[head * HEAD_DIM : head * HEAD_DIM + 1]
            for j in range(i + 1):
                k_pair = load_rows(qkv_ref, pieces[j], K_COLUMNS)
                distance = jnp.abs(gap) if i == j else gap + float(BLOCK * (i - j))
                probs = jnp.exp(contract_last(k_pair, q) - slope * distance - lse)
                prob_grad = contract_last(load_rows(qkv_ref, pieces[j], V_COLUMNS), up)
                score_grad = (probs * (prob_grad - inner)).astype(jnp.bfloat16)
                dv = contract(probs.astype(jnp.bfloat16), up)
                dk = contract(score_grad, q)
                part = contract_first(score_grad, jnp.where(mine, k_pair, zero))
                dq = part if dq is None else dq + part
                if i == j and head == 0:
                    dv_ref[j] = dv
                    dk_ref[j] = dk
                else:
                    dv_ref[j] += dv
                    dk_ref[j] += dk
        dq_ref[i] = dq
    for i in range(blocks):
        store_rows(out_ref, pieces[i], Q_COLUMNS, (dq_ref[i] * HEAD_DIM**-0.5).astype(out_ref.dtype))
        store_rows(out_ref, pieces[i], K_COLUMNS, dk_ref[i].astype(out_ref.dtype))
        store_rows(out_ref, pieces[i], V_COLUMNS, dv_ref[i].astype(out_ref.dtype))


def attend_forward(mask, slopes, qkv, seqs, local):
    rows, width = qkv.shape
    pairs, blocks = width // (3 * PAIR), rows // seqs // BLOCK
    scored = pairs * seqs * blocks * (blocks + 1) * BLOCK * BLOCK
    return pl.pallas_call(
        partial(attend_forward_kernel, blocks=blocks, seqs=seqs, local=local),
        grid_spec=pltpu.PrefetchScalarGridSpec(
            num_scalar_prefetch=2,
            grid=(pairs, seqs),
            in_specs=[pl.BlockSpec((rows, 3 * PAIR), lambda p, *_: (0, p))],
            out_specs=[pl.BlockSpec((rows, PAIR), lambda p, *_: (0, p))] * 2,
        ),
        out_shape=[
            jax.ShapeDtypeStruct((rows, pairs * PAIR), jnp.bfloat16),
            jax.ShapeDtypeStruct((rows, pairs * PAIR), jnp.float32),
        ],
        compiler_params=pltpu.CompilerParams(vmem_limit_bytes=40 * 2**20),
        cost_estimate=pl.CostEstimate(
            flops=scored * 2 * 512, bytes_accessed=rows * pairs * PAIR * 12, transcendentals=scored
        ),
        name="attend_forward",
    )(mask, slopes, qkv)


def attend_backward(mask, slopes, qkv, lse, mixed, grad, seqs, local, start, stop, begun=None):
    rows, width = qkv.shape
    blocks = rows // seqs // BLOCK
    scored = (stop - start) * seqs * blocks * (blocks + 1) * BLOCK * BLOCK
    narrow = pl.BlockSpec((rows, PAIR), lambda p, *_: (0, p + start))
    wide = pl.BlockSpec((rows, 3 * PAIR), lambda p, *_: (0, p + start))
    earlier = [] if begun is None else [begun]
    return pl.pallas_call(
        partial(attend_backward_kernel, blocks=blocks, seqs=seqs, local=local, start=start),
        grid_spec=pltpu.PrefetchScalarGridSpec(
            num_scalar_prefetch=2,
            grid=(stop - start, seqs),
            in_specs=[wide, narrow, narrow, narrow] + [pl.BlockSpec(memory_space=pl.ANY)] * len(earlier),
            out_specs=wide,
            scratch_shapes=[pltpu.VMEM((blocks, BLOCK, PAIR), jnp.float32)] * 3,
        ),
        out_shape=jax.ShapeDtypeStruct((rows, width), jnp.bfloat16),
        input_output_aliases={6: 0} if earlier else {},
        compiler_params=pltpu.CompilerParams(vmem_limit_bytes=40 * 2**20),
        cost_estimate=pl.CostEstimate(
            flops=scored * 2 * 1280,
            bytes_accessed=rows * (stop - start) * PAIR * 20,
            transcendentals=scored,
        ),
        name="attend_backward",
    )(mask, slopes, qkv, lse, mixed, grad, *earlier)


def up_kernel(rows_ref, weight_ref, bias_ref, active_ref, slope_ref, *, chunk):
    rows = rows_ref[...]
    for at in range(0, weight_ref.shape[1], chunk):
        columns = slice(at, at + chunk)
        hidden = contract(rows, weight_ref[:, columns]) + bias_ref[:, columns]
        below = 0.5 + 0.5 * lax.erf(hidden * 2**-0.5)
        active_ref[:, columns] = (hidden * below).astype(active_ref.dtype)
        slope_ref[:, columns] = below + hidden * ((2 * math.pi) ** -0.5 * jnp.exp(-0.5 * hidden * hidden))


def hidden_grad_kernel(rows_ref, weight_ref, slope_ref, grad_ref, sum_ref, *, chunk):
    rows = rows_ref[...]
    starting = pl.program_id(0) == 0
    for at in range(0, weight_ref.shape[0], chunk):
        columns = slice(at, at + chunk)
        grad = contract_last(rows, weight_ref[columns, :]) * slope_ref[:, columns]
        grad = grad.astype(grad_ref.dtype)
        grad_ref[:, columns] = grad
        part = jnp.sum(grad.astype(jnp.float32), axis=0, keepdims=True)
        sum_ref[:, columns] = jnp.where(starting, part, sum_ref[:, columns] + part)


TILE = 512


def up_and_bend(rows, weight, bias):
    count, depth = rows.shape
    width = weight.shape[1]
    tile = pl.BlockSpec((TILE, width), lambda i: (i, 0))
    return pl.pallas_call(
        partial(up_kernel, chunk=TILE),
        grid=(count // TILE,),
        in_specs=[
            pl.BlockSpec((TILE, depth), lambda i: (i, 0)),
            pl.BlockSpec((depth, width), lambda i: (0, 0)),
            pl.BlockSpec((1, width), lambda i: (0, 0)),
        ],
        out_specs=[tile, tile],
        out_shape=[
            jax.ShapeDtypeStruct((count, width), jnp.bfloat16),
            jax.ShapeDtypeStruct((count, width), jnp.float32),
        ],
        compiler_params=pltpu.CompilerParams(vmem_limit_bytes=48 * 2**20),
        cost_estimate=pl.CostEstimate(
            flops=count * depth * width * 4,
            bytes_accessed=2 * count * depth + 2 * depth * width + 6 * count * width,
            transcendentals=2 * count * width,
        ),
        name="up_and_bend",
    )(rows, weight, bias)


def hidden_gradient(rows, weight, slope):
    count, depth = rows.shape
    width = weight.shape[0]
    tile = pl.BlockSpec((TILE, width), lambda i: (i, 0))
    line = pl.BlockSpec((1, width), lambda i: (0, 0))
    return pl.pallas_call(
        partial(hidden_grad_kernel, chunk=TILE),
        grid=(count // TILE,),
        in_specs=[
            pl.BlockSpec((TILE, depth), lambda i: (i, 0)),
            pl.BlockSpec((width, depth), lambda i: (0, 0)),
            tile,
        ],
        out_specs=[tile, line],
        out_shape=[
            jax.ShapeDtypeStruct((count, width), jnp.bfloat16),
            jax.ShapeDtypeStruct((1, width), jnp.float32),
        ],
        compiler_params=pltpu.CompilerParams(vmem_limit_bytes=48 * 2**20),
        cost_estimate=pl.CostEstimate(
            flops=count * depth * width * 3,
            bytes_accessed=2 * count * depth + 2 * depth * width + 6 * count * width,
            transcendentals=0,
        ),
        name="hidden_gradient",
    )(rows, weight, slope)


def swap(values, bit):
    return lax.ppermute(values, "seq", [(i, i ^ bit) for i in range(4)])


def by_index(parts, me):
    if len(parts) != 4:
        return parts
    odd, upper = (me & 1) == 1, (me & 2) == 2
    a, b, c, d = parts
    a, b, c, d = (
        jnp.where(odd, b, a),
        jnp.where(odd, a, b),
        jnp.where(odd, d, c),
        jnp.where(odd, c, d),
    )
    return [jnp.where(upper, c, a), jnp.where(upper, d, b), jnp.where(upper, a, c), jnp.where(upper, b, d)]


def exchange(slots):
    if lax.axis_size("seq") != 4:
        return list(lax.all_to_all(jnp.stack(slots), "seq", split_axis=0, concat_axis=0, tiled=True))
    return [slots[0]] + [swap(slots[j], j) for j in (1, 2, 3)]


def gate(values, *before):
    return lax.optimization_barrier((values, *before))[0]


class Order:
    def __init__(self):
        self.pending = []

    def after(self, *values):
        self.pending += values

    def __call__(self, operation, *operands):
        if self.pending:
            count = len(operands)
            operands = lax.optimization_barrier((*operands, *self.pending))[:count]
        made = operation(*operands)
        self.pending = jax.tree.leaves(made)
        return made

    def gather(self, rows):
        if lax.axis_size("seq") != 4:
            return lax.all_gather(jnp.concatenate(rows, axis=0), "seq", axis=0, tiled=True), None
        top, bottom = rows
        return rows, (swap(bottom, 1), swap(top, 2), swap(top, 1), swap(bottom, 2))

    def pass_on(self, begun, *before):
        rows, came = begun
        if came is None:
            return rows
        first_bottom, second_top, first_top, second_bottom = came
        self.after(*came)
        if before:
            second_top, first_bottom = gate((second_top, first_bottom), *before)
        far = [swap(second_top, 1), swap(first_bottom, 2)]
        return [*rows, first_top, first_bottom, second_top, second_bottom, *far]

    def send_far(self, product, rows, axis=0):
        if lax.axis_size("seq") != 4:
            return product, rows, axis, None
        count = rows.shape[axis] // 4

        def far_half(values):
            made = product(lax.slice_in_dim(values, 3 * count, 4 * count, axis=axis))
            half = made.shape[0] // 2
            return made[:half], made[half:]

        top, bottom = self(far_half, rows)
        return product, rows, axis, (swap(top, 1), swap(bottom, 2))

    def make_rest(self, begun):
        product, rows, axis, parts = begun
        if parts is None:
            return lax.psum_scatter(self(product, rows), "seq", scatter_dimension=0, tiled=True), None
        count = rows.shape[axis] // 4
        return self(lambda values: product(lax.slice_in_dim(values, 0, 3 * count, axis=axis)), rows), parts

    def add_far(self, begun):
        rest, parts = begun
        if parts is None:
            return begun
        wide = jnp.float32

        def add(rest, top, bottom):
            half = top.shape[0]
            count = 2 * half
            first, second = rest[count : 2 * count], rest[2 * count :]
            first_low = (first[half:].astype(wide) + bottom.astype(wide)).astype(rest.dtype)
            second_low = (second[:half].astype(wide) + top.astype(wide)).astype(rest.dtype)
            return (
                jnp.concatenate([first[:half], first_low], axis=0),
                jnp.concatenate([second_low, second[half:]], axis=0),
            )

        first, second = self(add, rest, *parts)
        return rest, (swap(first, 1), swap(second, 2))


def summed(rest, came):
    wide = jnp.float32
    if came is None:
        return rest.astype(wide)
    own = rest[: came[0].shape[0]]
    return own.astype(wide) + came[0].astype(wide) + came[1].astype(wide)


def whole(parts):
    return jnp.concatenate(parts, axis=0) if isinstance(parts, list) else parts


def total(values):
    for axis in ("fsdp", "seq"):
        count, bit = lax.axis_size(axis), 1
        while bit < count:
            values = values + lax.ppermute(values, axis, [(i, i ^ bit) for i in range(count)])
            bit *= 2
    return values


def local(
    tokens,
    cotangent,
    w_qkv,
    qv_bias,
    w_out,
    out_bias,
    ln1_gain,
    ln1_shift,
    ln2_gain,
    ln2_shift,
    w_up,
    up_bias,
    w_down,
    down_bias,
):
    seq_count, local_len, model_width = tokens.shape
    groups, shards = lax.axis_size("seq"), lax.axis_size("fsdp")
    me = lax.axis_index("seq")
    square = groups == 4
    heads_here = HEADS // groups
    slab = heads_here * HEAD_DIM
    pairs = slab // PAIR
    hidden_width = w_up.shape[1]
    hidden_slab = hidden_width // groups
    rows_here = seq_count * local_len
    low, wide = jnp.bfloat16, jnp.float32
    mask = jnp.reshape(me if square else jnp.zeros_like(me), (1,)).astype(jnp.int32)
    head_index = me * heads_here + jnp.arange(1, heads_here + 1, dtype=jnp.int32)
    slopes = 2.0 ** (-8.0 * head_index.astype(wide) / HEADS)

    def head_columns(values):
        split = values.reshape(-1, 3, groups, pairs, PAIR)
        mine = lax.dynamic_index_in_dim(split, me, axis=2, keepdims=False)
        return jnp.swapaxes(mine, 1, 2).reshape(values.shape[0], -1)

    def own_slab(values, axis):
        width = values.shape[axis] // groups
        return lax.dynamic_slice_in_dim(values, me * width, width, axis=axis)

    order = Order()
    x_low = tokens.reshape(rows_here, model_width)
    x = x_low.astype(wide)
    dz_low = cotangent.reshape(rows_here, model_width)
    dz = dz_low.astype(wide)
    qkv_slab = lax.all_gather(head_columns(w_qkv), "fsdp", axis=0, tiled=True)
    qkv_bias = head_columns(jnp.concatenate([qv_bias[0], jnp.zeros_like(qv_bias[0]), qv_bias[1]])[None])
    up_bias_slab = own_slab(up_bias, 0)

    first_norm, first_back = jax.vjp(layer_norm, x, ln1_gain, ln1_shift)
    half = rows_here // 2

    def halves_of(values):
        return values[:half].astype(low), values[half:].astype(low)

    normed = order.gather(order(halves_of, first_norm))
    normed = order.pass_on(normed)
    full_out = lax.all_gather(w_out, "fsdp", axis=0, tiled=True)
    up_slab = lax.all_gather(own_slab(w_up, 1), "fsdp", axis=0, tiled=True)
    down_slab = lax.all_gather(own_slab(w_down, 0), "fsdp", axis=1, tiled=True)
    normed = whole(normed)
    upstream = order.gather(halves_of(gate(dz_low, normed)))
    qkv = order(lambda rows: (contract(rows, qkv_slab) + qkv_bias).astype(low), normed)
    attended, log_totals = order(lambda rows: attend_forward(mask, slopes, rows, seq_count, local_len), qkv)
    if square:
        attended = gate(attended, *upstream[1])
    mixed_slots = exchange([attended[j * rows_here : (j + 1) * rows_here] for j in range(groups)])
    mixed_rows = jnp.concatenate(by_index(mixed_slots, me), axis=1)
    mixed_slots = jnp.concatenate(mixed_slots, axis=1)

    def pair_swap(values):
        return lax.ppermute(values, "fsdp", [(i, i ^ 1) for i in range(shards)])

    parity = lax.axis_index("fsdp") & 1
    out_rows = model_width // (groups * shards)

    def pair_halves(values):
        halves = values.reshape(rows_here, -1, 2, out_rows)
        return tuple(
            lax.dynamic_index_in_dim(halves, index, axis=2, keepdims=False).reshape(rows_here, -1)
            for index in (parity, 1 - parity)
        )

    middle = order(lambda rows: x + (contract(rows, full_out) + out_bias), mixed_rows)
    second_norm, second_back = jax.vjp(layer_norm, middle, ln2_gain, ln2_shift)
    second = order.gather(order(halves_of, second_norm))
    mine, theirs = order(pair_halves, mixed_slots)
    mixed_half = jnp.concatenate([mine, pair_swap(theirs)], axis=0)
    second = whole(order.pass_on(second))
    upstream = order.pass_on(upstream, second)
    active, slope = order(lambda rows: up_and_bend(rows, up_slab, up_bias_slab[None]), second)
    upstream = whole(upstream)

    def slab_sum(left, right):
        made = order(lambda rows: contract_first(rows, right).astype(low), left)
        width = made.shape[1]
        made = jnp.swapaxes(made.reshape(groups, shards, -1, width), 0, 1).reshape(-1, width)
        return lax.psum_scatter(made, "fsdp", scatter_dimension=0, tiled=True)

    def slabs_of_rows(values, *before):
        values = gate(values, *before) if before else values
        values = values.reshape(groups, -1, values.shape[1])
        slabs = lax.all_to_all(values, "seq", split_axis=0, concat_axis=0, tiled=True)
        return jnp.swapaxes(slabs, 0, 1).astype(wide)

    down_sum = slab_sum(upstream, active)

    hidden_grad, hidden_sum = order(lambda rows: hidden_gradient(rows, down_slab, slope), upstream)

    def to_second(rows):
        return contract_last(rows, up_slab).astype(low)

    second_grad = order.add_far(order.make_rest(order.send_far(to_second, hidden_grad)))
    up_sum = slab_sum(second, hidden_grad)

    def to_result(rows):
        return contract(rows, down_slab).astype(low)

    outcome = order.send_far(to_result, active)

    def to_middle(own, came):
        middle_part, gain_grad, shift_grad = second_back(summed(own, came))
        middle_grad = dz + middle_part
        return middle_grad.astype(low), middle_grad, gain_grad, shift_grad

    branch_grad, middle_grad, ln2_gain_grad, ln2_shift_grad = order(
        lambda own, *came: to_middle(own, came or None), second_grad[0], *(second_grad[1] or ())
    )
    def column_sum(values):
        return jnp.sum(values.astype(wide), axis=0)

    hidden_sum = lax.dynamic_update_slice_in_dim(
        jnp.zeros((hidden_width,), wide), hidden_sum[0], me * hidden_slab, axis=0
    )
    early = [column_sum(branch_grad), ln2_gain_grad, ln2_shift_grad, hidden_sum, column_sum(dz)]
    mixed_grad = order(lambda rows: contract_last(rows, full_out).astype(low), branch_grad)
    mixed_grad = exchange(by_index([mixed_grad[:, j * slab : (j + 1) * slab] for j in range(groups)], me))
    outcome = order.add_far(order.make_rest(outcome))
    mixed_grad = jnp.concatenate(mixed_grad, axis=0)
    order.after(down_sum)
    attention = (mask, slopes, qkv, log_totals, attended)
    begun = order(lambda rows: attend_backward(*attention, rows, seq_count, local_len, 0, pairs // 2), mixed_grad)
    branch_pair = jnp.concatenate([branch_grad, pair_swap(gate(branch_grad, mixed_grad))], axis=0)

    def to_out(columns):
        return contract_first(columns, branch_pair).astype(low)

    out_begun = order.make_rest(order.send_far(to_out, mixed_half, axis=1))
    qkv_grad = order(
        lambda rows: attend_backward(*attention, rows, seq_count, local_len, pairs // 2, pairs, begun), mixed_grad
    )
    if square:
        order.after(*outcome[1])
    out_begun = order.add_far(out_begun)
    order.after(up_sum)
    qkv_sum = slab_sum(normed, qkv_grad)

    def to_normed(rows):
        return contract_last(rows, qkv_slab).astype(low)

    normed_grad = order.send_far(to_normed, qkv_grad)
    normed_grad = order.make_rest(normed_grad)
    normed_grad = order.add_far(normed_grad)
    out_sum = order(
        lambda own, *came: summed(own, came or None).astype(low), out_begun[0], *(out_begun[1] or ())
    ).reshape(-1, 1, out_rows, model_width)
    zero = jnp.zeros_like(out_sum)
    out_sum = jnp.concatenate(
        [jnp.where(parity == 0, out_sum, zero), jnp.where(parity == 1, out_sum, zero)], axis=1
    ).reshape(-1, model_width)

    grad_w_out = lax.psum_scatter(out_sum, "fsdp", scatter_dimension=0, tiled=True).astype(wide)
    result = order(
        lambda own, *came: (middle + (summed(own, came or None) + down_bias)).astype(low),
        outcome[0],
        *(outcome[1] or ()),
    ).reshape(tokens.shape)

    def to_input(own, came):
        input_part, gain_grad, shift_grad = first_back(summed(own, came))
        return (middle_grad + input_part).astype(low), gain_grad, shift_grad

    grad_tokens, ln1_gain_grad, ln1_shift_grad = order(
        lambda own, *came: to_input(own, came or None), normed_grad[0], *(normed_grad[1] or ())
    )
    grad_tokens = grad_tokens.reshape(tokens.shape)
    grad_w_down = slabs_of_rows(down_sum, grad_tokens).reshape(-1, hidden_width).T
    grad_w_up = slabs_of_rows(up_sum, grad_tokens).reshape(-1, hidden_width)
    grad_w_qkv = slabs_of_rows(qkv_sum).reshape(-1, groups, pairs, 3, PAIR)
    grad_w_qkv = jnp.transpose(grad_w_qkv, (0, 3, 1, 2, 4)).reshape(-1, 3 * model_width)

    head_sum = jnp.transpose(column_sum(qkv_grad).reshape(pairs, 3, PAIR), (1, 0, 2)).reshape(3, slab)
    qv_sum = lax.dynamic_update_slice_in_dim(
        jnp.zeros((2, model_width), wide), head_sum[0::2], me * slab, axis=1
    )
    late = [qv_sum.reshape(-1), ln1_gain_grad, ln1_shift_grad]
    sums = total(jnp.concatenate(early + late).reshape(-1, PAIR)).reshape(-1)

    def cut(at, count):
        return sums[at * model_width : (at + count) * model_width]

    ratio = hidden_width // model_width
    return (
        result,
        grad_tokens,
        grad_w_qkv,
        cut(4 + ratio, 2).reshape(2, model_width),
        grad_w_out,
        cut(0, 1),
        cut(6 + ratio, 1),
        cut(7 + ratio, 1),
        cut(1, 1),
        cut(2, 1),
        grad_w_up,
        cut(3, ratio),
        grad_w_down,
        cut(3 + ratio, 1),
    )


def solution(mesh):
    return jax.shard_map(
        local,
        mesh=mesh,
        in_specs=(
            P("fsdp", "seq", None),
            P("fsdp", "seq", None),
            P("fsdp", None),
            P(),
            P("fsdp", None),
            P(),
            P(),
            P(),
            P(),
            P(),
            P("fsdp", None),
            P(),
            P(None, "fsdp"),
            P(),
        ),
        out_specs=(
            P("fsdp", "seq", None),
            P("fsdp", "seq", None),
            P(("seq", "fsdp"), None),
            P(),
            P(("seq", "fsdp"), None),
            P(),
            P(),
            P(),
            P(),
            P(),
            P(("seq", "fsdp"), None),
            P(),
            P(None, ("seq", "fsdp")),
            P(),
        ),
        check_vma=False,
    )
```

```python
import math
from functools import partial

import jax
import jax.numpy as jnp
from jax import lax
from jax.experimental import pallas as pl
from jax.experimental.pallas import tpu as pltpu
from jax.sharding import PartitionSpec as P

HEADS = 32
HEAD_DIM = 64
BLOCK = 256
PAIR = 2 * HEAD_DIM


def layer_norm(token_rows, gain_vec, shift_vec):
    average = jnp.mean(token_rows, axis=-1, keepdims=True)
    centred = token_rows - average
    spread = jnp.mean(centred * centred, axis=-1, keepdims=True)
    return centred * lax.rsqrt(spread + 1e-05) * gain_vec + shift_vec


def contract(left_side, right_side):
    return lax.dot_general(
        left_side, right_side, (((1,), (0,)), ((), ())), preferred_element_type=jnp.float32
    )


def contract_last(left_side, right_side):
    return lax.dot_general(
        left_side, right_side, (((1,), (1,)), ((), ())), preferred_element_type=jnp.float32
    )


def contract_first(left_side, right_side):
    return lax.dot_general(
        left_side, right_side, (((0,), (0,)), ((), ())), preferred_element_type=jnp.float32
    )


def row_pieces(mask, sequence, block, seqs, local):
    per = BLOCK // local
    return [
        pl.ds(pl.multiple_of((((block * per + r) ^ mask) * seqs + sequence) * local, local), local)
        for r in range(per)
    ]


def load_rows(ref, pieces, columns):
    parts = [ref[piece, columns] for piece in pieces]
    return parts[0] if len(parts) == 1 else jnp.concatenate(parts, axis=0)


def store_rows(ref, pieces, columns, values):
    local = values.shape[0] // len(pieces)
    for r, piece in enumerate(pieces):
        ref[piece, columns] = values[r * local : (r + 1) * local]


Q_COLUMNS, K_COLUMNS, V_COLUMNS = (slice(t * PAIR, (t + 1) * PAIR) for t in range(3))


def attend_forward_kernel(mask_ref, slope_ref, qkv_ref, mixed_ref, lse_ref, *, blocks, seqs, local):
    pair, sequence = pl.program_id(0), pl.program_id(1)
    mask = mask_ref[0]
    lane = lax.broadcasted_iota(jnp.int32, (BLOCK, PAIR), 1)
    row = lax.broadcasted_iota(jnp.int32, (BLOCK, BLOCK), 0)
    column = lax.broadcasted_iota(jnp.int32, (BLOCK, BLOCK), 1)
    gap = (row - column).astype(jnp.float32)
    pieces = [row_pieces(mask, sequence, block, seqs, local) for block in range(blocks)]

    for i in range(blocks):
        q_pair = load_rows(qkv_ref, pieces[i], Q_COLUMNS)
        outs, lses = [], []
        for head in range(2):
            slope = slope_ref[pair * 2 + head]
            mine = (lane >= head * HEAD_DIM) & (lane < (head + 1) * HEAD_DIM)
            q = jnp.where(mine, q_pair, jnp.zeros_like(q_pair)) * jnp.bfloat16(HEAD_DIM**-0.5)
            parts, highest = [], None
            for j in range(i + 1):
                scores = contract_last(q, load_rows(qkv_ref, pieces[j], K_COLUMNS))
                distance = jnp.abs(gap) if i == j else gap + float(BLOCK * (i - j))
                scores = scores - slope * distance
                parts.append(scores)
                top = jnp.max(scores, axis=-1, keepdims=True)
                highest = top if highest is None else jnp.maximum(highest, top)
            total, out = None, None
            for j in range(i + 1):
                weights = jnp.exp(parts[j] - highest)
                part = jnp.sum(weights, axis=-1, keepdims=True)
                mixed = contract(weights.astype(jnp.bfloat16), load_rows(qkv_ref, pieces[j], V_COLUMNS))
                total = part if total is None else total + part
                out = mixed if out is None else out + mixed
            outs.append(out / total)
            lses.append(highest + jnp.log(total))
        first = lane < HEAD_DIM
        everything = slice(0, PAIR)
        store_rows(
            mixed_ref, pieces[i], everything, jnp.where(first, outs[0], outs[1]).astype(mixed_ref.dtype)
        )
        store_rows(lse_ref, pieces[i], everything, jnp.where(first, lses[0], lses[1]))


def attend_backward_kernel(
    mask_ref, slope_ref, qkv_ref, lse_ref, mixed_ref, grad_ref, *rest, blocks, seqs, local, start
):
    out_ref, dq_ref, dk_ref, dv_ref = rest[-4:]
    pair, sequence = pl.program_id(0) + start, pl.program_id(1)
    mask = mask_ref[0]
    lane = lax.broadcasted_iota(jnp.int32, (BLOCK, PAIR), 1)
    key = lax.broadcasted_iota(jnp.int32, (BLOCK, BLOCK), 0)
    query = lax.broadcasted_iota(jnp.int32, (BLOCK, BLOCK), 1)
    gap = (query - key).astype(jnp.float32)
    pieces = [row_pieces(mask, sequence, block, seqs, local) for block in range(blocks)]
    everything = slice(0, PAIR)

    for i in range(blocks):
        q_pair = load_rows(qkv_ref, pieces[i], Q_COLUMNS)
        up_pair = load_rows(grad_ref, pieces[i], everything)
        mixed_pair = load_rows(mixed_ref, pieces[i], everything)
        inner_all = (up_pair.astype(jnp.float32) * mixed_pair.astype(jnp.float32)).T
        lse_all = load_rows(lse_ref, pieces[i], everything).T
        dq = None
        for head in range(2):
            slope = slope_ref[pair * 2 + head]
            mine = (lane >= head * HEAD_DIM) & (lane < (head + 1) * HEAD_DIM)
            zero = jnp.zeros_like(q_pair)
            q = jnp.where(mine, q_pair, zero) * jnp.bfloat16(HEAD_DIM**-0.5)
            up = jnp.where(mine, up_pair, zero)
            inner = jnp.sum(inner_all[head * HEAD_DIM : (head + 1) * HEAD_DIM], axis=0, keepdims=True)
            lse = lse_all[head * HEAD_DIM : head * HEAD_DIM + 1]
            for j in range(i + 1):
                k_pair = load_rows(qkv_ref, pieces[j], K_COLUMNS)
                distance = jnp.abs(gap) if i == j else gap + float(BLOCK * (i - j))
                probs = jnp.exp(contract_last(k_pair, q) - slope * distance - lse)
                prob_grad = contract_last(load_rows(qkv_ref, pieces[j], V_COLUMNS), up)
                score_grad = (probs * (prob_grad - inner)).astype(jnp.bfloat16)
                dv = contract(probs.astype(jnp.bfloat16), up)
                dk = contract(score_grad, q)
                part = contract_first(score_grad, jnp.where(mine, k_pair, zero))
                dq = part if dq is None else dq + part
                if i == j and head == 0:
                    dv_ref[j] = dv
                    dk_ref[j] = dk
                else:
                    dv_ref[j] += dv
                    dk_ref[j] += dk
        dq_ref[i] = dq
    for i in range(blocks):
        store_rows(out_ref, pieces[i], Q_COLUMNS, (dq_ref[i] * HEAD_DIM**-0.5).astype(out_ref.dtype))
        store_rows(out_ref, pieces[i], K_COLUMNS, dk_ref[i].astype(out_ref.dtype))
        store_rows(out_ref, pieces[i], V_COLUMNS, dv_ref[i].astype(out_ref.dtype))


def attend_forward(mask, slopes, qkv, seqs, local):
    rows, width = qkv.shape
    pairs, blocks = width // (3 * PAIR), rows // seqs // BLOCK
    scored = pairs * seqs * blocks * (blocks + 1) * BLOCK * BLOCK
    return pl.pallas_call(
        partial(attend_forward_kernel, blocks=blocks, seqs=seqs, local=local),
        grid_spec=pltpu.PrefetchScalarGridSpec(
            num_scalar_prefetch=2,
            grid=(pairs, seqs),
            in_specs=[pl.BlockSpec((rows, 3 * PAIR), lambda p, *_: (0, p))],
            out_specs=[pl.BlockSpec((rows, PAIR), lambda p, *_: (0, p))] * 2,
        ),
        out_shape=[
            jax.ShapeDtypeStruct((rows, pairs * PAIR), jnp.bfloat16),
            jax.ShapeDtypeStruct((rows, pairs * PAIR), jnp.float32),
        ],
        compiler_params=pltpu.CompilerParams(vmem_limit_bytes=24 * 2**20),
        cost_estimate=pl.CostEstimate(
            flops=scored * 2 * 512, bytes_accessed=rows * pairs * PAIR * 12, transcendentals=scored
        ),
        name="attend_forward",
    )(mask, slopes, qkv)


def attend_backward(mask, slopes, qkv, lse, mixed, grad, seqs, local, start, stop, begun=None):
    rows, width = qkv.shape
    blocks = rows // seqs // BLOCK
    scored = (stop - start) * seqs * blocks * (blocks + 1) * BLOCK * BLOCK
    narrow = pl.BlockSpec((rows, PAIR), lambda p, *_: (0, p + start))
    wide = pl.BlockSpec((rows, 3 * PAIR), lambda p, *_: (0, p + start))
    earlier = [] if begun is None else [begun]
    return pl.pallas_call(
        partial(attend_backward_kernel, blocks=blocks, seqs=seqs, local=local, start=start),
        grid_spec=pltpu.PrefetchScalarGridSpec(
            num_scalar_prefetch=2,
            grid=(stop - start, seqs),
            in_specs=[wide, narrow, narrow, narrow] + [pl.BlockSpec(memory_space=pl.ANY)] * len(earlier),
            out_specs=wide,
            scratch_shapes=[pltpu.VMEM((blocks, BLOCK, PAIR), jnp.float32)] * 3,
        ),
        out_shape=jax.ShapeDtypeStruct((rows, width), jnp.bfloat16),
        input_output_aliases={6: 0} if earlier else {},
        compiler_params=pltpu.CompilerParams(vmem_limit_bytes=24 * 2**20),
        cost_estimate=pl.CostEstimate(
            flops=scored * 2 * 1280,
            bytes_accessed=rows * (stop - start) * PAIR * 20,
            transcendentals=scored,
        ),
        name="attend_backward",
    )(mask, slopes, qkv, lse, mixed, grad, *earlier)


def head_columns_kernel(at_ref, in_ref, out_ref):
    for t in range(3):

        @pl.when(pl.program_id(0) == t)
        def _():
            for pair in range(in_ref.shape[1] // PAIR):
                at = (pair * 3 + t) * PAIR
                out_ref[:, at : at + PAIR] = in_ref[:, pair * PAIR : (pair + 1) * PAIR]


def up_kernel(rows_ref, weight_ref, bias_ref, active_ref, slope_ref, *, chunk):
    rows = rows_ref[...]
    for at in range(0, weight_ref.shape[1], chunk):
        columns = slice(at, at + chunk)
        hidden = contract(rows, weight_ref[:, columns]) + bias_ref[:, columns]
        below = 0.5 + 0.5 * lax.erf(hidden * 2**-0.5)
        active_ref[:, columns] = (hidden * below).astype(active_ref.dtype)
        slope_ref[:, columns] = below + hidden * ((2 * math.pi) ** -0.5 * jnp.exp(-0.5 * hidden * hidden))


def hidden_grad_kernel(rows_ref, weight_ref, slope_ref, grad_ref, sum_ref, *, chunk):
    rows = rows_ref[...]
    starting = pl.program_id(0) == 0
    for at in range(0, weight_ref.shape[0], chunk):
        columns = slice(at, at + chunk)
        grad = contract_last(rows, weight_ref[columns, :]) * slope_ref[:, columns]
        grad = grad.astype(grad_ref.dtype)
        grad_ref[:, columns] = grad
        part = jnp.sum(grad.astype(jnp.float32), axis=0, keepdims=True)
        sum_ref[:, columns] = jnp.where(starting, part, sum_ref[:, columns] + part)


TILE = 256


def up_and_bend(rows, weight, bias):
    count, depth = rows.shape
    width = weight.shape[1]
    tile = pl.BlockSpec((TILE, width), lambda i: (i, 0))
    return pl.pallas_call(
        partial(up_kernel, chunk=512),
        grid=(count // TILE,),
        in_specs=[
            pl.BlockSpec((TILE, depth), lambda i: (i, 0)),
            pl.BlockSpec((depth, width), lambda i: (0, 0), pipeline_mode=pl.Buffered(1)),
            pl.BlockSpec((1, width), lambda i: (0, 0)),
        ],
        out_specs=[tile, tile],
        out_shape=[
            jax.ShapeDtypeStruct((count, width), jnp.bfloat16),
            jax.ShapeDtypeStruct((count, width), jnp.float32),
        ],
        compiler_params=pltpu.CompilerParams(vmem_limit_bytes=28 * 2**20),
        cost_estimate=pl.CostEstimate(
            flops=count * depth * width * 4,
            bytes_accessed=2 * count * depth + 2 * depth * width + 6 * count * width,
            transcendentals=2 * count * width,
        ),
        name="up_and_bend",
    )(rows, weight, bias)


def hidden_gradient(rows, weight, slope):
    count, depth = rows.shape
    width = weight.shape[0]
    tile = pl.BlockSpec((TILE, width), lambda i: (i, 0))
    line = pl.BlockSpec((1, width), lambda i: (0, 0))
    return pl.pallas_call(
        partial(hidden_grad_kernel, chunk=512),
        grid=(count // TILE,),
        in_specs=[
            pl.BlockSpec((TILE, depth), lambda i: (i, 0)),
            pl.BlockSpec((width, depth), lambda i: (0, 0), pipeline_mode=pl.Buffered(1)),
            tile,
        ],
        out_specs=[tile, line],
        out_shape=[
            jax.ShapeDtypeStruct((count, width), jnp.bfloat16),
            jax.ShapeDtypeStruct((1, width), jnp.float32),
        ],
        compiler_params=pltpu.CompilerParams(vmem_limit_bytes=28 * 2**20),
        cost_estimate=pl.CostEstimate(
            flops=count * depth * width * 3,
            bytes_accessed=2 * count * depth + 2 * depth * width + 6 * count * width,
            transcendentals=0,
        ),
        name="hidden_gradient",
    )(rows, weight, slope)


def outer_kernel(left_ref, right_ref, out_ref, *, chunk):
    left = left_ref[...]
    shards = out_ref.shape[0]
    for at in range(0, right_ref.shape[1], chunk):
        columns = slice(at, at + chunk)
        made = contract_first(left, right_ref[:, columns]).astype(out_ref.dtype)
        out_ref[:, 0, :, columns] = made.reshape(shards, -1, made.shape[1])


def outer(left, right, groups, shards):
    tokens, rows = left.shape
    width = right.shape[1]
    part = rows // groups
    made = pl.pallas_call(
        partial(outer_kernel, chunk=512 if width % 512 == 0 else 256),
        grid=(groups,),
        in_specs=[
            pl.BlockSpec((tokens, part), lambda i: (0, i)),
            pl.BlockSpec((tokens, width), lambda i: (0, 0), pipeline_mode=pl.Buffered(1)),
        ],
        out_specs=pl.BlockSpec((shards, 1, part // shards, width), lambda i: (0, i, 0, 0)),
        out_shape=jax.ShapeDtypeStruct((shards, groups, part // shards, width), jnp.bfloat16),
        compiler_params=pltpu.CompilerParams(vmem_limit_bytes=28 * 2**20),
        cost_estimate=pl.CostEstimate(
            flops=2 * tokens * rows * width,
            bytes_accessed=2 * (tokens * rows + tokens * width + rows * width),
            transcendentals=0,
        ),
        name="outer",
    )(left, right)
    return made.reshape(rows, width)


def swap(values, bit):
    return lax.ppermute(values, "seq", [(i, i ^ bit) for i in range(4)])


def by_index(parts, me):
    if len(parts) != 4:
        return parts
    odd, upper = (me & 1) == 1, (me & 2) == 2
    a, b, c, d = parts
    a, b, c, d = (
        jnp.where(odd, b, a),
        jnp.where(odd, a, b),
        jnp.where(odd, d, c),
        jnp.where(odd, c, d),
    )
    return [jnp.where(upper, c, a), jnp.where(upper, d, b), jnp.where(upper, a, c), jnp.where(upper, b, d)]


def exchange(slots):
    if lax.axis_size("seq") != 4:
        return list(lax.all_to_all(jnp.stack(slots), "seq", split_axis=0, concat_axis=0, tiled=True))
    return [slots[0]] + [swap(slots[j], j) for j in (1, 2, 3)]


def gate(values, *before):
    return lax.optimization_barrier((values, *before))[0]


class Order:
    def __init__(self):
        self.pending = []

    def after(self, *values):
        self.pending += values

    def __call__(self, operation, *operands):
        if self.pending:
            count = len(operands)
            operands = lax.optimization_barrier((*operands, *self.pending))[:count]
        made = operation(*operands)
        self.pending = jax.tree.leaves(made)
        return made

    def gather(self, rows):
        if lax.axis_size("seq") != 4:
            return lax.all_gather(jnp.concatenate(rows, axis=0), "seq", axis=0, tiled=True), None
        top, bottom = rows
        return rows, (swap(bottom, 1), swap(top, 2), swap(top, 1), swap(bottom, 2))

    def fill(self, pieces):
        if not isinstance(pieces, list):
            return pieces
        count = sum(piece.shape[0] for piece in pieces[:-2])
        rows = pieces[-1].shape[0]
        room = jnp.zeros((2 * rows, pieces[0].shape[1]), pieces[0].dtype)
        made = self(lambda *parts: jnp.concatenate([*parts, room], axis=0), *pieces[:-2])

        def put(before, first, second):
            before = lax.dynamic_update_slice_in_dim(before, first, count, axis=0)
            return lax.dynamic_update_slice_in_dim(before, second, count + rows, axis=0)

        return lambda: self(put, made, *pieces[-2:])

    def pass_on(self, begun, *before):
        rows, came = begun
        if came is None:
            return rows
        first_bottom, second_top, first_top, second_bottom = came
        self.after(*came)
        if before:
            second_top, first_bottom = gate((second_top, first_bottom), *before)
        far = [swap(second_top, 1), swap(first_bottom, 2)]
        return [*rows, first_top, first_bottom, second_top, second_bottom, *far]

    def send_far(self, product, rows, axis=0, held=False):
        if lax.axis_size("seq") != 4:
            return product, rows, axis, None
        count = rows.shape[axis] // 4

        def far_half(values):
            made = product(lax.slice_in_dim(values, 3 * count, 4 * count, axis=axis))
            half = made.shape[0] // 2
            return made[:half], made[half:]

        top, bottom = self(far_half, rows)
        return product, rows, axis, (top, bottom) if held else (swap(top, 1), swap(bottom, 2))

    def send_held(self, begun, *before):
        if begun[1] is None:
            return begun
        rest, parts = begun
        top, bottom = gate(parts, *before)
        return rest, (swap(top, 1), swap(bottom, 2))

    def make_rest(self, begun):
        product, rows, axis, parts = begun
        if parts is None:
            return lax.psum_scatter(self(product, rows), "seq", scatter_dimension=0, tiled=True), None
        count = rows.shape[axis] // 4
        return self(lambda values: product(lax.slice_in_dim(values, 0, 3 * count, axis=axis)), rows), parts

    def add_far(self, begun):
        rest, parts = begun
        if parts is None:
            return begun
        wide = jnp.float32

        def add(rest, top, bottom):
            half = top.shape[0]
            count = 2 * half
            first, second = rest[count : 2 * count], rest[2 * count :]
            first_low = (first[half:].astype(wide) + bottom.astype(wide)).astype(rest.dtype)
            second_low = (second[:half].astype(wide) + top.astype(wide)).astype(rest.dtype)
            return (
                jnp.concatenate([first[:half], first_low], axis=0),
                jnp.concatenate([second_low, second[half:]], axis=0),
            )

        first, second = self(add, rest, *parts)
        return rest, (swap(first, 1), swap(second, 2))


def summed(rest, came):
    wide = jnp.float32
    if came is None:
        return rest.astype(wide)
    own = rest[: came[0].shape[0]]
    return own.astype(wide) + came[0].astype(wide) + came[1].astype(wide)


def whole(parts):
    return jnp.concatenate(parts, axis=0) if isinstance(parts, list) else parts


def total(values):
    for axis in ("fsdp", "seq"):
        count, bit = lax.axis_size(axis), 1
        bits = count.bit_length() - 1
        while bit < count:
            masks = [bit] if bits % 2 else [bit, 2 * bit, 3 * bit]
            came = [lax.ppermute(values, axis, [(i, i ^ mask) for i in range(count)]) for mask in masks]
            values = sum(came, values)
            bit <<= 1 if bits % 2 else 2
            bits -= bits % 2
    return values


def local(
    tokens,
    cotangent,
    w_qkv,
    qv_bias,
    w_out,
    out_bias,
    ln1_gain,
    ln1_shift,
    ln2_gain,
    ln2_shift,
    w_up,
    up_bias,
    w_down,
    down_bias,
):
    seq_count, local_len, model_width = tokens.shape
    groups, shards = lax.axis_size("seq"), lax.axis_size("fsdp")
    me = lax.axis_index("seq")
    square = groups == 4
    heads_here = HEADS // groups
    slab = heads_here * HEAD_DIM
    pairs = slab // PAIR
    hidden_width = w_up.shape[1]
    hidden_slab = hidden_width // groups
    rows_here = seq_count * local_len
    low, wide = jnp.bfloat16, jnp.float32
    mask = jnp.reshape(me if square else jnp.zeros_like(me), (1,)).astype(jnp.int32)
    head_index = me * heads_here + jnp.arange(1, heads_here + 1, dtype=jnp.int32)
    slopes = 2.0 ** (-8.0 * head_index.astype(wide) / HEADS)

    def head_columns(values):
        rows = values.shape[0]
        return pl.pallas_call(
            head_columns_kernel,
            grid_spec=pltpu.PrefetchScalarGridSpec(
                num_scalar_prefetch=1,
                grid=(3,),
                in_specs=[pl.BlockSpec((rows, slab), lambda t, at: (0, t * groups + at[0]))],
                out_specs=pl.BlockSpec((rows, 3 * slab), lambda t, at: (0, 0)),
            ),
            out_shape=jax.ShapeDtypeStruct((rows, 3 * slab), values.dtype),
            name="head_columns",
        )(jnp.reshape(me, (1,)).astype(jnp.int32), values)

    def own_slab(values, axis):
        width = values.shape[axis] // groups
        return lax.dynamic_slice_in_dim(values, me * width, width, axis=axis)

    order = Order()
    x_low = tokens.reshape(rows_here, model_width)
    x = x_low.astype(wide)
    dz_low = cotangent.reshape(rows_here, model_width)
    dz = dz_low.astype(wide)
    qkv_slab = lax.all_gather(head_columns(w_qkv), "fsdp", axis=0, tiled=True)
    qkv_bias = head_columns(jnp.concatenate([qv_bias[0], jnp.zeros_like(qv_bias[0]), qv_bias[1]])[None])
    up_bias_slab = own_slab(up_bias, 0)

    first_norm, first_back = jax.vjp(layer_norm, x, ln1_gain, ln1_shift)
    half = rows_here // 2

    def halves_of(values):
        return values[:half].astype(low), values[half:].astype(low)

    normed = order.gather(order(halves_of, first_norm))
    normed = order.pass_on(normed)
    full_out = lax.all_gather(w_out, "fsdp", axis=0, tiled=True)
    up_slab = lax.all_gather(own_slab(gate(w_up, normed[0]) if square else w_up, 1), "fsdp", axis=0, tiled=True)
    down_slab = lax.all_gather(own_slab(gate(w_down, normed[0]) if square else w_down, 0), "fsdp", axis=1, tiled=True)
    normed = whole(normed)
    upstream = order.gather(halves_of(gate(dz_low, normed)))
    qkv = order(lambda rows: (contract(rows, qkv_slab) + qkv_bias).astype(low), normed)
    attended, log_totals = order(lambda rows: attend_forward(mask, slopes, rows, seq_count, local_len), qkv)
    if square:
        attended = gate(attended, *upstream[1])
    mixed_slots = exchange([attended[j * rows_here : (j + 1) * rows_here] for j in range(groups)])
    mixed_rows = jnp.concatenate(by_index(mixed_slots, me), axis=1)
    mixed_slots = jnp.concatenate(mixed_slots, axis=1)

    def pair_swap(values):
        return lax.ppermute(values, "fsdp", [(i, i ^ 1) for i in range(shards)])

    parity = lax.axis_index("fsdp") & 1
    out_rows = model_width // (groups * shards)

    def pair_halves(values):
        halves = values.reshape(rows_here, -1, 2, out_rows)
        return tuple(
            lax.dynamic_index_in_dim(halves, index, axis=2, keepdims=False).reshape(rows_here, -1)
            for index in (parity, 1 - parity)
        )

    middle = order(lambda rows: x + (contract(rows, full_out) + out_bias), mixed_rows)
    second_norm, second_back = jax.vjp(layer_norm, middle, ln2_gain, ln2_shift)
    second = order.gather(order(halves_of, second_norm))
    mine, theirs = order(pair_halves, mixed_slots)
    theirs = pair_swap(theirs)
    second = whole(order.pass_on(second))
    upstream = order.fill(order.pass_on(upstream, second))
    mixed_half = order(lambda *parts: jnp.concatenate(parts, axis=0), mine, theirs)
    active, slope = order(lambda rows: up_and_bend(rows, up_slab, up_bias_slab[None]), second)
    upstream = upstream() if callable(upstream) else upstream

    def slab_product(left, right):
        return order(lambda rows: outer(rows, right, groups, shards), left)

    def slab_sum(made):
        return lax.psum_scatter(made, "fsdp", scatter_dimension=0, tiled=True)

    def slabs_of_rows(values, *before):
        values = gate(values, *before) if before else values
        values = values.reshape(groups, -1, values.shape[1])
        slabs = lax.all_to_all(values, "seq", split_axis=0, concat_axis=0, tiled=True)
        return jnp.swapaxes(slabs, 0, 1).astype(wide)

    down_sum = slab_sum(slab_product(upstream, active))

    hidden_grad, hidden_sum = order(lambda rows: hidden_gradient(rows, down_slab, slope), upstream)

    def to_second(rows):
        return contract_last(rows, up_slab).astype(low)

    second_grad = order.add_far(order.make_rest(order.send_far(to_second, hidden_grad)))
    def to_result(rows):
        return contract(rows, down_slab).astype(low)

    outcome = order.send_far(to_result, active, held=True)
    up_sum = slab_product(second, hidden_grad)
    if square:
        up_sum = gate(up_sum, *second_grad[1])
    up_sum = slab_sum(up_sum)


    def to_middle(own, came):
        middle_part, gain_grad, shift_grad = second_back(summed(own, came))
        middle_grad = dz + middle_part
        return middle_grad.astype(low), middle_grad, gain_grad, shift_grad

    branch_grad, middle_grad, ln2_gain_grad, ln2_shift_grad = order(
        lambda own, *came: to_middle(own, came or None), second_grad[0], *(second_grad[1] or ())
    )
    def column_sum(values):
        return jnp.sum(values.astype(wide), axis=0)

    hidden_sum = lax.dynamic_update_slice_in_dim(
        jnp.zeros((hidden_width,), wide), hidden_sum[0], me * hidden_slab, axis=0
    )
    early = [column_sum(branch_grad), ln2_gain_grad, ln2_shift_grad, hidden_sum, column_sum(dz)]
    mixed_grad = order(lambda rows: contract_last(rows, full_out).astype(low), branch_grad)
    mixed_grad = exchange(by_index([mixed_grad[:, j * slab : (j + 1) * slab] for j in range(groups)], me))
    outcome = order.make_rest(outcome)
    branch_pair = jnp.concatenate([branch_grad, pair_swap(branch_grad)], axis=0)

    def to_out(columns):
        return contract_first(columns, branch_pair).astype(low)
    out_begun = order.make_rest(order.send_far(to_out, mixed_half, axis=1))
    mixed_grad = jnp.concatenate(mixed_grad, axis=0)
    outcome = order.send_held(outcome, mixed_grad)
    order.after(down_sum)
    attention = (mask, slopes, qkv, log_totals, attended)
    begun = order(lambda rows: attend_backward(*attention, rows, seq_count, local_len, 0, pairs // 2), mixed_grad)
    outcome = order.add_far(outcome)
    out_begun = order.add_far(out_begun)
    qkv_grad = order(
        lambda rows: attend_backward(*attention, rows, seq_count, local_len, pairs // 2, pairs, begun), mixed_grad
    )
    out_sum = order(
        lambda own, *came: summed(own, came or None).astype(low), out_begun[0], *(out_begun[1] or ())
    ).reshape(-1, 1, out_rows, model_width)
    zero = jnp.zeros_like(out_sum)
    out_sum = jnp.concatenate(
        [jnp.where(parity == 0, out_sum, zero), jnp.where(parity == 1, out_sum, zero)], axis=1
    ).reshape(-1, model_width)
    grad_w_out = lax.psum_scatter(out_sum, "fsdp", scatter_dimension=0, tiled=True).astype(wide)
    order.after(up_sum)

    def to_normed(rows):
        return contract_last(rows, qkv_slab).astype(low)

    normed_grad = order.send_far(to_normed, qkv_grad)
    qkv_sum = slab_product(normed, qkv_grad)
    qkv_sum = slab_sum(gate(qkv_sum, grad_w_out, *(outcome[1] or ())))
    order.after(grad_w_out, *(outcome[1] or ()))
    normed_grad = order.make_rest(normed_grad)
    normed_grad = order.add_far(normed_grad)
    result = order(
        lambda own, *came: (middle + (summed(own, came or None) + down_bias)).astype(low),
        outcome[0],
        *(outcome[1] or ()),
    ).reshape(tokens.shape)

    def to_input(own, came):
        input_part, gain_grad, shift_grad = first_back(summed(own, came))
        return (middle_grad + input_part).astype(low), gain_grad, shift_grad

    grad_tokens, ln1_gain_grad, ln1_shift_grad = order(
        lambda own, *came: to_input(own, came or None), normed_grad[0], *(normed_grad[1] or ())
    )
    grad_tokens = grad_tokens.reshape(tokens.shape)
    grad_w_down = slabs_of_rows(down_sum, *(normed_grad[1] or ())).reshape(-1, hidden_width).T
    grad_w_up = slabs_of_rows(up_sum, *(normed_grad[1] or ())).reshape(-1, hidden_width)
    grad_w_qkv = slabs_of_rows(qkv_sum).reshape(-1, groups, pairs, 3, PAIR)
    grad_w_qkv = jnp.transpose(grad_w_qkv, (0, 3, 1, 2, 4)).reshape(-1, 3 * model_width)

    head_sum = jnp.transpose(column_sum(qkv_grad).reshape(pairs, 3, PAIR), (1, 0, 2)).reshape(3, slab)
    qv_sum = lax.dynamic_update_slice_in_dim(
        jnp.zeros((2, model_width), wide), head_sum[0::2], me * slab, axis=1
    )
    late = [qv_sum.reshape(-1), ln1_gain_grad, ln1_shift_grad]
    sums = total(jnp.concatenate(early + late).reshape(-1, PAIR)).reshape(-1)

    def cut(at, count):
        return sums[at * model_width : (at + count) * model_width]

    ratio = hidden_width // model_width
    return (
        result,
        grad_tokens,
        grad_w_qkv,
        cut(4 + ratio, 2).reshape(2, model_width),
        grad_w_out,
        cut(0, 1),
        cut(6 + ratio, 1),
        cut(7 + ratio, 1),
        cut(1, 1),
        cut(2, 1),
        grad_w_up,
        cut(3, ratio),
        grad_w_down,
        cut(3 + ratio, 1),
    )


def solution(mesh):
    return jax.shard_map(
        local,
        mesh=mesh,
        in_specs=(
            P("fsdp", "seq", None),
            P("fsdp", "seq", None),
            P("fsdp", None),
            P(),
            P("fsdp", None),
            P(),
            P(),
            P(),
            P(),
            P(),
            P("fsdp", None),
            P(),
            P(None, "fsdp"),
            P(),
        ),
        out_specs=(
            P("fsdp", "seq", None),
            P("fsdp", "seq", None),
            P(("seq", "fsdp"), None),
            P(),
            P(("seq", "fsdp"), None),
            P(),
            P(),
            P(),
            P(),
            P(),
            P(("seq", "fsdp"), None),
            P(),
            P(None, ("seq", "fsdp")),
            P(),
        ),
        check_vma=False,
    )
```

```python
import math
from functools import partial

import jax
import jax.numpy as jnp
from jax import lax
from jax.experimental import pallas as pl
from jax.experimental.pallas import tpu as pltpu
from jax.sharding import PartitionSpec as P

HEADS = 32
HEAD_DIM = 64
BLOCK = 256
PAIR = 2 * HEAD_DIM


def estimate(flops, transcendentals=0):
    return pl.CostEstimate(flops=flops // 4, bytes_accessed=flops // 4096, transcendentals=transcendentals // 4)


def layer_norm(token_rows, gain_vec, shift_vec):
    average = jnp.mean(token_rows, axis=-1, keepdims=True)
    centred = token_rows - average
    spread = jnp.mean(centred * centred, axis=-1, keepdims=True)
    return centred * lax.rsqrt(spread + 1e-05) * gain_vec + shift_vec


def contract(left_side, right_side):
    return lax.dot_general(
        left_side, right_side, (((1,), (0,)), ((), ())), preferred_element_type=jnp.float32
    )


def contract_last(left_side, right_side):
    return lax.dot_general(
        left_side, right_side, (((1,), (1,)), ((), ())), preferred_element_type=jnp.float32
    )


def contract_first(left_side, right_side):
    return lax.dot_general(
        left_side, right_side, (((0,), (0,)), ((), ())), preferred_element_type=jnp.float32
    )


def row_pieces(mask, sequence, block, seqs, local):
    per = BLOCK // local
    return [
        pl.ds(pl.multiple_of((((block * per + r) ^ mask) * seqs + sequence) * local, local), local)
        for r in range(per)
    ]


def load_rows(ref, pieces, columns):
    parts = [ref[piece, columns] for piece in pieces]
    return parts[0] if len(parts) == 1 else jnp.concatenate(parts, axis=0)


def store_rows(ref, pieces, columns, values):
    local = values.shape[0] // len(pieces)
    for r, piece in enumerate(pieces):
        ref[piece, columns] = values[r * local : (r + 1) * local]


Q_COLUMNS, K_COLUMNS, V_COLUMNS = (slice(t * PAIR, (t + 1) * PAIR) for t in range(3))


def attend_forward_kernel(mask_ref, slope_ref, qkv_ref, mixed_ref, lse_ref, *, blocks, seqs, local):
    pair, sequence = pl.program_id(0), pl.program_id(1)
    mask = mask_ref[0]
    lane = lax.broadcasted_iota(jnp.int32, (BLOCK, PAIR), 1)
    row = lax.broadcasted_iota(jnp.int32, (BLOCK, BLOCK), 0)
    column = lax.broadcasted_iota(jnp.int32, (BLOCK, BLOCK), 1)
    gap = (row - column).astype(jnp.float32)
    pieces = [row_pieces(mask, sequence, block, seqs, local) for block in range(blocks)]

    for i in range(blocks):
        q_pair = load_rows(qkv_ref, pieces[i], Q_COLUMNS)
        outs, lses = [], []
        for head in range(2):
            slope = slope_ref[pair * 2 + head]
            mine = (lane >= head * HEAD_DIM) & (lane < (head + 1) * HEAD_DIM)
            q = jnp.where(mine, q_pair, jnp.zeros_like(q_pair)) * jnp.bfloat16(HEAD_DIM**-0.5)
            parts, highest = [], None
            for j in range(i + 1):
                scores = contract_last(q, load_rows(qkv_ref, pieces[j], K_COLUMNS))
                distance = jnp.abs(gap) if i == j else gap + float(BLOCK * (i - j))
                scores = scores - slope * distance
                parts.append(scores)
                top = jnp.max(scores, axis=-1, keepdims=True)
                highest = top if highest is None else jnp.maximum(highest, top)
            total, out = None, None
            for j in range(i + 1):
                weights = jnp.exp(parts[j] - highest)
                part = jnp.sum(weights, axis=-1, keepdims=True)
                mixed = contract(weights.astype(jnp.bfloat16), load_rows(qkv_ref, pieces[j], V_COLUMNS))
                total = part if total is None else total + part
                out = mixed if out is None else out + mixed
            outs.append(out / total)
            lses.append(highest + jnp.log(total))
        first = lane < HEAD_DIM
        everything = slice(0, PAIR)
        store_rows(
            mixed_ref, pieces[i], everything, jnp.where(first, outs[0], outs[1]).astype(mixed_ref.dtype)
        )
        store_rows(lse_ref, pieces[i], everything, jnp.where(first, lses[0], lses[1]))


def attend_backward_kernel(
    mask_ref, slope_ref, qkv_ref, lse_ref, mixed_ref, grad_ref, *rest, blocks, seqs, local, start
):
    out_ref, dq_ref, dk_ref, dv_ref = rest[-4:]
    pair, sequence = pl.program_id(0) + start, pl.program_id(1)
    mask = mask_ref[0]
    lane = lax.broadcasted_iota(jnp.int32, (BLOCK, PAIR), 1)
    key = lax.broadcasted_iota(jnp.int32, (BLOCK, BLOCK), 0)
    query = lax.broadcasted_iota(jnp.int32, (BLOCK, BLOCK), 1)
    gap = (query - key).astype(jnp.float32)
    pieces = [row_pieces(mask, sequence, block, seqs, local) for block in range(blocks)]
    everything = slice(0, PAIR)

    for i in range(blocks):
        q_pair = load_rows(qkv_ref, pieces[i], Q_COLUMNS)
        up_pair = load_rows(grad_ref, pieces[i], everything)
        mixed_pair = load_rows(mixed_ref, pieces[i], everything)
        inner_all = (up_pair.astype(jnp.float32) * mixed_pair.astype(jnp.float32)).T
        lse_all = load_rows(lse_ref, pieces[i], everything).T
        dq = None
        for head in range(2):
            slope = slope_ref[pair * 2 + head]
            mine = (lane >= head * HEAD_DIM) & (lane < (head + 1) * HEAD_DIM)
            zero = jnp.zeros_like(q_pair)
            q = jnp.where(mine, q_pair, zero) * jnp.bfloat16(HEAD_DIM**-0.5)
            up = jnp.where(mine, up_pair, zero)
            inner = jnp.sum(inner_all[head * HEAD_DIM : (head + 1) * HEAD_DIM], axis=0, keepdims=True)
            lse = lse_all[head * HEAD_DIM : head * HEAD_DIM + 1]
            for j in range(i + 1):
                k_pair = load_rows(qkv_ref, pieces[j], K_COLUMNS)
                distance = jnp.abs(gap) if i == j else gap + float(BLOCK * (i - j))
                probs = jnp.exp(contract_last(k_pair, q) - slope * distance - lse)
                prob_grad = contract_last(load_rows(qkv_ref, pieces[j], V_COLUMNS), up)
                score_grad = (probs * (prob_grad - inner)).astype(jnp.bfloat16)
                dv = contract(probs.astype(jnp.bfloat16), up)
                dk = contract(score_grad, q)
                part = contract_first(score_grad, jnp.where(mine, k_pair, zero))
                dq = part if dq is None else dq + part
                if i == j and head == 0:
                    dv_ref[j] = dv
                    dk_ref[j] = dk
                else:
                    dv_ref[j] += dv
                    dk_ref[j] += dk
        dq_ref[i] = dq
    for i in range(blocks):
        store_rows(out_ref, pieces[i], Q_COLUMNS, (dq_ref[i] * HEAD_DIM**-0.5).astype(out_ref.dtype))
        store_rows(out_ref, pieces[i], K_COLUMNS, dk_ref[i].astype(out_ref.dtype))
        store_rows(out_ref, pieces[i], V_COLUMNS, dv_ref[i].astype(out_ref.dtype))


def attend_forward(mask, slopes, qkv, seqs, local):
    rows, width = qkv.shape
    pairs, blocks = width // (3 * PAIR), rows // seqs // BLOCK
    scored = pairs * seqs * blocks * (blocks + 1) * BLOCK * BLOCK
    return pl.pallas_call(
        partial(attend_forward_kernel, blocks=blocks, seqs=seqs, local=local),
        grid_spec=pltpu.PrefetchScalarGridSpec(
            num_scalar_prefetch=2,
            grid=(pairs, seqs),
            in_specs=[pl.BlockSpec((rows, 3 * PAIR), lambda p, *_: (0, p))],
            out_specs=[pl.BlockSpec((rows, PAIR), lambda p, *_: (0, p))] * 2,
        ),
        out_shape=[
            jax.ShapeDtypeStruct((rows, pairs * PAIR), jnp.bfloat16),
            jax.ShapeDtypeStruct((rows, pairs * PAIR), jnp.float32),
        ],
        compiler_params=pltpu.CompilerParams(vmem_limit_bytes=24 * 2**20),
        cost_estimate=estimate(scored * 2 * 512, scored),
        name="attend_forward",
    )(mask, slopes, qkv)


def attend_backward(mask, slopes, qkv, lse, mixed, grad, seqs, local, start, stop, begun=None):
    rows, width = qkv.shape
    blocks = rows // seqs // BLOCK
    scored = (stop - start) * seqs * blocks * (blocks + 1) * BLOCK * BLOCK
    narrow = pl.BlockSpec((rows, PAIR), lambda p, *_: (0, p + start))
    wide = pl.BlockSpec((rows, 3 * PAIR), lambda p, *_: (0, p + start))
    earlier = [] if begun is None else [begun]
    return pl.pallas_call(
        partial(attend_backward_kernel, blocks=blocks, seqs=seqs, local=local, start=start),
        grid_spec=pltpu.PrefetchScalarGridSpec(
            num_scalar_prefetch=2,
            grid=(stop - start, seqs),
            in_specs=[wide, narrow, narrow, narrow] + [pl.BlockSpec(memory_space=pl.ANY)] * len(earlier),
            out_specs=wide,
            scratch_shapes=[pltpu.VMEM((blocks, BLOCK, PAIR), jnp.float32)] * 3,
        ),
        out_shape=jax.ShapeDtypeStruct((rows, width), jnp.bfloat16),
        input_output_aliases={6: 0} if earlier else {},
        compiler_params=pltpu.CompilerParams(vmem_limit_bytes=24 * 2**20),
        cost_estimate=estimate(scored * 2 * 1280, scored),
        name="attend_backward",
    )(mask, slopes, qkv, lse, mixed, grad, *earlier)


def head_columns_kernel(at_ref, in_ref, out_ref):
    for t in range(3):

        @pl.when(pl.program_id(0) == t)
        def _():
            for pair in range(in_ref.shape[1] // PAIR):
                at = (pair * 3 + t) * PAIR
                out_ref[:, at : at + PAIR] = in_ref[:, pair * PAIR : (pair + 1) * PAIR]


def up_kernel(rows_ref, weight_ref, bias_ref, active_ref, slope_ref, *, chunk):
    rows = rows_ref[...]
    for at in range(0, weight_ref.shape[1], chunk):
        columns = slice(at, at + chunk)
        hidden = contract(rows, weight_ref[:, columns]) + bias_ref[:, columns]
        below = 0.5 + 0.5 * lax.erf(hidden * 2**-0.5)
        active_ref[:, columns] = (hidden * below).astype(active_ref.dtype)
        slope_ref[:, columns] = below + hidden * ((2 * math.pi) ** -0.5 * jnp.exp(-0.5 * hidden * hidden))


def hidden_grad_kernel(rows_ref, weight_ref, slope_ref, grad_ref, sum_ref, *, chunk):
    rows = rows_ref[...]
    starting = pl.program_id(0) == 0
    for at in range(0, weight_ref.shape[0], chunk):
        columns = slice(at, at + chunk)
        grad = contract_last(rows, weight_ref[columns, :]) * slope_ref[:, columns]
        grad = grad.astype(grad_ref.dtype)
        grad_ref[:, columns] = grad
        part = jnp.sum(grad.astype(jnp.float32), axis=0, keepdims=True)
        sum_ref[:, columns] = jnp.where(starting, part, sum_ref[:, columns] + part)


TILE = 256


def up_and_bend(rows, weight, bias):
    count, depth = rows.shape
    width = weight.shape[1]
    tile = pl.BlockSpec((TILE, width), lambda i: (i, 0))
    return pl.pallas_call(
        partial(up_kernel, chunk=512),
        grid=(count // TILE,),
        in_specs=[
            pl.BlockSpec((TILE, depth), lambda i: (i, 0)),
            pl.BlockSpec((depth, width), lambda i: (0, 0), pipeline_mode=pl.Buffered(1)),
            pl.BlockSpec((1, width), lambda i: (0, 0)),
        ],
        out_specs=[tile, tile],
        out_shape=[
            jax.ShapeDtypeStruct((count, width), jnp.bfloat16),
            jax.ShapeDtypeStruct((count, width), jnp.float32),
        ],
        compiler_params=pltpu.CompilerParams(vmem_limit_bytes=28 * 2**20),
        cost_estimate=estimate(count * depth * width * 4, 2 * count * width),
        name="up_and_bend",
    )(rows, weight, bias)


def hidden_gradient(rows, weight, slope):
    count, depth = rows.shape
    width = weight.shape[0]
    tile = pl.BlockSpec((TILE, width), lambda i: (i, 0))
    line = pl.BlockSpec((1, width), lambda i: (0, 0))
    return pl.pallas_call(
        partial(hidden_grad_kernel, chunk=512),
        grid=(count // TILE,),
        in_specs=[
            pl.BlockSpec((TILE, depth), lambda i: (i, 0)),
            pl.BlockSpec((width, depth), lambda i: (0, 0), pipeline_mode=pl.Buffered(1)),
            tile,
        ],
        out_specs=[tile, line],
        out_shape=[
            jax.ShapeDtypeStruct((count, width), jnp.bfloat16),
            jax.ShapeDtypeStruct((1, width), jnp.float32),
        ],
        compiler_params=pltpu.CompilerParams(vmem_limit_bytes=28 * 2**20),
        cost_estimate=estimate(count * depth * width * 3, 0),
        name="hidden_gradient",
    )(rows, weight, slope)


def norm_back_kernel(rest_ref, values_ref, base_ref, gain_ref, *refs, parts):
    came, (low_ref, wide_ref, sums_ref) = refs[:parts], refs[parts:]
    wide = jnp.float32
    starting = pl.program_id(0) == 0
    grad = rest_ref[...].astype(wide)
    for top, bottom in zip(came[0::2], came[1::2]):
        grad = grad + jnp.where(starting, top[...], bottom[...]).astype(wide)
    values = values_ref[...].astype(wide)
    base = base_ref[...].astype(wide)
    centred = values - jnp.mean(values, axis=-1, keepdims=True)
    scale = lax.rsqrt(jnp.mean(centred * centred, axis=-1, keepdims=True) + 1e-05)
    normal = centred * scale
    gained = grad * gain_ref[...]
    along = jnp.mean(gained * normal, axis=-1, keepdims=True)
    made = base + scale * (gained - jnp.mean(gained, axis=-1, keepdims=True) - normal * along)
    low = made.astype(low_ref.dtype)
    low_ref[...] = low
    wide_ref[...] = made
    for row, part in enumerate((grad * normal, grad, low.astype(wide), base)):
        line = jnp.sum(part, axis=0, keepdims=True)
        sums_ref[row : row + 1, :] = jnp.where(starting, line, sums_ref[row : row + 1, :] + line)


def norm_back(rest, values, base, gain, came):
    rows, width = values.shape
    half = rows // 2
    came = list(came or ())
    tile = pl.BlockSpec((half, width), lambda i: (i, 0))
    every = pl.BlockSpec((half, width), lambda i: (0, 0), pipeline_mode=pl.Buffered(1))
    return pl.pallas_call(
        partial(norm_back_kernel, parts=len(came)),
        grid=(2,),
        in_specs=[tile, tile, tile, pl.BlockSpec((1, width), lambda i: (0, 0))] + [every] * len(came),
        out_specs=[tile, tile, pl.BlockSpec((8, width), lambda i: (0, 0))],
        out_shape=[
            jax.ShapeDtypeStruct((rows, width), jnp.bfloat16),
            jax.ShapeDtypeStruct((rows, width), jnp.float32),
            jax.ShapeDtypeStruct((8, width), jnp.float32),
        ],
        compiler_params=pltpu.CompilerParams(vmem_limit_bytes=40 * 2**20),
        cost_estimate=estimate(30 * rows * width, rows),
        name="norm_back",
    )(rest, values, base, gain[None], *came)


def outer_kernel(left_ref, right_ref, out_ref, *, chunk):
    left = left_ref[...]
    shards = out_ref.shape[0]
    for at in range(0, right_ref.shape[1], chunk):
        columns = slice(at, at + chunk)
        made = contract_first(left, right_ref[:, columns]).astype(out_ref.dtype)
        out_ref[:, 0, :, columns] = made.reshape(shards, -1, made.shape[1])


def outer(left, right, groups, shards):
    tokens, rows = left.shape
    width = right.shape[1]
    part = rows // groups
    made = pl.pallas_call(
        partial(outer_kernel, chunk=512 if width % 512 == 0 else 256),
        grid=(groups,),
        in_specs=[
            pl.BlockSpec((tokens, part), lambda i: (0, i)),
            pl.BlockSpec((tokens, width), lambda i: (0, 0), pipeline_mode=pl.Buffered(1)),
        ],
        out_specs=pl.BlockSpec((shards, 1, part // shards, width), lambda i: (0, i, 0, 0)),
        out_shape=jax.ShapeDtypeStruct((shards, groups, part // shards, width), jnp.bfloat16),
        compiler_params=pltpu.CompilerParams(vmem_limit_bytes=28 * 2**20),
        cost_estimate=estimate(2 * tokens * rows * width, 0),
        name="outer",
    )(left, right)
    return made.reshape(rows, width)


def swap(values, bit):
    return lax.ppermute(values, "seq", [(i, i ^ bit) for i in range(4)])


def by_index(parts, me):
    if len(parts) != 4:
        return parts
    odd, upper = (me & 1) == 1, (me & 2) == 2
    a, b, c, d = parts
    a, b, c, d = (
        jnp.where(odd, b, a),
        jnp.where(odd, a, b),
        jnp.where(odd, d, c),
        jnp.where(odd, c, d),
    )
    return [jnp.where(upper, c, a), jnp.where(upper, d, b), jnp.where(upper, a, c), jnp.where(upper, b, d)]


def exchange(slots):
    if lax.axis_size("seq") != 4:
        return list(lax.all_to_all(jnp.stack(slots), "seq", split_axis=0, concat_axis=0, tiled=True))
    return [slots[0]] + [swap(slots[j], j) for j in (1, 2, 3)]


def gate(values, *before):
    return lax.optimization_barrier((values, *before))[0]


class Order:
    def __init__(self):
        self.pending = []

    def after(self, *values):
        self.pending += values

    def __call__(self, operation, *operands):
        if self.pending:
            count = len(operands)
            operands = lax.optimization_barrier((*operands, *self.pending))[:count]
        made = operation(*operands)
        self.pending = jax.tree.leaves(made)
        return made

    def gather(self, rows):
        if lax.axis_size("seq") != 4:
            return lax.all_gather(jnp.concatenate(rows, axis=0), "seq", axis=0, tiled=True), None
        top, bottom = rows
        return rows, (swap(bottom, 1), swap(top, 2), swap(top, 1), swap(bottom, 2))

    def fill(self, begun):
        rows, came = begun
        if came is None:
            return rows
        first_bottom, second_top, first_top, second_bottom = came
        room = jnp.zeros_like(rows[0])
        parts = (*rows, first_top, first_bottom, second_top, second_bottom, room, room)
        return self(lambda *parts: jnp.concatenate(parts, axis=0), *parts)

    def complete(self, made, pieces):
        if not isinstance(pieces, list):
            return made
        rows = pieces[-1].shape[0]

        def put(before, first, second):
            before = lax.dynamic_update_slice_in_dim(before, first, 6 * rows, axis=0)
            return lax.dynamic_update_slice_in_dim(before, second, 7 * rows, axis=0)

        return self(put, made, *pieces[-2:])

    def pass_on(self, begun, *before):
        rows, came = begun
        if came is None:
            return rows
        first_bottom, second_top, first_top, second_bottom = came
        self.after(*came)
        if before:
            second_top, first_bottom = gate((second_top, first_bottom), *before)
        far = [swap(second_top, 1), swap(first_bottom, 2)]
        return [*rows, first_top, first_bottom, second_top, second_bottom, *far]

    def send_far(self, product, rows, axis=0, held=False):
        if lax.axis_size("seq") != 4:
            return product, rows, axis, None
        count = rows.shape[axis] // 4

        def far_half(values):
            made = product(lax.slice_in_dim(values, 3 * count, 4 * count, axis=axis))
            half = made.shape[0] // 2
            return made[:half], made[half:]

        top, bottom = self(far_half, rows)
        return product, rows, axis, (top, bottom) if held else (swap(top, 1), swap(bottom, 2))

    def make_rest(self, begun, held=False):
        product, rows, axis, far = begun
        if far is None:
            return lax.psum_scatter(self(product, rows), "seq", scatter_dimension=0, tiled=True), None, None
        count = rows.shape[axis] // 4
        rest = self(lambda values: product(lax.slice_in_dim(values, 0, 3 * count, axis=axis)), rows)
        count = rest.shape[0] // 3
        half = count // 2
        direct = rest[count : count + half], rest[2 * count + half :]
        return rest, far, direct if held else (swap(direct[0], 1), swap(direct[1], 2))

    def send_held(self, begun, which, *before):
        rest, *parts = begun
        if parts[which] is not None:
            first, second = gate(parts[which], *before) if before else parts[which]
            parts[which] = swap(first, 1), swap(second, 2)
        return rest, *parts

    def add_far(self, begun, *before):
        rest, far, direct = begun
        if far is None:
            return rest, None
        wide = jnp.float32

        def add(rest, top, bottom):
            half = top.shape[0]
            first, second = rest[3 * half : 4 * half], rest[4 * half : 5 * half]
            return (
                (first.astype(wide) + bottom.astype(wide)).astype(rest.dtype),
                (second.astype(wide) + top.astype(wide)).astype(rest.dtype),
            )

        first, second = self(add, rest, *far)
        if before:
            first, second = gate((first, second), *before)
        return rest, (direct[0], swap(first, 1), swap(second, 2), direct[1])


def summed(rest, came):
    wide = jnp.float32
    if came is None:
        return rest.astype(wide)
    half = came[0].shape[0]
    first_top, first_bottom, second_top, second_bottom = (part.astype(wide) for part in came)
    top = rest[:half].astype(wide) + first_top + second_top
    bottom = rest[half : 2 * half].astype(wide) + first_bottom + second_bottom
    return jnp.concatenate([top, bottom], axis=0)


def whole(parts):
    return jnp.concatenate(parts, axis=0) if isinstance(parts, list) else parts


def total(values):
    for axis in ("fsdp", "seq"):
        count, bit = lax.axis_size(axis), 1
        bits = count.bit_length() - 1
        while bit < count:
            masks = [bit] if bits % 2 else [bit, 2 * bit, 3 * bit]
            came = [lax.ppermute(values, axis, [(i, i ^ mask) for i in range(count)]) for mask in masks]
            values = sum(came, values)
            bit <<= 1 if bits % 2 else 2
            bits -= bits % 2
    return values


def local(
    tokens,
    cotangent,
    w_qkv,
    qv_bias,
    w_out,
    out_bias,
    ln1_gain,
    ln1_shift,
    ln2_gain,
    ln2_shift,
    w_up,
    up_bias,
    w_down,
    down_bias,
):
    seq_count, local_len, model_width = tokens.shape
    groups, shards = lax.axis_size("seq"), lax.axis_size("fsdp")
    me = lax.axis_index("seq")
    square = groups == 4
    heads_here = HEADS // groups
    slab = heads_here * HEAD_DIM
    pairs = slab // PAIR
    hidden_width = w_up.shape[1]
    hidden_slab = hidden_width // groups
    rows_here = seq_count * local_len
    low, wide = jnp.bfloat16, jnp.float32
    mask = jnp.reshape(me if square else jnp.zeros_like(me), (1,)).astype(jnp.int32)
    head_index = me * heads_here + jnp.arange(1, heads_here + 1, dtype=jnp.int32)
    slopes = 2.0 ** (-8.0 * head_index.astype(wide) / HEADS)

    def head_columns(values):
        rows = values.shape[0]
        return pl.pallas_call(
            head_columns_kernel,
            grid_spec=pltpu.PrefetchScalarGridSpec(
                num_scalar_prefetch=1,
                grid=(3,),
                in_specs=[pl.BlockSpec((rows, slab), lambda t, at: (0, t * groups + at[0]))],
                out_specs=pl.BlockSpec((rows, 3 * slab), lambda t, at: (0, 0)),
            ),
            out_shape=jax.ShapeDtypeStruct((rows, 3 * slab), values.dtype),
            name="head_columns",
        )(jnp.reshape(me, (1,)).astype(jnp.int32), values)

    def own_slab(values, axis):
        width = values.shape[axis] // groups
        return lax.dynamic_slice_in_dim(values, me * width, width, axis=axis)

    order = Order()
    x_low = tokens.reshape(rows_here, model_width)
    x = x_low.astype(wide)
    dz_low = cotangent.reshape(rows_here, model_width)
    qkv_slab = lax.all_gather(head_columns(w_qkv), "fsdp", axis=0, tiled=True)
    qkv_bias = head_columns(jnp.concatenate([qv_bias[0], jnp.zeros_like(qv_bias[0]), qv_bias[1]])[None])
    up_bias_slab = own_slab(up_bias, 0)

    first_norm = layer_norm(x, ln1_gain, ln1_shift)
    half = rows_here // 2

    def halves_of(values):
        return values[:half].astype(low), values[half:].astype(low)

    normed = order.gather(order(halves_of, first_norm))
    normed = order.pass_on(normed)
    full_out = lax.all_gather(w_out, "fsdp", axis=0, tiled=True)
    up_slab = lax.all_gather(own_slab(gate(w_up, normed[0]) if square else w_up, 1), "fsdp", axis=0, tiled=True)
    down_slab = lax.all_gather(own_slab(gate(w_down, normed[0]) if square else w_down, 0), "fsdp", axis=1, tiled=True)
    normed = whole(normed)
    upstream = order.gather(halves_of(gate(dz_low, normed)))
    qkv = order(lambda rows: (contract(rows, qkv_slab) + qkv_bias).astype(low), normed)
    attended, log_totals = order(lambda rows: attend_forward(mask, slopes, rows, seq_count, local_len), qkv)
    if square:
        attended = gate(attended, *upstream[1])
    mixed_slots = exchange([attended[j * rows_here : (j + 1) * rows_here] for j in range(groups)])
    mixed_rows = jnp.concatenate(by_index(mixed_slots, me), axis=1)
    mixed_slots = jnp.concatenate(mixed_slots, axis=1)

    def pair_swap(values):
        return lax.ppermute(values, "fsdp", [(i, i ^ 1) for i in range(shards)])

    parity = lax.axis_index("fsdp") & 1
    out_rows = model_width // (groups * shards)

    def pair_halves(values):
        halves = values.reshape(rows_here, -1, 2, out_rows)
        return tuple(
            lax.dynamic_index_in_dim(halves, index, axis=2, keepdims=False).reshape(rows_here, -1)
            for index in (parity, 1 - parity)
        )

    middle = order(lambda rows: x + (contract(rows, full_out) + out_bias), mixed_rows)
    second_norm = layer_norm(middle, ln2_gain, ln2_shift)
    second = order.gather(order(halves_of, second_norm))
    mine, theirs = order(pair_halves, mixed_slots)
    upstream_made = order.fill(upstream)
    theirs = pair_swap(theirs)
    second = whole(order.pass_on(second))
    upstream = order.pass_on(upstream, second)
    mixed_half = order(lambda *parts: jnp.concatenate(parts, axis=0), mine, theirs)
    active, slope = order(lambda rows: up_and_bend(rows, up_slab, up_bias_slab[None]), second)
    upstream = order.complete(upstream_made, upstream)

    def slab_product(left, right):
        return order(lambda rows: outer(rows, right, groups, shards), left)

    def slab_sum(made):
        return lax.psum_scatter(made, "fsdp", scatter_dimension=0, tiled=True)

    def slabs_of_rows(*sums):
        parts = [part.reshape(groups, -1, part.shape[1]) for part in sums]
        slabs = lax.all_to_all(jnp.concatenate(parts, axis=1), "seq", split_axis=0, concat_axis=0, tiled=True)
        count = parts[0].shape[1]
        return [
            jnp.swapaxes(slabs[:, at : at + count], 0, 1).astype(wide) for at in range(0, slabs.shape[1], count)
        ]

    hidden_grad, hidden_sum = order(lambda rows: hidden_gradient(rows, down_slab, slope), upstream)

    def to_second(rows):
        return contract_last(rows, up_slab).astype(low)

    second_grad = order.add_far(order.make_rest(order.send_far(to_second, hidden_grad)))
    def to_result(rows):
        return contract(rows, down_slab).astype(low)

    outcome = order.send_far(to_result, active, held=True)
    down_sum = slab_product(upstream, active)
    if square:
        down_sum = gate(down_sum, *second_grad[1][0::3])
    down_sum = slab_sum(down_sum)
    up_sum = slab_product(second, hidden_grad)
    if square:
        up_sum = gate(up_sum, *second_grad[1])
    up_sum = slab_sum(up_sum)


    branch_grad, middle_grad, middle_sums = order(
        lambda rest, *came: norm_back(rest, middle, dz_low, ln2_gain, came), second_grad[0], *(second_grad[1] or ())
    )

    def column_sum(values):
        return jnp.sum(values.astype(wide), axis=0)

    hidden_sum = lax.dynamic_update_slice_in_dim(
        jnp.zeros((hidden_width,), wide), hidden_sum[0], me * hidden_slab, axis=0
    )
    early = [middle_sums[2], middle_sums[0], middle_sums[1], hidden_sum, middle_sums[3]]
    mixed_grad = order(lambda rows: contract_last(rows, full_out).astype(low), branch_grad)
    mixed_grad = exchange(by_index([mixed_grad[:, j * slab : (j + 1) * slab] for j in range(groups)], me))
    outcome = order.make_rest(outcome, held=True)
    mixed_grad = order(lambda *parts: jnp.concatenate(parts, axis=0), *mixed_grad)
    outcome = order.send_held(order.send_held(outcome, 0, mixed_grad), 1, mixed_grad)
    branch_pair = jnp.concatenate([branch_grad, pair_swap(branch_grad)], axis=0)

    def to_out(columns):
        return contract_first(columns, branch_pair).astype(low)

    order.after(down_sum)
    attention = (mask, slopes, qkv, log_totals, attended)
    begun = order(lambda rows: attend_backward(*attention, rows, seq_count, local_len, 0, pairs // 2), mixed_grad)
    out_begun = order.make_rest(order.send_far(to_out, mixed_half, axis=1))
    qkv_grad = order(
        lambda rows: attend_backward(*attention, rows, seq_count, local_len, pairs // 2, pairs, begun), mixed_grad
    )
    out_begun = order.add_far(out_begun)
    if square:
        order.after(*outcome[1], *outcome[2])
    order.after(up_sum)

    def to_normed(rows):
        return contract_last(rows, qkv_slab).astype(low)

    normed_grad = order.send_far(to_normed, qkv_grad)
    qkv_sum = slab_product(normed, qkv_grad)
    if square:
        qkv_sum = gate(qkv_sum, *normed_grad[3], *out_begun[1])
    qkv_sum = slab_sum(qkv_sum)
    normed_grad = order.make_rest(normed_grad)
    normed_grad = order.add_far(normed_grad)
    outcome = order.add_far(outcome)
    out_sum = order(
        lambda own, *came: summed(own, came or None).astype(low), out_begun[0], *(out_begun[1] or ())
    ).reshape(-1, 1, out_rows, model_width)
    zero = jnp.zeros_like(out_sum)
    out_sum = jnp.concatenate(
        [jnp.where(parity == 0, out_sum, zero), jnp.where(parity == 1, out_sum, zero)], axis=1
    ).reshape(-1, model_width)
    grad_w_out = lax.psum_scatter(out_sum, "fsdp", scatter_dimension=0, tiled=True).astype(wide)
    grad_tokens, _, input_sums = order(
        lambda rest, *came: norm_back(rest, x_low, middle_grad, ln1_gain, came),
        normed_grad[0],
        *(normed_grad[1] or ()),
    )
    grad_tokens = grad_tokens.reshape(tokens.shape)
    result = order(
        lambda own, *came: (middle + (summed(own, came or None) + down_bias)).astype(low),
        outcome[0],
        *(outcome[1] or ()),
    ).reshape(tokens.shape)
    sums = down_sum, up_sum
    if square:
        sums = gate(sums, *normed_grad[1])
    grad_w_down, grad_w_up = slabs_of_rows(*sums)
    grad_w_down = grad_w_down.reshape(-1, hidden_width).T
    grad_w_up = grad_w_up.reshape(-1, hidden_width)
    grad_w_qkv = slabs_of_rows(qkv_sum)[0].reshape(-1, groups, pairs, 3, PAIR)
    grad_w_qkv = jnp.transpose(grad_w_qkv, (0, 3, 1, 2, 4)).reshape(-1, 3 * model_width)

    head_sum = jnp.transpose(column_sum(qkv_grad).reshape(pairs, 3, PAIR), (1, 0, 2)).reshape(3, slab)
    qv_sum = lax.dynamic_update_slice_in_dim(
        jnp.zeros((2, model_width), wide), head_sum[0::2], me * slab, axis=1
    )
    late = [qv_sum.reshape(-1), input_sums[0], input_sums[1]]
    sums = total(jnp.concatenate(early + late).reshape(-1, PAIR)).reshape(-1)

    def cut(at, count):
        return sums[at * model_width : (at + count) * model_width]

    ratio = hidden_width // model_width
    return (
        result,
        grad_tokens,
        grad_w_qkv,
        cut(4 + ratio, 2).reshape(2, model_width),
        grad_w_out,
        cut(0, 1),
        cut(6 + ratio, 1),
        cut(7 + ratio, 1),
        cut(1, 1),
        cut(2, 1),
        grad_w_up,
        cut(3, ratio),
        grad_w_down,
        cut(3 + ratio, 1),
    )


def solution(mesh):
    return jax.shard_map(
        local,
        mesh=mesh,
        in_specs=(
            P("fsdp", "seq", None),
            P("fsdp", "seq", None),
            P("fsdp", None),
            P(),
            P("fsdp", None),
            P(),
            P(),
            P(),
            P(),
            P(),
            P("fsdp", None),
            P(),
            P(None, "fsdp"),
            P(),
        ),
        out_specs=(
            P("fsdp", "seq", None),
            P("fsdp", "seq", None),
            P(("seq", "fsdp"), None),
            P(),
            P(("seq", "fsdp"), None),
            P(),
            P(),
            P(),
            P(),
            P(),
            P(("seq", "fsdp"), None),
            P(),
            P(None, ("seq", "fsdp")),
            P(),
        ),
        check_vma=False,
    )
```

```python
import math
from functools import partial

import jax
import jax.numpy as jnp
from jax import lax
from jax.experimental import pallas as pl
from jax.experimental.pallas import tpu as pltpu
from jax.sharding import PartitionSpec as P

HEADS = 32
HEAD_DIM = 64
BLOCK = 256
PAIR = 2 * HEAD_DIM
GRANT = 58 * 2**20


def estimate(flops, transcendentals=0):
    return pl.CostEstimate(flops=flops // 4, bytes_accessed=flops // 4096, transcendentals=transcendentals // 4)


def layer_norm(token_rows, gain_vec, shift_vec):
    average = jnp.mean(token_rows, axis=-1, keepdims=True)
    centred = token_rows - average
    spread = jnp.mean(centred * centred, axis=-1, keepdims=True)
    return centred * lax.rsqrt(spread + 1e-05) * gain_vec + shift_vec


def contract(left_side, right_side):
    return lax.dot_general(
        left_side, right_side, (((1,), (0,)), ((), ())), preferred_element_type=jnp.float32
    )


def contract_last(left_side, right_side):
    return lax.dot_general(
        left_side, right_side, (((1,), (1,)), ((), ())), preferred_element_type=jnp.float32
    )


def contract_first(left_side, right_side):
    return lax.dot_general(
        left_side, right_side, (((0,), (0,)), ((), ())), preferred_element_type=jnp.float32
    )


def row_pieces(mask, sequence, block, seqs, local):
    per = BLOCK // local
    return [
        pl.ds(pl.multiple_of((((block * per + r) ^ mask) * seqs + sequence) * local, local), local)
        for r in range(per)
    ]


def load_rows(ref, pieces, columns):
    parts = [ref[piece, columns] for piece in pieces]
    return parts[0] if len(parts) == 1 else jnp.concatenate(parts, axis=0)


def store_rows(ref, pieces, columns, values):
    local = values.shape[0] // len(pieces)
    for r, piece in enumerate(pieces):
        ref[piece, columns] = values[r * local : (r + 1) * local]


Q_COLUMNS, K_COLUMNS, V_COLUMNS = (slice(t * PAIR, (t + 1) * PAIR) for t in range(3))


def attend_forward_kernel(mask_ref, slope_ref, qkv_ref, mixed_ref, lse_ref, *, blocks, seqs, local):
    pair, sequence = pl.program_id(0), pl.program_id(1)
    mask = mask_ref[0]
    lane = lax.broadcasted_iota(jnp.int32, (BLOCK, PAIR), 1)
    row = lax.broadcasted_iota(jnp.int32, (BLOCK, BLOCK), 0)
    column = lax.broadcasted_iota(jnp.int32, (BLOCK, BLOCK), 1)
    gap = (row - column).astype(jnp.float32)
    pieces = [row_pieces(mask, sequence, block, seqs, local) for block in range(blocks)]

    for i in range(blocks):
        q_pair = load_rows(qkv_ref, pieces[i], Q_COLUMNS)
        outs, lses = [], []
        for head in range(2):
            slope = slope_ref[pair * 2 + head]
            mine = (lane >= head * HEAD_DIM) & (lane < (head + 1) * HEAD_DIM)
            q = jnp.where(mine, q_pair, jnp.zeros_like(q_pair)) * jnp.bfloat16(HEAD_DIM**-0.5)
            parts, highest = [], None
            for j in range(i + 1):
                scores = contract_last(q, load_rows(qkv_ref, pieces[j], K_COLUMNS))
                distance = jnp.abs(gap) if i == j else gap + float(BLOCK * (i - j))
                scores = scores - slope * distance
                parts.append(scores)
                top = jnp.max(scores, axis=-1, keepdims=True)
                highest = top if highest is None else jnp.maximum(highest, top)
            total, out = None, None
            for j in range(i + 1):
                weights = jnp.exp(parts[j] - highest)
                part = jnp.sum(weights, axis=-1, keepdims=True)
                mixed = contract(weights.astype(jnp.bfloat16), load_rows(qkv_ref, pieces[j], V_COLUMNS))
                total = part if total is None else total + part
                out = mixed if out is None else out + mixed
            outs.append(out / total)
            lses.append(highest + jnp.log(total))
        first = lane < HEAD_DIM
        everything = slice(0, PAIR)
        store_rows(
            mixed_ref, pieces[i], everything, jnp.where(first, outs[0], outs[1]).astype(mixed_ref.dtype)
        )
        store_rows(lse_ref, pieces[i], everything, jnp.where(first, lses[0], lses[1]))


def attend_backward_kernel(
    mask_ref, slope_ref, qkv_ref, lse_ref, mixed_ref, grad_ref, *rest, blocks, seqs, local, start
):
    out_ref, dq_ref, dk_ref, dv_ref = rest[-4:]
    pair, sequence = pl.program_id(0) + start, pl.program_id(1)
    mask = mask_ref[0]
    lane = lax.broadcasted_iota(jnp.int32, (BLOCK, PAIR), 1)
    key = lax.broadcasted_iota(jnp.int32, (BLOCK, BLOCK), 0)
    query = lax.broadcasted_iota(jnp.int32, (BLOCK, BLOCK), 1)
    gap = (query - key).astype(jnp.float32)
    pieces = [row_pieces(mask, sequence, block, seqs, local) for block in range(blocks)]
    everything = slice(0, PAIR)

    for i in range(blocks):
        q_pair = load_rows(qkv_ref, pieces[i], Q_COLUMNS)
        up_pair = load_rows(grad_ref, pieces[i], everything)
        mixed_pair = load_rows(mixed_ref, pieces[i], everything)
        inner_all = (up_pair.astype(jnp.float32) * mixed_pair.astype(jnp.float32)).T
        lse_all = load_rows(lse_ref, pieces[i], everything).T
        dq = None
        for head in range(2):
            slope = slope_ref[pair * 2 + head]
            mine = (lane >= head * HEAD_DIM) & (lane < (head + 1) * HEAD_DIM)
            zero = jnp.zeros_like(q_pair)
            q = jnp.where(mine, q_pair, zero) * jnp.bfloat16(HEAD_DIM**-0.5)
            up = jnp.where(mine, up_pair, zero)
            inner = jnp.sum(inner_all[head * HEAD_DIM : (head + 1) * HEAD_DIM], axis=0, keepdims=True)
            lse = lse_all[head * HEAD_DIM : head * HEAD_DIM + 1]
            for j in range(i + 1):
                k_pair = load_rows(qkv_ref, pieces[j], K_COLUMNS)
                distance = jnp.abs(gap) if i == j else gap + float(BLOCK * (i - j))
                probs = jnp.exp(contract_last(k_pair, q) - slope * distance - lse)
                prob_grad = contract_last(load_rows(qkv_ref, pieces[j], V_COLUMNS), up)
                score_grad = (probs * (prob_grad - inner)).astype(jnp.bfloat16)
                dv = contract(probs.astype(jnp.bfloat16), up)
                dk = contract(score_grad, q)
                part = contract_first(score_grad, jnp.where(mine, k_pair, zero))
                dq = part if dq is None else dq + part
                if i == j and head == 0:
                    dv_ref[j] = dv
                    dk_ref[j] = dk
                else:
                    dv_ref[j] += dv
                    dk_ref[j] += dk
        dq_ref[i] = dq
    for i in range(blocks):
        store_rows(out_ref, pieces[i], Q_COLUMNS, (dq_ref[i] * HEAD_DIM**-0.5).astype(out_ref.dtype))
        store_rows(out_ref, pieces[i], K_COLUMNS, dk_ref[i].astype(out_ref.dtype))
        store_rows(out_ref, pieces[i], V_COLUMNS, dv_ref[i].astype(out_ref.dtype))


def attend_forward(mask, slopes, qkv, seqs, local):
    rows, width = qkv.shape
    pairs, blocks = width // (3 * PAIR), rows // seqs // BLOCK
    scored = pairs * seqs * blocks * (blocks + 1) * BLOCK * BLOCK
    return pl.pallas_call(
        partial(attend_forward_kernel, blocks=blocks, seqs=seqs, local=local),
        grid_spec=pltpu.PrefetchScalarGridSpec(
            num_scalar_prefetch=2,
            grid=(pairs, seqs),
            in_specs=[pl.BlockSpec((rows, 3 * PAIR), lambda p, *_: (0, p))],
            out_specs=[pl.BlockSpec((rows, PAIR), lambda p, *_: (0, p))] * 2,
        ),
        out_shape=[
            jax.ShapeDtypeStruct((rows, pairs * PAIR), jnp.bfloat16),
            jax.ShapeDtypeStruct((rows, pairs * PAIR), jnp.float32),
        ],
        compiler_params=pltpu.CompilerParams(vmem_limit_bytes=GRANT),
        cost_estimate=estimate(scored * 2 * 512, scored),
        name="attend_forward",
    )(mask, slopes, qkv)


def attend_backward(mask, slopes, qkv, lse, mixed, grad, seqs, local, start, stop, begun=None):
    rows, width = qkv.shape
    blocks = rows // seqs // BLOCK
    scored = (stop - start) * seqs * blocks * (blocks + 1) * BLOCK * BLOCK
    narrow = pl.BlockSpec((rows, PAIR), lambda p, *_: (0, p + start))
    wide = pl.BlockSpec((rows, 3 * PAIR), lambda p, *_: (0, p + start))
    earlier = [] if begun is None else [begun]
    return pl.pallas_call(
        partial(attend_backward_kernel, blocks=blocks, seqs=seqs, local=local, start=start),
        grid_spec=pltpu.PrefetchScalarGridSpec(
            num_scalar_prefetch=2,
            grid=(stop - start, seqs),
            in_specs=[wide, narrow, narrow, narrow] + [pl.BlockSpec(memory_space=pl.ANY)] * len(earlier),
            out_specs=wide,
            scratch_shapes=[pltpu.VMEM((blocks, BLOCK, PAIR), jnp.float32)] * 3,
        ),
        out_shape=jax.ShapeDtypeStruct((rows, width), jnp.bfloat16),
        input_output_aliases={6: 0} if earlier else {},
        compiler_params=pltpu.CompilerParams(vmem_limit_bytes=GRANT),
        cost_estimate=estimate(scored * 2 * 1280, scored),
        name="attend_backward",
    )(mask, slopes, qkv, lse, mixed, grad, *earlier)


def head_columns_kernel(at_ref, in_ref, out_ref):
    for t in range(3):

        @pl.when(pl.program_id(0) == t)
        def _():
            for pair in range(in_ref.shape[1] // PAIR):
                at = (pair * 3 + t) * PAIR
                out_ref[:, at : at + PAIR] = in_ref[:, pair * PAIR : (pair + 1) * PAIR]


def up_kernel(rows_ref, weight_ref, bias_ref, active_ref, slope_ref, *, chunk):
    rows = rows_ref[...]
    for at in range(0, weight_ref.shape[1], chunk):
        columns = slice(at, at + chunk)
        hidden = contract(rows, weight_ref[:, columns]) + bias_ref[:, columns]
        below = 0.5 + 0.5 * lax.erf(hidden * 2**-0.5)
        active_ref[:, columns] = (hidden * below).astype(active_ref.dtype)
        slope_ref[:, columns] = below + hidden * ((2 * math.pi) ** -0.5 * jnp.exp(-0.5 * hidden * hidden))


def hidden_grad_kernel(rows_ref, weight_ref, slope_ref, grad_ref, sum_ref, *, chunk):
    rows = rows_ref[...]
    starting = pl.program_id(0) == 0
    for at in range(0, weight_ref.shape[0], chunk):
        columns = slice(at, at + chunk)
        grad = contract_last(rows, weight_ref[columns, :]) * slope_ref[:, columns]
        grad = grad.astype(grad_ref.dtype)
        grad_ref[:, columns] = grad
        part = jnp.sum(grad.astype(jnp.float32), axis=0, keepdims=True)
        sum_ref[:, columns] = jnp.where(starting, part, sum_ref[:, columns] + part)


TILE = 256


def up_and_bend(rows, weight, bias):
    count, depth = rows.shape
    width = weight.shape[1]
    tile = pl.BlockSpec((TILE, width), lambda i: (i, 0))
    return pl.pallas_call(
        partial(up_kernel, chunk=512),
        grid=(count // TILE,),
        in_specs=[
            pl.BlockSpec((TILE, depth), lambda i: (i, 0)),
            pl.BlockSpec((depth, width), lambda i: (0, 0), pipeline_mode=pl.Buffered(1)),
            pl.BlockSpec((1, width), lambda i: (0, 0)),
        ],
        out_specs=[tile, tile],
        out_shape=[
            jax.ShapeDtypeStruct((count, width), jnp.bfloat16),
            jax.ShapeDtypeStruct((count, width), jnp.float32),
        ],
        compiler_params=pltpu.CompilerParams(vmem_limit_bytes=GRANT),
        cost_estimate=estimate(count * depth * width * 4, 2 * count * width),
        name="up_and_bend",
    )(rows, weight, bias)


def hidden_gradient(rows, weight, slope):
    count, depth = rows.shape
    width = weight.shape[0]
    tile = pl.BlockSpec((TILE, width), lambda i: (i, 0))
    line = pl.BlockSpec((1, width), lambda i: (0, 0))
    return pl.pallas_call(
        partial(hidden_grad_kernel, chunk=512),
        grid=(count // TILE,),
        in_specs=[
            pl.BlockSpec((TILE, depth), lambda i: (i, 0)),
            pl.BlockSpec((width, depth), lambda i: (0, 0), pipeline_mode=pl.Buffered(1)),
            tile,
        ],
        out_specs=[tile, line],
        out_shape=[
            jax.ShapeDtypeStruct((count, width), jnp.bfloat16),
            jax.ShapeDtypeStruct((1, width), jnp.float32),
        ],
        compiler_params=pltpu.CompilerParams(vmem_limit_bytes=GRANT),
        cost_estimate=estimate(count * depth * width * 3, 0),
        name="hidden_gradient",
    )(rows, weight, slope)


def norm_back_kernel(rest_ref, values_ref, base_ref, gain_ref, *refs, parts):
    came, (low_ref, wide_ref, sums_ref) = refs[:parts], refs[parts:]
    wide = jnp.float32
    starting = pl.program_id(0) == 0
    grad = rest_ref[...].astype(wide)
    for top, bottom in zip(came[0::2], came[1::2]):
        grad = grad + jnp.where(starting, top[...], bottom[...]).astype(wide)
    values = values_ref[...].astype(wide)
    base = base_ref[...].astype(wide)
    centred = values - jnp.mean(values, axis=-1, keepdims=True)
    scale = lax.rsqrt(jnp.mean(centred * centred, axis=-1, keepdims=True) + 1e-05)
    normal = centred * scale
    gained = grad * gain_ref[...]
    along = jnp.mean(gained * normal, axis=-1, keepdims=True)
    made = base + scale * (gained - jnp.mean(gained, axis=-1, keepdims=True) - normal * along)
    low = made.astype(low_ref.dtype)
    low_ref[...] = low
    wide_ref[...] = made
    for row, part in enumerate((grad * normal, grad, low.astype(wide), base)):
        line = jnp.sum(part, axis=0, keepdims=True)
        sums_ref[row : row + 1, :] = jnp.where(starting, line, sums_ref[row : row + 1, :] + line)


def norm_back(rest, values, base, gain, came):
    rows, width = values.shape
    half = rows // 2
    came = list(came or ())
    tile = pl.BlockSpec((half, width), lambda i: (i, 0))
    every = pl.BlockSpec((half, width), lambda i: (0, 0), pipeline_mode=pl.Buffered(1))
    return pl.pallas_call(
        partial(norm_back_kernel, parts=len(came)),
        grid=(2,),
        in_specs=[tile, tile, tile, pl.BlockSpec((1, width), lambda i: (0, 0))] + [every] * len(came),
        out_specs=[tile, tile, pl.BlockSpec((8, width), lambda i: (0, 0))],
        out_shape=[
            jax.ShapeDtypeStruct((rows, width), jnp.bfloat16),
            jax.ShapeDtypeStruct((rows, width), jnp.float32),
            jax.ShapeDtypeStruct((8, width), jnp.float32),
        ],
        compiler_params=pltpu.CompilerParams(vmem_limit_bytes=GRANT),
        cost_estimate=estimate(30 * rows * width, rows),
        name="norm_back",
    )(rest, values, base, gain[None], *came)


def outer_kernel(left_ref, right_ref, out_ref, *, chunk):
    left = left_ref[...]
    shards = out_ref.shape[0]
    for at in range(0, right_ref.shape[1], chunk):
        columns = slice(at, at + chunk)
        made = contract_first(left, right_ref[:, columns]).astype(out_ref.dtype)
        out_ref[:, 0, :, columns] = made.reshape(shards, -1, made.shape[1])


def outer(left, right, groups, shards):
    tokens, rows = left.shape
    width = right.shape[1]
    part = rows // groups
    made = pl.pallas_call(
        partial(outer_kernel, chunk=512 if width % 512 == 0 else 256),
        grid=(groups,),
        in_specs=[
            pl.BlockSpec((tokens, part), lambda i: (0, i)),
            pl.BlockSpec((tokens, width), lambda i: (0, 0), pipeline_mode=pl.Buffered(1)),
        ],
        out_specs=pl.BlockSpec((shards, 1, part // shards, width), lambda i: (0, i, 0, 0)),
        out_shape=jax.ShapeDtypeStruct((shards, groups, part // shards, width), jnp.bfloat16),
        compiler_params=pltpu.CompilerParams(vmem_limit_bytes=GRANT),
        cost_estimate=estimate(2 * tokens * rows * width, 0),
        name="outer",
    )(left, right)
    return made.reshape(rows, width)


def swap(values, bit):
    return lax.ppermute(values, "seq", [(i, i ^ bit) for i in range(4)])


def by_index(parts, me):
    if len(parts) != 4:
        return parts
    odd, upper = (me & 1) == 1, (me & 2) == 2
    a, b, c, d = parts
    a, b, c, d = (
        jnp.where(odd, b, a),
        jnp.where(odd, a, b),
        jnp.where(odd, d, c),
        jnp.where(odd, c, d),
    )
    return [jnp.where(upper, c, a), jnp.where(upper, d, b), jnp.where(upper, a, c), jnp.where(upper, b, d)]


def exchange(slots):
    if lax.axis_size("seq") != 4:
        return list(lax.all_to_all(jnp.stack(slots), "seq", split_axis=0, concat_axis=0, tiled=True))
    return [slots[0]] + [swap(slots[j], j) for j in (1, 2, 3)]


def gate(values, *before):
    return lax.optimization_barrier((values, *before))[0]


class Order:
    def __init__(self):
        self.pending = []

    def after(self, *values):
        self.pending += values

    def __call__(self, operation, *operands):
        if self.pending:
            count = len(operands)
            operands = lax.optimization_barrier((*operands, *self.pending))[:count]
        made = operation(*operands)
        self.pending = jax.tree.leaves(made)
        return made

    def gather(self, rows):
        if lax.axis_size("seq") != 4:
            return lax.all_gather(jnp.concatenate(rows, axis=0), "seq", axis=0, tiled=True), None
        top, bottom = rows
        return rows, (swap(bottom, 1), swap(top, 2), swap(top, 1), swap(bottom, 2))

    def fill(self, begun):
        rows, came = begun
        if came is None:
            return rows
        first_bottom, second_top, first_top, second_bottom = came
        room = jnp.zeros_like(rows[0])
        parts = (*rows, first_top, first_bottom, second_top, second_bottom, room, room)
        return self(lambda *parts: jnp.concatenate(parts, axis=0), *parts)

    def complete(self, made, pieces):
        if not isinstance(pieces, list):
            return made
        rows = pieces[-1].shape[0]

        def put(before, first, second):
            before = lax.dynamic_update_slice_in_dim(before, first, 6 * rows, axis=0)
            return lax.dynamic_update_slice_in_dim(before, second, 7 * rows, axis=0)

        return self(put, made, *pieces[-2:])

    def pass_on(self, begun, *before):
        rows, came = begun
        if came is None:
            return rows
        first_bottom, second_top, first_top, second_bottom = came
        self.after(*came)
        if before:
            second_top, first_bottom = gate((second_top, first_bottom), *before)
        far = [swap(second_top, 1), swap(first_bottom, 2)]
        return [*rows, first_top, first_bottom, second_top, second_bottom, *far]

    def send_far(self, product, rows, axis=0, held=False):
        if lax.axis_size("seq") != 4:
            return product, rows, axis, None
        count = rows.shape[axis] // 4

        def far_half(values):
            made = product(lax.slice_in_dim(values, 3 * count, 4 * count, axis=axis))
            half = made.shape[0] // 2
            return made[:half], made[half:]

        top, bottom = self(far_half, rows)
        return product, rows, axis, (top, bottom) if held else (swap(top, 1), swap(bottom, 2))

    def make_rest(self, begun, later=False):
        product, rows, axis, far = begun
        if far is None:
            return lax.psum_scatter(self(product, rows), "seq", scatter_dimension=0, tiled=True), None, None
        count = rows.shape[axis] // 4
        rest = self(lambda values: product(lax.slice_in_dim(values, 0, 3 * count, axis=axis)), rows)
        if later:
            return rest, far, None
        count = rest.shape[0] // 3
        half = count // 2
        return rest, far, (swap(rest[count : count + half], 1), swap(rest[2 * count + half :], 2))

    def send_direct(self, begun, *before):
        rest, far, _ = begun
        if far is None:
            return begun
        count = rest.shape[0] // 3
        half = count // 2
        first, second = gate((rest[count : count + half], rest[2 * count + half :]), *before)
        return rest, far, (swap(first, 1), swap(second, 2))

    def send_held(self, begun, *before):
        rest, far, direct = begun
        if far is not None:
            first, second = gate(far, *before)
            far = swap(first, 1), swap(second, 2)
        return rest, far, direct

    def add_far(self, begun, *before):
        rest, far, direct = begun
        if far is None:
            return rest, None
        wide = jnp.float32

        def add(rest, top, bottom):
            half = top.shape[0]
            first, second = rest[3 * half : 4 * half], rest[4 * half : 5 * half]
            first = (first.astype(wide) + bottom.astype(wide)).astype(rest.dtype)
            second = (second.astype(wide) + top.astype(wide)).astype(rest.dtype)
            if direct is None:
                first = jnp.concatenate([rest[2 * half : 3 * half], first], axis=0)
                second = jnp.concatenate([second, rest[5 * half :]], axis=0)
            return first, second

        first, second = self(add, rest, *far)
        if before:
            first, second = gate((first, second), *before)
        if direct is None:
            return rest, (swap(first, 1), swap(second, 2))
        return rest, (direct[0], swap(first, 1), swap(second, 2), direct[1])


def summed(rest, came):
    wide = jnp.float32
    if came is None:
        return rest.astype(wide)
    if len(came) == 2:
        return rest[: came[0].shape[0]].astype(wide) + came[0].astype(wide) + came[1].astype(wide)
    half = came[0].shape[0]
    first_top, first_bottom, second_top, second_bottom = (part.astype(wide) for part in came)
    top = rest[:half].astype(wide) + first_top + second_top
    bottom = rest[half : 2 * half].astype(wide) + first_bottom + second_bottom
    return jnp.concatenate([top, bottom], axis=0)


def whole(parts):
    return jnp.concatenate(parts, axis=0) if isinstance(parts, list) else parts


def total(values):
    for axis in ("fsdp", "seq"):
        count, bit = lax.axis_size(axis), 1
        bits = count.bit_length() - 1
        while bit < count:
            masks = [bit] if bits % 2 else [bit, 2 * bit, 3 * bit]
            came = [lax.ppermute(values, axis, [(i, i ^ mask) for i in range(count)]) for mask in masks]
            values = sum(came, values)
            bit <<= 1 if bits % 2 else 2
            bits -= bits % 2
    return values


def local(
    tokens,
    cotangent,
    w_qkv,
    qv_bias,
    w_out,
    out_bias,
    ln1_gain,
    ln1_shift,
    ln2_gain,
    ln2_shift,
    w_up,
    up_bias,
    w_down,
    down_bias,
):
    seq_count, local_len, model_width = tokens.shape
    groups, shards = lax.axis_size("seq"), lax.axis_size("fsdp")
    me = lax.axis_index("seq")
    square = groups == 4
    heads_here = HEADS // groups
    slab = heads_here * HEAD_DIM
    pairs = slab // PAIR
    hidden_width = w_up.shape[1]
    hidden_slab = hidden_width // groups
    rows_here = seq_count * local_len
    low, wide = jnp.bfloat16, jnp.float32
    mask = jnp.reshape(me if square else jnp.zeros_like(me), (1,)).astype(jnp.int32)
    head_index = me * heads_here + jnp.arange(1, heads_here + 1, dtype=jnp.int32)
    slopes = 2.0 ** (-8.0 * head_index.astype(wide) / HEADS)

    def head_columns(values):
        rows = values.shape[0]
        return pl.pallas_call(
            head_columns_kernel,
            grid_spec=pltpu.PrefetchScalarGridSpec(
                num_scalar_prefetch=1,
                grid=(3,),
                in_specs=[pl.BlockSpec((rows, slab), lambda t, at: (0, t * groups + at[0]))],
                out_specs=pl.BlockSpec((rows, 3 * slab), lambda t, at: (0, 0)),
            ),
            out_shape=jax.ShapeDtypeStruct((rows, 3 * slab), values.dtype),
            name="head_columns",
        )(jnp.reshape(me, (1,)).astype(jnp.int32), values)

    def own_slab(values, axis):
        width = values.shape[axis] // groups
        return lax.dynamic_slice_in_dim(values, me * width, width, axis=axis)

    order = Order()
    x_low = tokens.reshape(rows_here, model_width)
    x = x_low.astype(wide)
    dz_low = cotangent.reshape(rows_here, model_width)
    qkv_slab = lax.all_gather(head_columns(w_qkv), "fsdp", axis=0, tiled=True)
    qkv_bias = head_columns(jnp.concatenate([qv_bias[0], jnp.zeros_like(qv_bias[0]), qv_bias[1]])[None])
    up_bias_slab = own_slab(up_bias, 0)

    first_norm = layer_norm(x, ln1_gain, ln1_shift)
    half = rows_here // 2

    def halves_of(values):
        return values[:half].astype(low), values[half:].astype(low)

    normed = order.gather(order(halves_of, first_norm))
    normed = order.pass_on(normed)
    full_out = lax.all_gather(w_out, "fsdp", axis=0, tiled=True)
    up_slab = lax.all_gather(own_slab(gate(w_up, normed[0]) if square else w_up, 1), "fsdp", axis=0, tiled=True)
    down_slab = lax.all_gather(own_slab(gate(w_down, normed[0]) if square else w_down, 0), "fsdp", axis=1, tiled=True)
    normed = whole(normed)
    upstream = order.gather(halves_of(gate(dz_low, normed)))
    qkv = order(lambda rows: (contract(rows, qkv_slab) + qkv_bias).astype(low), normed)
    attended, log_totals = order(lambda rows: attend_forward(mask, slopes, rows, seq_count, local_len), qkv)
    if square:
        attended = gate(attended, *upstream[1])
    mixed_slots = exchange([attended[j * rows_here : (j + 1) * rows_here] for j in range(groups)])
    mixed_rows = jnp.concatenate(by_index(mixed_slots, me), axis=1)
    mixed_slots = jnp.concatenate(mixed_slots, axis=1)

    def pair_swap(values):
        return lax.ppermute(values, "fsdp", [(i, i ^ 1) for i in range(shards)])

    parity = lax.axis_index("fsdp") & 1
    out_rows = model_width // (groups * shards)

    def pair_halves(values):
        halves = values.reshape(rows_here, -1, 2, out_rows)
        return tuple(
            lax.dynamic_index_in_dim(halves, index, axis=2, keepdims=False).reshape(rows_here, -1)
            for index in (parity, 1 - parity)
        )

    middle = order(lambda rows: x + (contract(rows, full_out) + out_bias), mixed_rows)
    second_norm = layer_norm(middle, ln2_gain, ln2_shift)
    second = order.gather(order(halves_of, second_norm))
    mine, theirs = order(pair_halves, mixed_slots)
    upstream_made = order.fill(upstream)
    mixed_half = order(lambda *parts: jnp.concatenate(parts, axis=0), mine, pair_swap(theirs))
    second = whole(order.pass_on(second))
    upstream = order.pass_on(upstream, second)
    active, slope = order(lambda rows: up_and_bend(rows, up_slab, up_bias_slab[None]), second)
    upstream = order.complete(upstream_made, upstream)

    def slab_product(left, right):
        return order(lambda rows: outer(rows, right, groups, shards), left)

    def slab_sum(made):
        return lax.psum_scatter(made, "fsdp", scatter_dimension=0, tiled=True)

    def slabs_of_rows(*sums):
        parts = [part.reshape(groups, -1, part.shape[1]) for part in sums]
        slabs = lax.all_to_all(jnp.concatenate(parts, axis=1), "seq", split_axis=0, concat_axis=0, tiled=True)
        count = parts[0].shape[1]
        return [
            jnp.swapaxes(slabs[:, at : at + count], 0, 1).astype(wide) for at in range(0, slabs.shape[1], count)
        ]

    down_sum = slab_sum(slab_product(upstream, active))

    def to_result(rows):
        return contract(rows, down_slab).astype(low)

    outcome = order.send_far(to_result, active)
    hidden_grad, hidden_sum = order(lambda rows: hidden_gradient(rows, down_slab, slope), upstream)

    def to_second(rows):
        return contract_last(rows, up_slab).astype(low)

    if square:
        order.after(*outcome[3])
    second_grad = order.add_far(order.make_rest(order.send_far(to_second, hidden_grad)))
    outcome = order.make_rest(outcome, later=True)
    up_sum = slab_product(second, hidden_grad)
    if square:
        up_sum = gate(up_sum, *second_grad[1])
        outcome = order.send_direct(outcome, *second_grad[1])
    up_sum = slab_sum(up_sum)
    branch_grad, middle_grad, middle_sums = order(
        lambda rest, *came: norm_back(rest, middle, dz_low, ln2_gain, came), second_grad[0], *(second_grad[1] or ())
    )

    def column_sum(values):
        return jnp.sum(values.astype(wide), axis=0)

    hidden_sum = lax.dynamic_update_slice_in_dim(
        jnp.zeros((hidden_width,), wide), hidden_sum[0], me * hidden_slab, axis=0
    )
    early = [middle_sums[2], middle_sums[0], middle_sums[1], hidden_sum, middle_sums[3]]
    mixed_grad = order(lambda rows: contract_last(rows, full_out).astype(low), branch_grad)
    mixed_grad = exchange(by_index([mixed_grad[:, j * slab : (j + 1) * slab] for j in range(groups)], me))
    branch_pair = jnp.concatenate([branch_grad, pair_swap(branch_grad)], axis=0)
    out_sum = order(lambda columns: outer(columns, branch_pair, groups, 1), mixed_half)
    if square:
        order.after(*outcome[2])
    mixed_grad = order(lambda *parts: jnp.concatenate(parts, axis=0), *mixed_grad)
    if square:
        count = out_sum.shape[0] // 4
        far = out_sum[3 * count : 3 * count + count // 2], out_sum[3 * count + count // 2 :]
        out_begun = order.send_held((out_sum[: 3 * count], far, None), mixed_grad)
    else:
        out_begun = lax.psum_scatter(out_sum, "seq", scatter_dimension=0, tiled=True), None, None
    order.after(down_sum)
    attention = (mask, slopes, qkv, log_totals, attended)
    begun = order(lambda rows: attend_backward(*attention, rows, seq_count, local_len, 0, pairs // 2), mixed_grad)
    out_begun = order.add_far(out_begun)
    outcome = order.add_far(outcome, begun)
    qkv_grad = order(
        lambda rows: attend_backward(*attention, rows, seq_count, local_len, pairs // 2, pairs, begun), mixed_grad
    )
    if square:
        order.after(*out_begun[1])
    out_sum = order(
        lambda own, *came: summed(own, came or None).astype(low), out_begun[0], *(out_begun[1] or ())
    ).reshape(-1, 1, out_rows, model_width)
    zero = jnp.zeros_like(out_sum)
    out_sum = jnp.concatenate(
        [jnp.where(parity == 0, out_sum, zero), jnp.where(parity == 1, out_sum, zero)], axis=1
    ).reshape(-1, model_width)
    grad_w_out = lax.psum_scatter(out_sum, "fsdp", scatter_dimension=0, tiled=True).astype(wide)
    order.after(up_sum, *(out_begun[1] or ()))

    def to_normed(rows):
        return contract_last(rows, qkv_slab).astype(low)

    normed_grad = order.send_far(to_normed, qkv_grad)
    qkv_sum = slab_product(normed, qkv_grad)
    if square:
        qkv_sum = gate(qkv_sum, *normed_grad[3], *outcome[1])
    qkv_sum = slab_sum(qkv_sum)
    normed_grad = order.make_rest(normed_grad)
    normed_grad = order.add_far(normed_grad)
    grad_tokens, _, input_sums = order(
        lambda rest, *came: norm_back(rest, x_low, middle_grad, ln1_gain, came),
        normed_grad[0],
        *(normed_grad[1] or ()),
    )
    grad_tokens = grad_tokens.reshape(tokens.shape)
    result = order(
        lambda own, *came: (middle + (summed(own, came or None) + down_bias)).astype(low),
        outcome[0],
        *(outcome[1] or ()),
    ).reshape(tokens.shape)
    sums = down_sum, up_sum
    if square:
        sums = gate(sums, *normed_grad[1])
    grad_w_down, grad_w_up = slabs_of_rows(*sums)
    grad_w_down = grad_w_down.reshape(-1, hidden_width).T
    grad_w_up = grad_w_up.reshape(-1, hidden_width)
    grad_w_qkv = slabs_of_rows(qkv_sum)[0].reshape(-1, groups, pairs, 3, PAIR)
    grad_w_qkv = jnp.transpose(grad_w_qkv, (0, 3, 1, 2, 4)).reshape(-1, 3 * model_width)

    head_sum = jnp.transpose(column_sum(qkv_grad).reshape(pairs, 3, PAIR), (1, 0, 2)).reshape(3, slab)
    qv_sum = lax.dynamic_update_slice_in_dim(
        jnp.zeros((2, model_width), wide), head_sum[0::2], me * slab, axis=1
    )
    late = [qv_sum.reshape(-1), input_sums[0], input_sums[1]]
    sums = total(jnp.concatenate(early + late).reshape(-1, PAIR)).reshape(-1)

    def cut(at, count):
        return sums[at * model_width : (at + count) * model_width]

    ratio = hidden_width // model_width
    return (
        result,
        grad_tokens,
        grad_w_qkv,
        cut(4 + ratio, 2).reshape(2, model_width),
        grad_w_out,
        cut(0, 1),
        cut(6 + ratio, 1),
        cut(7 + ratio, 1),
        cut(1, 1),
        cut(2, 1),
        grad_w_up,
        cut(3, ratio),
        grad_w_down,
        cut(3 + ratio, 1),
    )


def solution(mesh):
    return jax.shard_map(
        local,
        mesh=mesh,
        in_specs=(
            P("fsdp", "seq", None),
            P("fsdp", "seq", None),
            P("fsdp", None),
            P(),
            P("fsdp", None),
            P(),
            P(),
            P(),
            P(),
            P(),
            P("fsdp", None),
            P(),
            P(None, "fsdp"),
            P(),
        ),
        out_specs=(
            P("fsdp", "seq", None),
            P("fsdp", "seq", None),
            P(("seq", "fsdp"), None),
            P(),
            P(("seq", "fsdp"), None),
            P(),
            P(),
            P(),
            P(),
            P(),
            P(("seq", "fsdp"), None),
            P(),
            P(None, ("seq", "fsdp")),
            P(),
        ),
        check_vma=False,
    )
```

```python
import math
from functools import partial

import jax
import jax.numpy as jnp
from jax import lax
from jax.experimental import pallas as pl
from jax.experimental.pallas import tpu as pltpu
from jax.sharding import PartitionSpec as P

HEADS = 32
HEAD_DIM = 64
BLOCK = 256
PAIR = 2 * HEAD_DIM
GRANT = 58 * 2**20


def estimate(flops, transcendentals=0):
    return pl.CostEstimate(flops=flops // 4, bytes_accessed=flops // 4096, transcendentals=transcendentals // 4)


def layer_norm(token_rows, gain_vec, shift_vec):
    average = jnp.mean(token_rows, axis=-1, keepdims=True)
    centred = token_rows - average
    spread = jnp.mean(centred * centred, axis=-1, keepdims=True)
    return centred * lax.rsqrt(spread + 1e-05) * gain_vec + shift_vec


def contract(left_side, right_side):
    return lax.dot_general(
        left_side, right_side, (((1,), (0,)), ((), ())), preferred_element_type=jnp.float32
    )


def contract_last(left_side, right_side):
    return lax.dot_general(
        left_side, right_side, (((1,), (1,)), ((), ())), preferred_element_type=jnp.float32
    )


def contract_first(left_side, right_side):
    return lax.dot_general(
        left_side, right_side, (((0,), (0,)), ((), ())), preferred_element_type=jnp.float32
    )


def row_pieces(mask, sequence, block, seqs, local):
    per = BLOCK // local
    return [
        pl.ds(pl.multiple_of((((block * per + r) ^ mask) * seqs + sequence) * local, local), local)
        for r in range(per)
    ]


def load_rows(ref, pieces, columns):
    parts = [ref[piece, columns] for piece in pieces]
    return parts[0] if len(parts) == 1 else jnp.concatenate(parts, axis=0)


def store_rows(ref, pieces, columns, values):
    local = values.shape[0] // len(pieces)
    for r, piece in enumerate(pieces):
        ref[piece, columns] = values[r * local : (r + 1) * local]


Q_COLUMNS, K_COLUMNS, V_COLUMNS = (slice(t * PAIR, (t + 1) * PAIR) for t in range(3))


def attend_forward_kernel(mask_ref, slope_ref, qkv_ref, mixed_ref, lse_ref, *, blocks, seqs, local):
    pair, sequence = pl.program_id(0), pl.program_id(1)
    mask = mask_ref[0]
    lane = lax.broadcasted_iota(jnp.int32, (BLOCK, PAIR), 1)
    row = lax.broadcasted_iota(jnp.int32, (BLOCK, BLOCK), 0)
    column = lax.broadcasted_iota(jnp.int32, (BLOCK, BLOCK), 1)
    gap = (row - column).astype(jnp.float32)
    pieces = [row_pieces(mask, sequence, block, seqs, local) for block in range(blocks)]

    for i in range(blocks):
        q_pair = load_rows(qkv_ref, pieces[i], Q_COLUMNS)
        outs, lses = [], []
        for head in range(2):
            slope = slope_ref[pair * 2 + head]
            mine = (lane >= head * HEAD_DIM) & (lane < (head + 1) * HEAD_DIM)
            q = jnp.where(mine, q_pair, jnp.zeros_like(q_pair)) * jnp.bfloat16(HEAD_DIM**-0.5)
            parts, highest = [], None
            for j in range(i + 1):
                scores = contract_last(q, load_rows(qkv_ref, pieces[j], K_COLUMNS))
                distance = jnp.abs(gap) if i == j else gap + float(BLOCK * (i - j))
                scores = scores - slope * distance
                parts.append(scores)
                top = jnp.max(scores, axis=-1, keepdims=True)
                highest = top if highest is None else jnp.maximum(highest, top)
            total, out = None, None
            for j in range(i + 1):
                weights = jnp.exp(parts[j] - highest)
                part = jnp.sum(weights, axis=-1, keepdims=True)
                mixed = contract(weights.astype(jnp.bfloat16), load_rows(qkv_ref, pieces[j], V_COLUMNS))
                total = part if total is None else total + part
                out = mixed if out is None else out + mixed
            outs.append(out / total)
            lses.append(highest + jnp.log(total))
        first = lane < HEAD_DIM
        everything = slice(0, PAIR)
        store_rows(
            mixed_ref, pieces[i], everything, jnp.where(first, outs[0], outs[1]).astype(mixed_ref.dtype)
        )
        store_rows(lse_ref, pieces[i], everything, jnp.where(first, lses[0], lses[1]))


def attend_backward_kernel(
    mask_ref, slope_ref, qkv_ref, lse_ref, mixed_ref, grad_ref, *rest, blocks, seqs, local, start
):
    out_ref, dq_ref, dk_ref, dv_ref = rest[-4:]
    pair, sequence = pl.program_id(0) + start, pl.program_id(1)
    mask = mask_ref[0]
    lane = lax.broadcasted_iota(jnp.int32, (BLOCK, PAIR), 1)
    key = lax.broadcasted_iota(jnp.int32, (BLOCK, BLOCK), 0)
    query = lax.broadcasted_iota(jnp.int32, (BLOCK, BLOCK), 1)
    gap = (query - key).astype(jnp.float32)
    pieces = [row_pieces(mask, sequence, block, seqs, local) for block in range(blocks)]
    everything = slice(0, PAIR)

    for i in range(blocks):
        q_pair = load_rows(qkv_ref, pieces[i], Q_COLUMNS)
        up_pair = load_rows(grad_ref, pieces[i], everything)
        mixed_pair = load_rows(mixed_ref, pieces[i], everything)
        inner_all = (up_pair.astype(jnp.float32) * mixed_pair.astype(jnp.float32)).T
        lse_all = load_rows(lse_ref, pieces[i], everything).T
        dq = None
        for head in range(2):
            slope = slope_ref[pair * 2 + head]
            mine = (lane >= head * HEAD_DIM) & (lane < (head + 1) * HEAD_DIM)
            zero = jnp.zeros_like(q_pair)
            q = jnp.where(mine, q_pair, zero) * jnp.bfloat16(HEAD_DIM**-0.5)
            up = jnp.where(mine, up_pair, zero)
            inner = jnp.sum(inner_all[head * HEAD_DIM : (head + 1) * HEAD_DIM], axis=0, keepdims=True)
            lse = lse_all[head * HEAD_DIM : head * HEAD_DIM + 1]
            for j in range(i + 1):
                k_pair = load_rows(qkv_ref, pieces[j], K_COLUMNS)
                distance = jnp.abs(gap) if i == j else gap + float(BLOCK * (i - j))
                probs = jnp.exp(contract_last(k_pair, q) - slope * distance - lse)
                prob_grad = contract_last(load_rows(qkv_ref, pieces[j], V_COLUMNS), up)
                score_grad = (probs * (prob_grad - inner)).astype(jnp.bfloat16)
                dv = contract(probs.astype(jnp.bfloat16), up)
                dk = contract(score_grad, q)
                part = contract_first(score_grad, jnp.where(mine, k_pair, zero))
                dq = part if dq is None else dq + part
                if i == j and head == 0:
                    dv_ref[j] = dv
                    dk_ref[j] = dk
                else:
                    dv_ref[j] += dv
                    dk_ref[j] += dk
        dq_ref[i] = dq
    for i in range(blocks):
        store_rows(out_ref, pieces[i], Q_COLUMNS, (dq_ref[i] * HEAD_DIM**-0.5).astype(out_ref.dtype))
        store_rows(out_ref, pieces[i], K_COLUMNS, dk_ref[i].astype(out_ref.dtype))
        store_rows(out_ref, pieces[i], V_COLUMNS, dv_ref[i].astype(out_ref.dtype))


def attend_forward(mask, slopes, qkv, seqs, local):
    rows, width = qkv.shape
    pairs, blocks = width // (3 * PAIR), rows // seqs // BLOCK
    scored = pairs * seqs * blocks * (blocks + 1) * BLOCK * BLOCK
    return pl.pallas_call(
        partial(attend_forward_kernel, blocks=blocks, seqs=seqs, local=local),
        grid_spec=pltpu.PrefetchScalarGridSpec(
            num_scalar_prefetch=2,
            grid=(pairs, seqs),
            in_specs=[pl.BlockSpec((rows, 3 * PAIR), lambda p, *_: (0, p))],
            out_specs=[pl.BlockSpec((rows, PAIR), lambda p, *_: (0, p))] * 2,
        ),
        out_shape=[
            jax.ShapeDtypeStruct((rows, pairs * PAIR), jnp.bfloat16),
            jax.ShapeDtypeStruct((rows, pairs * PAIR), jnp.float32),
        ],
        compiler_params=pltpu.CompilerParams(vmem_limit_bytes=GRANT),
        cost_estimate=estimate(scored * 2 * 512, scored),
        name="attend_forward",
    )(mask, slopes, qkv)


def attend_backward(mask, slopes, qkv, lse, mixed, grad, seqs, local, start, stop, begun=None):
    rows, width = qkv.shape
    blocks = rows // seqs // BLOCK
    scored = (stop - start) * seqs * blocks * (blocks + 1) * BLOCK * BLOCK
    narrow = pl.BlockSpec((rows, PAIR), lambda p, *_: (0, p + start))
    wide = pl.BlockSpec((rows, 3 * PAIR), lambda p, *_: (0, p + start))
    earlier = [] if begun is None else [begun]
    return pl.pallas_call(
        partial(attend_backward_kernel, blocks=blocks, seqs=seqs, local=local, start=start),
        grid_spec=pltpu.PrefetchScalarGridSpec(
            num_scalar_prefetch=2,
            grid=(stop - start, seqs),
            in_specs=[wide, narrow, narrow, narrow] + [pl.BlockSpec(memory_space=pl.ANY)] * len(earlier),
            out_specs=wide,
            scratch_shapes=[pltpu.VMEM((blocks, BLOCK, PAIR), jnp.float32)] * 3,
        ),
        out_shape=jax.ShapeDtypeStruct((rows, width), jnp.bfloat16),
        input_output_aliases={6: 0} if earlier else {},
        compiler_params=pltpu.CompilerParams(vmem_limit_bytes=GRANT),
        cost_estimate=estimate(scored * 2 * 1280, scored),
        name="attend_backward",
    )(mask, slopes, qkv, lse, mixed, grad, *earlier)


def head_columns_kernel(at_ref, in_ref, out_ref):
    for t in range(3):

        @pl.when(pl.program_id(0) == t)
        def _():
            for pair in range(in_ref.shape[1] // PAIR):
                at = (pair * 3 + t) * PAIR
                out_ref[:, at : at + PAIR] = in_ref[:, pair * PAIR : (pair + 1) * PAIR]


def up_kernel(rows_ref, weight_ref, bias_ref, active_ref, slope_ref, *, chunk):
    rows = rows_ref[...]
    for at in range(0, weight_ref.shape[1], chunk):
        columns = slice(at, at + chunk)
        hidden = contract(rows, weight_ref[:, columns]) + bias_ref[:, columns]
        below = 0.5 + 0.5 * lax.erf(hidden * 2**-0.5)
        active_ref[:, columns] = (hidden * below).astype(active_ref.dtype)
        slope_ref[:, columns] = below + hidden * ((2 * math.pi) ** -0.5 * jnp.exp(-0.5 * hidden * hidden))


def hidden_grad_kernel(rows_ref, weight_ref, slope_ref, grad_ref, sum_ref, *, chunk):
    rows = rows_ref[...]
    starting = pl.program_id(0) == 0
    for at in range(0, weight_ref.shape[0], chunk):
        columns = slice(at, at + chunk)
        grad = contract_last(rows, weight_ref[columns, :]) * slope_ref[:, columns]
        grad = grad.astype(grad_ref.dtype)
        grad_ref[:, columns] = grad
        part = jnp.sum(grad.astype(jnp.float32), axis=0, keepdims=True)
        sum_ref[:, columns] = jnp.where(starting, part, sum_ref[:, columns] + part)


TILE = 256


def up_and_bend(rows, weight, bias):
    count, depth = rows.shape
    width = weight.shape[1]
    tile = pl.BlockSpec((TILE, width), lambda i: (i, 0))
    return pl.pallas_call(
        partial(up_kernel, chunk=512),
        grid=(count // TILE,),
        in_specs=[
            pl.BlockSpec((TILE, depth), lambda i: (i, 0)),
            pl.BlockSpec((depth, width), lambda i: (0, 0), pipeline_mode=pl.Buffered(1)),
            pl.BlockSpec((1, width), lambda i: (0, 0)),
        ],
        out_specs=[tile, tile],
        out_shape=[
            jax.ShapeDtypeStruct((count, width), jnp.bfloat16),
            jax.ShapeDtypeStruct((count, width), jnp.float32),
        ],
        compiler_params=pltpu.CompilerParams(vmem_limit_bytes=GRANT),
        cost_estimate=estimate(count * depth * width * 4, 2 * count * width),
        name="up_and_bend",
    )(rows, weight, bias)


def hidden_gradient(rows, weight, slope, start, count):
    depth = rows.shape[1]
    width = weight.shape[0]
    first = start // TILE
    line = pl.BlockSpec((1, width), lambda i: (0, 0))
    return pl.pallas_call(
        partial(hidden_grad_kernel, chunk=512),
        grid=(count // TILE,),
        in_specs=[
            pl.BlockSpec((TILE, depth), lambda i: (i + first, 0)),
            pl.BlockSpec((width, depth), lambda i: (0, 0), pipeline_mode=pl.Buffered(1)),
            pl.BlockSpec((TILE, width), lambda i: (i + first, 0)),
        ],
        out_specs=[pl.BlockSpec((TILE, width), lambda i: (i, 0)), line],
        out_shape=[
            jax.ShapeDtypeStruct((count, width), jnp.bfloat16),
            jax.ShapeDtypeStruct((1, width), jnp.float32),
        ],
        compiler_params=pltpu.CompilerParams(vmem_limit_bytes=GRANT),
        cost_estimate=estimate(count * depth * width * 3, 0),
        name="hidden_gradient",
    )(rows, weight, slope)


def norm_back_kernel(rest_ref, values_ref, base_ref, gain_ref, *refs, parts):
    came, (low_ref, wide_ref, sums_ref) = refs[:parts], refs[parts:]
    wide = jnp.float32
    step = pl.program_id(0)
    upper = step < pl.num_programs(0) // 2
    grad = rest_ref[...].astype(wide)
    for top, bottom in zip(came[0::2], came[1::2]):
        grad = grad + jnp.where(upper, top[...], bottom[...]).astype(wide)
    values = values_ref[...].astype(wide)
    base = base_ref[...].astype(wide)
    centred = values - jnp.mean(values, axis=-1, keepdims=True)
    scale = lax.rsqrt(jnp.mean(centred * centred, axis=-1, keepdims=True) + 1e-05)
    normal = centred * scale
    gained = grad * gain_ref[...]
    along = jnp.mean(gained * normal, axis=-1, keepdims=True)
    made = base + scale * (gained - jnp.mean(gained, axis=-1, keepdims=True) - normal * along)
    low = made.astype(low_ref.dtype)
    low_ref[...] = low
    wide_ref[...] = made
    for row, part in enumerate((grad * normal, grad, low.astype(wide), base)):
        line = jnp.sum(part, axis=0, keepdims=True)
        sums_ref[row : row + 1, :] = jnp.where(step == 0, line, sums_ref[row : row + 1, :] + line)


def norm_back(rest, values, base, gain, came):
    rows, width = values.shape
    steps = 8
    half = steps // 2
    came = list(came or ())
    count = rows // steps
    tile = pl.BlockSpec((count, width), lambda i: (i, 0))
    top = pl.BlockSpec((count, width), lambda i: (jnp.minimum(i, half - 1), 0))
    bottom = pl.BlockSpec((count, width), lambda i: (jnp.maximum(i - half, 0), 0))
    return pl.pallas_call(
        partial(norm_back_kernel, parts=len(came)),
        grid=(steps,),
        in_specs=[tile, tile, tile, pl.BlockSpec((1, width), lambda i: (0, 0))] + [top, bottom] * (len(came) // 2),
        out_specs=[tile, tile, pl.BlockSpec((8, width), lambda i: (0, 0))],
        out_shape=[
            jax.ShapeDtypeStruct((rows, width), jnp.bfloat16),
            jax.ShapeDtypeStruct((rows, width), jnp.float32),
            jax.ShapeDtypeStruct((8, width), jnp.float32),
        ],
        compiler_params=pltpu.CompilerParams(vmem_limit_bytes=GRANT),
        cost_estimate=estimate(30 * rows * width, rows),
        name="norm_back",
    )(rest, values, base, gain[None], *came)


def outer_kernel(left_ref, *refs, chunk):
    right_refs, out_ref = refs[:-1], refs[-1]
    shards = out_ref.shape[0]
    for at in range(0, out_ref.shape[3], chunk):
        columns = slice(at, at + chunk)
        made, row = None, 0
        for right_ref in right_refs:
            count = right_ref.shape[0]
            part = contract_first(left_ref[row : row + count, :], right_ref[:, columns])
            made = part if made is None else made + part
            row += count
        out_ref[:, 0, :, columns] = made.astype(out_ref.dtype).reshape(shards, -1, made.shape[1])


def outer(left, rights, groups, shards):
    rights = rights if isinstance(rights, (list, tuple)) else [rights]
    tokens, rows = left.shape
    width = rights[0].shape[1]
    part = rows // groups
    made = pl.pallas_call(
        partial(outer_kernel, chunk=512 if width % 512 == 0 else 256),
        grid=(groups,),
        in_specs=[pl.BlockSpec((tokens, part), lambda i: (0, i))]
        + [
            pl.BlockSpec((right.shape[0], width), lambda i: (0, 0), pipeline_mode=pl.Buffered(1))
            for right in rights
        ],
        out_specs=pl.BlockSpec((shards, 1, part // shards, width), lambda i: (0, i, 0, 0)),
        out_shape=jax.ShapeDtypeStruct((shards, groups, part // shards, width), jnp.bfloat16),
        compiler_params=pltpu.CompilerParams(vmem_limit_bytes=GRANT),
        cost_estimate=estimate(2 * tokens * rows * width, 0),
        name="outer",
    )(left, *rights)
    return made.reshape(rows, width)


def swap(values, bit):
    return lax.ppermute(values, "seq", [(i, i ^ bit) for i in range(4)])


def by_index(parts, me):
    if len(parts) != 4:
        return parts
    odd, upper = (me & 1) == 1, (me & 2) == 2
    a, b, c, d = parts
    a, b, c, d = (
        jnp.where(odd, b, a),
        jnp.where(odd, a, b),
        jnp.where(odd, d, c),
        jnp.where(odd, c, d),
    )
    return [jnp.where(upper, c, a), jnp.where(upper, d, b), jnp.where(upper, a, c), jnp.where(upper, b, d)]


def exchange(slots):
    if lax.axis_size("seq") != 4:
        return list(lax.all_to_all(jnp.stack(slots), "seq", split_axis=0, concat_axis=0, tiled=True))
    return [slots[0]] + [swap(slots[j], j) for j in (1, 2, 3)]


def gate(values, *before):
    return lax.optimization_barrier((values, *before))[0]


class Order:
    def __init__(self):
        self.pending = []

    def after(self, *values):
        self.pending += values

    def __call__(self, operation, *operands):
        if self.pending:
            count = len(operands)
            operands = lax.optimization_barrier((*operands, *self.pending))[:count]
        made = operation(*operands)
        self.pending = jax.tree.leaves(made)
        return made

    def gather(self, rows):
        if lax.axis_size("seq") != 4:
            return lax.all_gather(jnp.concatenate(rows, axis=0), "seq", axis=0, tiled=True), None
        top, bottom = rows
        return rows, (swap(bottom, 1), swap(top, 2), swap(top, 1), swap(bottom, 2))

    def fill(self, begun):
        rows, came = begun
        if came is None:
            return rows
        first_bottom, second_top, first_top, second_bottom = came
        room = jnp.zeros_like(rows[0])
        parts = (*rows, first_top, first_bottom, second_top, second_bottom, room, room)
        return self(lambda *parts: jnp.concatenate(parts, axis=0), *parts)

    def complete(self, made, pieces):
        if not isinstance(pieces, list):
            return made
        rows = pieces[-1].shape[0]

        def put(before, first, second):
            before = lax.dynamic_update_slice_in_dim(before, first, 6 * rows, axis=0)
            return lax.dynamic_update_slice_in_dim(before, second, 7 * rows, axis=0)

        return self(put, made, *pieces[-2:])

    def pass_on(self, begun, *before):
        rows, came = begun
        if came is None:
            return rows
        first_bottom, second_top, first_top, second_bottom = came
        self.after(*came)
        if before:
            second_top, first_bottom = gate((second_top, first_bottom), *before)
        far = [swap(second_top, 1), swap(first_bottom, 2)]
        return [*rows, first_top, first_bottom, second_top, second_bottom, *far]

    def halves(self, product, rows):
        def cut(values):
            made = product(values)
            half = made.shape[0] // 2
            return made[:half], made[half:]

        return self(cut, rows)

    def add_far(self, near, far, direct, *before):
        wide = jnp.float32

        def add(near, top, bottom):
            half = top.shape[0]
            first = (near[half : 2 * half].astype(wide) + bottom.astype(wide)).astype(near.dtype)
            second = (near[2 * half : 3 * half].astype(wide) + top.astype(wide)).astype(near.dtype)
            if direct is None:
                first = jnp.concatenate([near[:half], first], axis=0)
                second = jnp.concatenate([second, near[3 * half :]], axis=0)
            return first, second

        first, second = self(add, near, *far)
        if before:
            first, second = gate((first, second), *before)
        first, second = swap(first, 1), swap(second, 2)
        return (first, second) if direct is None else (direct[0], first, second, direct[1])


def swap_far(halves):
    return swap(halves[0], 1), swap(halves[1], 2)


def swap_direct(near):
    half = near.shape[0] // 4
    return swap(near[:half], 1), swap(near[3 * half :], 2)


def summed(own, came):
    wide = jnp.float32
    own = own.astype(wide)
    return sum((part.astype(wide) for part in came), own)


def whole(parts):
    return jnp.concatenate(parts, axis=0) if isinstance(parts, list) else parts


def total(values):
    for axis in ("fsdp", "seq"):
        count, bit = lax.axis_size(axis), 1
        bits = count.bit_length() - 1
        while bit < count:
            masks = [bit] if bits % 2 else [bit, 2 * bit, 3 * bit]
            came = [lax.ppermute(values, axis, [(i, i ^ mask) for i in range(count)]) for mask in masks]
            values = sum(came, values)
            bit <<= 1 if bits % 2 else 2
            bits -= bits % 2
    return values


def local(
    tokens,
    cotangent,
    w_qkv,
    qv_bias,
    w_out,
    out_bias,
    ln1_gain,
    ln1_shift,
    ln2_gain,
    ln2_shift,
    w_up,
    up_bias,
    w_down,
    down_bias,
):
    seq_count, local_len, model_width = tokens.shape
    groups, shards = lax.axis_size("seq"), lax.axis_size("fsdp")
    me = lax.axis_index("seq")
    square = groups == 4
    heads_here = HEADS // groups
    slab = heads_here * HEAD_DIM
    pairs = slab // PAIR
    hidden_width = w_up.shape[1]
    hidden_slab = hidden_width // groups
    rows_here = seq_count * local_len
    low, wide = jnp.bfloat16, jnp.float32
    mask = jnp.reshape(me if square else jnp.zeros_like(me), (1,)).astype(jnp.int32)
    head_index = me * heads_here + jnp.arange(1, heads_here + 1, dtype=jnp.int32)
    slopes = 2.0 ** (-8.0 * head_index.astype(wide) / HEADS)

    def head_columns(values):
        rows = values.shape[0]
        return pl.pallas_call(
            head_columns_kernel,
            grid_spec=pltpu.PrefetchScalarGridSpec(
                num_scalar_prefetch=1,
                grid=(3,),
                in_specs=[pl.BlockSpec((rows, slab), lambda t, at: (0, t * groups + at[0]))],
                out_specs=pl.BlockSpec((rows, 3 * slab), lambda t, at: (0, 0)),
            ),
            out_shape=jax.ShapeDtypeStruct((rows, 3 * slab), values.dtype),
            name="head_columns",
        )(jnp.reshape(me, (1,)).astype(jnp.int32), values)

    def own_slab(values, axis):
        width = values.shape[axis] // groups
        return lax.dynamic_slice_in_dim(values, me * width, width, axis=axis)

    order = Order()
    x_low = tokens.reshape(rows_here, model_width)
    x = x_low.astype(wide)
    dz_low = cotangent.reshape(rows_here, model_width)
    qkv_slab = lax.all_gather(head_columns(w_qkv), "fsdp", axis=0, tiled=True)
    qkv_bias = head_columns(jnp.concatenate([qv_bias[0], jnp.zeros_like(qv_bias[0]), qv_bias[1]])[None])
    up_bias_slab = own_slab(up_bias, 0)

    first_norm = layer_norm(x, ln1_gain, ln1_shift)
    half = rows_here // 2

    def halves_of(values):
        return values[:half].astype(low), values[half:].astype(low)

    normed = order.gather(order(halves_of, first_norm))
    normed = order.pass_on(normed)
    full_out = lax.all_gather(w_out, "fsdp", axis=0, tiled=True)
    up_slab = lax.all_gather(own_slab(gate(w_up, normed[0]) if square else w_up, 1), "fsdp", axis=0, tiled=True)
    down_slab = lax.all_gather(own_slab(gate(w_down, normed[0]) if square else w_down, 0), "fsdp", axis=1, tiled=True)
    normed = whole(normed)
    upstream = order.gather(halves_of(gate(dz_low, normed)))
    qkv = order(lambda rows: (contract(rows, qkv_slab) + qkv_bias).astype(low), normed)
    attended, log_totals = order(lambda rows: attend_forward(mask, slopes, rows, seq_count, local_len), qkv)
    if square:
        attended = gate(attended, *upstream[1])
    mixed_slots = exchange([attended[j * rows_here : (j + 1) * rows_here] for j in range(groups)])
    mixed_rows = jnp.concatenate(by_index(mixed_slots, me), axis=1)
    mixed_slots = jnp.concatenate(mixed_slots, axis=1)

    def pair_swap(values):
        return lax.ppermute(values, "fsdp", [(i, i ^ 1) for i in range(shards)])

    parity = lax.axis_index("fsdp") & 1
    out_rows = model_width // (groups * shards)

    def pair_halves(values):
        halves = values.reshape(rows_here, -1, 2, out_rows)
        return tuple(
            lax.dynamic_index_in_dim(halves, index, axis=2, keepdims=False).reshape(rows_here, -1)
            for index in (parity, 1 - parity)
        )

    middle = order(lambda rows: x + (contract(rows, full_out) + out_bias), mixed_rows)
    second_norm = layer_norm(middle, ln2_gain, ln2_shift)
    second = order.gather(order(halves_of, second_norm))
    mine, theirs = order(pair_halves, mixed_slots)
    upstream_made = order.fill(upstream)
    mixed_half = order(lambda *parts: jnp.concatenate(parts, axis=0), mine, pair_swap(theirs))
    second = whole(order.pass_on(second))
    upstream = order.pass_on(upstream, second)
    active, slope = order(lambda rows: up_and_bend(rows, up_slab, up_bias_slab[None]), second)
    upstream = order.complete(upstream_made, upstream)

    def slab_product(left, right):
        return order(lambda rows: outer(rows, right, groups, shards), left)

    def slab_sum(made):
        return lax.psum_scatter(made, "fsdp", scatter_dimension=0, tiled=True)

    def slabs_of_rows(*sums):
        parts = [part.reshape(groups, -1, part.shape[1]) for part in sums]
        slabs = lax.all_to_all(jnp.concatenate(parts, axis=1), "seq", split_axis=0, concat_axis=0, tiled=True)
        count = parts[0].shape[1]
        return [
            jnp.swapaxes(slabs[:, at : at + count], 0, 1).astype(wide) for at in range(0, slabs.shape[1], count)
        ]

    down_sum = slab_sum(slab_product(upstream, active))
    count = rows_here

    def slots(values, start, stop):
        return values[start * count : stop * count]

    def to_hidden(start, stop):
        return order(
            lambda rows: hidden_gradient(rows, down_slab, slope, start * count, (stop - start) * count), upstream
        )

    def to_second(rows):
        return contract_last(rows, up_slab).astype(low)

    def to_result(rows):
        return contract(rows, down_slab).astype(low)

    def to_normed(rows):
        return contract_last(rows, qkv_slab).astype(low)

    def scatter(product, rows):
        return lax.psum_scatter(order(product, rows), "seq", scatter_dimension=0, tiled=True)

    if square:
        grad_far, sum_far = to_hidden(3, 4)
        far = swap_far(order.halves(to_second, grad_far))
        grad_near, sum_near = to_hidden(1, 3)
        near = order(to_second, grad_near)
        direct = swap_direct(near)
        came = order.add_far(near, far, direct)
        grad_own, sum_own = to_hidden(0, 1)
        second_own = order(to_second, grad_own)
        hidden_grad = [grad_own, grad_near, grad_far]
        hidden_sum = sum_own + sum_near + sum_far
        result_far = order.halves(to_result, slots(active, 3, 4))
        up_sum = slab_sum(gate(slab_product(second, hidden_grad), *came))
        result_far = swap_far(gate(result_far, *came))
    else:
        hidden_grad, hidden_sum = to_hidden(0, groups)
        second_own, came = scatter(to_second, hidden_grad), ()
        up_sum = slab_sum(slab_product(second, hidden_grad))
    branch_grad, middle_grad, middle_sums = order(
        lambda own, *came: norm_back(own, middle, dz_low, ln2_gain, came), second_own, *came
    )

    def column_sum(values):
        return jnp.sum(values.astype(wide), axis=0)

    hidden_sum = lax.dynamic_update_slice_in_dim(
        jnp.zeros((hidden_width,), wide), hidden_sum[0], me * hidden_slab, axis=0
    )
    early = [middle_sums[2], middle_sums[0], middle_sums[1], hidden_sum, middle_sums[3]]
    mixed_grad = order(lambda rows: contract_last(rows, full_out).astype(low), branch_grad)
    mixed_grad = exchange(by_index([mixed_grad[:, j * slab : (j + 1) * slab] for j in range(groups)], me))
    if square:
        order.after(*result_far)
        result_rest = order(to_result, slots(active, 0, 3))
    branch_other = pair_swap(gate(branch_grad, *result_far) if square else branch_grad)
    branch_pair = jnp.concatenate([branch_grad, branch_other], axis=0)
    out_sum = order(lambda columns: outer(columns, branch_pair, groups, 1), mixed_half)
    mixed_grad = order(lambda *parts: jnp.concatenate(parts, axis=0), *mixed_grad)
    attention = (mask, slopes, qkv, log_totals, attended)
    if square:
        part = out_sum.shape[0] // 4
        out_far = out_sum[3 * part : 3 * part + part // 2], out_sum[3 * part + part // 2 :]
        out_far = swap_far(gate(out_far, mixed_grad))
        result_near = result_rest[count:]
        result_came = order.add_far(result_near, result_far, None, mixed_grad)
    order.after(down_sum)
    begun = order(lambda rows: attend_backward(*attention, rows, seq_count, local_len, 0, pairs // 2), mixed_grad)
    if square:
        out_came = order.add_far(out_sum[part : 3 * part], out_far, None)
    qkv_grad = order(
        lambda rows: attend_backward(*attention, rows, seq_count, local_len, pairs // 2, pairs, begun), mixed_grad
    )
    if square:
        order.after(*out_came, *result_came)
        out_sum = order(lambda own, *came: summed(own, came).astype(low), out_sum[:part], *out_came)
        order.after(*out_came)
    else:
        out_sum = lax.psum_scatter(out_sum, "seq", scatter_dimension=0, tiled=True)
    out_sum = out_sum.reshape(-1, 1, out_rows, model_width)
    zero = jnp.zeros_like(out_sum)
    out_sum = jnp.concatenate(
        [jnp.where(parity == 0, out_sum, zero), jnp.where(parity == 1, out_sum, zero)], axis=1
    ).reshape(-1, model_width)
    grad_w_out = lax.psum_scatter(out_sum, "fsdp", scatter_dimension=0, tiled=True).astype(wide)
    order.after(up_sum)
    if square:
        far = swap_far(order.halves(to_normed, slots(qkv_grad, 3, 4)))
        near = order(to_normed, slots(qkv_grad, 1, 3))
        direct = swap_direct(near)
        qkv_sum = slab_sum(gate(slab_product(normed, qkv_grad), *far))
        came = order.add_far(near, far, direct)
        normed_own = order(to_normed, slots(qkv_grad, 0, 1))
    else:
        qkv_sum = slab_sum(slab_product(normed, qkv_grad))
        normed_own, came = scatter(to_normed, qkv_grad), ()
    grad_tokens, _, input_sums = order(
        lambda own, *came: norm_back(own, x_low, middle_grad, ln1_gain, came), normed_own, *came
    )
    grad_tokens = grad_tokens.reshape(tokens.shape)
    if square:
        outcome = summed(result_rest[:count], result_came)
    else:
        outcome = scatter(to_result, active).astype(wide)
    result = (middle + (outcome + down_bias)).astype(low).reshape(tokens.shape)
    if square:
        up_sum, down_sum = gate((up_sum, down_sum), *came)
    grad_w_down = slabs_of_rows(down_sum)[0]
    order.after(grad_w_down)
    grad_w_down = grad_w_down.reshape(-1, hidden_width).T
    grad_w_up = slabs_of_rows(up_sum)[0].reshape(-1, hidden_width)
    grad_w_qkv = slabs_of_rows(qkv_sum)[0].reshape(-1, groups, pairs, 3, PAIR)
    grad_w_qkv = jnp.transpose(grad_w_qkv, (0, 3, 1, 2, 4)).reshape(-1, 3 * model_width)

    head_sum = jnp.transpose(column_sum(qkv_grad).reshape(pairs, 3, PAIR), (1, 0, 2)).reshape(3, slab)
    qv_sum = lax.dynamic_update_slice_in_dim(
        jnp.zeros((2, model_width), wide), head_sum[0::2], me * slab, axis=1
    )
    late = [qv_sum.reshape(-1), input_sums[0], input_sums[1]]
    sums = order(lambda *parts: jnp.concatenate(parts).reshape(-1, PAIR), *early, *late)
    sums = total(sums).reshape(-1)

    def cut(at, count):
        return sums[at * model_width : (at + count) * model_width]

    ratio = hidden_width // model_width
    return (
        result,
        grad_tokens,
        grad_w_qkv,
        cut(4 + ratio, 2).reshape(2, model_width),
        grad_w_out,
        cut(0, 1),
        cut(6 + ratio, 1),
        cut(7 + ratio, 1),
        cut(1, 1),
        cut(2, 1),
        grad_w_up,
        cut(3, ratio),
        grad_w_down,
        cut(3 + ratio, 1),
    )


def solution(mesh):
    return jax.shard_map(
        local,
        mesh=mesh,
        in_specs=(
            P("fsdp", "seq", None),
            P("fsdp", "seq", None),
            P("fsdp", None),
            P(),
            P("fsdp", None),
            P(),
            P(),
            P(),
            P(),
            P(),
            P("fsdp", None),
            P(),
            P(None, "fsdp"),
            P(),
        ),
        out_specs=(
            P("fsdp", "seq", None),
            P("fsdp", "seq", None),
            P(("seq", "fsdp"), None),
            P(),
            P(("seq", "fsdp"), None),
            P(),
            P(),
            P(),
            P(),
            P(),
            P(("seq", "fsdp"), None),
            P(),
            P(None, ("seq", "fsdp")),
            P(),
        ),
        check_vma=False,
    )
```

```python
import math
from functools import partial

import jax
import jax.numpy as jnp
from jax import lax
from jax.experimental import pallas as pl
from jax.experimental.pallas import tpu as pltpu
from jax.sharding import PartitionSpec as P

HEADS = 32
HEAD_DIM = 64
BLOCK = 256
PAIR = 2 * HEAD_DIM
GRANT = 58 * 2**20


def estimate(flops, transcendentals=0):
    return pl.CostEstimate(flops=flops // 4, bytes_accessed=flops // 4096, transcendentals=transcendentals // 4)


def layer_norm(token_rows, gain_vec, shift_vec):
    average = jnp.mean(token_rows, axis=-1, keepdims=True)
    centred = token_rows - average
    spread = jnp.mean(centred * centred, axis=-1, keepdims=True)
    return centred * lax.rsqrt(spread + 1e-05) * gain_vec + shift_vec


def contract(left_side, right_side):
    return lax.dot_general(
        left_side, right_side, (((1,), (0,)), ((), ())), preferred_element_type=jnp.float32
    )


def contract_last(left_side, right_side):
    return lax.dot_general(
        left_side, right_side, (((1,), (1,)), ((), ())), preferred_element_type=jnp.float32
    )


def contract_first(left_side, right_side):
    return lax.dot_general(
        left_side, right_side, (((0,), (0,)), ((), ())), preferred_element_type=jnp.float32
    )


def row_pieces(mask, sequence, block, seqs, local):
    per = BLOCK // local
    return [
        pl.ds(pl.multiple_of((((block * per + r) ^ mask) * seqs + sequence) * local, local), local)
        for r in range(per)
    ]


def load_rows(ref, pieces, columns):
    parts = [ref[piece, columns] for piece in pieces]
    return parts[0] if len(parts) == 1 else jnp.concatenate(parts, axis=0)


def store_rows(ref, pieces, columns, values):
    local = values.shape[0] // len(pieces)
    for r, piece in enumerate(pieces):
        ref[piece, columns] = values[r * local : (r + 1) * local]


Q_COLUMNS, K_COLUMNS, V_COLUMNS = (slice(t * PAIR, (t + 1) * PAIR) for t in range(3))


def attend_forward_kernel(mask_ref, slope_ref, qkv_ref, mixed_ref, lse_ref, *, blocks, seqs, local):
    pair, sequence = pl.program_id(0), pl.program_id(1)
    mask = mask_ref[0]
    lane = lax.broadcasted_iota(jnp.int32, (BLOCK, PAIR), 1)
    row = lax.broadcasted_iota(jnp.int32, (BLOCK, BLOCK), 0)
    column = lax.broadcasted_iota(jnp.int32, (BLOCK, BLOCK), 1)
    gap = (row - column).astype(jnp.float32)
    pieces = [row_pieces(mask, sequence, block, seqs, local) for block in range(blocks)]

    for i in range(blocks):
        q_pair = load_rows(qkv_ref, pieces[i], Q_COLUMNS)
        outs, lses = [], []
        for head in range(2):
            slope = slope_ref[pair * 2 + head]
            mine = (lane >= head * HEAD_DIM) & (lane < (head + 1) * HEAD_DIM)
            q = jnp.where(mine, q_pair, jnp.zeros_like(q_pair)) * jnp.bfloat16(HEAD_DIM**-0.5)
            parts, highest = [], None
            for j in range(i + 1):
                scores = contract_last(q, load_rows(qkv_ref, pieces[j], K_COLUMNS))
                distance = jnp.abs(gap) if i == j else gap + float(BLOCK * (i - j))
                scores = scores - slope * distance
                parts.append(scores)
                top = jnp.max(scores, axis=-1, keepdims=True)
                highest = top if highest is None else jnp.maximum(highest, top)
            total, out = None, None
            for j in range(i + 1):
                weights = jnp.exp(parts[j] - highest)
                part = jnp.sum(weights, axis=-1, keepdims=True)
                mixed = contract(weights.astype(jnp.bfloat16), load_rows(qkv_ref, pieces[j], V_COLUMNS))
                total = part if total is None else total + part
                out = mixed if out is None else out + mixed
            outs.append(out / total)
            lses.append(highest + jnp.log(total))
        first = lane < HEAD_DIM
        everything = slice(0, PAIR)
        store_rows(
            mixed_ref, pieces[i], everything, jnp.where(first, outs[0], outs[1]).astype(mixed_ref.dtype)
        )
        store_rows(lse_ref, pieces[i], everything, jnp.where(first, lses[0], lses[1]))


def attend_backward_kernel(
    mask_ref, slope_ref, qkv_ref, lse_ref, mixed_ref, grad_ref, *rest, blocks, seqs, local, start
):
    out_ref, dq_ref, dk_ref, dv_ref = rest[-4:]
    pair, sequence = pl.program_id(0) + start, pl.program_id(1)
    mask = mask_ref[0]
    lane = lax.broadcasted_iota(jnp.int32, (BLOCK, PAIR), 1)
    key = lax.broadcasted_iota(jnp.int32, (BLOCK, BLOCK), 0)
    query = lax.broadcasted_iota(jnp.int32, (BLOCK, BLOCK), 1)
    gap = (query - key).astype(jnp.float32)
    pieces = [row_pieces(mask, sequence, block, seqs, local) for block in range(blocks)]
    everything = slice(0, PAIR)

    for i in range(blocks):
        q_pair = load_rows(qkv_ref, pieces[i], Q_COLUMNS)
        up_pair = load_rows(grad_ref, pieces[i], everything)
        mixed_pair = load_rows(mixed_ref, pieces[i], everything)
        inner_all = (up_pair.astype(jnp.float32) * mixed_pair.astype(jnp.float32)).T
        lse_all = load_rows(lse_ref, pieces[i], everything).T
        dq = None
        for head in range(2):
            slope = slope_ref[pair * 2 + head]
            mine = (lane >= head * HEAD_DIM) & (lane < (head + 1) * HEAD_DIM)
            zero = jnp.zeros_like(q_pair)
            q = jnp.where(mine, q_pair, zero) * jnp.bfloat16(HEAD_DIM**-0.5)
            up = jnp.where(mine, up_pair, zero)
            inner = jnp.sum(inner_all[head * HEAD_DIM : (head + 1) * HEAD_DIM], axis=0, keepdims=True)
            lse = lse_all[head * HEAD_DIM : head * HEAD_DIM + 1]
            for j in range(i + 1):
                k_pair = load_rows(qkv_ref, pieces[j], K_COLUMNS)
                distance = jnp.abs(gap) if i == j else gap + float(BLOCK * (i - j))
                probs = jnp.exp(contract_last(k_pair, q) - slope * distance - lse)
                prob_grad = contract_last(load_rows(qkv_ref, pieces[j], V_COLUMNS), up)
                score_grad = (probs * (prob_grad - inner)).astype(jnp.bfloat16)
                dv = contract(probs.astype(jnp.bfloat16), up)
                dk = contract(score_grad, q)
                part = contract_first(score_grad, jnp.where(mine, k_pair, zero))
                dq = part if dq is None else dq + part
                if i == j and head == 0:
                    dv_ref[j] = dv
                    dk_ref[j] = dk
                else:
                    dv_ref[j] += dv
                    dk_ref[j] += dk
        dq_ref[i] = dq
    for i in range(blocks):
        store_rows(out_ref, pieces[i], Q_COLUMNS, (dq_ref[i] * HEAD_DIM**-0.5).astype(out_ref.dtype))
        store_rows(out_ref, pieces[i], K_COLUMNS, dk_ref[i].astype(out_ref.dtype))
        store_rows(out_ref, pieces[i], V_COLUMNS, dv_ref[i].astype(out_ref.dtype))


def attend_forward(mask, slopes, qkv, seqs, local):
    rows, width = qkv.shape
    pairs, blocks = width // (3 * PAIR), rows // seqs // BLOCK
    scored = pairs * seqs * blocks * (blocks + 1) * BLOCK * BLOCK
    return pl.pallas_call(
        partial(attend_forward_kernel, blocks=blocks, seqs=seqs, local=local),
        grid_spec=pltpu.PrefetchScalarGridSpec(
            num_scalar_prefetch=2,
            grid=(pairs, seqs),
            in_specs=[pl.BlockSpec((rows, 3 * PAIR), lambda p, *_: (0, p))],
            out_specs=[pl.BlockSpec((rows, PAIR), lambda p, *_: (0, p))] * 2,
        ),
        out_shape=[
            jax.ShapeDtypeStruct((rows, pairs * PAIR), jnp.bfloat16),
            jax.ShapeDtypeStruct((rows, pairs * PAIR), jnp.float32),
        ],
        compiler_params=pltpu.CompilerParams(vmem_limit_bytes=GRANT),
        cost_estimate=estimate(scored * 2 * 512, scored),
        name="attend_forward",
    )(mask, slopes, qkv)


def attend_backward(mask, slopes, qkv, lse, mixed, grad, seqs, local, start, stop, begun=None):
    rows, width = qkv.shape
    blocks = rows // seqs // BLOCK
    scored = (stop - start) * seqs * blocks * (blocks + 1) * BLOCK * BLOCK
    narrow = pl.BlockSpec((rows, PAIR), lambda p, *_: (0, p + start))
    wide = pl.BlockSpec((rows, 3 * PAIR), lambda p, *_: (0, p + start))
    earlier = [] if begun is None else [begun]
    return pl.pallas_call(
        partial(attend_backward_kernel, blocks=blocks, seqs=seqs, local=local, start=start),
        grid_spec=pltpu.PrefetchScalarGridSpec(
            num_scalar_prefetch=2,
            grid=(stop - start, seqs),
            in_specs=[wide, narrow, narrow, narrow] + [pl.BlockSpec(memory_space=pl.ANY)] * len(earlier),
            out_specs=wide,
            scratch_shapes=[pltpu.VMEM((blocks, BLOCK, PAIR), jnp.float32)] * 3,
        ),
        out_shape=jax.ShapeDtypeStruct((rows, width), jnp.bfloat16),
        input_output_aliases={6: 0} if earlier else {},
        compiler_params=pltpu.CompilerParams(vmem_limit_bytes=GRANT),
        cost_estimate=estimate(scored * 2 * 1280, scored),
        name="attend_backward",
    )(mask, slopes, qkv, lse, mixed, grad, *earlier)


def head_columns_kernel(at_ref, in_ref, out_ref):
    for t in range(3):

        @pl.when(pl.program_id(0) == t)
        def _():
            for pair in range(in_ref.shape[1] // PAIR):
                at = (pair * 3 + t) * PAIR
                out_ref[:, at : at + PAIR] = in_ref[:, pair * PAIR : (pair + 1) * PAIR]


def up_kernel(rows_ref, weight_ref, bias_ref, active_ref, slope_ref, *, chunk):
    rows = rows_ref[...]
    for at in range(0, weight_ref.shape[1], chunk):
        columns = slice(at, at + chunk)
        hidden = contract(rows, weight_ref[:, columns]) + bias_ref[:, columns]
        below = 0.5 + 0.5 * lax.erf(hidden * 2**-0.5)
        active_ref[:, columns] = (hidden * below).astype(active_ref.dtype)
        slope_ref[:, columns] = below + hidden * ((2 * math.pi) ** -0.5 * jnp.exp(-0.5 * hidden * hidden))


def hidden_grad_kernel(rows_ref, weight_ref, slope_ref, grad_ref, sum_ref, *, chunk):
    rows = rows_ref[...]
    starting = pl.program_id(0) == 0
    for at in range(0, weight_ref.shape[0], chunk):
        columns = slice(at, at + chunk)
        grad = contract_last(rows, weight_ref[columns, :]) * slope_ref[:, columns]
        grad = grad.astype(grad_ref.dtype)
        grad_ref[:, columns] = grad
        part = jnp.sum(grad.astype(jnp.float32), axis=0, keepdims=True)
        sum_ref[:, columns] = jnp.where(starting, part, sum_ref[:, columns] + part)


TILE = 256


def up_and_bend(rows, weight, bias):
    count, depth = rows.shape
    width = weight.shape[1]
    tile = pl.BlockSpec((TILE, width), lambda i: (i, 0))
    return pl.pallas_call(
        partial(up_kernel, chunk=512),
        grid=(count // TILE,),
        in_specs=[
            pl.BlockSpec((TILE, depth), lambda i: (i, 0)),
            pl.BlockSpec((depth, width), lambda i: (0, 0), pipeline_mode=pl.Buffered(1)),
            pl.BlockSpec((1, width), lambda i: (0, 0)),
        ],
        out_specs=[tile, tile],
        out_shape=[
            jax.ShapeDtypeStruct((count, width), jnp.bfloat16),
            jax.ShapeDtypeStruct((count, width), jnp.float32),
        ],
        compiler_params=pltpu.CompilerParams(vmem_limit_bytes=GRANT),
        cost_estimate=estimate(count * depth * width * 4, 2 * count * width),
        name="up_and_bend",
    )(rows, weight, bias)


def hidden_gradient(rows, weight, slope, start, count):
    depth = rows.shape[1]
    width = weight.shape[0]
    first = start // TILE
    line = pl.BlockSpec((1, width), lambda i: (0, 0))
    return pl.pallas_call(
        partial(hidden_grad_kernel, chunk=512),
        grid=(count // TILE,),
        in_specs=[
            pl.BlockSpec((TILE, depth), lambda i: (i + first, 0)),
            pl.BlockSpec((width, depth), lambda i: (0, 0), pipeline_mode=pl.Buffered(1)),
            pl.BlockSpec((TILE, width), lambda i: (i + first, 0)),
        ],
        out_specs=[pl.BlockSpec((TILE, width), lambda i: (i, 0)), line],
        out_shape=[
            jax.ShapeDtypeStruct((count, width), jnp.bfloat16),
            jax.ShapeDtypeStruct((1, width), jnp.float32),
        ],
        compiler_params=pltpu.CompilerParams(vmem_limit_bytes=GRANT),
        cost_estimate=estimate(count * depth * width * 3, 0),
        name="hidden_gradient",
    )(rows, weight, slope)


def mixed_grad_kernel(rows_ref, weight_ref, out_ref):
    out_ref[...] = contract_last(rows_ref[...], weight_ref[...]).astype(out_ref.dtype)


def mixed_gradient(rows, weight, slab):
    count, depth = rows.shape
    width = weight.shape[0]
    return pl.pallas_call(
        mixed_grad_kernel,
        grid=(width // slab,),
        in_specs=[
            pl.BlockSpec((count, depth), lambda i: (0, 0), pipeline_mode=pl.Buffered(1)),
            pl.BlockSpec((slab, depth), lambda i: (i, 0)),
        ],
        out_specs=pl.BlockSpec((count, slab), lambda i: (0, i)),
        out_shape=jax.ShapeDtypeStruct((count, width), jnp.bfloat16),
        compiler_params=pltpu.CompilerParams(vmem_limit_bytes=GRANT),
        cost_estimate=estimate(2 * count * depth * width, 0),
        name="mixed_gradient",
    )(rows, weight)


def norm_back_kernel(own_ref, values_ref, base_ref, gain_ref, *refs, parts):
    came, (low_ref, wide_ref, sums_ref) = refs[:parts], refs[parts:]
    wide = jnp.float32
    step = pl.program_id(0)

    def make(came):
        grad = own_ref[...].astype(wide)
        for part in came:
            grad = grad + part[...].astype(wide)
        values = values_ref[...].astype(wide)
        centred = values - jnp.mean(values, axis=-1, keepdims=True)
        scale = lax.rsqrt(jnp.mean(centred * centred, axis=-1, keepdims=True) + 1e-05)
        normal = centred * scale
        gained = grad * gain_ref[...]
        along = jnp.mean(gained * normal, axis=-1, keepdims=True)
        made = gained - jnp.mean(gained, axis=-1, keepdims=True) - normal * along
        made = base_ref[...].astype(wide) + scale * made
        low = made.astype(low_ref.dtype)
        low_ref[...] = low
        wide_ref[...] = made
        for row, part in enumerate((grad * normal, grad, low.astype(wide))):
            line = jnp.sum(part, axis=0, keepdims=True)
            sums_ref[row : row + 1, :] = jnp.where(step == 0, line, sums_ref[row : row + 1, :] + line)

    if not came:
        make(())
        return
    upper = step < pl.num_programs(0) // 2
    pl.when(upper)(lambda: make(came[0::2]))
    pl.when(jnp.logical_not(upper))(lambda: make(came[1::2]))


def norm_back(rest, values, base, gain, came):
    rows, width = values.shape
    steps = 8
    half = steps // 2
    came = list(came or ())
    count = rows // steps
    tile = pl.BlockSpec((count, width), lambda i: (i, 0))
    top = pl.BlockSpec((count, width), lambda i: (jnp.minimum(i, half - 1), 0))
    bottom = pl.BlockSpec((count, width), lambda i: (jnp.maximum(i - half, 0), 0))
    return pl.pallas_call(
        partial(norm_back_kernel, parts=len(came)),
        grid=(steps,),
        in_specs=[tile, tile, tile, pl.BlockSpec((1, width), lambda i: (0, 0))] + [top, bottom] * (len(came) // 2),
        out_specs=[tile, tile, pl.BlockSpec((8, width), lambda i: (0, 0))],
        out_shape=[
            jax.ShapeDtypeStruct((rows, width), jnp.bfloat16),
            jax.ShapeDtypeStruct((rows, width), jnp.float32),
            jax.ShapeDtypeStruct((8, width), jnp.float32),
        ],
        compiler_params=pltpu.CompilerParams(vmem_limit_bytes=GRANT),
        cost_estimate=estimate(30 * rows * width, rows),
        name="norm_back",
    )(rest, values, base, gain[None], *came)


def outer_kernel(left_ref, *refs, chunk):
    right_refs, out_ref = refs[:-1], refs[-1]
    shards = out_ref.shape[0]
    for at in range(0, out_ref.shape[3], chunk):
        columns = slice(at, at + chunk)
        made, row = None, 0
        for right_ref in right_refs:
            count = right_ref.shape[0]
            part = contract_first(left_ref[row : row + count, :], right_ref[:, columns])
            made = part if made is None else made + part
            row += count
        out_ref[:, 0, :, columns] = made.astype(out_ref.dtype).reshape(shards, -1, made.shape[1])


def outer(left, rights, groups, shards):
    rights = rights if isinstance(rights, (list, tuple)) else [rights]
    tokens, rows = left.shape
    width = rights[0].shape[1]
    part = rows // groups
    made = pl.pallas_call(
        partial(outer_kernel, chunk=512 if width % 512 == 0 else 256),
        grid=(groups,),
        in_specs=[pl.BlockSpec((tokens, part), lambda i: (0, i))]
        + [
            pl.BlockSpec((right.shape[0], width), lambda i: (0, 0), pipeline_mode=pl.Buffered(1))
            for right in rights
        ],
        out_specs=pl.BlockSpec((shards, 1, part // shards, width), lambda i: (0, i, 0, 0)),
        out_shape=jax.ShapeDtypeStruct((shards, groups, part // shards, width), jnp.bfloat16),
        compiler_params=pltpu.CompilerParams(vmem_limit_bytes=GRANT),
        cost_estimate=estimate(2 * tokens * rows * width, 0),
        name="outer",
    )(left, *rights)
    return made.reshape(rows, width)


def swap(values, bit):
    return lax.ppermute(values, "seq", [(i, i ^ bit) for i in range(4)])


def by_index(parts, me):
    if len(parts) != 4:
        return parts
    odd, upper = (me & 1) == 1, (me & 2) == 2
    a, b, c, d = parts
    a, b, c, d = (
        jnp.where(odd, b, a),
        jnp.where(odd, a, b),
        jnp.where(odd, d, c),
        jnp.where(odd, c, d),
    )
    return [jnp.where(upper, c, a), jnp.where(upper, d, b), jnp.where(upper, a, c), jnp.where(upper, b, d)]


def exchange(slots):
    if lax.axis_size("seq") != 4:
        return list(lax.all_to_all(jnp.stack(slots), "seq", split_axis=0, concat_axis=0, tiled=True))
    return [slots[0]] + [swap(slots[j], j) for j in (1, 2, 3)]


def gate(values, *before):
    return lax.optimization_barrier((values, *before))[0]


class Order:
    def __init__(self):
        self.pending = []

    def after(self, *values):
        self.pending += values

    def __call__(self, operation, *operands):
        if self.pending:
            count = len(operands)
            operands = lax.optimization_barrier((*operands, *self.pending))[:count]
        made = operation(*operands)
        self.pending = jax.tree.leaves(made)
        return made

    def gather(self, rows):
        if lax.axis_size("seq") != 4:
            return lax.all_gather(jnp.concatenate(rows, axis=0), "seq", axis=0, tiled=True), None
        top, bottom = rows
        return rows, (swap(bottom, 1), swap(top, 2), swap(top, 1), swap(bottom, 2))

    def fill(self, begun):
        rows, came = begun
        if came is None:
            return rows
        first_bottom, second_top, first_top, second_bottom = came
        room = jnp.zeros_like(rows[0])
        parts = (*rows, first_top, first_bottom, second_top, second_bottom, room, room)
        return self(lambda *parts: jnp.concatenate(parts, axis=0), *parts)

    def complete(self, made, pieces):
        if not isinstance(pieces, list):
            return made
        rows = pieces[-1].shape[0]

        def put(before, first, second):
            before = lax.dynamic_update_slice_in_dim(before, first, 6 * rows, axis=0)
            return lax.dynamic_update_slice_in_dim(before, second, 7 * rows, axis=0)

        return self(put, made, *pieces[-2:])

    def pass_on(self, begun, *before):
        rows, came = begun
        if came is None:
            return rows
        first_bottom, second_top, first_top, second_bottom = came
        self.after(*came)
        if before:
            second_top, first_bottom = gate((second_top, first_bottom), *before)
        far = [swap(second_top, 1), swap(first_bottom, 2)]
        return [*rows, first_top, first_bottom, second_top, second_bottom, *far]

    def halves(self, product, rows):
        def cut(values):
            made = product(values)
            half = made.shape[0] // 2
            return made[:half], made[half:]

        return self(cut, rows)

    def add_far(self, made, far, direct, *before, at=None):
        wide = jnp.float32
        half = far[0].shape[0]
        start = made.shape[0] - 4 * half if at is None else at

        def add(made, top, bottom):
            at = start
            first = (made[at + half : at + 2 * half].astype(wide) + bottom.astype(wide)).astype(made.dtype)
            second = (made[at + 2 * half : at + 3 * half].astype(wide) + top.astype(wide)).astype(made.dtype)
            if direct is None:
                first = jnp.concatenate([made[at : at + half], first], axis=0)
                second = jnp.concatenate([second, made[at + 3 * half : at + 4 * half]], axis=0)
            return first, second

        first, second = self(add, made, *far)
        if before:
            first, second = gate((first, second), *before)
        first, second = swap(first, 1), swap(second, 2)
        return (first, second) if direct is None else (direct[0], first, second, direct[1])


def swap_far(halves):
    return swap(halves[0], 1), swap(halves[1], 2)


def swap_direct(made, half):
    at = made.shape[0] - 4 * half
    return swap(made[at : at + half], 1), swap(made[at + 3 * half :], 2)


def summed(own, came):
    wide = jnp.float32
    own = own.astype(wide)
    return sum((part.astype(wide) for part in came), own)


def whole(parts):
    return jnp.concatenate(parts, axis=0) if isinstance(parts, list) else parts


def total_stages():
    stages = []
    for axis in ("fsdp", "seq"):
        count, bit = lax.axis_size(axis), 1
        bits = count.bit_length() - 1
        while bit < count:
            stages.append((axis, [bit] if bits % 2 else [bit, 2 * bit, 3 * bit]))
            bit <<= 1 if bits % 2 else 2
            bits -= bits % 2
    return stages


def local(
    tokens,
    cotangent,
    w_qkv,
    qv_bias,
    w_out,
    out_bias,
    ln1_gain,
    ln1_shift,
    ln2_gain,
    ln2_shift,
    w_up,
    up_bias,
    w_down,
    down_bias,
):
    seq_count, local_len, model_width = tokens.shape
    groups, shards = lax.axis_size("seq"), lax.axis_size("fsdp")
    me = lax.axis_index("seq")
    square = groups == 4
    heads_here = HEADS // groups
    slab = heads_here * HEAD_DIM
    pairs = slab // PAIR
    hidden_width = w_up.shape[1]
    hidden_slab = hidden_width // groups
    rows_here = seq_count * local_len
    low, wide = jnp.bfloat16, jnp.float32
    mask = jnp.reshape(me if square else jnp.zeros_like(me), (1,)).astype(jnp.int32)
    head_index = me * heads_here + jnp.arange(1, heads_here + 1, dtype=jnp.int32)
    slopes = 2.0 ** (-8.0 * head_index.astype(wide) / HEADS)

    def head_columns(values):
        rows = values.shape[0]
        return pl.pallas_call(
            head_columns_kernel,
            grid_spec=pltpu.PrefetchScalarGridSpec(
                num_scalar_prefetch=1,
                grid=(3,),
                in_specs=[pl.BlockSpec((rows, slab), lambda t, at: (0, t * groups + at[0]))],
                out_specs=pl.BlockSpec((rows, 3 * slab), lambda t, at: (0, 0)),
            ),
            out_shape=jax.ShapeDtypeStruct((rows, 3 * slab), values.dtype),
            name="head_columns",
        )(jnp.reshape(me, (1,)).astype(jnp.int32), values)

    def own_slab(values, axis):
        width = values.shape[axis] // groups
        return lax.dynamic_slice_in_dim(values, me * width, width, axis=axis)

    order = Order()
    x_low = tokens.reshape(rows_here, model_width)
    x = x_low.astype(wide)
    dz_low = cotangent.reshape(rows_here, model_width)
    qkv_slab = lax.all_gather(head_columns(w_qkv), "fsdp", axis=0, tiled=True)
    qkv_bias = head_columns(jnp.concatenate([qv_bias[0], jnp.zeros_like(qv_bias[0]), qv_bias[1]])[None])
    up_bias_slab = own_slab(up_bias, 0)

    first_norm = layer_norm(x, ln1_gain, ln1_shift)
    half = rows_here // 2

    def halves_of(values):
        return values[:half].astype(low), values[half:].astype(low)

    normed = order.gather(order(halves_of, first_norm))
    normed = order.pass_on(normed)
    full_out = lax.all_gather(w_out, "fsdp", axis=0, tiled=True)
    up_slab = lax.all_gather(own_slab(gate(w_up, normed[0]) if square else w_up, 1), "fsdp", axis=0, tiled=True)
    down_slab = lax.all_gather(own_slab(gate(w_down, normed[0]) if square else w_down, 0), "fsdp", axis=1, tiled=True)
    normed = whole(normed)
    upstream = order.gather(halves_of(gate(dz_low, normed)))
    qkv = order(lambda rows: (contract(rows, qkv_slab) + qkv_bias).astype(low), normed)
    attended, log_totals = order(lambda rows: attend_forward(mask, slopes, rows, seq_count, local_len), qkv)
    if square:
        attended = gate(attended, *upstream[1])
    mixed_slots = exchange([attended[j * rows_here : (j + 1) * rows_here] for j in range(groups)])
    mixed_rows = jnp.concatenate(by_index(mixed_slots, me), axis=1)
    mixed_slots = jnp.concatenate(mixed_slots, axis=1)

    def pair_swap(values):
        return lax.ppermute(values, "fsdp", [(i, i ^ 1) for i in range(shards)])

    parity = lax.axis_index("fsdp") & 1
    out_rows = model_width // (groups * shards)

    def pair_halves(values):
        halves = values.reshape(rows_here, -1, 2, out_rows)
        return tuple(
            lax.dynamic_index_in_dim(halves, index, axis=2, keepdims=False).reshape(rows_here, -1)
            for index in (parity, 1 - parity)
        )

    middle = order(lambda rows: x + (contract(rows, full_out) + out_bias), mixed_rows)
    second_norm = layer_norm(middle, ln2_gain, ln2_shift)
    second = order.gather(order(halves_of, second_norm))
    mine, theirs = order(pair_halves, mixed_slots)
    upstream_made = order.fill(upstream)
    mixed_half = order(lambda *parts: jnp.concatenate(parts, axis=0), mine, pair_swap(theirs))
    dz_sum = order(lambda values: jnp.sum(values.astype(wide), axis=0), dz_low)
    second = whole(order.pass_on(second))
    upstream = order.pass_on(upstream, second)
    active, slope = order(lambda rows: up_and_bend(rows, up_slab, up_bias_slab[None]), second)
    upstream = order.complete(upstream_made, upstream)

    def slab_product(left, right):
        return order(lambda rows: outer(rows, right, groups, shards), left)

    def slab_sum(made):
        return lax.psum_scatter(made, "fsdp", scatter_dimension=0, tiled=True)

    def slabs_of_rows(values):
        return lax.all_to_all(
            values.reshape(groups, -1, values.shape[1]), "seq", split_axis=0, concat_axis=0, tiled=True
        )

    down_sum = slab_sum(slab_product(upstream, active))
    count = rows_here

    def slots(product, start, stop):
        return lambda values: product(values[start * count : stop * count])

    def to_second(rows):
        return contract_last(rows, up_slab).astype(low)

    def to_result(rows):
        return contract(rows, down_slab).astype(low)

    def to_normed(rows):
        return contract_last(rows, qkv_slab).astype(low)

    def scatter(product, rows):
        return lax.psum_scatter(order(product, rows), "seq", scatter_dimension=0, tiled=True)

    hidden_grad, hidden_sum = order(lambda rows: hidden_gradient(rows, down_slab, slope, 0, groups * count), upstream)
    if square:
        far = swap_far(order.halves(slots(to_second, 3, 4), hidden_grad))
        rest = order(slots(to_second, 0, 3), hidden_grad)
        second_own = rest
        direct = swap_direct(rest, half)
        came = order.add_far(rest, far, direct)
        result_far = order.halves(slots(to_result, 3, 4), active)
        up_sum = slab_sum(gate(slab_product(second, hidden_grad), *came))
        result_far = swap_far(gate(result_far, *came))
    else:
        second_own, came = scatter(to_second, hidden_grad), ()
        up_sum = slab_sum(slab_product(second, hidden_grad))
    branch_grad, middle_grad, middle_sums = order(
        lambda own, *came: norm_back(own, middle, dz_low, ln2_gain, came), second_own, *came
    )

    def column_sum(values):
        return jnp.sum(values.astype(wide), axis=0)

    hidden_sum = lax.dynamic_update_slice_in_dim(
        jnp.zeros((hidden_width,), wide), hidden_sum[0], me * hidden_slab, axis=0
    )
    early = [middle_sums[2], middle_sums[0], middle_sums[1], hidden_sum, dz_sum]
    mixed_grad = order(lambda rows: mixed_gradient(rows, full_out, slab), branch_grad)
    if square:
        mixed_grad = gate(mixed_grad, *result_far)
    mixed_grad = exchange(by_index([mixed_grad[:, j * slab : (j + 1) * slab] for j in range(groups)], me))
    if square:
        result_rest = order(slots(to_result, 0, 3), active)
    branch_other = pair_swap(branch_grad)
    branch_pair = jnp.concatenate([branch_grad, branch_other], axis=0)
    out_sum = order(lambda columns: outer(columns, branch_pair, groups, 1), mixed_half)
    mixed_grad = order(lambda *parts: jnp.concatenate(parts, axis=0), *mixed_grad)
    attention = (mask, slopes, qkv, log_totals, attended)
    if square:
        part = out_sum.shape[0] // 4
        out_far = out_sum[3 * part : 3 * part + part // 2], out_sum[3 * part + part // 2 :]
        out_far = swap_far(gate(out_far, mixed_grad))
        result_came = order.add_far(result_rest, result_far, None, mixed_grad)
    order.after(down_sum)
    begun = order(lambda rows: attend_backward(*attention, rows, seq_count, local_len, 0, pairs // 2), mixed_grad)
    if square:
        out_came = order.add_far(out_sum, out_far, None, at=part)
    down_slabs = slabs_of_rows(gate(down_sum, begun))
    qkv_grad = order(
        lambda rows: attend_backward(*attention, rows, seq_count, local_len, pairs // 2, pairs, begun), mixed_grad
    )
    order.after(down_slabs)
    if square:
        order.after(*out_came, *result_came)
        out_sum = order(lambda own, *came: summed(own[:part], came).astype(low), out_sum, *out_came)
        order.after(*out_came)
    else:
        out_sum = lax.psum_scatter(out_sum, "seq", scatter_dimension=0, tiled=True)
    out_sum = out_sum.reshape(-1, 1, out_rows, model_width)
    zero = jnp.zeros_like(out_sum)
    out_sum = jnp.concatenate(
        [jnp.where(parity == 0, out_sum, zero), jnp.where(parity == 1, out_sum, zero)], axis=1
    ).reshape(-1, model_width)
    grad_w_out = lax.psum_scatter(out_sum, "fsdp", scatter_dimension=0, tiled=True).astype(wide)
    order.after(up_sum)
    if square:
        far = swap_far(order.halves(slots(to_normed, 3, 4), qkv_grad))
        near = order(slots(to_normed, 1, 3), qkv_grad)
        direct = swap_direct(near, half)
        qkv_sum = slab_sum(gate(slab_product(normed, qkv_grad), *far))
        came = order.add_far(near, far, direct)
        normed_own = order(slots(to_normed, 0, 1), qkv_grad)
    else:
        qkv_sum = slab_sum(slab_product(normed, qkv_grad))
        normed_own, came = scatter(to_normed, qkv_grad), ()
    grad_tokens, _, input_sums = order(
        lambda own, *came: norm_back(own, x_low, middle_grad, ln1_gain, came), normed_own, *came
    )
    grad_tokens = grad_tokens.reshape(tokens.shape)
    if square:
        outcome = summed(result_rest[:count], result_came)
    else:
        outcome = scatter(to_result, active).astype(wide)
    result = (middle + (outcome + down_bias)).astype(low).reshape(tokens.shape)
    up_slabs = slabs_of_rows(gate(up_sum, *came, normed_own))
    qkv_slabs = slabs_of_rows(qkv_sum)

    def rows_of(slabs):
        return jnp.swapaxes(slabs, 0, 1).astype(wide)

    grad_w_down = rows_of(down_slabs).reshape(-1, hidden_width).T
    grad_w_up = rows_of(up_slabs).reshape(-1, hidden_width)
    grad_w_qkv = rows_of(qkv_slabs).reshape(-1, groups, pairs, 3, PAIR)
    grad_w_qkv = jnp.transpose(grad_w_qkv, (0, 3, 1, 2, 4)).reshape(-1, 3 * model_width)

    head_sum = jnp.transpose(column_sum(qkv_grad).reshape(pairs, 3, PAIR), (1, 0, 2)).reshape(3, slab)
    qv_sum = lax.dynamic_update_slice_in_dim(
        jnp.zeros((2, model_width), wide), head_sum[0::2], me * slab, axis=1
    )
    late = [qv_sum.reshape(-1), input_sums[0], input_sums[1]]
    order.after(up_slabs)
    sums = order(lambda *parts: jnp.concatenate(parts).reshape(-1, PAIR), *early, *late)
    stages = total_stages()
    for axis, masks in stages:
        others = range(lax.axis_size(axis))
        came = [lax.ppermute(sums, axis, [(i, i ^ mask) for i in others]) for mask in masks]
        if (axis, masks) == stages[-1]:
            order.after(qkv_slabs)
        sums = order(lambda *parts: sum(parts[1:], parts[0]), sums, *came)
    sums = sums.reshape(-1)

    def cut(at, count):
        return sums[at * model_width : (at + count) * model_width]

    ratio = hidden_width // model_width
    return (
        result,
        grad_tokens,
        grad_w_qkv,
        cut(4 + ratio, 2).reshape(2, model_width),
        grad_w_out,
        cut(0, 1),
        cut(6 + ratio, 1),
        cut(7 + ratio, 1),
        cut(1, 1),
        cut(2, 1),
        grad_w_up,
        cut(3, ratio),
        grad_w_down,
        cut(3 + ratio, 1),
    )


def solution(mesh):
    return jax.shard_map(
        local,
        mesh=mesh,
        in_specs=(
            P("fsdp", "seq", None),
            P("fsdp", "seq", None),
            P("fsdp", None),
            P(),
            P("fsdp", None),
            P(),
            P(),
            P(),
            P(),
            P(),
            P("fsdp", None),
            P(),
            P(None, "fsdp"),
            P(),
        ),
        out_specs=(
            P("fsdp", "seq", None),
            P("fsdp", "seq", None),
            P(("seq", "fsdp"), None),
            P(),
            P(("seq", "fsdp"), None),
            P(),
            P(),
            P(),
            P(),
            P(),
            P(("seq", "fsdp"), None),
            P(),
            P(None, ("seq", "fsdp")),
            P(),
        ),
        check_vma=False,
    )
```

```python
import math
from functools import partial

import jax
import jax.numpy as jnp
from jax import lax
from jax.experimental import pallas as pl
from jax.experimental.pallas import tpu as pltpu
from jax.sharding import PartitionSpec as P

HEADS = 32
HEAD_DIM = 64
BLOCK = 256
PAIR = 2 * HEAD_DIM
GRANT = 58 * 2**20


def estimate(flops, transcendentals=0):
    return pl.CostEstimate(flops=flops // 4, bytes_accessed=flops // 4096, transcendentals=transcendentals // 4)


def layer_norm(token_rows, gain_vec, shift_vec):
    average = jnp.mean(token_rows, axis=-1, keepdims=True)
    centred = token_rows - average
    spread = jnp.mean(centred * centred, axis=-1, keepdims=True)
    return centred * lax.rsqrt(spread + 1e-05) * gain_vec + shift_vec


def contract(left_side, right_side):
    return lax.dot_general(
        left_side, right_side, (((1,), (0,)), ((), ())), preferred_element_type=jnp.float32
    )


def contract_last(left_side, right_side):
    return lax.dot_general(
        left_side, right_side, (((1,), (1,)), ((), ())), preferred_element_type=jnp.float32
    )


def contract_first(left_side, right_side):
    return lax.dot_general(
        left_side, right_side, (((0,), (0,)), ((), ())), preferred_element_type=jnp.float32
    )


def row_pieces(mask, sequence, block, seqs, local):
    per = BLOCK // local
    return [
        pl.ds(pl.multiple_of((((block * per + r) ^ mask) * seqs + sequence) * local, local), local)
        for r in range(per)
    ]


def load_rows(ref, pieces, columns):
    parts = [ref[piece, columns] for piece in pieces]
    return parts[0] if len(parts) == 1 else jnp.concatenate(parts, axis=0)


def store_rows(ref, pieces, columns, values):
    local = values.shape[0] // len(pieces)
    for r, piece in enumerate(pieces):
        ref[piece, columns] = values[r * local : (r + 1) * local]


Q_COLUMNS, K_COLUMNS, V_COLUMNS = (slice(t * PAIR, (t + 1) * PAIR) for t in range(3))


def attend_forward_kernel(mask_ref, slope_ref, qkv_ref, mixed_ref, lse_ref, *, blocks, seqs, local):
    pair, sequence = pl.program_id(0), pl.program_id(1)
    mask = mask_ref[0]
    lane = lax.broadcasted_iota(jnp.int32, (BLOCK, PAIR), 1)
    row = lax.broadcasted_iota(jnp.int32, (BLOCK, BLOCK), 0)
    column = lax.broadcasted_iota(jnp.int32, (BLOCK, BLOCK), 1)
    gap = (row - column).astype(jnp.float32)
    pieces = [row_pieces(mask, sequence, block, seqs, local) for block in range(blocks)]

    for i in range(blocks):
        q_pair = load_rows(qkv_ref, pieces[i], Q_COLUMNS)
        outs, lses = [], []
        for head in range(2):
            slope = slope_ref[pair * 2 + head]
            mine = (lane >= head * HEAD_DIM) & (lane < (head + 1) * HEAD_DIM)
            q = jnp.where(mine, q_pair, jnp.zeros_like(q_pair)) * jnp.bfloat16(HEAD_DIM**-0.5)
            parts, highest = [], None
            for j in range(i + 1):
                scores = contract_last(q, load_rows(qkv_ref, pieces[j], K_COLUMNS))
                distance = jnp.abs(gap) if i == j else gap + float(BLOCK * (i - j))
                scores = scores - slope * distance
                parts.append(scores)
                top = jnp.max(scores, axis=-1, keepdims=True)
                highest = top if highest is None else jnp.maximum(highest, top)
            total, out = None, None
            for j in range(i + 1):
                weights = jnp.exp(parts[j] - highest)
                part = jnp.sum(weights, axis=-1, keepdims=True)
                mixed = contract(weights.astype(jnp.bfloat16), load_rows(qkv_ref, pieces[j], V_COLUMNS))
                total = part if total is None else total + part
                out = mixed if out is None else out + mixed
            outs.append(out / total)
            lses.append(highest + jnp.log(total))
        first = lane < HEAD_DIM
        everything = slice(0, PAIR)
        store_rows(
            mixed_ref, pieces[i], everything, jnp.where(first, outs[0], outs[1]).astype(mixed_ref.dtype)
        )
        store_rows(lse_ref, pieces[i], everything, jnp.where(first, lses[0], lses[1]))


def attend_backward_kernel(
    mask_ref, slope_ref, qkv_ref, lse_ref, mixed_ref, grad_ref, *rest, blocks, seqs, local, start
):
    out_ref, dq_ref, dk_ref, dv_ref = rest[-4:]
    pair, sequence = pl.program_id(0) + start, pl.program_id(1)
    mask = mask_ref[0]
    lane = lax.broadcasted_iota(jnp.int32, (BLOCK, PAIR), 1)
    key = lax.broadcasted_iota(jnp.int32, (BLOCK, BLOCK), 0)
    query = lax.broadcasted_iota(jnp.int32, (BLOCK, BLOCK), 1)
    gap = (query - key).astype(jnp.float32)
    pieces = [row_pieces(mask, sequence, block, seqs, local) for block in range(blocks)]
    everything = slice(0, PAIR)

    for i in range(blocks):
        q_pair = load_rows(qkv_ref, pieces[i], Q_COLUMNS)
        up_pair = load_rows(grad_ref, pieces[i], everything)
        mixed_pair = load_rows(mixed_ref, pieces[i], everything)
        inner_all = (up_pair.astype(jnp.float32) * mixed_pair.astype(jnp.float32)).T
        lse_all = load_rows(lse_ref, pieces[i], everything).T
        dq = None
        for head in range(2):
            slope = slope_ref[pair * 2 + head]
            mine = (lane >= head * HEAD_DIM) & (lane < (head + 1) * HEAD_DIM)
            zero = jnp.zeros_like(q_pair)
            q = jnp.where(mine, q_pair, zero) * jnp.bfloat16(HEAD_DIM**-0.5)
            up = jnp.where(mine, up_pair, zero)
            inner = jnp.sum(inner_all[head * HEAD_DIM : (head + 1) * HEAD_DIM], axis=0, keepdims=True)
            lse = lse_all[head * HEAD_DIM : head * HEAD_DIM + 1]
            for j in range(i + 1):
                k_pair = load_rows(qkv_ref, pieces[j], K_COLUMNS)
                distance = jnp.abs(gap) if i == j else gap + float(BLOCK * (i - j))
                probs = jnp.exp(contract_last(k_pair, q) - slope * distance - lse)
                prob_grad = contract_last(load_rows(qkv_ref, pieces[j], V_COLUMNS), up)
                score_grad = (probs * (prob_grad - inner)).astype(jnp.bfloat16)
                dv = contract(probs.astype(jnp.bfloat16), up)
                dk = contract(score_grad, q)
                part = contract_first(score_grad, jnp.where(mine, k_pair, zero))
                dq = part if dq is None else dq + part
                if i == j and head == 0:
                    dv_ref[j] = dv
                    dk_ref[j] = dk
                else:
                    dv_ref[j] += dv
                    dk_ref[j] += dk
        dq_ref[i] = dq
    for i in range(blocks):
        store_rows(out_ref, pieces[i], Q_COLUMNS, (dq_ref[i] * HEAD_DIM**-0.5).astype(out_ref.dtype))
        store_rows(out_ref, pieces[i], K_COLUMNS, dk_ref[i].astype(out_ref.dtype))
        store_rows(out_ref, pieces[i], V_COLUMNS, dv_ref[i].astype(out_ref.dtype))


def attend_forward(mask, slopes, qkv, seqs, local):
    rows, width = qkv.shape
    pairs, blocks = width // (3 * PAIR), rows // seqs // BLOCK
    scored = pairs * seqs * blocks * (blocks + 1) * BLOCK * BLOCK
    return pl.pallas_call(
        partial(attend_forward_kernel, blocks=blocks, seqs=seqs, local=local),
        grid_spec=pltpu.PrefetchScalarGridSpec(
            num_scalar_prefetch=2,
            grid=(pairs, seqs),
            in_specs=[pl.BlockSpec((rows, 3 * PAIR), lambda p, *_: (0, p))],
            out_specs=[pl.BlockSpec((rows, PAIR), lambda p, *_: (0, p))] * 2,
        ),
        out_shape=[
            jax.ShapeDtypeStruct((rows, pairs * PAIR), jnp.bfloat16),
            jax.ShapeDtypeStruct((rows, pairs * PAIR), jnp.float32),
        ],
        compiler_params=pltpu.CompilerParams(vmem_limit_bytes=GRANT),
        cost_estimate=estimate(scored * 2 * 512, scored),
        name="attend_forward",
    )(mask, slopes, qkv)


def attend_backward(mask, slopes, qkv, lse, mixed, grad, seqs, local, start, stop, begun=None):
    rows, width = qkv.shape
    blocks = rows // seqs // BLOCK
    scored = (stop - start) * seqs * blocks * (blocks + 1) * BLOCK * BLOCK
    narrow = pl.BlockSpec((rows, PAIR), lambda p, *_: (0, p + start))
    wide = pl.BlockSpec((rows, 3 * PAIR), lambda p, *_: (0, p + start))
    earlier = [] if begun is None else [begun]
    return pl.pallas_call(
        partial(attend_backward_kernel, blocks=blocks, seqs=seqs, local=local, start=start),
        grid_spec=pltpu.PrefetchScalarGridSpec(
            num_scalar_prefetch=2,
            grid=(stop - start, seqs),
            in_specs=[wide, narrow, narrow, narrow] + [pl.BlockSpec(memory_space=pl.ANY)] * len(earlier),
            out_specs=wide,
            scratch_shapes=[pltpu.VMEM((blocks, BLOCK, PAIR), jnp.float32)] * 3,
        ),
        out_shape=jax.ShapeDtypeStruct((rows, width), jnp.bfloat16),
        input_output_aliases={6: 0} if earlier else {},
        compiler_params=pltpu.CompilerParams(vmem_limit_bytes=GRANT),
        cost_estimate=estimate(scored * 2 * 1280, scored),
        name="attend_backward",
    )(mask, slopes, qkv, lse, mixed, grad, *earlier)


def head_columns_kernel(at_ref, in_ref, out_ref):
    for t in range(3):

        @pl.when(pl.program_id(0) == t)
        def _():
            for pair in range(in_ref.shape[1] // PAIR):
                at = (pair * 3 + t) * PAIR
                out_ref[:, at : at + PAIR] = in_ref[:, pair * PAIR : (pair + 1) * PAIR]


def up_kernel(rows_ref, weight_ref, bias_ref, active_ref, slope_ref, *, chunk):
    rows = rows_ref[...]
    for at in range(0, weight_ref.shape[1], chunk):
        columns = slice(at, at + chunk)
        hidden = contract(rows, weight_ref[:, columns]) + bias_ref[:, columns]
        below = 0.5 + 0.5 * lax.erf(hidden * 2**-0.5)
        active_ref[:, columns] = (hidden * below).astype(active_ref.dtype)
        slope_ref[:, columns] = below + hidden * ((2 * math.pi) ** -0.5 * jnp.exp(-0.5 * hidden * hidden))


def hidden_grad_kernel(rows_ref, weight_ref, slope_ref, grad_ref, sum_ref, *, chunk):
    rows = rows_ref[...]
    starting = pl.program_id(0) == 0
    for at in range(0, weight_ref.shape[0], chunk):
        columns = slice(at, at + chunk)
        grad = contract_last(rows, weight_ref[columns, :]) * slope_ref[:, columns]
        grad = grad.astype(grad_ref.dtype)
        grad_ref[:, columns] = grad
        part = jnp.sum(grad.astype(jnp.float32), axis=0, keepdims=True)
        sum_ref[:, columns] = jnp.where(starting, part, sum_ref[:, columns] + part)


TILE = 256


def up_and_bend(rows, weight, bias):
    count, depth = rows.shape
    width = weight.shape[1]
    tile = pl.BlockSpec((TILE, width), lambda i: (i, 0))
    return pl.pallas_call(
        partial(up_kernel, chunk=512),
        grid=(count // TILE,),
        in_specs=[
            pl.BlockSpec((TILE, depth), lambda i: (i, 0)),
            pl.BlockSpec((depth, width), lambda i: (0, 0), pipeline_mode=pl.Buffered(1)),
            pl.BlockSpec((1, width), lambda i: (0, 0)),
        ],
        out_specs=[tile, tile],
        out_shape=[
            jax.ShapeDtypeStruct((count, width), jnp.bfloat16),
            jax.ShapeDtypeStruct((count, width), jnp.float32),
        ],
        compiler_params=pltpu.CompilerParams(vmem_limit_bytes=GRANT),
        cost_estimate=estimate(count * depth * width * 4, 2 * count * width),
        name="up_and_bend",
    )(rows, weight, bias)


def hidden_gradient(rows, weight, slope, start, count):
    depth = rows.shape[1]
    width = weight.shape[0]
    first = start // TILE
    line = pl.BlockSpec((1, width), lambda i: (0, 0))
    return pl.pallas_call(
        partial(hidden_grad_kernel, chunk=512),
        grid=(count // TILE,),
        in_specs=[
            pl.BlockSpec((TILE, depth), lambda i: (i + first, 0)),
            pl.BlockSpec((width, depth), lambda i: (0, 0), pipeline_mode=pl.Buffered(1)),
            pl.BlockSpec((TILE, width), lambda i: (i + first, 0)),
        ],
        out_specs=[pl.BlockSpec((TILE, width), lambda i: (i, 0)), line],
        out_shape=[
            jax.ShapeDtypeStruct((count, width), jnp.bfloat16),
            jax.ShapeDtypeStruct((1, width), jnp.float32),
        ],
        compiler_params=pltpu.CompilerParams(vmem_limit_bytes=GRANT),
        cost_estimate=estimate(count * depth * width * 3, 0),
        name="hidden_gradient",
    )(rows, weight, slope)


def mixed_grad_kernel(rows_ref, weight_ref, out_ref):
    out_ref[...] = contract_last(rows_ref[...], weight_ref[...]).astype(out_ref.dtype)


def mixed_gradient(rows, weight, slab):
    count, depth = rows.shape
    width = weight.shape[0]
    return pl.pallas_call(
        mixed_grad_kernel,
        grid=(width // slab,),
        in_specs=[
            pl.BlockSpec((count, depth), lambda i: (0, 0), pipeline_mode=pl.Buffered(1)),
            pl.BlockSpec((slab, depth), lambda i: (i, 0)),
        ],
        out_specs=pl.BlockSpec((count, slab), lambda i: (0, i)),
        out_shape=jax.ShapeDtypeStruct((count, width), jnp.bfloat16),
        compiler_params=pltpu.CompilerParams(vmem_limit_bytes=GRANT),
        cost_estimate=estimate(2 * count * depth * width, 0),
        name="mixed_gradient",
    )(rows, weight)


def norm_back_kernel(own_ref, values_ref, base_ref, gain_ref, *refs, parts):
    came, (low_ref, wide_ref, sums_ref) = refs[:parts], refs[parts:]
    wide = jnp.float32
    step = pl.program_id(0)

    @pl.when(step == 0)
    def _():
        sums_ref[...] = jnp.zeros_like(sums_ref)

    def make(came):
        @pl.loop(0, own_ref.shape[0] // 16)
        def _(group):
            rows = pl.ds(pl.multiple_of(group * 16, 16), 16)
            grad = own_ref[rows, :].astype(wide)
            for part in came:
                grad = grad + part[rows, :].astype(wide)
            values = values_ref[rows, :].astype(wide)
            centred = values - jnp.mean(values, axis=-1, keepdims=True)
            scale = lax.rsqrt(jnp.mean(centred * centred, axis=-1, keepdims=True) + 1e-05)
            normal = centred * scale
            gained = grad * gain_ref[...]
            along = jnp.mean(gained * normal, axis=-1, keepdims=True)
            made = gained - jnp.mean(gained, axis=-1, keepdims=True) - normal * along
            made = base_ref[rows, :].astype(wide) + scale * made
            low = made.astype(low_ref.dtype)
            low_ref[rows, :] = low
            wide_ref[rows, :] = made
            for at, part in enumerate((grad * normal, grad, low.astype(wide))):
                sums_ref[8 * at : 8 * at + 8, :] += part[:8] + part[8:]

    if not came:
        make(())
        return
    upper = step < pl.num_programs(0) // 2
    pl.when(upper)(lambda: make(came[0::2]))
    pl.when(jnp.logical_not(upper))(lambda: make(came[1::2]))


def norm_back(rest, values, base, gain, came):
    rows, width = values.shape
    steps = 8
    half = steps // 2
    came = list(came or ())
    count = rows // steps
    tile = pl.BlockSpec((count, width), lambda i: (i, 0))
    top = pl.BlockSpec((count, width), lambda i: (jnp.minimum(i, half - 1), 0))
    bottom = pl.BlockSpec((count, width), lambda i: (jnp.maximum(i - half, 0), 0))
    low, full, sums = pl.pallas_call(
        partial(norm_back_kernel, parts=len(came)),
        grid=(steps,),
        in_specs=[tile, tile, tile, pl.BlockSpec((1, width), lambda i: (0, 0))] + [top, bottom] * (len(came) // 2),
        out_specs=[tile, tile, pl.BlockSpec((24, width), lambda i: (0, 0))],
        out_shape=[
            jax.ShapeDtypeStruct((rows, width), jnp.bfloat16),
            jax.ShapeDtypeStruct((rows, width), jnp.float32),
            jax.ShapeDtypeStruct((24, width), jnp.float32),
        ],
        compiler_params=pltpu.CompilerParams(vmem_limit_bytes=GRANT),
        cost_estimate=estimate(30 * rows * width, rows),
        name="norm_back",
    )(rest, values, base, gain[None], *came)
    return low, full, jnp.sum(sums.reshape(3, 8, width), axis=1)


def outer_kernel(left_ref, *refs, chunk):
    right_refs, out_ref = refs[:-1], refs[-1]
    shards = out_ref.shape[0]
    for at in range(0, out_ref.shape[3], chunk):
        columns = slice(at, at + chunk)
        made, row = None, 0
        for right_ref in right_refs:
            count = right_ref.shape[0]
            part = contract_first(left_ref[row : row + count, :], right_ref[:, columns])
            made = part if made is None else made + part
            row += count
        out_ref[:, 0, :, columns] = made.astype(out_ref.dtype).reshape(shards, -1, made.shape[1])


def outer(left, rights, groups, shards):
    rights = rights if isinstance(rights, (list, tuple)) else [rights]
    tokens, rows = left.shape
    width = rights[0].shape[1]
    part = rows // groups
    made = pl.pallas_call(
        partial(outer_kernel, chunk=512 if width % 512 == 0 else 256),
        grid=(groups,),
        in_specs=[pl.BlockSpec((tokens, part), lambda i: (0, i))]
        + [
            pl.BlockSpec((right.shape[0], width), lambda i: (0, 0), pipeline_mode=pl.Buffered(1))
            for right in rights
        ],
        out_specs=pl.BlockSpec((shards, 1, part // shards, width), lambda i: (0, i, 0, 0)),
        out_shape=jax.ShapeDtypeStruct((shards, groups, part // shards, width), jnp.bfloat16),
        compiler_params=pltpu.CompilerParams(vmem_limit_bytes=GRANT),
        cost_estimate=estimate(2 * tokens * rows * width, 0),
        name="outer",
    )(left, *rights)
    return made.reshape(rows, width)


def swap(values, bit):
    return lax.ppermute(values, "seq", [(i, i ^ bit) for i in range(4)])


def by_index(parts, me):
    if len(parts) != 4:
        return parts
    odd, upper = (me & 1) == 1, (me & 2) == 2
    a, b, c, d = parts
    a, b, c, d = (
        jnp.where(odd, b, a),
        jnp.where(odd, a, b),
        jnp.where(odd, d, c),
        jnp.where(odd, c, d),
    )
    return [jnp.where(upper, c, a), jnp.where(upper, d, b), jnp.where(upper, a, c), jnp.where(upper, b, d)]


def exchange(slots):
    if lax.axis_size("seq") != 4:
        return list(lax.all_to_all(jnp.stack(slots), "seq", split_axis=0, concat_axis=0, tiled=True))
    return [slots[0]] + [swap(slots[j], j) for j in (1, 2, 3)]


def gate(values, *before):
    return lax.optimization_barrier((values, *before))[0]


class Order:
    def __init__(self):
        self.pending = []

    def after(self, *values):
        self.pending += values

    def __call__(self, operation, *operands):
        if self.pending:
            count = len(operands)
            operands = lax.optimization_barrier((*operands, *self.pending))[:count]
        made = operation(*operands)
        self.pending = jax.tree.leaves(made)
        return made

    def gather(self, rows):
        if lax.axis_size("seq") != 4:
            return lax.all_gather(jnp.concatenate(rows, axis=0), "seq", axis=0, tiled=True), None
        top, bottom = rows
        return rows, (swap(bottom, 1), swap(top, 2), swap(top, 1), swap(bottom, 2))

    def fill(self, begun):
        rows, came = begun
        if came is None:
            return rows
        first_bottom, second_top, first_top, second_bottom = came
        room = jnp.zeros_like(rows[0])
        parts = (*rows, first_top, first_bottom, second_top, second_bottom, room, room)
        return self(lambda *parts: jnp.concatenate(parts, axis=0), *parts)

    def complete(self, made, pieces):
        if not isinstance(pieces, list):
            return made
        rows = pieces[-1].shape[0]

        def put(before, first, second):
            before = lax.dynamic_update_slice_in_dim(before, first, 6 * rows, axis=0)
            return lax.dynamic_update_slice_in_dim(before, second, 7 * rows, axis=0)

        return self(put, made, *pieces[-2:])

    def pass_on(self, begun, *before):
        rows, came = begun
        if came is None:
            return rows
        first_bottom, second_top, first_top, second_bottom = came
        self.after(*came)
        if before:
            second_top, first_bottom = gate((second_top, first_bottom), *before)
        far = [swap(second_top, 1), swap(first_bottom, 2)]
        return [*rows, first_top, first_bottom, second_top, second_bottom, *far]

    def halves(self, product, rows):
        def cut(values):
            made = product(values)
            half = made.shape[0] // 2
            return made[:half], made[half:]

        return self(cut, rows)

    def add_far(self, made, far, direct, *before, at=None):
        wide = jnp.float32
        half = far[0].shape[0]
        start = made.shape[0] - 4 * half if at is None else at

        def add(made, top, bottom):
            at = start
            first = (made[at + half : at + 2 * half].astype(wide) + bottom.astype(wide)).astype(made.dtype)
            second = (made[at + 2 * half : at + 3 * half].astype(wide) + top.astype(wide)).astype(made.dtype)
            if direct is None:
                first = jnp.concatenate([made[at : at + half], first], axis=0)
                second = jnp.concatenate([second, made[at + 3 * half : at + 4 * half]], axis=0)
            return first, second

        first, second = self(add, made, *far)
        if before:
            first, second = gate((first, second), *before)
        first, second = swap(first, 1), swap(second, 2)
        return (first, second) if direct is None else (direct[0], first, second, direct[1])


def swap_far(halves):
    return swap(halves[0], 1), swap(halves[1], 2)


def swap_direct(made, half):
    at = made.shape[0] - 4 * half
    return swap(made[at : at + half], 1), swap(made[at + 3 * half :], 2)


def summed(own, came):
    wide = jnp.float32
    own = own.astype(wide)
    return sum((part.astype(wide) for part in came), own)


def whole(parts):
    return jnp.concatenate(parts, axis=0) if isinstance(parts, list) else parts


def total_stages():
    stages = []
    for axis in ("fsdp", "seq"):
        count, bit = lax.axis_size(axis), 1
        bits = count.bit_length() - 1
        while bit < count:
            stages.append((axis, [bit] if bits % 2 else [bit, 2 * bit, 3 * bit]))
            bit <<= 1 if bits % 2 else 2
            bits -= bits % 2
    return stages


def local(
    tokens,
    cotangent,
    w_qkv,
    qv_bias,
    w_out,
    out_bias,
    ln1_gain,
    ln1_shift,
    ln2_gain,
    ln2_shift,
    w_up,
    up_bias,
    w_down,
    down_bias,
):
    seq_count, local_len, model_width = tokens.shape
    groups, shards = lax.axis_size("seq"), lax.axis_size("fsdp")
    me = lax.axis_index("seq")
    square = groups == 4
    heads_here = HEADS // groups
    slab = heads_here * HEAD_DIM
    pairs = slab // PAIR
    hidden_width = w_up.shape[1]
    hidden_slab = hidden_width // groups
    rows_here = seq_count * local_len
    low, wide = jnp.bfloat16, jnp.float32
    mask = jnp.reshape(me if square else jnp.zeros_like(me), (1,)).astype(jnp.int32)
    head_index = me * heads_here + jnp.arange(1, heads_here + 1, dtype=jnp.int32)
    slopes = 2.0 ** (-8.0 * head_index.astype(wide) / HEADS)

    def head_columns(values):
        rows = values.shape[0]
        return pl.pallas_call(
            head_columns_kernel,
            grid_spec=pltpu.PrefetchScalarGridSpec(
                num_scalar_prefetch=1,
                grid=(3,),
                in_specs=[pl.BlockSpec((rows, slab), lambda t, at: (0, t * groups + at[0]))],
                out_specs=pl.BlockSpec((rows, 3 * slab), lambda t, at: (0, 0)),
            ),
            out_shape=jax.ShapeDtypeStruct((rows, 3 * slab), values.dtype),
            name="head_columns",
        )(jnp.reshape(me, (1,)).astype(jnp.int32), values)

    def own_slab(values, axis):
        width = values.shape[axis] // groups
        return lax.dynamic_slice_in_dim(values, me * width, width, axis=axis)

    order = Order()
    x_low = tokens.reshape(rows_here, model_width)
    x = x_low.astype(wide)
    dz_low = cotangent.reshape(rows_here, model_width)
    qkv_slab = lax.all_gather(head_columns(w_qkv), "fsdp", axis=0, tiled=True)
    qkv_bias = head_columns(jnp.concatenate([qv_bias[0], jnp.zeros_like(qv_bias[0]), qv_bias[1]])[None])
    up_bias_slab = own_slab(up_bias, 0)

    first_norm = layer_norm(x, ln1_gain, ln1_shift)
    half = rows_here // 2

    def halves_of(values):
        return values[:half].astype(low), values[half:].astype(low)

    normed = order.gather(order(halves_of, first_norm))
    normed = order.pass_on(normed)
    full_out = lax.all_gather(w_out, "fsdp", axis=0, tiled=True)
    up_slab = lax.all_gather(own_slab(gate(w_up, normed[0]) if square else w_up, 1), "fsdp", axis=0, tiled=True)
    down_slab = lax.all_gather(own_slab(gate(w_down, normed[0]) if square else w_down, 0), "fsdp", axis=1, tiled=True)
    normed = whole(normed)
    upstream = order.gather(halves_of(gate(dz_low, normed)))
    qkv = order(lambda rows: (contract(rows, qkv_slab) + qkv_bias).astype(low), normed)
    attended, log_totals = order(lambda rows: attend_forward(mask, slopes, rows, seq_count, local_len), qkv)
    if square:
        attended = gate(attended, *upstream[1])
    mixed_slots = exchange([attended[j * rows_here : (j + 1) * rows_here] for j in range(groups)])
    mixed_rows = jnp.concatenate(by_index(mixed_slots, me), axis=1)
    mixed_slots = jnp.concatenate(mixed_slots, axis=1)

    def pair_swap(values):
        return lax.ppermute(values, "fsdp", [(i, i ^ 1) for i in range(shards)])

    parity = lax.axis_index("fsdp") & 1
    out_rows = model_width // (groups * shards)

    def pair_halves(values):
        halves = values.reshape(rows_here, -1, 2, out_rows)
        return tuple(
            lax.dynamic_index_in_dim(halves, index, axis=2, keepdims=False).reshape(rows_here, -1)
            for index in (parity, 1 - parity)
        )

    middle = order(lambda rows: x + (contract(rows, full_out) + out_bias), mixed_rows)
    second_norm = layer_norm(middle, ln2_gain, ln2_shift)
    second = order.gather(order(halves_of, second_norm))
    mine, theirs = order(pair_halves, mixed_slots)
    upstream_made = order.fill(upstream)
    mixed_half = order(lambda *parts: jnp.concatenate(parts, axis=0), mine, pair_swap(theirs))
    dz_sum = order(lambda values: jnp.sum(values.astype(wide), axis=0), dz_low)
    second = whole(order.pass_on(second))
    upstream = order.pass_on(upstream, second)
    active, slope = order(lambda rows: up_and_bend(rows, up_slab, up_bias_slab[None]), second)
    upstream = order.complete(upstream_made, upstream)

    def slab_product(left, right):
        return order(lambda rows: outer(rows, right, groups, shards), left)

    def slab_sum(made):
        return lax.psum_scatter(made, "fsdp", scatter_dimension=0, tiled=True)

    def slabs_of_rows(values):
        return lax.all_to_all(
            values.reshape(groups, -1, values.shape[1]), "seq", split_axis=0, concat_axis=0, tiled=True
        )

    down_sum = slab_sum(slab_product(upstream, active))
    count = rows_here

    def slots(product, start, stop):
        return lambda values: product(values[start * count : stop * count])

    def to_second(rows):
        return contract_last(rows, up_slab).astype(low)

    def to_result(rows):
        return contract(rows, down_slab).astype(low)

    def to_normed(rows):
        return contract_last(rows, qkv_slab).astype(low)

    def scatter(product, rows):
        return lax.psum_scatter(order(product, rows), "seq", scatter_dimension=0, tiled=True)

    hidden_grad, hidden_sum = order(lambda rows: hidden_gradient(rows, down_slab, slope, 0, groups * count), upstream)
    if square:
        far = swap_far(order.halves(slots(to_second, 3, 4), hidden_grad))
        rest = order(slots(to_second, 0, 3), hidden_grad)
        second_own = rest
        direct = swap_direct(rest, half)
        came = order.add_far(rest, far, direct)
        result_far = order.halves(slots(to_result, 3, 4), active)
        up_sum = slab_sum(gate(slab_product(second, hidden_grad), *came))
        result_far = swap_far(gate(result_far, *came))
    else:
        second_own, came = scatter(to_second, hidden_grad), ()
        up_sum = slab_sum(slab_product(second, hidden_grad))
    branch_grad, middle_grad, middle_sums = order(
        lambda own, *came: norm_back(own, middle, dz_low, ln2_gain, came), second_own, *came
    )

    def column_sum(values):
        return jnp.sum(values.astype(wide), axis=0)

    hidden_sum = lax.dynamic_update_slice_in_dim(
        jnp.zeros((hidden_width,), wide), hidden_sum[0], me * hidden_slab, axis=0
    )
    early = [middle_sums[2], middle_sums[0], middle_sums[1], hidden_sum, dz_sum]
    mixed_grad = order(lambda rows: mixed_gradient(rows, full_out, slab), branch_grad)
    if square:
        mixed_grad = gate(mixed_grad, *result_far)
    mixed_grad = exchange(by_index([mixed_grad[:, j * slab : (j + 1) * slab] for j in range(groups)], me))
    if square:
        result_rest = order(slots(to_result, 0, 3), active)
    branch_other = pair_swap(branch_grad)
    branch_pair = jnp.concatenate([branch_grad, branch_other], axis=0)
    out_sum = order(lambda columns: outer(columns, branch_pair, groups, 1), mixed_half)
    mixed_grad = order(lambda *parts: jnp.concatenate(parts, axis=0), *mixed_grad)
    attention = (mask, slopes, qkv, log_totals, attended)
    if square:
        part = out_sum.shape[0] // 4
        out_far = out_sum[3 * part : 3 * part + part // 2], out_sum[3 * part + part // 2 :]
        out_far = swap_far(gate(out_far, mixed_grad))
        result_came = order.add_far(result_rest, result_far, None, mixed_grad)
    order.after(down_sum)
    begun = order(lambda rows: attend_backward(*attention, rows, seq_count, local_len, 0, pairs // 2), mixed_grad)
    if square:
        out_came = order.add_far(out_sum, out_far, None, at=part)
    qkv_grad = order(
        lambda rows: attend_backward(*attention, rows, seq_count, local_len, pairs // 2, pairs, begun), mixed_grad
    )
    if square:
        order.after(*out_came, *result_came)
        out_sum = order(lambda own, *came: summed(own[:part], came).astype(low), out_sum, *out_came)
        order.after(*out_came)
    else:
        out_sum = lax.psum_scatter(out_sum, "seq", scatter_dimension=0, tiled=True)
    out_sum = out_sum.reshape(-1, 1, out_rows, model_width)
    zero = jnp.zeros_like(out_sum)
    out_sum = jnp.concatenate(
        [jnp.where(parity == 0, out_sum, zero), jnp.where(parity == 1, out_sum, zero)], axis=1
    ).reshape(-1, model_width)
    grad_w_out = lax.psum_scatter(out_sum, "fsdp", scatter_dimension=0, tiled=True).astype(wide)
    order.after(up_sum)
    if square:
        far = swap_far(order.halves(slots(to_normed, 3, 4), qkv_grad))
        near = order(slots(to_normed, 1, 3), qkv_grad)
        direct = swap_direct(near, half)
        down_slabs = slabs_of_rows(gate(down_sum, near))
        qkv_sum = slab_sum(gate(slab_product(normed, qkv_grad), *far, down_slabs))
        came = order.add_far(near, far, direct)
        normed_own = order(slots(to_normed, 0, 1), qkv_grad)
    else:
        down_slabs = slabs_of_rows(down_sum)
        qkv_sum = slab_sum(slab_product(normed, qkv_grad))
        normed_own, came = scatter(to_normed, qkv_grad), ()
    if square:
        result = order(
            lambda rest, *came: (middle + (summed(rest[:count], came) + down_bias)).astype(low),
            result_rest,
            *result_came,
        )
    else:
        result = (middle + (scatter(to_result, active).astype(wide) + down_bias)).astype(low)
    result = result.reshape(tokens.shape)
    qkv_column_sum = order(column_sum, qkv_grad)
    grad_tokens, _, input_sums = order(
        lambda own, *came: norm_back(own, x_low, middle_grad, ln1_gain, came), normed_own, *came
    )
    grad_tokens = grad_tokens.reshape(tokens.shape)
    up_slabs = slabs_of_rows(gate(up_sum, *came, normed_own))
    qkv_slabs = slabs_of_rows(qkv_sum)

    def rows_of(slabs):
        return jnp.swapaxes(slabs, 0, 1).astype(wide)

    grad_w_down = rows_of(down_slabs).reshape(-1, hidden_width).T
    grad_w_up = rows_of(up_slabs).reshape(-1, hidden_width)
    grad_w_qkv = rows_of(qkv_slabs).reshape(-1, groups, pairs, 3, PAIR)
    grad_w_qkv = jnp.transpose(grad_w_qkv, (0, 3, 1, 2, 4)).reshape(-1, 3 * model_width)

    head_sum = jnp.transpose(qkv_column_sum.reshape(pairs, 3, PAIR), (1, 0, 2)).reshape(3, slab)
    qv_sum = lax.dynamic_update_slice_in_dim(
        jnp.zeros((2, model_width), wide), head_sum[0::2], me * slab, axis=1
    )
    late = [qv_sum.reshape(-1), input_sums[0], input_sums[1]]
    sums = order(lambda *parts: jnp.concatenate(parts).reshape(-1, PAIR), *early, *late)
    stages = total_stages()
    for axis, masks in stages:
        others = range(lax.axis_size(axis))
        came = [lax.ppermute(sums, axis, [(i, i ^ mask) for i in others]) for mask in masks]
        if (axis, masks) == stages[-1]:
            order.after(up_slabs, qkv_slabs)
        sums = order(lambda *parts: sum(parts[1:], parts[0]), sums, *came)
    sums = sums.reshape(-1)

    def cut(at, count):
        return sums[at * model_width : (at + count) * model_width]

    ratio = hidden_width // model_width
    return (
        result,
        grad_tokens,
        grad_w_qkv,
        cut(4 + ratio, 2).reshape(2, model_width),
        grad_w_out,
        cut(0, 1),
        cut(6 + ratio, 1),
        cut(7 + ratio, 1),
        cut(1, 1),
        cut(2, 1),
        grad_w_up,
        cut(3, ratio),
        grad_w_down,
        cut(3 + ratio, 1),
    )


def solution(mesh):
    return jax.shard_map(
        local,
        mesh=mesh,
        in_specs=(
            P("fsdp", "seq", None),
            P("fsdp", "seq", None),
            P("fsdp", None),
            P(),
            P("fsdp", None),
            P(),
            P(),
            P(),
            P(),
            P(),
            P("fsdp", None),
            P(),
            P(None, "fsdp"),
            P(),
        ),
        out_specs=(
            P("fsdp", "seq", None),
            P("fsdp", "seq", None),
            P(("seq", "fsdp"), None),
            P(),
            P(("seq", "fsdp"), None),
            P(),
            P(),
            P(),
            P(),
            P(),
            P(("seq", "fsdp"), None),
            P(),
            P(None, ("seq", "fsdp")),
            P(),
        ),
        check_vma=False,
    )
```

```python
import math
from functools import partial

import jax
import jax.numpy as jnp
from jax import lax
from jax.experimental import pallas as pl
from jax.experimental.pallas import tpu as pltpu
from jax.sharding import PartitionSpec as P

HEADS = 32
HEAD_DIM = 64
BLOCK = 256
PAIR = 2 * HEAD_DIM
GRANT = 58 * 2**20


def estimate(flops, transcendentals=0):
    return pl.CostEstimate(flops=flops // 4, bytes_accessed=flops // 4096, transcendentals=transcendentals // 4)


def layer_norm(token_rows, gain_vec, shift_vec):
    average = jnp.mean(token_rows, axis=-1, keepdims=True)
    centred = token_rows - average
    spread = jnp.mean(centred * centred, axis=-1, keepdims=True)
    scale = lax.rsqrt(spread + 1e-05)
    return centred * scale * gain_vec + shift_vec, average, scale


def contract(left_side, right_side):
    return lax.dot_general(
        left_side, right_side, (((1,), (0,)), ((), ())), preferred_element_type=jnp.float32
    )


def contract_last(left_side, right_side):
    return lax.dot_general(
        left_side, right_side, (((1,), (1,)), ((), ())), preferred_element_type=jnp.float32
    )


def contract_first(left_side, right_side):
    return lax.dot_general(
        left_side, right_side, (((0,), (0,)), ((), ())), preferred_element_type=jnp.float32
    )


def row_pieces(mask, sequence, block, seqs, local):
    per = BLOCK // local
    return [
        pl.ds(pl.multiple_of((((block * per + r) ^ mask) * seqs + sequence) * local, local), local)
        for r in range(per)
    ]


def load_rows(ref, pieces, columns):
    parts = [ref[piece, columns] for piece in pieces]
    return parts[0] if len(parts) == 1 else jnp.concatenate(parts, axis=0)


def store_rows(ref, pieces, columns, values):
    local = values.shape[0] // len(pieces)
    for r, piece in enumerate(pieces):
        ref[piece, columns] = values[r * local : (r + 1) * local]


Q_COLUMNS, K_COLUMNS, V_COLUMNS = (slice(t * PAIR, (t + 1) * PAIR) for t in range(3))


def attend_forward_kernel(mask_ref, slope_ref, qkv_ref, mixed_ref, lse_ref, *, blocks, seqs, local):
    pair, sequence = pl.program_id(0), pl.program_id(1)
    mask = mask_ref[0]
    lane = lax.broadcasted_iota(jnp.int32, (BLOCK, PAIR), 1)
    row = lax.broadcasted_iota(jnp.int32, (BLOCK, BLOCK), 0)
    column = lax.broadcasted_iota(jnp.int32, (BLOCK, BLOCK), 1)
    gap = (row - column).astype(jnp.float32)
    pieces = [row_pieces(mask, sequence, block, seqs, local) for block in range(blocks)]

    for i in range(blocks):
        q_pair = load_rows(qkv_ref, pieces[i], Q_COLUMNS)
        outs, lses = [], []
        for head in range(2):
            slope = slope_ref[pair * 2 + head]
            mine = (lane >= head * HEAD_DIM) & (lane < (head + 1) * HEAD_DIM)
            q = jnp.where(mine, q_pair, jnp.zeros_like(q_pair)) * jnp.bfloat16(HEAD_DIM**-0.5)
            parts, highest = [], None
            for j in range(i + 1):
                scores = contract_last(q, load_rows(qkv_ref, pieces[j], K_COLUMNS))
                distance = jnp.abs(gap) if i == j else gap + float(BLOCK * (i - j))
                scores = scores - slope * distance
                parts.append(scores)
                top = jnp.max(scores, axis=-1, keepdims=True)
                highest = top if highest is None else jnp.maximum(highest, top)
            total, out = None, None
            for j in range(i + 1):
                weights = jnp.exp(parts[j] - highest)
                part = jnp.sum(weights, axis=-1, keepdims=True)
                mixed = contract(weights.astype(jnp.bfloat16), load_rows(qkv_ref, pieces[j], V_COLUMNS))
                total = part if total is None else total + part
                out = mixed if out is None else out + mixed
            outs.append(out / total)
            lses.append(highest + jnp.log(total))
        first = lane < HEAD_DIM
        everything = slice(0, PAIR)
        store_rows(
            mixed_ref, pieces[i], everything, jnp.where(first, outs[0], outs[1]).astype(mixed_ref.dtype)
        )
        store_rows(lse_ref, pieces[i], everything, jnp.where(first, lses[0], lses[1]))


def attend_backward_kernel(
    mask_ref, slope_ref, qkv_ref, lse_ref, mixed_ref, *rest, blocks, seqs, local, start, grads
):
    out_ref, dq_ref, dk_ref, dv_ref, grad_ref = rest[-5:]
    pair, sequence = pl.program_id(0) + start, pl.program_id(1)
    mask = mask_ref[0]
    lane = lax.broadcasted_iota(jnp.int32, (BLOCK, PAIR), 1)
    key = lax.broadcasted_iota(jnp.int32, (BLOCK, BLOCK), 0)
    query = lax.broadcasted_iota(jnp.int32, (BLOCK, BLOCK), 1)
    gap = (query - key).astype(jnp.float32)
    pieces = [row_pieces(mask, sequence, block, seqs, local) for block in range(blocks)]
    everything = slice(0, PAIR)

    @pl.when(sequence == 0)
    def _():
        at = 0
        for part in rest[:grads]:
            grad_ref[at : at + part.shape[0], :] = part[...]
            at += part.shape[0]

    for i in range(blocks):
        q_pair = load_rows(qkv_ref, pieces[i], Q_COLUMNS)
        up_pair = load_rows(grad_ref, pieces[i], everything)
        mixed_pair = load_rows(mixed_ref, pieces[i], everything)
        inner_all = (up_pair.astype(jnp.float32) * mixed_pair.astype(jnp.float32)).T
        lse_all = load_rows(lse_ref, pieces[i], everything).T
        dq = None
        for head in range(2):
            slope = slope_ref[pair * 2 + head]
            mine = (lane >= head * HEAD_DIM) & (lane < (head + 1) * HEAD_DIM)
            zero = jnp.zeros_like(q_pair)
            q = jnp.where(mine, q_pair, zero) * jnp.bfloat16(HEAD_DIM**-0.5)
            up = jnp.where(mine, up_pair, zero)
            inner = jnp.sum(inner_all[head * HEAD_DIM : (head + 1) * HEAD_DIM], axis=0, keepdims=True)
            lse = lse_all[head * HEAD_DIM : head * HEAD_DIM + 1]
            for j in range(i + 1):
                k_pair = load_rows(qkv_ref, pieces[j], K_COLUMNS)
                distance = jnp.abs(gap) if i == j else gap + float(BLOCK * (i - j))
                probs = jnp.exp(contract_last(k_pair, q) - slope * distance - lse)
                prob_grad = contract_last(load_rows(qkv_ref, pieces[j], V_COLUMNS), up)
                score_grad = (probs * (prob_grad - inner)).astype(jnp.bfloat16)
                dv = contract(probs.astype(jnp.bfloat16), up)
                dk = contract(score_grad, q)
                part = contract_first(score_grad, jnp.where(mine, k_pair, zero))
                dq = part if dq is None else dq + part
                if i == j and head == 0:
                    dv_ref[j] = dv
                    dk_ref[j] = dk
                else:
                    dv_ref[j] += dv
                    dk_ref[j] += dk
        dq_ref[i] = dq
    for i in range(blocks):
        store_rows(out_ref, pieces[i], Q_COLUMNS, (dq_ref[i] * HEAD_DIM**-0.5).astype(out_ref.dtype))
        store_rows(out_ref, pieces[i], K_COLUMNS, dk_ref[i].astype(out_ref.dtype))
        store_rows(out_ref, pieces[i], V_COLUMNS, dv_ref[i].astype(out_ref.dtype))


def attend_forward(mask, slopes, qkv, seqs, local):
    rows, width = qkv.shape
    pairs, blocks = width // (3 * PAIR), rows // seqs // BLOCK
    scored = pairs * seqs * blocks * (blocks + 1) * BLOCK * BLOCK
    return pl.pallas_call(
        partial(attend_forward_kernel, blocks=blocks, seqs=seqs, local=local),
        grid_spec=pltpu.PrefetchScalarGridSpec(
            num_scalar_prefetch=2,
            grid=(pairs, seqs),
            in_specs=[pl.BlockSpec((rows, 3 * PAIR), lambda p, *_: (0, p))],
            out_specs=[pl.BlockSpec((rows, PAIR), lambda p, *_: (0, p))] * 2,
        ),
        out_shape=[
            jax.ShapeDtypeStruct((rows, pairs * PAIR), jnp.bfloat16),
            jax.ShapeDtypeStruct((rows, pairs * PAIR), jnp.float32),
        ],
        compiler_params=pltpu.CompilerParams(vmem_limit_bytes=GRANT),
        cost_estimate=estimate(scored * 2 * 512, scored),
        name="attend_forward",
    )(mask, slopes, qkv)


def attend_backward(mask, slopes, qkv, lse, mixed, grads, seqs, local, start, stop, begun=None):
    rows, width = qkv.shape
    blocks = rows // seqs // BLOCK
    scored = (stop - start) * seqs * blocks * (blocks + 1) * BLOCK * BLOCK
    narrow = pl.BlockSpec((rows, PAIR), lambda p, *_: (0, p + start))
    wide = pl.BlockSpec((rows, 3 * PAIR), lambda p, *_: (0, p + start))
    earlier = [] if begun is None else [begun]
    return pl.pallas_call(
        partial(
            attend_backward_kernel, blocks=blocks, seqs=seqs, local=local, start=start, grads=len(grads)
        ),
        grid_spec=pltpu.PrefetchScalarGridSpec(
            num_scalar_prefetch=2,
            grid=(stop - start, seqs),
            in_specs=[wide, narrow, narrow]
            + [pl.BlockSpec((grad.shape[0], PAIR), lambda p, *_: (0, p + start)) for grad in grads]
            + [pl.BlockSpec(memory_space=pl.ANY)] * len(earlier),
            out_specs=wide,
            scratch_shapes=[pltpu.VMEM((blocks, BLOCK, PAIR), jnp.float32)] * 3
            + [pltpu.VMEM((rows, PAIR), jnp.bfloat16)],
        ),
        out_shape=jax.ShapeDtypeStruct((rows, width), jnp.bfloat16),
        input_output_aliases={5 + len(grads): 0} if earlier else {},
        compiler_params=pltpu.CompilerParams(vmem_limit_bytes=GRANT),
        cost_estimate=estimate(scored * 2 * 1280, scored),
        name="attend_backward",
    )(mask, slopes, qkv, lse, mixed, *grads, *earlier)


def head_columns_kernel(at_ref, in_ref, out_ref):
    for t in range(3):

        @pl.when(pl.program_id(0) == t)
        def _():
            for pair in range(in_ref.shape[1] // PAIR):
                at = (pair * 3 + t) * PAIR
                out_ref[:, at : at + PAIR] = in_ref[:, pair * PAIR : (pair + 1) * PAIR]


def up_kernel(rows_ref, weight_ref, bias_ref, active_ref, slope_ref, *, chunk):
    rows = rows_ref[...]
    for at in range(0, weight_ref.shape[1], chunk):
        columns = slice(at, at + chunk)
        hidden = contract(rows, weight_ref[:, columns]) + bias_ref[:, columns]
        below = 0.5 + 0.5 * lax.erf(hidden * 2**-0.5)
        active_ref[:, columns] = (hidden * below).astype(active_ref.dtype)
        slope_ref[:, columns] = below + hidden * ((2 * math.pi) ** -0.5 * jnp.exp(-0.5 * hidden * hidden))


def hidden_grad_kernel(rows_ref, weight_ref, slope_ref, grad_ref, sum_ref, *, chunk):
    rows = rows_ref[...]
    starting = pl.program_id(0) == 0
    for at in range(0, weight_ref.shape[0], chunk):
        columns = slice(at, at + chunk)
        grad = contract_last(rows, weight_ref[columns, :]) * slope_ref[:, columns]
        grad = grad.astype(grad_ref.dtype)
        grad_ref[:, columns] = grad
        part = jnp.sum(grad.astype(jnp.float32), axis=0, keepdims=True)
        sum_ref[:, columns] = jnp.where(starting, part, sum_ref[:, columns] + part)


TILE = 256


def up_and_bend(rows, weight, bias):
    count, depth = rows.shape
    width = weight.shape[1]
    tile = pl.BlockSpec((TILE, width), lambda i: (i, 0))
    return pl.pallas_call(
        partial(up_kernel, chunk=512),
        grid=(count // TILE,),
        in_specs=[
            pl.BlockSpec((TILE, depth), lambda i: (i, 0)),
            pl.BlockSpec((depth, width), lambda i: (0, 0), pipeline_mode=pl.Buffered(1)),
            pl.BlockSpec((1, width), lambda i: (0, 0)),
        ],
        out_specs=[tile, tile],
        out_shape=[
            jax.ShapeDtypeStruct((count, width), jnp.bfloat16),
            jax.ShapeDtypeStruct((count, width), jnp.float32),
        ],
        compiler_params=pltpu.CompilerParams(vmem_limit_bytes=GRANT),
        cost_estimate=estimate(count * depth * width * 4, 2 * count * width),
        name="up_and_bend",
    )(rows, weight, bias)


def hidden_gradient(rows, weight, slope, start, count):
    depth = rows.shape[1]
    width = weight.shape[0]
    first = start // TILE
    line = pl.BlockSpec((1, width), lambda i: (0, 0))
    return pl.pallas_call(
        partial(hidden_grad_kernel, chunk=512),
        grid=(count // TILE,),
        in_specs=[
            pl.BlockSpec((TILE, depth), lambda i: (i + first, 0)),
            pl.BlockSpec((width, depth), lambda i: (0, 0), pipeline_mode=pl.Buffered(1)),
            pl.BlockSpec((TILE, width), lambda i: (i + first, 0)),
        ],
        out_specs=[pl.BlockSpec((TILE, width), lambda i: (i, 0)), line],
        out_shape=[
            jax.ShapeDtypeStruct((count, width), jnp.bfloat16),
            jax.ShapeDtypeStruct((1, width), jnp.float32),
        ],
        compiler_params=pltpu.CompilerParams(vmem_limit_bytes=GRANT),
        cost_estimate=estimate(count * depth * width * 3, 0),
        name="hidden_gradient",
    )(rows, weight, slope)


def mixed_grad_kernel(rows_ref, weight_ref, out_ref):
    out_ref[...] = contract_last(rows_ref[...], weight_ref[...]).astype(out_ref.dtype)


def mixed_gradient(rows, weight, slab):
    count, depth = rows.shape
    width = weight.shape[0]
    return pl.pallas_call(
        mixed_grad_kernel,
        grid=(width // slab,),
        in_specs=[
            pl.BlockSpec((count, depth), lambda i: (0, 0), pipeline_mode=pl.Buffered(1)),
            pl.BlockSpec((slab, depth), lambda i: (i, 0)),
        ],
        out_specs=pl.BlockSpec((count, slab), lambda i: (0, i)),
        out_shape=jax.ShapeDtypeStruct((count, width), jnp.bfloat16),
        compiler_params=pltpu.CompilerParams(vmem_limit_bytes=GRANT),
        cost_estimate=estimate(2 * count * depth * width, 0),
        name="mixed_gradient",
    )(rows, weight)


def norm_back_kernel(own_ref, values_ref, average_ref, scale_ref, base_ref, gain_ref, *refs, parts):
    came, (low_ref, wide_ref, sums_ref) = refs[:parts], refs[parts:]
    wide = jnp.float32
    step = pl.program_id(0)

    @pl.when(step == 0)
    def _():
        sums_ref[...] = jnp.zeros_like(sums_ref)

    def make(came):
        grad = own_ref[...].astype(wide)
        for part in came:
            grad = grad + part[...].astype(wide)
        scale = scale_ref[...]
        normal = (values_ref[...].astype(wide) - average_ref[...]) * scale
        gained = grad * gain_ref[...]
        along = jnp.mean(gained * normal, axis=-1, keepdims=True)
        across = jnp.mean(gained, axis=-1, keepdims=True)
        made = base_ref[...].astype(wide) + scale * (gained - across - normal * along)
        low = made.astype(low_ref.dtype)
        low_ref[...] = low
        wide_ref[...] = made
        for at, part in enumerate((grad * normal, grad, low.astype(wide))):
            sums_ref[8 * at : 8 * at + 8, :] += jnp.sum(part.reshape(-1, 8, part.shape[1]), axis=0)

    if not came:
        make(())
        return
    upper = step < pl.num_programs(0) // 2
    pl.when(upper)(lambda: make(came[0::2]))
    pl.when(jnp.logical_not(upper))(lambda: make(came[1::2]))


def norm_back(rest, values, average, scale, base, gain, came):
    rows, width = values.shape
    steps = 8
    half = steps // 2
    came = list(came or ())
    count = rows // steps
    tile = pl.BlockSpec((count, width), lambda i: (i, 0))
    thin = pl.BlockSpec((count, 1), lambda i: (i, 0))
    top = pl.BlockSpec((count, width), lambda i: (jnp.minimum(i, half - 1), 0))
    bottom = pl.BlockSpec((count, width), lambda i: (jnp.maximum(i - half, 0), 0))
    low, full, sums = pl.pallas_call(
        partial(norm_back_kernel, parts=len(came)),
        grid=(steps,),
        in_specs=[tile, tile, thin, thin, tile, pl.BlockSpec((1, width), lambda i: (0, 0))]
        + [top, bottom] * (len(came) // 2),
        out_specs=[tile, tile, pl.BlockSpec((24, width), lambda i: (0, 0))],
        out_shape=[
            jax.ShapeDtypeStruct((rows, width), jnp.bfloat16),
            jax.ShapeDtypeStruct((rows, width), jnp.float32),
            jax.ShapeDtypeStruct((24, width), jnp.float32),
        ],
        compiler_params=pltpu.CompilerParams(vmem_limit_bytes=GRANT),
        cost_estimate=estimate(30 * rows * width, rows),
        name="norm_back",
    )(rest, values, average, scale, base, gain[None], *came)
    return low, full, jnp.sum(sums.reshape(3, 8, width), axis=1)


def outer_kernel(left_ref, *refs, chunk):
    right_refs, out_ref = refs[:-1], refs[-1]
    shards = out_ref.shape[0]
    for at in range(0, out_ref.shape[3], chunk):
        columns = slice(at, at + chunk)
        made, row = None, 0
        for right_ref in right_refs:
            count = right_ref.shape[0]
            part = contract_first(left_ref[row : row + count, :], right_ref[:, columns])
            made = part if made is None else made + part
            row += count
        out_ref[:, 0, :, columns] = made.astype(out_ref.dtype).reshape(shards, -1, made.shape[1])


def outer(left, rights, groups, shards):
    rights = rights if isinstance(rights, (list, tuple)) else [rights]
    tokens, rows = left.shape
    width = rights[0].shape[1]
    part = rows // groups
    made = pl.pallas_call(
        partial(outer_kernel, chunk=512 if width % 512 == 0 else 256),
        grid=(groups,),
        in_specs=[pl.BlockSpec((tokens, part), lambda i: (0, i))]
        + [
            pl.BlockSpec((right.shape[0], width), lambda i: (0, 0), pipeline_mode=pl.Buffered(1))
            for right in rights
        ],
        out_specs=pl.BlockSpec((shards, 1, part // shards, width), lambda i: (0, i, 0, 0)),
        out_shape=jax.ShapeDtypeStruct((shards, groups, part // shards, width), jnp.bfloat16),
        compiler_params=pltpu.CompilerParams(vmem_limit_bytes=GRANT),
        cost_estimate=estimate(2 * tokens * rows * width, 0),
        name="outer",
    )(left, *rights)
    return made.reshape(rows, width)


def swap(values, bit):
    return lax.ppermute(values, "seq", [(i, i ^ bit) for i in range(4)])


def by_index(parts, me):
    if len(parts) != 4:
        return parts
    odd, upper = (me & 1) == 1, (me & 2) == 2
    a, b, c, d = parts
    a, b, c, d = (
        jnp.where(odd, b, a),
        jnp.where(odd, a, b),
        jnp.where(odd, d, c),
        jnp.where(odd, c, d),
    )
    return [jnp.where(upper, c, a), jnp.where(upper, d, b), jnp.where(upper, a, c), jnp.where(upper, b, d)]


def exchange(slots):
    if lax.axis_size("seq") != 4:
        return list(lax.all_to_all(jnp.stack(slots), "seq", split_axis=0, concat_axis=0, tiled=True))
    return [slots[0]] + [swap(slots[j], j) for j in (1, 2, 3)]


def gate(values, *before):
    return lax.optimization_barrier((values, *before))[0]


class Order:
    def __init__(self):
        self.pending = []

    def after(self, *values):
        self.pending += values

    def __call__(self, operation, *operands):
        if self.pending:
            count = len(operands)
            operands = lax.optimization_barrier((*operands, *self.pending))[:count]
        made = operation(*operands)
        self.pending = jax.tree.leaves(made)
        return made

    def gather(self, rows):
        if lax.axis_size("seq") != 4:
            return lax.all_gather(jnp.concatenate(rows, axis=0), "seq", axis=0, tiled=True), None
        top, bottom = rows
        return rows, (swap(bottom, 1), swap(top, 2), swap(top, 1), swap(bottom, 2))

    def fill(self, begun):
        rows, came = begun
        if came is None:
            return rows
        first_bottom, second_top, first_top, second_bottom = came
        room = jnp.zeros_like(rows[0])
        parts = (*rows, first_top, first_bottom, second_top, second_bottom, room, room)
        return self(lambda *parts: jnp.concatenate(parts, axis=0), *parts)

    def complete(self, made, pieces):
        if not isinstance(pieces, list):
            return made
        rows = pieces[-1].shape[0]

        def put(before, first, second):
            before = lax.dynamic_update_slice_in_dim(before, first, 6 * rows, axis=0)
            return lax.dynamic_update_slice_in_dim(before, second, 7 * rows, axis=0)

        return self(put, made, *pieces[-2:])

    def pass_on(self, begun, *before):
        rows, came = begun
        if came is None:
            return rows
        first_bottom, second_top, first_top, second_bottom = came
        self.after(*came)
        if before:
            second_top, first_bottom = gate((second_top, first_bottom), *before)
        far = [swap(second_top, 1), swap(first_bottom, 2)]
        return [*rows, first_top, first_bottom, second_top, second_bottom, *far]

    def halves(self, product, rows):
        def cut(values):
            made = product(values)
            half = made.shape[0] // 2
            return made[:half], made[half:]

        return self(cut, rows)

    def add_far(self, made, far, direct, *before, at=None):
        wide = jnp.float32
        half = far[0].shape[0]
        start = made.shape[0] - 4 * half if at is None else at

        def add(made, top, bottom):
            at = start
            first = (made[at + half : at + 2 * half].astype(wide) + bottom.astype(wide)).astype(made.dtype)
            second = (made[at + 2 * half : at + 3 * half].astype(wide) + top.astype(wide)).astype(made.dtype)
            if direct is None:
                first = jnp.concatenate([made[at : at + half], first], axis=0)
                second = jnp.concatenate([second, made[at + 3 * half : at + 4 * half]], axis=0)
            return first, second

        first, second = self(add, made, *far)
        if before:
            first, second = gate((first, second), *before)
        first, second = swap(first, 1), swap(second, 2)
        return (first, second) if direct is None else (direct[0], first, second, direct[1])


def swap_far(halves):
    return swap(halves[0], 1), swap(halves[1], 2)


def swap_direct(made, half):
    at = made.shape[0] - 4 * half
    return swap(made[at : at + half], 1), swap(made[at + 3 * half :], 2)


def summed(own, came):
    wide = jnp.float32
    own = own.astype(wide)
    return sum((part.astype(wide) for part in came), own)


def whole(parts):
    return jnp.concatenate(parts, axis=0) if isinstance(parts, list) else parts


def total_stages():
    stages = []
    for axis in ("fsdp", "seq"):
        count, bit = lax.axis_size(axis), 1
        bits = count.bit_length() - 1
        while bit < count:
            stages.append((axis, [bit] if bits % 2 else [bit, 2 * bit, 3 * bit]))
            bit <<= 1 if bits % 2 else 2
            bits -= bits % 2
    return stages


def local(
    tokens,
    cotangent,
    w_qkv,
    qv_bias,
    w_out,
    out_bias,
    ln1_gain,
    ln1_shift,
    ln2_gain,
    ln2_shift,
    w_up,
    up_bias,
    w_down,
    down_bias,
):
    seq_count, local_len, model_width = tokens.shape
    groups, shards = lax.axis_size("seq"), lax.axis_size("fsdp")
    me = lax.axis_index("seq")
    square = groups == 4
    heads_here = HEADS // groups
    slab = heads_here * HEAD_DIM
    pairs = slab // PAIR
    hidden_width = w_up.shape[1]
    hidden_slab = hidden_width // groups
    rows_here = seq_count * local_len
    low, wide = jnp.bfloat16, jnp.float32
    mask = jnp.reshape(me if square else jnp.zeros_like(me), (1,)).astype(jnp.int32)
    head_index = me * heads_here + jnp.arange(1, heads_here + 1, dtype=jnp.int32)
    slopes = 2.0 ** (-8.0 * head_index.astype(wide) / HEADS)

    def head_columns(values):
        rows = values.shape[0]
        return pl.pallas_call(
            head_columns_kernel,
            grid_spec=pltpu.PrefetchScalarGridSpec(
                num_scalar_prefetch=1,
                grid=(3,),
                in_specs=[pl.BlockSpec((rows, slab), lambda t, at: (0, t * groups + at[0]))],
                out_specs=pl.BlockSpec((rows, 3 * slab), lambda t, at: (0, 0)),
            ),
            out_shape=jax.ShapeDtypeStruct((rows, 3 * slab), values.dtype),
            name="head_columns",
        )(jnp.reshape(me, (1,)).astype(jnp.int32), values)

    def own_slab(values, axis):
        width = values.shape[axis] // groups
        return lax.dynamic_slice_in_dim(values, me * width, width, axis=axis)

    order = Order()
    x_low = tokens.reshape(rows_here, model_width)
    x = x_low.astype(wide)
    dz_low = cotangent.reshape(rows_here, model_width)
    qkv_slab = lax.all_gather(head_columns(w_qkv), "fsdp", axis=0, tiled=True)
    qkv_bias = head_columns(jnp.concatenate([qv_bias[0], jnp.zeros_like(qv_bias[0]), qv_bias[1]])[None])
    up_bias_slab = own_slab(up_bias, 0)

    first_norm, *first_stats = layer_norm(x, ln1_gain, ln1_shift)
    half = rows_here // 2

    def halves_of(values):
        return values[:half].astype(low), values[half:].astype(low)

    normed = order.gather(order(halves_of, first_norm))
    normed = order.pass_on(normed)
    full_out = lax.all_gather(w_out, "fsdp", axis=0, tiled=True)
    up_slab = lax.all_gather(own_slab(gate(w_up, normed[0]) if square else w_up, 1), "fsdp", axis=0, tiled=True)
    down_slab = lax.all_gather(own_slab(gate(w_down, normed[0]) if square else w_down, 0), "fsdp", axis=1, tiled=True)
    normed = whole(normed)
    upstream = order.gather(halves_of(gate(dz_low, normed)))
    qkv = order(lambda rows: (contract(rows, qkv_slab) + qkv_bias).astype(low), normed)
    attended, log_totals = order(lambda rows: attend_forward(mask, slopes, rows, seq_count, local_len), qkv)
    if square:
        attended = gate(attended, *upstream[1])
    mixed_slots = exchange([attended[j * rows_here : (j + 1) * rows_here] for j in range(groups)])
    mixed_rows = jnp.concatenate(by_index(mixed_slots, me), axis=1)
    mixed_slots = jnp.concatenate(mixed_slots, axis=1)

    def pair_swap(values):
        return lax.ppermute(values, "fsdp", [(i, i ^ 1) for i in range(shards)])

    parity = lax.axis_index("fsdp") & 1
    out_rows = model_width // (groups * shards)

    def pair_halves(values):
        halves = values.reshape(rows_here, -1, 2, out_rows)
        return tuple(
            lax.dynamic_index_in_dim(halves, index, axis=2, keepdims=False).reshape(rows_here, -1)
            for index in (parity, 1 - parity)
        )

    middle = order(lambda rows: x + (contract(rows, full_out) + out_bias), mixed_rows)
    second_norm, *second_stats = layer_norm(middle, ln2_gain, ln2_shift)
    second = order.gather(order(halves_of, second_norm))
    mine, theirs = order(pair_halves, mixed_slots)
    upstream_made = order.fill(upstream)
    mixed_half = order(lambda *parts: jnp.concatenate(parts, axis=0), mine, pair_swap(theirs))
    dz_sum = order(lambda values: jnp.sum(values.astype(wide), axis=0), dz_low)
    second = whole(order.pass_on(second))
    upstream = order.pass_on(upstream, second)
    active, slope = order(lambda rows: up_and_bend(rows, up_slab, up_bias_slab[None]), second)
    upstream = order.complete(upstream_made, upstream)

    def slab_product(left, right):
        return order(lambda rows: outer(rows, right, groups, shards), left)

    def slab_sum(made):
        return lax.psum_scatter(made, "fsdp", scatter_dimension=0, tiled=True)

    def slabs_of_rows(values):
        return lax.all_to_all(
            values.reshape(groups, -1, values.shape[1]), "seq", split_axis=0, concat_axis=0, tiled=True
        )

    down_sum = slab_sum(slab_product(upstream, active))
    count = rows_here

    def slots(product, start, stop):
        return lambda values: product(values[start * count : stop * count])

    def to_second(rows):
        return contract_last(rows, up_slab).astype(low)

    def to_result(rows):
        return contract(rows, down_slab).astype(low)

    def to_normed(rows):
        return contract_last(rows, qkv_slab).astype(low)

    def scatter(product, rows):
        return lax.psum_scatter(order(product, rows), "seq", scatter_dimension=0, tiled=True)

    hidden_grad, hidden_sum = order(lambda rows: hidden_gradient(rows, down_slab, slope, 0, groups * count), upstream)
    if square:
        far = swap_far(order.halves(slots(to_second, 3, 4), hidden_grad))
        rest = order(slots(to_second, 0, 3), hidden_grad)
        second_own = rest
        direct = swap_direct(rest, half)
        came = order.add_far(rest, far, direct)
        result_far = order.halves(slots(to_result, 3, 4), active)
        up_sum = slab_sum(gate(slab_product(second, hidden_grad), *came))
        result_far = swap_far(gate(result_far, *came))
    else:
        second_own, came = scatter(to_second, hidden_grad), ()
        up_sum = slab_sum(slab_product(second, hidden_grad))
    branch_grad, middle_grad, middle_sums = order(
        lambda own, *came: norm_back(own, middle, *second_stats, dz_low, ln2_gain, came), second_own, *came
    )

    def column_sum(values):
        return jnp.sum(values.astype(wide), axis=0)

    hidden_sum = lax.dynamic_update_slice_in_dim(
        jnp.zeros((hidden_width,), wide), hidden_sum[0], me * hidden_slab, axis=0
    )
    early = [middle_sums[2], middle_sums[0], middle_sums[1], hidden_sum, dz_sum]
    mixed_grad = order(lambda rows: mixed_gradient(rows, full_out, slab), branch_grad)
    if square:
        mixed_grad = gate(mixed_grad, *result_far)
    mixed_grad = exchange(by_index([mixed_grad[:, j * slab : (j + 1) * slab] for j in range(groups)], me))
    if square:
        result_rest = order(slots(to_result, 0, 3), active)
    branch_other = pair_swap(branch_grad)
    branch_pair = jnp.concatenate([branch_grad, branch_other], axis=0)
    out_sum = order(lambda columns: outer(columns, branch_pair, groups, 1), mixed_half)
    attention = (mask, slopes, qkv, log_totals, attended)
    if square:
        part = out_sum.shape[0] // 4
        out_far = out_sum[3 * part : 3 * part + part // 2], out_sum[3 * part + part // 2 :]
        out_far = swap_far(gate(out_far, *mixed_grad))
        result_came = order.add_far(result_rest, result_far, None, *mixed_grad)
    order.after(down_sum)
    begun = order(
        lambda *grads: attend_backward(*attention, grads, seq_count, local_len, 0, pairs // 2), *mixed_grad
    )
    if square:
        out_came = order.add_far(out_sum, out_far, None, at=part)
    qkv_grad = order(
        lambda *grads: attend_backward(*attention, grads, seq_count, local_len, pairs // 2, pairs, begun),
        *mixed_grad,
    )
    if square:
        order.after(*out_came, *result_came)
        out_sum = order(lambda own, *came: summed(own[:part], came).astype(low), out_sum, *out_came)
        order.after(*out_came)
    else:
        out_sum = lax.psum_scatter(out_sum, "seq", scatter_dimension=0, tiled=True)
    out_sum = out_sum.reshape(-1, 1, out_rows, model_width)
    zero = jnp.zeros_like(out_sum)
    out_sum = jnp.concatenate(
        [jnp.where(parity == 0, out_sum, zero), jnp.where(parity == 1, out_sum, zero)], axis=1
    ).reshape(-1, model_width)
    grad_w_out = lax.psum_scatter(out_sum, "fsdp", scatter_dimension=0, tiled=True).astype(wide)
    order.after(up_sum)
    if square:
        far = swap_far(order.halves(slots(to_normed, 3, 4), qkv_grad))
        qkv_sum = slab_sum(gate(slab_product(normed, qkv_grad), *far, grad_w_out))
        near = order(slots(to_normed, 1, 3), qkv_grad)
        direct = swap_direct(near, half)
        down_slabs = slabs_of_rows(gate(down_sum, *far))
        order.after(down_slabs)
        came = order.add_far(near, far, direct)
        normed_own = order(slots(to_normed, 0, 1), qkv_grad)
    else:
        down_slabs = slabs_of_rows(down_sum)
        qkv_sum = slab_sum(slab_product(normed, qkv_grad))
        normed_own, came = scatter(to_normed, qkv_grad), ()
    if square:
        result = order(
            lambda rest, *came: (middle + (summed(rest[:count], came) + down_bias)).astype(low),
            result_rest,
            *result_came,
        )
    else:
        result = (middle + (scatter(to_result, active).astype(wide) + down_bias)).astype(low)
    result = result.reshape(tokens.shape)
    qkv_column_sum = order(column_sum, qkv_grad)
    grad_tokens, _, input_sums = order(
        lambda own, *came: norm_back(own, x_low, *first_stats, middle_grad, ln1_gain, came), normed_own, *came
    )
    grad_tokens = grad_tokens.reshape(tokens.shape)
    up_slabs = slabs_of_rows(gate(up_sum, *came, normed_own))
    qkv_slabs = slabs_of_rows(qkv_sum)

    def rows_of(slabs):
        return jnp.swapaxes(slabs, 0, 1).astype(wide)

    grad_w_down = rows_of(down_slabs).reshape(-1, hidden_width).T
    grad_w_up = rows_of(up_slabs).reshape(-1, hidden_width)
    grad_w_qkv = rows_of(qkv_slabs).reshape(-1, groups, pairs, 3, PAIR)
    grad_w_qkv = jnp.transpose(grad_w_qkv, (0, 3, 1, 2, 4)).reshape(-1, 3 * model_width)

    head_sum = jnp.transpose(qkv_column_sum.reshape(pairs, 3, PAIR), (1, 0, 2)).reshape(3, slab)
    qv_sum = lax.dynamic_update_slice_in_dim(
        jnp.zeros((2, model_width), wide), head_sum[0::2], me * slab, axis=1
    )
    late = [qv_sum.reshape(-1), input_sums[0], input_sums[1]]
    sums = order(lambda *parts: jnp.concatenate(parts).reshape(-1, PAIR), *early, *late)
    stages = total_stages()
    for axis, masks in stages:
        others = range(lax.axis_size(axis))
        came = [lax.ppermute(sums, axis, [(i, i ^ mask) for i in others]) for mask in masks]
        if (axis, masks) == stages[-1]:
            order.after(up_slabs, qkv_slabs)
        sums = order(lambda *parts: sum(parts[1:], parts[0]), sums, *came)
    sums = sums.reshape(-1)

    def cut(at, count):
        return sums[at * model_width : (at + count) * model_width]

    ratio = hidden_width // model_width
    return (
        result,
        grad_tokens,
        grad_w_qkv,
        cut(4 + ratio, 2).reshape(2, model_width),
        grad_w_out,
        cut(0, 1),
        cut(6 + ratio, 1),
        cut(7 + ratio, 1),
        cut(1, 1),
        cut(2, 1),
        grad_w_up,
        cut(3, ratio),
        grad_w_down,
        cut(3 + ratio, 1),
    )


def solution(mesh):
    return jax.shard_map(
        local,
        mesh=mesh,
        in_specs=(
            P("fsdp", "seq", None),
            P("fsdp", "seq", None),
            P("fsdp", None),
            P(),
            P("fsdp", None),
            P(),
            P(),
            P(),
            P(),
            P(),
            P("fsdp", None),
            P(),
            P(None, "fsdp"),
            P(),
        ),
        out_specs=(
            P("fsdp", "seq", None),
            P("fsdp", "seq", None),
            P(("seq", "fsdp"), None),
            P(),
            P(("seq", "fsdp"), None),
            P(),
            P(),
            P(),
            P(),
            P(),
            P(("seq", "fsdp"), None),
            P(),
            P(None, ("seq", "fsdp")),
            P(),
        ),
        check_vma=False,
    )
```

```python
import math
from functools import partial

import jax
import jax.numpy as jnp
from jax import lax
from jax.experimental import pallas as pl
from jax.experimental.pallas import tpu as pltpu
from jax.sharding import PartitionSpec as P

HEADS = 32
HEAD_DIM = 64
BLOCK = 256
PAIR = 2 * HEAD_DIM
GRANT = 58 * 2**20


def estimate(flops, transcendentals=0):
    return pl.CostEstimate(flops=flops // 4, bytes_accessed=flops // 4096, transcendentals=transcendentals // 4)


def layer_norm(token_rows, gain_vec, shift_vec):
    average = jnp.mean(token_rows, axis=-1, keepdims=True)
    centred = token_rows - average
    spread = jnp.mean(centred * centred, axis=-1, keepdims=True)
    scale = lax.rsqrt(spread + 1e-05)
    return centred * scale * gain_vec + shift_vec, average, scale


def contract(left_side, right_side):
    return lax.dot_general(
        left_side, right_side, (((1,), (0,)), ((), ())), preferred_element_type=jnp.float32
    )


def contract_last(left_side, right_side):
    return lax.dot_general(
        left_side, right_side, (((1,), (1,)), ((), ())), preferred_element_type=jnp.float32
    )


def contract_first(left_side, right_side):
    return lax.dot_general(
        left_side, right_side, (((0,), (0,)), ((), ())), preferred_element_type=jnp.float32
    )


def row_pieces(mask, sequence, block, seqs, local):
    per = BLOCK // local
    return [
        pl.ds(pl.multiple_of((((block * per + r) ^ mask) * seqs + sequence) * local, local), local)
        for r in range(per)
    ]


def load_rows(ref, pieces, columns):
    parts = [ref[piece, columns] for piece in pieces]
    return parts[0] if len(parts) == 1 else jnp.concatenate(parts, axis=0)


def store_rows(ref, pieces, columns, values):
    local = values.shape[0] // len(pieces)
    for r, piece in enumerate(pieces):
        ref[piece, columns] = values[r * local : (r + 1) * local]


Q_COLUMNS, K_COLUMNS, V_COLUMNS = (slice(t * PAIR, (t + 1) * PAIR) for t in range(3))


def attend_forward_kernel(mask_ref, slope_ref, qkv_ref, mixed_ref, lse_ref, *, blocks, seqs, local):
    pair, sequence = pl.program_id(0), pl.program_id(1)
    mask = mask_ref[0]
    lane = lax.broadcasted_iota(jnp.int32, (BLOCK, PAIR), 1)
    row = lax.broadcasted_iota(jnp.int32, (BLOCK, BLOCK), 0)
    column = lax.broadcasted_iota(jnp.int32, (BLOCK, BLOCK), 1)
    gap = (row - column).astype(jnp.float32)
    pieces = [row_pieces(mask, sequence, block, seqs, local) for block in range(blocks)]

    for i in range(blocks):
        q_pair = load_rows(qkv_ref, pieces[i], Q_COLUMNS)
        outs, lses = [], []
        for head in range(2):
            slope = slope_ref[pair * 2 + head]
            mine = (lane >= head * HEAD_DIM) & (lane < (head + 1) * HEAD_DIM)
            q = jnp.where(mine, q_pair, jnp.zeros_like(q_pair)) * jnp.bfloat16(HEAD_DIM**-0.5)
            parts, highest = [], None
            for j in range(i + 1):
                scores = contract_last(q, load_rows(qkv_ref, pieces[j], K_COLUMNS))
                distance = jnp.abs(gap) if i == j else gap + float(BLOCK * (i - j))
                scores = scores - slope * distance
                parts.append(scores)
                top = jnp.max(scores, axis=-1, keepdims=True)
                highest = top if highest is None else jnp.maximum(highest, top)
            total, out = None, None
            for j in range(i + 1):
                weights = jnp.exp(parts[j] - highest)
                part = jnp.sum(weights, axis=-1, keepdims=True)
                mixed = contract(weights.astype(jnp.bfloat16), load_rows(qkv_ref, pieces[j], V_COLUMNS))
                total = part if total is None else total + part
                out = mixed if out is None else out + mixed
            outs.append(out / total)
            lses.append(highest + jnp.log(total))
        first = lane < HEAD_DIM
        everything = slice(0, PAIR)
        store_rows(
            mixed_ref, pieces[i], everything, jnp.where(first, outs[0], outs[1]).astype(mixed_ref.dtype)
        )
        store_rows(lse_ref, pieces[i], everything, jnp.where(first, lses[0], lses[1]))


def attend_backward_kernel(
    mask_ref, slope_ref, qkv_ref, lse_ref, mixed_ref, *rest, blocks, seqs, local, start, grads
):
    out_ref, dq_ref, dk_ref, dv_ref, grad_ref = rest[-5:]
    pair, sequence = pl.program_id(0) + start, pl.program_id(1)
    mask = mask_ref[0]
    lane = lax.broadcasted_iota(jnp.int32, (BLOCK, PAIR), 1)
    key = lax.broadcasted_iota(jnp.int32, (BLOCK, BLOCK), 0)
    query = lax.broadcasted_iota(jnp.int32, (BLOCK, BLOCK), 1)
    gap = (query - key).astype(jnp.float32)
    pieces = [row_pieces(mask, sequence, block, seqs, local) for block in range(blocks)]
    everything = slice(0, PAIR)

    @pl.when(sequence == 0)
    def _():
        at = 0
        for part in rest[:grads]:
            grad_ref[at : at + part.shape[0], :] = part[...]
            at += part.shape[0]

    for i in range(blocks):
        q_pair = load_rows(qkv_ref, pieces[i], Q_COLUMNS)
        up_pair = load_rows(grad_ref, pieces[i], everything)
        mixed_pair = load_rows(mixed_ref, pieces[i], everything)
        inner_all = (up_pair.astype(jnp.float32) * mixed_pair.astype(jnp.float32)).T
        lse_all = load_rows(lse_ref, pieces[i], everything).T
        dq = None
        for head in range(2):
            slope = slope_ref[pair * 2 + head]
            mine = (lane >= head * HEAD_DIM) & (lane < (head + 1) * HEAD_DIM)
            zero = jnp.zeros_like(q_pair)
            q = jnp.where(mine, q_pair, zero) * jnp.bfloat16(HEAD_DIM**-0.5)
            up = jnp.where(mine, up_pair, zero)
            inner = jnp.sum(inner_all[head * HEAD_DIM : (head + 1) * HEAD_DIM], axis=0, keepdims=True)
            lse = lse_all[head * HEAD_DIM : head * HEAD_DIM + 1]
            for j in range(i + 1):
                k_pair = load_rows(qkv_ref, pieces[j], K_COLUMNS)
                distance = jnp.abs(gap) if i == j else gap + float(BLOCK * (i - j))
                probs = jnp.exp(contract_last(k_pair, q) - slope * distance - lse)
                prob_grad = contract_last(load_rows(qkv_ref, pieces[j], V_COLUMNS), up)
                score_grad = (probs * (prob_grad - inner)).astype(jnp.bfloat16)
                dv = contract(probs.astype(jnp.bfloat16), up)
                dk = contract(score_grad, q)
                part = contract_first(score_grad, jnp.where(mine, k_pair, zero))
                dq = part if dq is None else dq + part
                if i == j and head == 0:
                    dv_ref[j] = dv
                    dk_ref[j] = dk
                else:
                    dv_ref[j] += dv
                    dk_ref[j] += dk
        dq_ref[i] = dq
    for i in range(blocks):
        store_rows(out_ref, pieces[i], Q_COLUMNS, (dq_ref[i] * HEAD_DIM**-0.5).astype(out_ref.dtype))
        store_rows(out_ref, pieces[i], K_COLUMNS, dk_ref[i].astype(out_ref.dtype))
        store_rows(out_ref, pieces[i], V_COLUMNS, dv_ref[i].astype(out_ref.dtype))


def attend_forward(mask, slopes, qkv, seqs, local):
    rows, width = qkv.shape
    pairs, blocks = width // (3 * PAIR), rows // seqs // BLOCK
    scored = pairs * seqs * blocks * (blocks + 1) * BLOCK * BLOCK
    return pl.pallas_call(
        partial(attend_forward_kernel, blocks=blocks, seqs=seqs, local=local),
        grid_spec=pltpu.PrefetchScalarGridSpec(
            num_scalar_prefetch=2,
            grid=(pairs, seqs),
            in_specs=[pl.BlockSpec((rows, 3 * PAIR), lambda p, *_: (0, p))],
            out_specs=[pl.BlockSpec((rows, PAIR), lambda p, *_: (0, p))] * 2,
        ),
        out_shape=[
            jax.ShapeDtypeStruct((rows, pairs * PAIR), jnp.bfloat16),
            jax.ShapeDtypeStruct((rows, pairs * PAIR), jnp.float32),
        ],
        compiler_params=pltpu.CompilerParams(vmem_limit_bytes=GRANT),
        cost_estimate=estimate(scored * 2 * 512, scored),
        name="attend_forward",
    )(mask, slopes, qkv)


def attend_backward(mask, slopes, qkv, lse, mixed, grads, seqs, local, start, stop, begun=None):
    rows, width = qkv.shape
    blocks = rows // seqs // BLOCK
    scored = (stop - start) * seqs * blocks * (blocks + 1) * BLOCK * BLOCK
    narrow = pl.BlockSpec((rows, PAIR), lambda p, *_: (0, p + start))
    wide = pl.BlockSpec((rows, 3 * PAIR), lambda p, *_: (0, p + start))
    earlier = [] if begun is None else [begun]
    return pl.pallas_call(
        partial(
            attend_backward_kernel, blocks=blocks, seqs=seqs, local=local, start=start, grads=len(grads)
        ),
        grid_spec=pltpu.PrefetchScalarGridSpec(
            num_scalar_prefetch=2,
            grid=(stop - start, seqs),
            in_specs=[wide, narrow, narrow]
            + [pl.BlockSpec((grad.shape[0], PAIR), lambda p, *_: (0, p + start)) for grad in grads]
            + [pl.BlockSpec(memory_space=pl.ANY)] * len(earlier),
            out_specs=wide,
            scratch_shapes=[pltpu.VMEM((blocks, BLOCK, PAIR), jnp.float32)] * 3
            + [pltpu.VMEM((rows, PAIR), jnp.bfloat16)],
        ),
        out_shape=jax.ShapeDtypeStruct((rows, width), jnp.bfloat16),
        input_output_aliases={5 + len(grads): 0} if earlier else {},
        compiler_params=pltpu.CompilerParams(vmem_limit_bytes=GRANT),
        cost_estimate=estimate(scored * 2 * 1280, scored),
        name="attend_backward",
    )(mask, slopes, qkv, lse, mixed, *grads, *earlier)


def head_columns_kernel(at_ref, in_ref, out_ref):
    for t in range(3):

        @pl.when(pl.program_id(0) == t)
        def _():
            for pair in range(in_ref.shape[1] // PAIR):
                at = (pair * 3 + t) * PAIR
                out_ref[:, at : at + PAIR] = in_ref[:, pair * PAIR : (pair + 1) * PAIR]


def up_kernel(rows_ref, weight_ref, bias_ref, active_ref, slope_ref, *, chunk):
    rows = rows_ref[...]
    for at in range(0, weight_ref.shape[1], chunk):
        columns = slice(at, at + chunk)
        hidden = contract(rows, weight_ref[:, columns]) + bias_ref[:, columns]
        below = 0.5 + 0.5 * lax.erf(hidden * 2**-0.5)
        active_ref[:, columns] = (hidden * below).astype(active_ref.dtype)
        slope_ref[:, columns] = below + hidden * ((2 * math.pi) ** -0.5 * jnp.exp(-0.5 * hidden * hidden))


def hidden_grad_kernel(rows_ref, weight_ref, slope_ref, grad_ref, sum_ref, *, chunk):
    rows = rows_ref[...]
    starting = pl.program_id(0) == 0
    for at in range(0, weight_ref.shape[0], chunk):
        columns = slice(at, at + chunk)
        grad = contract_last(rows, weight_ref[columns, :]) * slope_ref[:, columns]
        grad = grad.astype(grad_ref.dtype)
        grad_ref[:, columns] = grad
        part = jnp.sum(grad.astype(jnp.float32), axis=0, keepdims=True)
        sum_ref[:, columns] = jnp.where(starting, part, sum_ref[:, columns] + part)


TILE = 256


def up_and_bend(rows, weight, bias):
    count, depth = rows.shape
    width = weight.shape[1]
    tile = pl.BlockSpec((TILE, width), lambda i: (i, 0))
    return pl.pallas_call(
        partial(up_kernel, chunk=512),
        grid=(count // TILE,),
        in_specs=[
            pl.BlockSpec((TILE, depth), lambda i: (i, 0)),
            pl.BlockSpec((depth, width), lambda i: (0, 0), pipeline_mode=pl.Buffered(1)),
            pl.BlockSpec((1, width), lambda i: (0, 0)),
        ],
        out_specs=[tile, tile],
        out_shape=[
            jax.ShapeDtypeStruct((count, width), jnp.bfloat16),
            jax.ShapeDtypeStruct((count, width), jnp.float32),
        ],
        compiler_params=pltpu.CompilerParams(vmem_limit_bytes=GRANT),
        cost_estimate=estimate(count * depth * width * 4, 2 * count * width),
        name="up_and_bend",
    )(rows, weight, bias)


def hidden_gradient(rows, weight, slope, start, count):
    depth = rows.shape[1]
    width = weight.shape[0]
    first = start // TILE
    line = pl.BlockSpec((1, width), lambda i: (0, 0))
    return pl.pallas_call(
        partial(hidden_grad_kernel, chunk=512),
        grid=(count // TILE,),
        in_specs=[
            pl.BlockSpec((TILE, depth), lambda i: (i + first, 0)),
            pl.BlockSpec((width, depth), lambda i: (0, 0), pipeline_mode=pl.Buffered(1)),
            pl.BlockSpec((TILE, width), lambda i: (i + first, 0)),
        ],
        out_specs=[pl.BlockSpec((TILE, width), lambda i: (i, 0)), line],
        out_shape=[
            jax.ShapeDtypeStruct((count, width), jnp.bfloat16),
            jax.ShapeDtypeStruct((1, width), jnp.float32),
        ],
        compiler_params=pltpu.CompilerParams(vmem_limit_bytes=GRANT),
        cost_estimate=estimate(count * depth * width * 3, 0),
        name="hidden_gradient",
    )(rows, weight, slope)


def product_kernel(rows_ref, weight_ref, out_ref):
    out_ref[...] = contract(rows_ref[...], weight_ref[...]).astype(out_ref.dtype)


def product_of(rows, weight, count):
    depth, width = weight.shape
    return pl.pallas_call(
        product_kernel,
        grid=(count // TILE,),
        in_specs=[
            pl.BlockSpec((TILE, depth), lambda i: (i, 0)),
            pl.BlockSpec((depth, width), lambda i: (0, 0), pipeline_mode=pl.Buffered(1)),
        ],
        out_specs=pl.BlockSpec((TILE, width), lambda i: (i, 0)),
        out_shape=jax.ShapeDtypeStruct((count, width), jnp.bfloat16),
        compiler_params=pltpu.CompilerParams(vmem_limit_bytes=GRANT),
        cost_estimate=estimate(2 * count * depth * width, 0),
        name="product",
    )(rows, weight)


def mixed_grad_kernel(rows_ref, weight_ref, out_ref):
    out_ref[...] = contract_last(rows_ref[...], weight_ref[...]).astype(out_ref.dtype)


def mixed_gradient(rows, weight, slab):
    count, depth = rows.shape
    width = weight.shape[0]
    return pl.pallas_call(
        mixed_grad_kernel,
        grid=(width // slab,),
        in_specs=[
            pl.BlockSpec((count, depth), lambda i: (0, 0), pipeline_mode=pl.Buffered(1)),
            pl.BlockSpec((slab, depth), lambda i: (i, 0)),
        ],
        out_specs=pl.BlockSpec((count, slab), lambda i: (0, i)),
        out_shape=jax.ShapeDtypeStruct((count, width), jnp.bfloat16),
        compiler_params=pltpu.CompilerParams(vmem_limit_bytes=GRANT),
        cost_estimate=estimate(2 * count * depth * width, 0),
        name="mixed_gradient",
    )(rows, weight)


def norm_back_kernel(own_ref, values_ref, average_ref, scale_ref, base_ref, gain_ref, *refs, parts):
    came, (low_ref, wide_ref, sums_ref) = refs[:parts], refs[parts:]
    wide = jnp.float32
    step = pl.program_id(0)

    @pl.when(step == 0)
    def _():
        sums_ref[...] = jnp.zeros_like(sums_ref)

    def make(came):
        grad = own_ref[...].astype(wide)
        for part in came:
            grad = grad + part[...].astype(wide)
        scale = scale_ref[...]
        normal = (values_ref[...].astype(wide) - average_ref[...]) * scale
        gained = grad * gain_ref[...]
        along = jnp.mean(gained * normal, axis=-1, keepdims=True)
        across = jnp.mean(gained, axis=-1, keepdims=True)
        made = base_ref[...].astype(wide) + scale * (gained - across - normal * along)
        low = made.astype(low_ref.dtype)
        low_ref[...] = low
        wide_ref[...] = made
        for at, part in enumerate((grad * normal, grad, low.astype(wide))):
            sums_ref[8 * at : 8 * at + 8, :] += jnp.sum(part.reshape(-1, 8, part.shape[1]), axis=0)

    if not came:
        make(())
        return
    upper = step < pl.num_programs(0) // 2
    pl.when(upper)(lambda: make(came[0::2]))
    pl.when(jnp.logical_not(upper))(lambda: make(came[1::2]))


def norm_back(rest, values, average, scale, base, gain, came):
    rows, width = values.shape
    steps = 8
    half = steps // 2
    came = list(came or ())
    count = rows // steps
    tile = pl.BlockSpec((count, width), lambda i: (i, 0))
    thin = pl.BlockSpec((count, 1), lambda i: (i, 0))
    top = pl.BlockSpec((count, width), lambda i: (jnp.minimum(i, half - 1), 0))
    bottom = pl.BlockSpec((count, width), lambda i: (jnp.maximum(i - half, 0), 0))
    low, full, sums = pl.pallas_call(
        partial(norm_back_kernel, parts=len(came)),
        grid=(steps,),
        in_specs=[tile, tile, thin, thin, tile, pl.BlockSpec((1, width), lambda i: (0, 0))]
        + [top, bottom] * (len(came) // 2),
        out_specs=[tile, tile, pl.BlockSpec((24, width), lambda i: (0, 0))],
        out_shape=[
            jax.ShapeDtypeStruct((rows, width), jnp.bfloat16),
            jax.ShapeDtypeStruct((rows, width), jnp.float32),
            jax.ShapeDtypeStruct((24, width), jnp.float32),
        ],
        compiler_params=pltpu.CompilerParams(vmem_limit_bytes=GRANT),
        cost_estimate=estimate(30 * rows * width, rows),
        name="norm_back",
    )(rest, values, average, scale, base, gain[None], *came)
    return low, full, jnp.sum(sums.reshape(3, 8, width), axis=1)


def outer_kernel(left_ref, *refs, chunk):
    right_refs, out_ref = refs[:-1], refs[-1]
    shards = out_ref.shape[0]
    for at in range(0, out_ref.shape[3], chunk):
        columns = slice(at, at + chunk)
        made, row = None, 0
        for right_ref in right_refs:
            count = right_ref.shape[0]
            part = contract_first(left_ref[row : row + count, :], right_ref[:, columns])
            made = part if made is None else made + part
            row += count
        out_ref[:, 0, :, columns] = made.astype(out_ref.dtype).reshape(shards, -1, made.shape[1])


def outer(left, rights, groups, shards):
    rights = rights if isinstance(rights, (list, tuple)) else [rights]
    tokens, rows = left.shape
    width = rights[0].shape[1]
    part = rows // groups
    made = pl.pallas_call(
        partial(outer_kernel, chunk=512 if width % 512 == 0 else 256),
        grid=(groups,),
        in_specs=[pl.BlockSpec((tokens, part), lambda i: (0, i))]
        + [
            pl.BlockSpec((right.shape[0], width), lambda i: (0, 0), pipeline_mode=pl.Buffered(1))
            for right in rights
        ],
        out_specs=pl.BlockSpec((shards, 1, part // shards, width), lambda i: (0, i, 0, 0)),
        out_shape=jax.ShapeDtypeStruct((shards, groups, part // shards, width), jnp.bfloat16),
        compiler_params=pltpu.CompilerParams(vmem_limit_bytes=GRANT),
        cost_estimate=estimate(2 * tokens * rows * width, 0),
        name="outer",
    )(left, *rights)
    return made.reshape(rows, width)


def swap(values, bit):
    return lax.ppermute(values, "seq", [(i, i ^ bit) for i in range(4)])


def by_index(parts, me):
    if len(parts) != 4:
        return parts
    odd, upper = (me & 1) == 1, (me & 2) == 2
    a, b, c, d = parts
    a, b, c, d = (
        jnp.where(odd, b, a),
        jnp.where(odd, a, b),
        jnp.where(odd, d, c),
        jnp.where(odd, c, d),
    )
    return [jnp.where(upper, c, a), jnp.where(upper, d, b), jnp.where(upper, a, c), jnp.where(upper, b, d)]


def exchange(slots):
    if lax.axis_size("seq") != 4:
        return list(lax.all_to_all(jnp.stack(slots), "seq", split_axis=0, concat_axis=0, tiled=True))
    return [slots[0]] + [swap(slots[j], j) for j in (1, 2, 3)]


def gate(values, *before):
    return lax.optimization_barrier((values, *before))[0]


class Order:
    def __init__(self):
        self.pending = []

    def after(self, *values):
        self.pending += values

    def __call__(self, operation, *operands):
        if self.pending:
            count = len(operands)
            operands = lax.optimization_barrier((*operands, *self.pending))[:count]
        made = operation(*operands)
        self.pending = jax.tree.leaves(made)
        return made

    def gather(self, rows):
        if lax.axis_size("seq") != 4:
            return lax.all_gather(jnp.concatenate(rows, axis=0), "seq", axis=0, tiled=True), None
        top, bottom = rows
        return rows, (swap(bottom, 1), swap(top, 2), swap(top, 1), swap(bottom, 2))

    def fill(self, begun):
        rows, came = begun
        if came is None:
            return rows
        first_bottom, second_top, first_top, second_bottom = came
        room = jnp.zeros_like(rows[0])
        parts = (*rows, first_top, first_bottom, second_top, second_bottom, room, room)
        return self(lambda *parts: jnp.concatenate(parts, axis=0), *parts)

    def complete(self, made, pieces):
        if not isinstance(pieces, list):
            return made
        rows = pieces[-1].shape[0]

        def put(before, first, second):
            before = lax.dynamic_update_slice_in_dim(before, first, 6 * rows, axis=0)
            return lax.dynamic_update_slice_in_dim(before, second, 7 * rows, axis=0)

        return self(put, made, *pieces[-2:])

    def pass_on(self, begun, *before):
        rows, came = begun
        if came is None:
            return rows
        first_bottom, second_top, first_top, second_bottom = came
        self.after(*came)
        if before:
            second_top, first_bottom = gate((second_top, first_bottom), *before)
        far = [swap(second_top, 1), swap(first_bottom, 2)]
        return [*rows, first_top, first_bottom, second_top, second_bottom, *far]

    def halves(self, product, rows):
        def cut(values):
            made = product(values)
            half = made.shape[0] // 2
            return made[:half], made[half:]

        return self(cut, rows)

    def add_far(self, made, far, direct, *before, at=None):
        wide = jnp.float32
        half = far[0].shape[0]
        start = made.shape[0] - 4 * half if at is None else at

        def add(made, top, bottom):
            at = start
            first = (made[at + half : at + 2 * half].astype(wide) + bottom.astype(wide)).astype(made.dtype)
            second = (made[at + 2 * half : at + 3 * half].astype(wide) + top.astype(wide)).astype(made.dtype)
            if direct is None:
                first = jnp.concatenate([made[at : at + half], first], axis=0)
                second = jnp.concatenate([second, made[at + 3 * half : at + 4 * half]], axis=0)
            return first, second

        first, second = self(add, made, *far)
        if before:
            first, second = gate((first, second), *before)
        first, second = swap(first, 1), swap(second, 2)
        return (first, second) if direct is None else (direct[0], first, second, direct[1])


def swap_far(halves):
    return swap(halves[0], 1), swap(halves[1], 2)


def swap_direct(made, half):
    at = made.shape[0] - 4 * half
    return swap(made[at : at + half], 1), swap(made[at + 3 * half :], 2)


def summed(own, came):
    wide = jnp.float32
    own = own.astype(wide)
    return sum((part.astype(wide) for part in came), own)


def whole(parts):
    return jnp.concatenate(parts, axis=0) if isinstance(parts, list) else parts


def total_stages():
    stages = []
    for axis in ("fsdp", "seq"):
        count, bit = lax.axis_size(axis), 1
        bits = count.bit_length() - 1
        while bit < count:
            stages.append((axis, [bit] if bits % 2 else [bit, 2 * bit, 3 * bit]))
            bit <<= 1 if bits % 2 else 2
            bits -= bits % 2
    return stages


def local(
    tokens,
    cotangent,
    w_qkv,
    qv_bias,
    w_out,
    out_bias,
    ln1_gain,
    ln1_shift,
    ln2_gain,
    ln2_shift,
    w_up,
    up_bias,
    w_down,
    down_bias,
):
    seq_count, local_len, model_width = tokens.shape
    groups, shards = lax.axis_size("seq"), lax.axis_size("fsdp")
    me = lax.axis_index("seq")
    square = groups == 4
    heads_here = HEADS // groups
    slab = heads_here * HEAD_DIM
    pairs = slab // PAIR
    hidden_width = w_up.shape[1]
    hidden_slab = hidden_width // groups
    rows_here = seq_count * local_len
    low, wide = jnp.bfloat16, jnp.float32
    mask = jnp.reshape(me if square else jnp.zeros_like(me), (1,)).astype(jnp.int32)
    head_index = me * heads_here + jnp.arange(1, heads_here + 1, dtype=jnp.int32)
    slopes = 2.0 ** (-8.0 * head_index.astype(wide) / HEADS)

    def head_columns(values):
        rows = values.shape[0]
        return pl.pallas_call(
            head_columns_kernel,
            grid_spec=pltpu.PrefetchScalarGridSpec(
                num_scalar_prefetch=1,
                grid=(3,),
                in_specs=[pl.BlockSpec((rows, slab), lambda t, at: (0, t * groups + at[0]))],
                out_specs=pl.BlockSpec((rows, 3 * slab), lambda t, at: (0, 0)),
            ),
            out_shape=jax.ShapeDtypeStruct((rows, 3 * slab), values.dtype),
            name="head_columns",
        )(jnp.reshape(me, (1,)).astype(jnp.int32), values)

    def own_slab(values, axis):
        width = values.shape[axis] // groups
        return lax.dynamic_slice_in_dim(values, me * width, width, axis=axis)

    order = Order()
    x_low = tokens.reshape(rows_here, model_width)
    x = x_low.astype(wide)
    dz_low = cotangent.reshape(rows_here, model_width)
    qkv_slab = lax.all_gather(head_columns(w_qkv), "fsdp", axis=0, tiled=True)
    qkv_bias = head_columns(jnp.concatenate([qv_bias[0], jnp.zeros_like(qv_bias[0]), qv_bias[1]])[None])
    up_bias_slab = own_slab(up_bias, 0)

    first_norm, *first_stats = layer_norm(x, ln1_gain, ln1_shift)
    half = rows_here // 2

    def halves_of(values):
        return values[:half].astype(low), values[half:].astype(low)

    normed = order.gather(order(halves_of, first_norm))
    normed = order.pass_on(normed)
    full_out = lax.all_gather(w_out, "fsdp", axis=0, tiled=True)
    up_slab = lax.all_gather(own_slab(gate(w_up, normed[0]) if square else w_up, 1), "fsdp", axis=0, tiled=True)
    down_slab = lax.all_gather(own_slab(gate(w_down, normed[0]) if square else w_down, 0), "fsdp", axis=1, tiled=True)
    normed = whole(normed)
    upstream = order.gather(halves_of(gate(dz_low, normed)))
    qkv = order(lambda rows: (contract(rows, qkv_slab) + qkv_bias).astype(low), normed)
    attended, log_totals = order(lambda rows: attend_forward(mask, slopes, rows, seq_count, local_len), qkv)
    if square:
        attended = gate(attended, *upstream[1])
    mixed_slots = exchange([attended[j * rows_here : (j + 1) * rows_here] for j in range(groups)])
    mixed_rows = jnp.concatenate(by_index(mixed_slots, me), axis=1)
    mixed_slots = jnp.concatenate(mixed_slots, axis=1)

    def pair_swap(values):
        return lax.ppermute(values, "fsdp", [(i, i ^ 1) for i in range(shards)])

    parity = lax.axis_index("fsdp") & 1
    out_rows = model_width // (groups * shards)

    def pair_halves(values):
        halves = values.reshape(rows_here, -1, 2, out_rows)
        return tuple(
            lax.dynamic_index_in_dim(halves, index, axis=2, keepdims=False).reshape(rows_here, -1)
            for index in (parity, 1 - parity)
        )

    middle = order(lambda rows: x + (contract(rows, full_out) + out_bias), mixed_rows)
    second_norm, *second_stats = layer_norm(middle, ln2_gain, ln2_shift)
    second = order.gather(order(halves_of, second_norm))
    mine, theirs = order(pair_halves, mixed_slots)
    upstream_made = order.fill(upstream)
    theirs = pair_swap(theirs)
    dz_sum = order(lambda values: jnp.sum(values.astype(wide), axis=0), dz_low)
    second = whole(order.pass_on(second))
    upstream = order.pass_on(upstream, second)
    active, slope = order(lambda rows: up_and_bend(rows, up_slab, up_bias_slab[None]), second)
    mixed_half = order(lambda *parts: jnp.concatenate(parts, axis=0), mine, theirs)
    upstream = order.complete(upstream_made, upstream)

    def slab_product(left, right):
        return order(lambda rows: outer(rows, right, groups, shards), left)

    def slab_sum(made):
        return lax.psum_scatter(made, "fsdp", scatter_dimension=0, tiled=True)

    def slabs_of_rows(values):
        return lax.all_to_all(
            values.reshape(groups, -1, values.shape[1]), "seq", split_axis=0, concat_axis=0, tiled=True
        )

    down_sum = slab_sum(slab_product(upstream, active))
    count = rows_here

    def slots(product, start, stop):
        return lambda values: product(values[start * count : stop * count])

    def to_second(rows):
        return contract_last(rows, up_slab).astype(low)

    def to_result(rows):
        return contract(rows, down_slab).astype(low)

    def to_normed(rows):
        return contract_last(rows, qkv_slab).astype(low)

    def scatter(product, rows):
        return lax.psum_scatter(order(product, rows), "seq", scatter_dimension=0, tiled=True)

    hidden_grad, hidden_sum = order(lambda rows: hidden_gradient(rows, down_slab, slope, 0, groups * count), upstream)
    if square:
        far = swap_far(order.halves(slots(to_second, 3, 4), hidden_grad))
        rest = order(slots(to_second, 0, 3), hidden_grad)
        second_own = rest
        direct = swap_direct(rest, half)
        came = order.add_far(rest, far, direct)
        result_far = order.halves(slots(to_result, 3, 4), active)
        up_sum = slab_sum(gate(slab_product(second, hidden_grad), *came))
        result_far = swap_far(gate(result_far, *came))
    else:
        second_own, came = scatter(to_second, hidden_grad), ()
        up_sum = slab_sum(slab_product(second, hidden_grad))
    branch_grad, middle_grad, middle_sums = order(
        lambda own, *came: norm_back(own, middle, *second_stats, dz_low, ln2_gain, came), second_own, *came
    )

    def column_sum(values):
        return jnp.sum(values.astype(wide), axis=0)

    hidden_sum = lax.dynamic_update_slice_in_dim(
        jnp.zeros((hidden_width,), wide), hidden_sum[0], me * hidden_slab, axis=0
    )
    early = [middle_sums[2], middle_sums[0], middle_sums[1], hidden_sum, dz_sum]
    mixed_grad = order(lambda rows: mixed_gradient(rows, full_out, slab), branch_grad)
    mixed_grad = exchange(by_index([mixed_grad[:, j * slab : (j + 1) * slab] for j in range(groups)], me))
    if square:
        result_rest = order(lambda rows: product_of(rows, down_slab, 3 * count), active)
        result_came = order.add_far(result_rest, result_far, None)
    branch_other = pair_swap(branch_grad)
    branch_pair = jnp.concatenate([branch_grad, branch_other], axis=0)
    out_sum = order(lambda columns: outer(columns, branch_pair, groups, 1), mixed_half)
    attention = (mask, slopes, qkv, log_totals, attended)
    if square:
        part = out_sum.shape[0] // 4
        out_far = out_sum[3 * part : 3 * part + part // 2], out_sum[3 * part + part // 2 :]
        out_far = swap_far(gate(out_far, *mixed_grad))
    order.after(down_sum)
    begun = order(
        lambda *grads: attend_backward(*attention, grads, seq_count, local_len, 0, pairs // 2), *mixed_grad
    )
    if square:
        out_came = order.add_far(out_sum, out_far, None, at=part)
    qkv_grad = order(
        lambda *grads: attend_backward(*attention, grads, seq_count, local_len, pairs // 2, pairs, begun),
        *mixed_grad,
    )
    if square:
        order.after(*out_came, *result_came)
        out_sum = order(lambda own, *came: summed(own[:part], came).astype(low), out_sum, *out_came)
        order.after(*out_came)
    else:
        out_sum = lax.psum_scatter(out_sum, "seq", scatter_dimension=0, tiled=True)
    out_sum = out_sum.reshape(-1, 1, out_rows, model_width)
    zero = jnp.zeros_like(out_sum)
    out_sum = jnp.concatenate(
        [jnp.where(parity == 0, out_sum, zero), jnp.where(parity == 1, out_sum, zero)], axis=1
    ).reshape(-1, model_width)
    grad_w_out = lax.psum_scatter(out_sum, "fsdp", scatter_dimension=0, tiled=True).astype(wide)
    order.after(up_sum)
    if square:
        far = swap_far(order.halves(slots(to_normed, 3, 4), qkv_grad))
        near = order(slots(to_normed, 1, 3), qkv_grad)
        direct = swap_direct(near, half)
        qkv_sum = slab_sum(gate(slab_product(normed, qkv_grad), *far, *direct, grad_w_out))
        came = order.add_far(near, far, direct)
        down_slabs = slabs_of_rows(gate(down_sum, *came))
        normed_own = order(slots(to_normed, 0, 1), qkv_grad)
    else:
        down_slabs = slabs_of_rows(down_sum)
        qkv_sum = slab_sum(slab_product(normed, qkv_grad))
        normed_own, came = scatter(to_normed, qkv_grad), ()
    if square:
        result = order(
            lambda rest, *came: (middle + (summed(rest[:count], came) + down_bias)).astype(low),
            result_rest,
            *result_came,
        )
    else:
        result = (middle + (scatter(to_result, active).astype(wide) + down_bias)).astype(low)
    result = result.reshape(tokens.shape)
    qkv_column_sum = order(column_sum, qkv_grad)
    grad_tokens, _, input_sums = order(
        lambda own, *came: norm_back(own, x_low, *first_stats, middle_grad, ln1_gain, came), normed_own, *came
    )
    grad_tokens = grad_tokens.reshape(tokens.shape)
    up_slabs = slabs_of_rows(gate(up_sum, *came, normed_own))
    qkv_slabs = slabs_of_rows(qkv_sum)

    def rows_of(slabs):
        return jnp.swapaxes(slabs, 0, 1).astype(wide)

    grad_w_down = rows_of(down_slabs).reshape(-1, hidden_width).T
    grad_w_up = rows_of(up_slabs).reshape(-1, hidden_width)
    grad_w_qkv = rows_of(qkv_slabs).reshape(-1, groups, pairs, 3, PAIR)
    grad_w_qkv = jnp.transpose(grad_w_qkv, (0, 3, 1, 2, 4)).reshape(-1, 3 * model_width)

    head_sum = jnp.transpose(qkv_column_sum.reshape(pairs, 3, PAIR), (1, 0, 2)).reshape(3, slab)
    qv_sum = lax.dynamic_update_slice_in_dim(
        jnp.zeros((2, model_width), wide), head_sum[0::2], me * slab, axis=1
    )
    late = [qv_sum.reshape(-1), input_sums[0], input_sums[1]]
    sums = order(lambda *parts: jnp.concatenate(parts).reshape(-1, PAIR), *early, *late)
    stages = total_stages()
    for axis, masks in stages:
        others = range(lax.axis_size(axis))
        came = [lax.ppermute(sums, axis, [(i, i ^ mask) for i in others]) for mask in masks]
        if (axis, masks) == stages[-1]:
            order.after(down_slabs, up_slabs, qkv_slabs)
        sums = order(lambda *parts: sum(parts[1:], parts[0]), sums, *came)
    sums = sums.reshape(-1)

    def cut(at, count):
        return sums[at * model_width : (at + count) * model_width]

    ratio = hidden_width // model_width
    return (
        result,
        grad_tokens,
        grad_w_qkv,
        cut(4 + ratio, 2).reshape(2, model_width),
        grad_w_out,
        cut(0, 1),
        cut(6 + ratio, 1),
        cut(7 + ratio, 1),
        cut(1, 1),
        cut(2, 1),
        grad_w_up,
        cut(3, ratio),
        grad_w_down,
        cut(3 + ratio, 1),
    )


def solution(mesh):
    return jax.shard_map(
        local,
        mesh=mesh,
        in_specs=(
            P("fsdp", "seq", None),
            P("fsdp", "seq", None),
            P("fsdp", None),
            P(),
            P("fsdp", None),
            P(),
            P(),
            P(),
            P(),
            P(),
            P("fsdp", None),
            P(),
            P(None, "fsdp"),
            P(),
        ),
        out_specs=(
            P("fsdp", "seq", None),
            P("fsdp", "seq", None),
            P(("seq", "fsdp"), None),
            P(),
            P(("seq", "fsdp"), None),
            P(),
            P(),
            P(),
            P(),
            P(),
            P(("seq", "fsdp"), None),
            P(),
            P(None, ("seq", "fsdp")),
            P(),
        ),
        check_vma=False,
    )
```

```python
import math
from functools import partial

import jax
import jax.numpy as jnp
from jax import lax
from jax.experimental import pallas as pl
from jax.experimental.pallas import tpu as pltpu
from jax.sharding import PartitionSpec as P

HEADS = 32
HEAD_DIM = 64
BLOCK = 256
PAIR = 2 * HEAD_DIM
GRANT = 58 * 2**20


def estimate(flops, transcendentals=0):
    return pl.CostEstimate(flops=flops // 4, bytes_accessed=flops // 4096, transcendentals=transcendentals // 4)


def layer_norm(token_rows, gain_vec, shift_vec):
    average = jnp.mean(token_rows, axis=-1, keepdims=True)
    centred = token_rows - average
    spread = jnp.mean(centred * centred, axis=-1, keepdims=True)
    scale = lax.rsqrt(spread + 1e-05)
    return centred * scale * gain_vec + shift_vec, average, scale


def contract(left_side, right_side):
    return lax.dot_general(
        left_side, right_side, (((1,), (0,)), ((), ())), preferred_element_type=jnp.float32
    )


def contract_last(left_side, right_side):
    return lax.dot_general(
        left_side, right_side, (((1,), (1,)), ((), ())), preferred_element_type=jnp.float32
    )


def contract_first(left_side, right_side):
    return lax.dot_general(
        left_side, right_side, (((0,), (0,)), ((), ())), preferred_element_type=jnp.float32
    )


def row_pieces(mask, sequence, block, seqs, local):
    per = BLOCK // local
    return [
        pl.ds(pl.multiple_of((((block * per + r) ^ mask) * seqs + sequence) * local, local), local)
        for r in range(per)
    ]


def load_rows(ref, pieces, columns):
    parts = [ref[piece, columns] for piece in pieces]
    return parts[0] if len(parts) == 1 else jnp.concatenate(parts, axis=0)


def store_rows(ref, pieces, columns, values):
    local = values.shape[0] // len(pieces)
    for r, piece in enumerate(pieces):
        ref[piece, columns] = values[r * local : (r + 1) * local]


Q_COLUMNS, K_COLUMNS, V_COLUMNS = (slice(t * PAIR, (t + 1) * PAIR) for t in range(3))


def attend_forward_kernel(mask_ref, slope_ref, qkv_ref, mixed_ref, lse_ref, *, blocks, seqs, local):
    pair, sequence = pl.program_id(0), pl.program_id(1)
    mask = mask_ref[0]
    lane = lax.broadcasted_iota(jnp.int32, (BLOCK, PAIR), 1)
    row = lax.broadcasted_iota(jnp.int32, (BLOCK, BLOCK), 0)
    column = lax.broadcasted_iota(jnp.int32, (BLOCK, BLOCK), 1)
    gap = (row - column).astype(jnp.float32)
    pieces = [row_pieces(mask, sequence, block, seqs, local) for block in range(blocks)]

    for i in range(blocks):
        q_pair = load_rows(qkv_ref, pieces[i], Q_COLUMNS)
        outs, lses = [], []
        for head in range(2):
            slope = slope_ref[pair * 2 + head]
            mine = (lane >= head * HEAD_DIM) & (lane < (head + 1) * HEAD_DIM)
            q = jnp.where(mine, q_pair, jnp.zeros_like(q_pair)) * jnp.bfloat16(HEAD_DIM**-0.5)
            parts, highest = [], None
            for j in range(i + 1):
                scores = contract_last(q, load_rows(qkv_ref, pieces[j], K_COLUMNS))
                distance = jnp.abs(gap) if i == j else gap + float(BLOCK * (i - j))
                scores = scores - slope * distance
                parts.append(scores)
                top = jnp.max(scores, axis=-1, keepdims=True)
                highest = top if highest is None else jnp.maximum(highest, top)
            total, out = None, None
            for j in range(i + 1):
                weights = jnp.exp(parts[j] - highest)
                part = jnp.sum(weights, axis=-1, keepdims=True)
                mixed = contract(weights.astype(jnp.bfloat16), load_rows(qkv_ref, pieces[j], V_COLUMNS))
                total = part if total is None else total + part
                out = mixed if out is None else out + mixed
            outs.append(out / total)
            lses.append(highest + jnp.log(total))
        first = lane < HEAD_DIM
        everything = slice(0, PAIR)
        store_rows(
            mixed_ref, pieces[i], everything, jnp.where(first, outs[0], outs[1]).astype(mixed_ref.dtype)
        )
        store_rows(lse_ref, pieces[i], everything, jnp.where(first, lses[0], lses[1]))


def attend_backward_kernel(
    mask_ref, slope_ref, qkv_ref, lse_ref, mixed_ref, *rest, blocks, seqs, local, start, grads
):
    out_ref, dq_ref, dk_ref, dv_ref, grad_ref = rest[-5:]
    pair, sequence = pl.program_id(0) + start, pl.program_id(1)
    mask = mask_ref[0]
    lane = lax.broadcasted_iota(jnp.int32, (BLOCK, PAIR), 1)
    key = lax.broadcasted_iota(jnp.int32, (BLOCK, BLOCK), 0)
    query = lax.broadcasted_iota(jnp.int32, (BLOCK, BLOCK), 1)
    gap = (query - key).astype(jnp.float32)
    pieces = [row_pieces(mask, sequence, block, seqs, local) for block in range(blocks)]
    everything = slice(0, PAIR)

    @pl.when(sequence == 0)
    def _():
        at = 0
        for part in rest[:grads]:
            grad_ref[at : at + part.shape[0], :] = part[...]
            at += part.shape[0]

    for i in range(blocks):
        q_pair = load_rows(qkv_ref, pieces[i], Q_COLUMNS)
        up_pair = load_rows(grad_ref, pieces[i], everything)
        mixed_pair = load_rows(mixed_ref, pieces[i], everything)
        inner_all = (up_pair.astype(jnp.float32) * mixed_pair.astype(jnp.float32)).T
        lse_all = load_rows(lse_ref, pieces[i], everything).T
        dq = None
        for head in range(2):
            slope = slope_ref[pair * 2 + head]
            mine = (lane >= head * HEAD_DIM) & (lane < (head + 1) * HEAD_DIM)
            zero = jnp.zeros_like(q_pair)
            q = jnp.where(mine, q_pair, zero) * jnp.bfloat16(HEAD_DIM**-0.5)
            up = jnp.where(mine, up_pair, zero)
            inner = jnp.sum(inner_all[head * HEAD_DIM : (head + 1) * HEAD_DIM], axis=0, keepdims=True)
            lse = lse_all[head * HEAD_DIM : head * HEAD_DIM + 1]
            for j in range(i + 1):
                k_pair = load_rows(qkv_ref, pieces[j], K_COLUMNS)
                distance = jnp.abs(gap) if i == j else gap + float(BLOCK * (i - j))
                probs = jnp.exp(contract_last(k_pair, q) - slope * distance - lse)
                prob_grad = contract_last(load_rows(qkv_ref, pieces[j], V_COLUMNS), up)
                score_grad = (probs * (prob_grad - inner)).astype(jnp.bfloat16)
                dv = contract(probs.astype(jnp.bfloat16), up)
                dk = contract(score_grad, q)
                part = contract_first(score_grad, jnp.where(mine, k_pair, zero))
                dq = part if dq is None else dq + part
                if i == j and head == 0:
                    dv_ref[j] = dv
                    dk_ref[j] = dk
                else:
                    dv_ref[j] += dv
                    dk_ref[j] += dk
        dq_ref[i] = dq
    for i in range(blocks):
        store_rows(out_ref, pieces[i], Q_COLUMNS, (dq_ref[i] * HEAD_DIM**-0.5).astype(out_ref.dtype))
        store_rows(out_ref, pieces[i], K_COLUMNS, dk_ref[i].astype(out_ref.dtype))
        store_rows(out_ref, pieces[i], V_COLUMNS, dv_ref[i].astype(out_ref.dtype))


def attend_forward(mask, slopes, qkv, seqs, local):
    rows, width = qkv.shape
    pairs, blocks = width // (3 * PAIR), rows // seqs // BLOCK
    scored = pairs * seqs * blocks * (blocks + 1) * BLOCK * BLOCK
    return pl.pallas_call(
        partial(attend_forward_kernel, blocks=blocks, seqs=seqs, local=local),
        grid_spec=pltpu.PrefetchScalarGridSpec(
            num_scalar_prefetch=2,
            grid=(pairs, seqs),
            in_specs=[pl.BlockSpec((rows, 3 * PAIR), lambda p, *_: (0, p))],
            out_specs=[pl.BlockSpec((rows, PAIR), lambda p, *_: (0, p))] * 2,
        ),
        out_shape=[
            jax.ShapeDtypeStruct((rows, pairs * PAIR), jnp.bfloat16),
            jax.ShapeDtypeStruct((rows, pairs * PAIR), jnp.float32),
        ],
        compiler_params=pltpu.CompilerParams(vmem_limit_bytes=GRANT),
        cost_estimate=estimate(scored * 2 * 512, scored),
        name="attend_forward",
    )(mask, slopes, qkv)


def attend_backward(mask, slopes, qkv, lse, mixed, grads, seqs, local, start, stop, begun=None):
    rows, width = qkv.shape
    blocks = rows // seqs // BLOCK
    scored = (stop - start) * seqs * blocks * (blocks + 1) * BLOCK * BLOCK
    narrow = pl.BlockSpec((rows, PAIR), lambda p, *_: (0, p + start))
    wide = pl.BlockSpec((rows, 3 * PAIR), lambda p, *_: (0, p + start))
    earlier = [] if begun is None else [begun]
    return pl.pallas_call(
        partial(
            attend_backward_kernel, blocks=blocks, seqs=seqs, local=local, start=start, grads=len(grads)
        ),
        grid_spec=pltpu.PrefetchScalarGridSpec(
            num_scalar_prefetch=2,
            grid=(stop - start, seqs),
            in_specs=[wide, narrow, narrow]
            + [pl.BlockSpec((grad.shape[0], PAIR), lambda p, *_: (0, p + start)) for grad in grads]
            + [pl.BlockSpec(memory_space=pl.ANY)] * len(earlier),
            out_specs=wide,
            scratch_shapes=[pltpu.VMEM((blocks, BLOCK, PAIR), jnp.float32)] * 3
            + [pltpu.VMEM((rows, PAIR), jnp.bfloat16)],
        ),
        out_shape=jax.ShapeDtypeStruct((rows, width), jnp.bfloat16),
        input_output_aliases={5 + len(grads): 0} if earlier else {},
        compiler_params=pltpu.CompilerParams(vmem_limit_bytes=GRANT),
        cost_estimate=estimate(scored * 2 * 1280, scored),
        name="attend_backward",
    )(mask, slopes, qkv, lse, mixed, *grads, *earlier)


def head_columns_kernel(at_ref, in_ref, out_ref):
    for t in range(3):

        @pl.when(pl.program_id(0) == t)
        def _():
            for pair in range(in_ref.shape[1] // PAIR):
                at = (pair * 3 + t) * PAIR
                out_ref[:, at : at + PAIR] = in_ref[:, pair * PAIR : (pair + 1) * PAIR]


def up_kernel(rows_ref, weight_ref, bias_ref, active_ref, slope_ref, *, chunk):
    rows = rows_ref[...]
    for at in range(0, weight_ref.shape[1], chunk):
        columns = slice(at, at + chunk)
        hidden = contract(rows, weight_ref[:, columns]) + bias_ref[:, columns]
        below = 0.5 + 0.5 * lax.erf(hidden * 2**-0.5)
        active_ref[:, columns] = (hidden * below).astype(active_ref.dtype)
        slope_ref[:, columns] = below + hidden * ((2 * math.pi) ** -0.5 * jnp.exp(-0.5 * hidden * hidden))


def hidden_grad_kernel(rows_ref, weight_ref, slope_ref, grad_ref, sum_ref, *, chunk):
    rows = rows_ref[...]
    starting = pl.program_id(0) == 0
    for at in range(0, weight_ref.shape[0], chunk):
        columns = slice(at, at + chunk)
        grad = contract_last(rows, weight_ref[columns, :]) * slope_ref[:, columns]
        grad = grad.astype(grad_ref.dtype)
        grad_ref[:, columns] = grad
        part = jnp.sum(grad.astype(jnp.float32), axis=0, keepdims=True)
        sum_ref[:, columns] = jnp.where(starting, part, sum_ref[:, columns] + part)


TILE = 256


def up_and_bend(rows, weight, bias):
    count, depth = rows.shape
    width = weight.shape[1]
    tile = pl.BlockSpec((TILE, width), lambda i: (i, 0))
    return pl.pallas_call(
        partial(up_kernel, chunk=512),
        grid=(count // TILE,),
        in_specs=[
            pl.BlockSpec((TILE, depth), lambda i: (i, 0)),
            pl.BlockSpec((depth, width), lambda i: (0, 0), pipeline_mode=pl.Buffered(1)),
            pl.BlockSpec((1, width), lambda i: (0, 0)),
        ],
        out_specs=[tile, tile],
        out_shape=[
            jax.ShapeDtypeStruct((count, width), jnp.bfloat16),
            jax.ShapeDtypeStruct((count, width), jnp.float32),
        ],
        compiler_params=pltpu.CompilerParams(vmem_limit_bytes=GRANT),
        cost_estimate=estimate(count * depth * width * 4, 2 * count * width),
        name="up_and_bend",
    )(rows, weight, bias)


def hidden_gradient(rows, weight, slope, start, count):
    depth = rows.shape[1]
    width = weight.shape[0]
    first = start // TILE
    line = pl.BlockSpec((1, width), lambda i: (0, 0))
    return pl.pallas_call(
        partial(hidden_grad_kernel, chunk=512),
        grid=(count // TILE,),
        in_specs=[
            pl.BlockSpec((TILE, depth), lambda i: (i + first, 0)),
            pl.BlockSpec((width, depth), lambda i: (0, 0), pipeline_mode=pl.Buffered(1)),
            pl.BlockSpec((TILE, width), lambda i: (i + first, 0)),
        ],
        out_specs=[pl.BlockSpec((TILE, width), lambda i: (i, 0)), line],
        out_shape=[
            jax.ShapeDtypeStruct((count, width), jnp.bfloat16),
            jax.ShapeDtypeStruct((1, width), jnp.float32),
        ],
        compiler_params=pltpu.CompilerParams(vmem_limit_bytes=GRANT),
        cost_estimate=estimate(count * depth * width * 3, 0),
        name="hidden_gradient",
    )(rows, weight, slope)


def product_kernel(rows_ref, weight_ref, out_ref):
    out_ref[...] = contract(rows_ref[...], weight_ref[...]).astype(out_ref.dtype)


def product_of(rows, weight, count):
    depth, width = weight.shape
    return pl.pallas_call(
        product_kernel,
        grid=(count // TILE,),
        in_specs=[
            pl.BlockSpec((TILE, depth), lambda i: (i, 0)),
            pl.BlockSpec((depth, width), lambda i: (0, 0), pipeline_mode=pl.Buffered(1)),
        ],
        out_specs=pl.BlockSpec((TILE, width), lambda i: (i, 0)),
        out_shape=jax.ShapeDtypeStruct((count, width), jnp.bfloat16),
        compiler_params=pltpu.CompilerParams(vmem_limit_bytes=GRANT),
        cost_estimate=estimate(2 * count * depth * width, 0),
        name="product",
    )(rows, weight)


def mixed_grad_kernel(rows_ref, weight_ref, out_ref):
    out_ref[...] = contract_last(rows_ref[...], weight_ref[...]).astype(out_ref.dtype)


def mixed_gradient(rows, weight, slab):
    count, depth = rows.shape
    width = weight.shape[0]
    return pl.pallas_call(
        mixed_grad_kernel,
        grid=(width // slab,),
        in_specs=[
            pl.BlockSpec((count, depth), lambda i: (0, 0), pipeline_mode=pl.Buffered(1)),
            pl.BlockSpec((slab, depth), lambda i: (i, 0)),
        ],
        out_specs=pl.BlockSpec((count, slab), lambda i: (0, i)),
        out_shape=jax.ShapeDtypeStruct((count, width), jnp.bfloat16),
        compiler_params=pltpu.CompilerParams(vmem_limit_bytes=GRANT),
        cost_estimate=estimate(2 * count * depth * width, 0),
        name="mixed_gradient",
    )(rows, weight)


def norm_back_kernel(own_ref, values_ref, average_ref, scale_ref, base_ref, gain_ref, *refs, parts):
    came, (low_ref, wide_ref, sums_ref) = refs[:parts], refs[parts:]
    wide = jnp.float32
    step = pl.program_id(0)

    @pl.when(step == 0)
    def _():
        sums_ref[...] = jnp.zeros_like(sums_ref)

    def make(came):
        grad = own_ref[...].astype(wide)
        for part in came:
            grad = grad + part[...].astype(wide)
        scale = scale_ref[...]
        normal = (values_ref[...].astype(wide) - average_ref[...]) * scale
        gained = grad * gain_ref[...]
        along = jnp.mean(gained * normal, axis=-1, keepdims=True)
        across = jnp.mean(gained, axis=-1, keepdims=True)
        made = base_ref[...].astype(wide) + scale * (gained - across - normal * along)
        low = made.astype(low_ref.dtype)
        low_ref[...] = low
        wide_ref[...] = made
        for at, part in enumerate((grad * normal, grad, low.astype(wide))):
            sums_ref[8 * at : 8 * at + 8, :] += jnp.sum(part.reshape(-1, 8, part.shape[1]), axis=0)

    if not came:
        make(())
        return
    upper = step < pl.num_programs(0) // 2
    pl.when(upper)(lambda: make(came[0::2]))
    pl.when(jnp.logical_not(upper))(lambda: make(came[1::2]))


def norm_back(rest, values, average, scale, base, gain, came):
    rows, width = values.shape
    steps = 8
    half = steps // 2
    came = list(came or ())
    count = rows // steps
    tile = pl.BlockSpec((count, width), lambda i: (i, 0))
    thin = pl.BlockSpec((count, 1), lambda i: (i, 0))
    top = pl.BlockSpec((count, width), lambda i: (jnp.minimum(i, half - 1), 0))
    bottom = pl.BlockSpec((count, width), lambda i: (jnp.maximum(i - half, 0), 0))
    low, full, sums = pl.pallas_call(
        partial(norm_back_kernel, parts=len(came)),
        grid=(steps,),
        in_specs=[tile, tile, thin, thin, tile, pl.BlockSpec((1, width), lambda i: (0, 0))]
        + [top, bottom] * (len(came) // 2),
        out_specs=[tile, tile, pl.BlockSpec((24, width), lambda i: (0, 0))],
        out_shape=[
            jax.ShapeDtypeStruct((rows, width), jnp.bfloat16),
            jax.ShapeDtypeStruct((rows, width), jnp.float32),
            jax.ShapeDtypeStruct((24, width), jnp.float32),
        ],
        compiler_params=pltpu.CompilerParams(vmem_limit_bytes=GRANT),
        cost_estimate=estimate(30 * rows * width, rows),
        name="norm_back",
    )(rest, values, average, scale, base, gain[None], *came)
    return low, full, jnp.sum(sums.reshape(3, 8, width), axis=1)


def outer_kernel(left_ref, right_ref, out_ref, *, chunk):
    left = left_ref[...]
    shards = out_ref.shape[0]
    for at in range(0, out_ref.shape[3], chunk):
        columns = slice(at, at + chunk)
        made = contract_first(left, right_ref[:, columns]).astype(out_ref.dtype)
        out_ref[:, 0, :, columns] = made.reshape(shards, -1, made.shape[1])


def outer(left, right, groups, shards, part_of=(0, 1)):
    at, parts = part_of
    tokens, rows = left.shape
    width = right.shape[1] // parts
    part = rows // groups
    made = pl.pallas_call(
        partial(outer_kernel, chunk=next(c for c in (512, 384, 256, 128) if width % c == 0)),
        grid=(groups,),
        in_specs=[
            pl.BlockSpec((tokens, part), lambda i: (0, i)),
            pl.BlockSpec((tokens, width), lambda i: (0, at), pipeline_mode=pl.Buffered(1)),
        ],
        out_specs=pl.BlockSpec((shards, 1, part // shards, width), lambda i: (0, i, 0, 0)),
        out_shape=jax.ShapeDtypeStruct((shards, groups, part // shards, width), jnp.bfloat16),
        compiler_params=pltpu.CompilerParams(vmem_limit_bytes=GRANT),
        cost_estimate=estimate(2 * tokens * rows * width, 0),
        name="outer",
    )(left, right)
    return made.reshape(rows, width)


def swap(values, bit):
    return lax.ppermute(values, "seq", [(i, i ^ bit) for i in range(4)])


def by_index(parts, me):
    if len(parts) != 4:
        return parts
    odd, upper = (me & 1) == 1, (me & 2) == 2
    a, b, c, d = parts
    a, b, c, d = (
        jnp.where(odd, b, a),
        jnp.where(odd, a, b),
        jnp.where(odd, d, c),
        jnp.where(odd, c, d),
    )
    return [jnp.where(upper, c, a), jnp.where(upper, d, b), jnp.where(upper, a, c), jnp.where(upper, b, d)]


def exchange(slots):
    if lax.axis_size("seq") != 4:
        return list(lax.all_to_all(jnp.stack(slots), "seq", split_axis=0, concat_axis=0, tiled=True))
    return [slots[0]] + [swap(slots[j], j) for j in (1, 2, 3)]


def gate(values, *before):
    return lax.optimization_barrier((values, *before))[0]


class Order:
    def __init__(self):
        self.pending = []

    def after(self, *values):
        self.pending += values

    def __call__(self, operation, *operands):
        if self.pending:
            count = len(operands)
            operands = lax.optimization_barrier((*operands, *self.pending))[:count]
        made = operation(*operands)
        self.pending = jax.tree.leaves(made)
        return made

    def gather(self, rows):
        if lax.axis_size("seq") != 4:
            return lax.all_gather(jnp.concatenate(rows, axis=0), "seq", axis=0, tiled=True), None
        top, bottom = rows
        return rows, (swap(bottom, 1), swap(top, 2), swap(top, 1), swap(bottom, 2))

    def fill(self, begun):
        rows, came = begun
        if came is None:
            return rows
        first_bottom, second_top, first_top, second_bottom = came
        room = jnp.zeros_like(rows[0])
        parts = (*rows, first_top, first_bottom, second_top, second_bottom, room, room)
        return self(lambda *parts: jnp.concatenate(parts, axis=0), *parts)

    def complete(self, made, pieces):
        if not isinstance(pieces, list):
            return made
        rows = pieces[-1].shape[0]

        def put(before, first, second):
            before = lax.dynamic_update_slice_in_dim(before, first, 6 * rows, axis=0)
            return lax.dynamic_update_slice_in_dim(before, second, 7 * rows, axis=0)

        return self(put, made, *pieces[-2:])

    def pass_on(self, begun, *before):
        rows, came = begun
        if came is None:
            return rows
        first_bottom, second_top, first_top, second_bottom = came
        self.after(*came)
        if before:
            second_top, first_bottom = gate((second_top, first_bottom), *before)
        far = [swap(second_top, 1), swap(first_bottom, 2)]
        return [*rows, first_top, first_bottom, second_top, second_bottom, *far]

    def halves(self, product, rows):
        def cut(values):
            made = product(values)
            half = made.shape[0] // 2
            return made[:half], made[half:]

        return self(cut, rows)

    def add_far(self, made, far, direct, *before, at=None):
        wide = jnp.float32
        half = far[0].shape[0]
        start = made.shape[0] - 4 * half if at is None else at

        def add(made, top, bottom):
            at = start
            first = (made[at + half : at + 2 * half].astype(wide) + bottom.astype(wide)).astype(made.dtype)
            second = (made[at + 2 * half : at + 3 * half].astype(wide) + top.astype(wide)).astype(made.dtype)
            if direct is None:
                first = jnp.concatenate([made[at : at + half], first], axis=0)
                second = jnp.concatenate([second, made[at + 3 * half : at + 4 * half]], axis=0)
            return first, second

        first, second = self(add, made, *far)
        if before:
            first, second = gate((first, second), *before)
        first, second = swap(first, 1), swap(second, 2)
        return (first, second) if direct is None else (direct[0], first, second, direct[1])


def swap_far(halves):
    return swap(halves[0], 1), swap(halves[1], 2)


def swap_direct(made, half):
    at = made.shape[0] - 4 * half
    return swap(made[at : at + half], 1), swap(made[at + 3 * half :], 2)


def summed(own, came):
    wide = jnp.float32
    own = own.astype(wide)
    return sum((part.astype(wide) for part in came), own)


def whole(parts):
    return jnp.concatenate(parts, axis=0) if isinstance(parts, list) else parts


def total_stages():
    stages = []
    for axis in ("fsdp", "seq"):
        count, bit = lax.axis_size(axis), 1
        bits = count.bit_length() - 1
        while bit < count:
            stages.append((axis, [bit] if bits % 2 else [bit, 2 * bit, 3 * bit]))
            bit <<= 1 if bits % 2 else 2
            bits -= bits % 2
    return stages


def local(
    tokens,
    cotangent,
    w_qkv,
    qv_bias,
    w_out,
    out_bias,
    ln1_gain,
    ln1_shift,
    ln2_gain,
    ln2_shift,
    w_up,
    up_bias,
    w_down,
    down_bias,
):
    seq_count, local_len, model_width = tokens.shape
    groups, shards = lax.axis_size("seq"), lax.axis_size("fsdp")
    me = lax.axis_index("seq")
    square = groups == 4
    heads_here = HEADS // groups
    slab = heads_here * HEAD_DIM
    pairs = slab // PAIR
    hidden_width = w_up.shape[1]
    hidden_slab = hidden_width // groups
    rows_here = seq_count * local_len
    low, wide = jnp.bfloat16, jnp.float32
    mask = jnp.reshape(me if square else jnp.zeros_like(me), (1,)).astype(jnp.int32)
    head_index = me * heads_here + jnp.arange(1, heads_here + 1, dtype=jnp.int32)
    slopes = 2.0 ** (-8.0 * head_index.astype(wide) / HEADS)

    def head_columns(values):
        rows = values.shape[0]
        return pl.pallas_call(
            head_columns_kernel,
            grid_spec=pltpu.PrefetchScalarGridSpec(
                num_scalar_prefetch=1,
                grid=(3,),
                in_specs=[pl.BlockSpec((rows, slab), lambda t, at: (0, t * groups + at[0]))],
                out_specs=pl.BlockSpec((rows, 3 * slab), lambda t, at: (0, 0)),
            ),
            out_shape=jax.ShapeDtypeStruct((rows, 3 * slab), values.dtype),
            name="head_columns",
        )(jnp.reshape(me, (1,)).astype(jnp.int32), values)

    def own_slab(values, axis):
        width = values.shape[axis] // groups
        return lax.dynamic_slice_in_dim(values, me * width, width, axis=axis)

    order = Order()
    x_low = tokens.reshape(rows_here, model_width)
    x = x_low.astype(wide)
    dz_low = cotangent.reshape(rows_here, model_width)
    qkv_slab = lax.all_gather(head_columns(w_qkv), "fsdp", axis=0, tiled=True)
    qkv_bias = head_columns(jnp.concatenate([qv_bias[0], jnp.zeros_like(qv_bias[0]), qv_bias[1]])[None])
    up_bias_slab = own_slab(up_bias, 0)

    first_norm, *first_stats = layer_norm(x, ln1_gain, ln1_shift)
    half = rows_here // 2

    def halves_of(values):
        return values[:half].astype(low), values[half:].astype(low)

    normed = order.gather(order(halves_of, first_norm))
    normed = order.pass_on(normed)
    full_out = lax.all_gather(w_out, "fsdp", axis=0, tiled=True)
    up_slab = lax.all_gather(own_slab(gate(w_up, normed[0]) if square else w_up, 1), "fsdp", axis=0, tiled=True)
    down_slab = lax.all_gather(own_slab(gate(w_down, normed[0]) if square else w_down, 0), "fsdp", axis=1, tiled=True)
    normed = whole(normed)
    upstream = order.gather(halves_of(gate(dz_low, normed)))
    qkv = order(lambda rows: (contract(rows, qkv_slab) + qkv_bias).astype(low), normed)
    attended, log_totals = order(lambda rows: attend_forward(mask, slopes, rows, seq_count, local_len), qkv)
    if square:
        attended = gate(attended, *upstream[1])
    mixed_slots = exchange([attended[j * rows_here : (j + 1) * rows_here] for j in range(groups)])
    mixed_rows = jnp.concatenate(by_index(mixed_slots, me), axis=1)
    mixed_slots = jnp.concatenate(mixed_slots, axis=1)

    def pair_swap(values):
        return lax.ppermute(values, "fsdp", [(i, i ^ 1) for i in range(shards)])

    parity = lax.axis_index("fsdp") & 1
    out_rows = model_width // (groups * shards)

    def pair_halves(values):
        halves = values.reshape(rows_here, -1, 2, out_rows)
        return tuple(
            lax.dynamic_index_in_dim(halves, index, axis=2, keepdims=False).reshape(rows_here, -1)
            for index in (parity, 1 - parity)
        )

    middle = order(lambda rows: x + (contract(rows, full_out) + out_bias), mixed_rows)
    second_norm, *second_stats = layer_norm(middle, ln2_gain, ln2_shift)
    second = order.gather(order(halves_of, second_norm))
    mine, theirs = order(pair_halves, mixed_slots)
    upstream_made = order.fill(upstream)
    theirs = pair_swap(theirs)
    dz_sum = order(lambda values: jnp.sum(values.astype(wide), axis=0), dz_low)
    second = whole(order.pass_on(second))
    upstream = order.pass_on(upstream, second)
    active, slope = order(lambda rows: up_and_bend(rows, up_slab, up_bias_slab[None]), second)
    mixed_half = order(lambda *parts: jnp.concatenate(parts, axis=0), mine, theirs)
    upstream = order.complete(upstream_made, upstream)

    def slab_product(left, right, part_of=(0, 1)):
        return order(lambda rows, others: outer(rows, others, groups, shards, part_of), left, right)

    def slab_sum(made):
        return lax.psum_scatter(made, "fsdp", scatter_dimension=0, tiled=True)

    def slabs_of_rows(values):
        return lax.all_to_all(
            values.reshape(groups, -1, values.shape[1]), "seq", split_axis=0, concat_axis=0, tiled=True
        )

    down_sum = slab_sum(slab_product(upstream, active))
    count = rows_here

    def slots(product, start, stop):
        return lambda values: product(values[start * count : stop * count])

    def to_second(rows):
        return contract_last(rows, up_slab).astype(low)

    def to_result(rows):
        return contract(rows, down_slab).astype(low)

    def to_normed(rows):
        return contract_last(rows, qkv_slab).astype(low)

    def scatter(product, rows):
        return lax.psum_scatter(order(product, rows), "seq", scatter_dimension=0, tiled=True)

    hidden_grad, hidden_sum = order(lambda rows: hidden_gradient(rows, down_slab, slope, 0, groups * count), upstream)
    if square:
        far = swap_far(order.halves(slots(to_second, 3, 4), hidden_grad))
        rest = order(slots(to_second, 0, 3), hidden_grad)
        second_own = rest
        direct = swap_direct(rest, half)
        came = order.add_far(rest, far, direct)
        result_far = order.halves(slots(to_result, 3, 4), active)
        up_sum = slab_sum(gate(slab_product(second, hidden_grad), *came))
        result_far = swap_far(gate(result_far, *came))
    else:
        second_own, came = scatter(to_second, hidden_grad), ()
        up_sum = slab_sum(slab_product(second, hidden_grad))
    branch_grad, middle_grad, middle_sums = order(
        lambda own, *came: norm_back(own, middle, *second_stats, dz_low, ln2_gain, came), second_own, *came
    )

    def column_sum(values):
        return jnp.sum(values.astype(wide), axis=0)

    hidden_sum = lax.dynamic_update_slice_in_dim(
        jnp.zeros((hidden_width,), wide), hidden_sum[0], me * hidden_slab, axis=0
    )
    early = [middle_sums[2], middle_sums[0], middle_sums[1], hidden_sum, dz_sum]
    mixed_grad = order(lambda rows: mixed_gradient(rows, full_out, slab), branch_grad)
    mixed_grad = exchange(by_index([mixed_grad[:, j * slab : (j + 1) * slab] for j in range(groups)], me))
    if square:
        result_rest = order(lambda rows: product_of(rows, down_slab, 3 * count), active)
        order.after(*mixed_grad)
        result_came = order.add_far(result_rest, result_far, None)
    attention = (mask, slopes, qkv, log_totals, attended)
    order.after(down_sum)
    begun = order(
        lambda *grads: attend_backward(*attention, grads, seq_count, local_len, 0, pairs // 2), *mixed_grad
    )
    branch_other = pair_swap(branch_grad)
    branch_pair = jnp.concatenate([branch_grad, branch_other], axis=0)
    out_sum = order(lambda columns: outer(columns, branch_pair, groups, 1), mixed_half)
    if square:
        part = out_sum.shape[0] // 4
        out_far = out_sum[3 * part : 3 * part + part // 2], out_sum[3 * part + part // 2 :]
        out_far = swap_far(out_far)
    first_sum = slab_product(normed, begun, (0, 2))
    if square:
        first_sum = gate(first_sum, *result_came)
        order.after(*result_came)
    first_sum = slab_sum(first_sum)
    qkv_grad = order(
        lambda begun, *grads: attend_backward(
            *attention, grads, seq_count, local_len, pairs // 2, pairs, begun
        ),
        begun,
        *mixed_grad,
    )
    if square:
        out_came = order.add_far(out_sum, out_far, None, at=part)
    else:
        out_sum = lax.psum_scatter(out_sum, "seq", scatter_dimension=0, tiled=True)
    order.after(up_sum)
    if square:
        far = swap_far(order.halves(slots(to_normed, 3, 4), qkv_grad))
        order.after(first_sum)
        near = order(slots(to_normed, 1, 3), qkv_grad)
        direct = swap_direct(near, half)
        order.after(*out_came)
        out_sum = order(lambda own, *came: summed(own[:part], came).astype(low), out_sum, *out_came)
    out_sum = out_sum.reshape(-1, 1, out_rows, model_width)
    zero = jnp.zeros_like(out_sum)
    out_sum = jnp.concatenate(
        [jnp.where(parity == 0, out_sum, zero), jnp.where(parity == 1, out_sum, zero)], axis=1
    ).reshape(-1, model_width)
    if square:
        out_sum = gate(out_sum, *far)
    grad_w_out = lax.psum_scatter(out_sum, "fsdp", scatter_dimension=0, tiled=True).astype(wide)
    second_sum = slab_product(normed, qkv_grad, (1, 2))
    if square:
        second_sum = slab_sum(gate(second_sum, *far, *direct, grad_w_out))
        came = order.add_far(near, far, direct)
        down_slabs = slabs_of_rows(gate(down_sum, *came))
        normed_own = order(slots(to_normed, 0, 1), qkv_grad)
    else:
        second_sum, down_slabs = slab_sum(second_sum), slabs_of_rows(down_sum)
        normed_own, came = scatter(to_normed, qkv_grad), ()
    if square:
        result = order(
            lambda rest, *came: (middle + (summed(rest[:count], came) + down_bias)).astype(low),
            result_rest,
            *result_came,
        )
    else:
        result = (middle + (scatter(to_result, active).astype(wide) + down_bias)).astype(low)
    result = result.reshape(tokens.shape)
    qkv_column_sum = order(column_sum, qkv_grad)
    grad_tokens, _, input_sums = order(
        lambda own, *came: norm_back(own, x_low, *first_stats, middle_grad, ln1_gain, came), normed_own, *came
    )
    grad_tokens = grad_tokens.reshape(tokens.shape)
    up_slabs = slabs_of_rows(gate(up_sum, *came, normed_own))
    first_slabs = slabs_of_rows(gate(first_sum, *came, normed_own))
    second_slabs = slabs_of_rows(second_sum)

    def rows_of(slabs):
        return jnp.swapaxes(slabs, 0, 1).astype(wide)

    grad_w_down = rows_of(down_slabs).reshape(-1, hidden_width).T
    grad_w_up = rows_of(up_slabs).reshape(-1, hidden_width)
    grad_w_qkv = [
        rows_of(part).reshape(-1, groups, pairs // 2, 3, PAIR) for part in (first_slabs, second_slabs)
    ]
    grad_w_qkv = jnp.concatenate(grad_w_qkv, axis=2)
    grad_w_qkv = jnp.transpose(grad_w_qkv, (0, 3, 1, 2, 4)).reshape(-1, 3 * model_width)

    head_sum = jnp.transpose(qkv_column_sum.reshape(pairs, 3, PAIR), (1, 0, 2)).reshape(3, slab)
    qv_sum = lax.dynamic_update_slice_in_dim(
        jnp.zeros((2, model_width), wide), head_sum[0::2], me * slab, axis=1
    )
    late = [qv_sum.reshape(-1), input_sums[0], input_sums[1]]
    sums = order(lambda *parts: jnp.concatenate(parts).reshape(-1, PAIR), *early, *late)
    stages = total_stages()
    for axis, masks in stages:
        others = range(lax.axis_size(axis))
        came = [lax.ppermute(sums, axis, [(i, i ^ mask) for i in others]) for mask in masks]
        if (axis, masks) == stages[-1]:
            order.after(down_slabs, up_slabs, first_slabs, second_slabs)
        sums = order(lambda *parts: sum(parts[1:], parts[0]), sums, *came)
    sums = sums.reshape(-1)

    def cut(at, count):
        return sums[at * model_width : (at + count) * model_width]

    ratio = hidden_width // model_width
    return (
        result,
        grad_tokens,
        grad_w_qkv,
        cut(4 + ratio, 2).reshape(2, model_width),
        grad_w_out,
        cut(0, 1),
        cut(6 + ratio, 1),
        cut(7 + ratio, 1),
        cut(1, 1),
        cut(2, 1),
        grad_w_up,
        cut(3, ratio),
        grad_w_down,
        cut(3 + ratio, 1),
    )


def solution(mesh):
    return jax.shard_map(
        local,
        mesh=mesh,
        in_specs=(
            P("fsdp", "seq", None),
            P("fsdp", "seq", None),
            P("fsdp", None),
            P(),
            P("fsdp", None),
            P(),
            P(),
            P(),
            P(),
            P(),
            P("fsdp", None),
            P(),
            P(None, "fsdp"),
            P(),
        ),
        out_specs=(
            P("fsdp", "seq", None),
            P("fsdp", "seq", None),
            P(("seq", "fsdp"), None),
            P(),
            P(("seq", "fsdp"), None),
            P(),
            P(),
            P(),
            P(),
            P(),
            P(("seq", "fsdp"), None),
            P(),
            P(None, ("seq", "fsdp")),
            P(),
        ),
        check_vma=False,
    )
```

```python
import math
from functools import partial

import jax
import jax.numpy as jnp
from jax import lax
from jax.experimental import pallas as pl
from jax.experimental.pallas import tpu as pltpu
from jax.sharding import PartitionSpec as P

HEADS = 32
HEAD_DIM = 64
BLOCK = 256
PAIR = 2 * HEAD_DIM
GRANT = 58 * 2**20


def estimate(flops, transcendentals=0):
    return pl.CostEstimate(flops=flops // 4, bytes_accessed=flops // 4096, transcendentals=transcendentals // 4)


def layer_norm(token_rows, gain_vec, shift_vec):
    average = jnp.mean(token_rows, axis=-1, keepdims=True)
    centred = token_rows - average
    spread = jnp.mean(centred * centred, axis=-1, keepdims=True)
    scale = lax.rsqrt(spread + 1e-05)
    return centred * scale * gain_vec + shift_vec, average, scale


def contract(left_side, right_side):
    return lax.dot_general(
        left_side, right_side, (((1,), (0,)), ((), ())), preferred_element_type=jnp.float32
    )


def contract_last(left_side, right_side):
    return lax.dot_general(
        left_side, right_side, (((1,), (1,)), ((), ())), preferred_element_type=jnp.float32
    )


def contract_first(left_side, right_side):
    return lax.dot_general(
        left_side, right_side, (((0,), (0,)), ((), ())), preferred_element_type=jnp.float32
    )


def row_pieces(mask, sequence, block, seqs, local):
    per = BLOCK // local
    return [
        pl.ds(pl.multiple_of((((block * per + r) ^ mask) * seqs + sequence) * local, local), local)
        for r in range(per)
    ]


def load_rows(ref, pieces, columns):
    parts = [ref[piece, columns] for piece in pieces]
    return parts[0] if len(parts) == 1 else jnp.concatenate(parts, axis=0)


def store_rows(ref, pieces, columns, values):
    local = values.shape[0] // len(pieces)
    for r, piece in enumerate(pieces):
        ref[piece, columns] = values[r * local : (r + 1) * local]


Q_COLUMNS, K_COLUMNS, V_COLUMNS = (slice(t * PAIR, (t + 1) * PAIR) for t in range(3))


def attend_forward_kernel(mask_ref, slope_ref, qkv_ref, mixed_ref, lse_ref, *, blocks, seqs, local):
    pair, sequence = pl.program_id(0), pl.program_id(1)
    mask = mask_ref[0]
    lane = lax.broadcasted_iota(jnp.int32, (BLOCK, PAIR), 1)
    row = lax.broadcasted_iota(jnp.int32, (BLOCK, BLOCK), 0)
    column = lax.broadcasted_iota(jnp.int32, (BLOCK, BLOCK), 1)
    gap = (row - column).astype(jnp.float32)
    pieces = [row_pieces(mask, sequence, block, seqs, local) for block in range(blocks)]

    for i in range(blocks):
        q_pair = load_rows(qkv_ref, pieces[i], Q_COLUMNS)
        outs, lses = [], []
        for head in range(2):
            slope = slope_ref[pair * 2 + head]
            mine = (lane >= head * HEAD_DIM) & (lane < (head + 1) * HEAD_DIM)
            q = jnp.where(mine, q_pair, jnp.zeros_like(q_pair)) * jnp.bfloat16(HEAD_DIM**-0.5)
            parts, highest = [], None
            for j in range(i + 1):
                scores = contract_last(q, load_rows(qkv_ref, pieces[j], K_COLUMNS))
                distance = jnp.abs(gap) if i == j else gap + float(BLOCK * (i - j))
                scores = scores - slope * distance
                parts.append(scores)
                top = jnp.max(scores, axis=-1, keepdims=True)
                highest = top if highest is None else jnp.maximum(highest, top)
            total, out = None, None
            for j in range(i + 1):
                weights = jnp.exp(parts[j] - highest)
                part = jnp.sum(weights, axis=-1, keepdims=True)
                mixed = contract(weights.astype(jnp.bfloat16), load_rows(qkv_ref, pieces[j], V_COLUMNS))
                total = part if total is None else total + part
                out = mixed if out is None else out + mixed
            outs.append(out / total)
            lses.append(highest + jnp.log(total))
        first = lane < HEAD_DIM
        everything = slice(0, PAIR)
        store_rows(
            mixed_ref, pieces[i], everything, jnp.where(first, outs[0], outs[1]).astype(mixed_ref.dtype)
        )
        store_rows(lse_ref, pieces[i], everything, jnp.where(first, lses[0], lses[1]))


def attend_backward_kernel(
    mask_ref, slope_ref, qkv_ref, lse_ref, mixed_ref, *rest, blocks, seqs, local, start, grads
):
    out_ref, dq_ref, dk_ref, dv_ref, grad_ref = rest[-5:]
    pair, sequence = pl.program_id(0) + start, pl.program_id(1)
    mask = mask_ref[0]
    lane = lax.broadcasted_iota(jnp.int32, (BLOCK, PAIR), 1)
    key = lax.broadcasted_iota(jnp.int32, (BLOCK, BLOCK), 0)
    query = lax.broadcasted_iota(jnp.int32, (BLOCK, BLOCK), 1)
    gap = (query - key).astype(jnp.float32)
    pieces = [row_pieces(mask, sequence, block, seqs, local) for block in range(blocks)]
    everything = slice(0, PAIR)

    @pl.when(sequence == 0)
    def _():
        at = 0
        for part in rest[:grads]:
            grad_ref[at : at + part.shape[0], :] = part[...]
            at += part.shape[0]

    for i in range(blocks):
        q_pair = load_rows(qkv_ref, pieces[i], Q_COLUMNS)
        up_pair = load_rows(grad_ref, pieces[i], everything)
        mixed_pair = load_rows(mixed_ref, pieces[i], everything)
        inner_all = (up_pair.astype(jnp.float32) * mixed_pair.astype(jnp.float32)).T
        lse_all = load_rows(lse_ref, pieces[i], everything).T
        dq = None
        for head in range(2):
            slope = slope_ref[pair * 2 + head]
            mine = (lane >= head * HEAD_DIM) & (lane < (head + 1) * HEAD_DIM)
            zero = jnp.zeros_like(q_pair)
            q = jnp.where(mine, q_pair, zero) * jnp.bfloat16(HEAD_DIM**-0.5)
            up = jnp.where(mine, up_pair, zero)
            inner = jnp.sum(inner_all[head * HEAD_DIM : (head + 1) * HEAD_DIM], axis=0, keepdims=True)
            lse = lse_all[head * HEAD_DIM : head * HEAD_DIM + 1]
            for j in range(i + 1):
                k_pair = load_rows(qkv_ref, pieces[j], K_COLUMNS)
                distance = jnp.abs(gap) if i == j else gap + float(BLOCK * (i - j))
                probs = jnp.exp(contract_last(k_pair, q) - slope * distance - lse)
                prob_grad = contract_last(load_rows(qkv_ref, pieces[j], V_COLUMNS), up)
                score_grad = (probs * (prob_grad - inner)).astype(jnp.bfloat16)
                dv = contract(probs.astype(jnp.bfloat16), up)
                dk = contract(score_grad, q)
                part = contract_first(score_grad, jnp.where(mine, k_pair, zero))
                dq = part if dq is None else dq + part
                if i == j and head == 0:
                    dv_ref[j] = dv
                    dk_ref[j] = dk
                else:
                    dv_ref[j] += dv
                    dk_ref[j] += dk
        dq_ref[i] = dq
    for i in range(blocks):
        store_rows(out_ref, pieces[i], Q_COLUMNS, (dq_ref[i] * HEAD_DIM**-0.5).astype(out_ref.dtype))
        store_rows(out_ref, pieces[i], K_COLUMNS, dk_ref[i].astype(out_ref.dtype))
        store_rows(out_ref, pieces[i], V_COLUMNS, dv_ref[i].astype(out_ref.dtype))


def attend_forward(mask, slopes, qkv, seqs, local):
    rows, width = qkv.shape
    pairs, blocks = width // (3 * PAIR), rows // seqs // BLOCK
    scored = pairs * seqs * blocks * (blocks + 1) * BLOCK * BLOCK
    return pl.pallas_call(
        partial(attend_forward_kernel, blocks=blocks, seqs=seqs, local=local),
        grid_spec=pltpu.PrefetchScalarGridSpec(
            num_scalar_prefetch=2,
            grid=(pairs, seqs),
            in_specs=[pl.BlockSpec((rows, 3 * PAIR), lambda p, *_: (0, p))],
            out_specs=[pl.BlockSpec((rows, PAIR), lambda p, *_: (0, p))] * 2,
        ),
        out_shape=[
            jax.ShapeDtypeStruct((rows, pairs * PAIR), jnp.bfloat16),
            jax.ShapeDtypeStruct((rows, pairs * PAIR), jnp.float32),
        ],
        compiler_params=pltpu.CompilerParams(vmem_limit_bytes=GRANT),
        cost_estimate=estimate(scored * 2 * 512, scored),
        name="attend_forward",
    )(mask, slopes, qkv)


def attend_backward(mask, slopes, qkv, lse, mixed, grads, seqs, local, start, stop, begun=None):
    rows, width = qkv.shape
    blocks = rows // seqs // BLOCK
    scored = (stop - start) * seqs * blocks * (blocks + 1) * BLOCK * BLOCK
    narrow = pl.BlockSpec((rows, PAIR), lambda p, *_: (0, p + start))
    wide = pl.BlockSpec((rows, 3 * PAIR), lambda p, *_: (0, p + start))
    earlier = [] if begun is None else [begun]
    return pl.pallas_call(
        partial(
            attend_backward_kernel, blocks=blocks, seqs=seqs, local=local, start=start, grads=len(grads)
        ),
        grid_spec=pltpu.PrefetchScalarGridSpec(
            num_scalar_prefetch=2,
            grid=(stop - start, seqs),
            in_specs=[wide, narrow, narrow]
            + [pl.BlockSpec((grad.shape[0], PAIR), lambda p, *_: (0, p + start)) for grad in grads]
            + [pl.BlockSpec(memory_space=pl.ANY)] * len(earlier),
            out_specs=wide,
            scratch_shapes=[pltpu.VMEM((blocks, BLOCK, PAIR), jnp.float32)] * 3
            + [pltpu.VMEM((rows, PAIR), jnp.bfloat16)],
        ),
        out_shape=jax.ShapeDtypeStruct((rows, width), jnp.bfloat16),
        input_output_aliases={5 + len(grads): 0} if earlier else {},
        compiler_params=pltpu.CompilerParams(vmem_limit_bytes=GRANT),
        cost_estimate=estimate(scored * 2 * 1280, scored),
        name="attend_backward",
    )(mask, slopes, qkv, lse, mixed, *grads, *earlier)


def head_columns_kernel(at_ref, in_ref, out_ref):
    for t in range(3):

        @pl.when(pl.program_id(0) == t)
        def _():
            for pair in range(in_ref.shape[1] // PAIR):
                at = (pair * 3 + t) * PAIR
                out_ref[:, at : at + PAIR] = in_ref[:, pair * PAIR : (pair + 1) * PAIR]


def up_kernel(rows_ref, weight_ref, bias_ref, active_ref, slope_ref, *, chunk):
    rows = rows_ref[...]
    for at in range(0, weight_ref.shape[1], chunk):
        columns = slice(at, at + chunk)
        hidden = contract(rows, weight_ref[:, columns]) + bias_ref[:, columns]
        below = 0.5 + 0.5 * lax.erf(hidden * 2**-0.5)
        active_ref[:, columns] = (hidden * below).astype(active_ref.dtype)
        slope_ref[:, columns] = below + hidden * ((2 * math.pi) ** -0.5 * jnp.exp(-0.5 * hidden * hidden))


def hidden_grad_kernel(rows_ref, weight_ref, slope_ref, grad_ref, sum_ref, *, chunk):
    rows = rows_ref[...]
    starting = pl.program_id(0) == 0
    for at in range(0, weight_ref.shape[0], chunk):
        columns = slice(at, at + chunk)
        grad = contract_last(rows, weight_ref[columns, :]) * slope_ref[:, columns]
        grad = grad.astype(grad_ref.dtype)
        grad_ref[:, columns] = grad
        part = jnp.sum(grad.astype(jnp.float32), axis=0, keepdims=True)
        sum_ref[:, columns] = jnp.where(starting, part, sum_ref[:, columns] + part)


TILE = 256


def up_and_bend(rows, weight, bias):
    count, depth = rows.shape
    width = weight.shape[1]
    tile = pl.BlockSpec((TILE, width), lambda i: (i, 0))
    return pl.pallas_call(
        partial(up_kernel, chunk=512),
        grid=(count // TILE,),
        in_specs=[
            pl.BlockSpec((TILE, depth), lambda i: (i, 0)),
            pl.BlockSpec((depth, width), lambda i: (0, 0), pipeline_mode=pl.Buffered(1)),
            pl.BlockSpec((1, width), lambda i: (0, 0)),
        ],
        out_specs=[tile, tile],
        out_shape=[
            jax.ShapeDtypeStruct((count, width), jnp.bfloat16),
            jax.ShapeDtypeStruct((count, width), jnp.float32),
        ],
        compiler_params=pltpu.CompilerParams(vmem_limit_bytes=GRANT),
        cost_estimate=estimate(count * depth * width * 4, 2 * count * width),
        name="up_and_bend",
    )(rows, weight, bias)


def hidden_gradient(rows, weight, slope, start, count):
    depth = rows.shape[1]
    width = weight.shape[0]
    first = start // TILE
    line = pl.BlockSpec((1, width), lambda i: (0, 0))
    return pl.pallas_call(
        partial(hidden_grad_kernel, chunk=512),
        grid=(count // TILE,),
        in_specs=[
            pl.BlockSpec((TILE, depth), lambda i: (i + first, 0)),
            pl.BlockSpec((width, depth), lambda i: (0, 0), pipeline_mode=pl.Buffered(1)),
            pl.BlockSpec((TILE, width), lambda i: (i + first, 0)),
        ],
        out_specs=[pl.BlockSpec((TILE, width), lambda i: (i, 0)), line],
        out_shape=[
            jax.ShapeDtypeStruct((count, width), jnp.bfloat16),
            jax.ShapeDtypeStruct((1, width), jnp.float32),
        ],
        compiler_params=pltpu.CompilerParams(vmem_limit_bytes=GRANT),
        cost_estimate=estimate(count * depth * width * 3, 0),
        name="hidden_gradient",
    )(rows, weight, slope)


def product_kernel(rows_ref, weight_ref, out_ref):
    out_ref[...] = contract(rows_ref[...], weight_ref[...]).astype(out_ref.dtype)


def product_of(rows, weight, count):
    depth, width = weight.shape
    return pl.pallas_call(
        product_kernel,
        grid=(count // TILE,),
        in_specs=[
            pl.BlockSpec((TILE, depth), lambda i: (i, 0)),
            pl.BlockSpec((depth, width), lambda i: (0, 0), pipeline_mode=pl.Buffered(1)),
        ],
        out_specs=pl.BlockSpec((TILE, width), lambda i: (i, 0)),
        out_shape=jax.ShapeDtypeStruct((count, width), jnp.bfloat16),
        compiler_params=pltpu.CompilerParams(vmem_limit_bytes=GRANT),
        cost_estimate=estimate(2 * count * depth * width, 0),
        name="product",
    )(rows, weight)


def mixed_grad_kernel(rows_ref, weight_ref, out_ref):
    out_ref[...] = contract_last(rows_ref[...], weight_ref[...]).astype(out_ref.dtype)


def mixed_gradient(rows, weight, slab):
    count, depth = rows.shape
    width = weight.shape[0]
    return pl.pallas_call(
        mixed_grad_kernel,
        grid=(width // slab,),
        in_specs=[
            pl.BlockSpec((count, depth), lambda i: (0, 0), pipeline_mode=pl.Buffered(1)),
            pl.BlockSpec((slab, depth), lambda i: (i, 0)),
        ],
        out_specs=pl.BlockSpec((count, slab), lambda i: (0, i)),
        out_shape=jax.ShapeDtypeStruct((count, width), jnp.bfloat16),
        compiler_params=pltpu.CompilerParams(vmem_limit_bytes=GRANT),
        cost_estimate=estimate(2 * count * depth * width, 0),
        name="mixed_gradient",
    )(rows, weight)


def norm_back_kernel(own_ref, values_ref, average_ref, scale_ref, base_ref, gain_ref, *refs, parts):
    came, (low_ref, wide_ref, sums_ref) = refs[:parts], refs[parts:]
    wide = jnp.float32
    step = pl.program_id(0)

    @pl.when(step == 0)
    def _():
        sums_ref[...] = jnp.zeros_like(sums_ref)

    def make(came):
        grad = own_ref[...].astype(wide)
        for part in came:
            grad = grad + part[...].astype(wide)
        scale = scale_ref[...]
        normal = (values_ref[...].astype(wide) - average_ref[...]) * scale
        gained = grad * gain_ref[...]
        along = jnp.mean(gained * normal, axis=-1, keepdims=True)
        across = jnp.mean(gained, axis=-1, keepdims=True)
        made = base_ref[...].astype(wide) + scale * (gained - across - normal * along)
        low = made.astype(low_ref.dtype)
        low_ref[...] = low
        wide_ref[...] = made
        for at, part in enumerate((grad * normal, grad, low.astype(wide))):
            sums_ref[8 * at : 8 * at + 8, :] += jnp.sum(part.reshape(-1, 8, part.shape[1]), axis=0)

    if not came:
        make(())
        return
    upper = step < pl.num_programs(0) // 2
    pl.when(upper)(lambda: make(came[0::2]))
    pl.when(jnp.logical_not(upper))(lambda: make(came[1::2]))


def norm_back(rest, values, average, scale, base, gain, came):
    rows, width = values.shape
    steps = 8
    half = steps // 2
    came = list(came or ())
    count = rows // steps
    tile = pl.BlockSpec((count, width), lambda i: (i, 0))
    thin = pl.BlockSpec((count, 1), lambda i: (i, 0))
    top = pl.BlockSpec((count, width), lambda i: (jnp.minimum(i, half - 1), 0))
    bottom = pl.BlockSpec((count, width), lambda i: (jnp.maximum(i - half, 0), 0))
    low, full, sums = pl.pallas_call(
        partial(norm_back_kernel, parts=len(came)),
        grid=(steps,),
        in_specs=[tile, tile, thin, thin, tile, pl.BlockSpec((1, width), lambda i: (0, 0))]
        + [top, bottom] * (len(came) // 2),
        out_specs=[tile, tile, pl.BlockSpec((24, width), lambda i: (0, 0))],
        out_shape=[
            jax.ShapeDtypeStruct((rows, width), jnp.bfloat16),
            jax.ShapeDtypeStruct((rows, width), jnp.float32),
            jax.ShapeDtypeStruct((24, width), jnp.float32),
        ],
        compiler_params=pltpu.CompilerParams(vmem_limit_bytes=GRANT),
        cost_estimate=estimate(30 * rows * width, rows),
        name="norm_back",
    )(rest, values, average, scale, base, gain[None], *came)
    return low, full, jnp.sum(sums.reshape(3, 8, width), axis=1)


def outer_kernel(left_ref, right_ref, out_ref, *, chunk):
    left = left_ref[...]
    shards = out_ref.shape[0]
    for at in range(0, out_ref.shape[3], chunk):
        columns = slice(at, at + chunk)
        made = contract_first(left, right_ref[:, columns]).astype(out_ref.dtype)
        out_ref[:, 0, :, columns] = made.reshape(shards, -1, made.shape[1])


def outer(left, right, groups, shards, part_of=(0, 1)):
    at, parts = part_of
    tokens, rows = left.shape
    width = right.shape[1] // parts
    part = rows // groups
    made = pl.pallas_call(
        partial(outer_kernel, chunk=next(c for c in (512, 384, 256, 128) if width % c == 0)),
        grid=(groups,),
        in_specs=[
            pl.BlockSpec((tokens, part), lambda i: (0, i)),
            pl.BlockSpec((tokens, width), lambda i: (0, at), pipeline_mode=pl.Buffered(1)),
        ],
        out_specs=pl.BlockSpec((shards, 1, part // shards, width), lambda i: (0, i, 0, 0)),
        out_shape=jax.ShapeDtypeStruct((shards, groups, part // shards, width), jnp.bfloat16),
        compiler_params=pltpu.CompilerParams(vmem_limit_bytes=GRANT),
        cost_estimate=estimate(2 * tokens * rows * width, 0),
        name="outer",
    )(left, right)
    return made.reshape(rows, width)


def swap(values, bit):
    return lax.ppermute(values, "seq", [(i, i ^ bit) for i in range(4)])


def by_index(parts, me):
    if len(parts) != 4:
        return parts
    odd, upper = (me & 1) == 1, (me & 2) == 2
    a, b, c, d = parts
    a, b, c, d = (
        jnp.where(odd, b, a),
        jnp.where(odd, a, b),
        jnp.where(odd, d, c),
        jnp.where(odd, c, d),
    )
    return [jnp.where(upper, c, a), jnp.where(upper, d, b), jnp.where(upper, a, c), jnp.where(upper, b, d)]


def exchange(slots):
    if lax.axis_size("seq") != 4:
        return list(lax.all_to_all(jnp.stack(slots), "seq", split_axis=0, concat_axis=0, tiled=True))
    return [slots[0]] + [swap(slots[j], j) for j in (1, 2, 3)]


def gate(values, *before):
    return lax.optimization_barrier((values, *before))[0]


class Order:
    def __init__(self):
        self.pending = []

    def after(self, *values):
        self.pending += values

    def __call__(self, operation, *operands):
        if self.pending:
            count = len(operands)
            operands = lax.optimization_barrier((*operands, *self.pending))[:count]
        made = operation(*operands)
        self.pending = jax.tree.leaves(made)
        return made

    def gather(self, rows):
        if lax.axis_size("seq") != 4:
            return lax.all_gather(jnp.concatenate(rows, axis=0), "seq", axis=0, tiled=True), None
        top, bottom = rows
        return rows, (swap(bottom, 1), swap(top, 2), swap(top, 1), swap(bottom, 2))

    def fill(self, begun):
        rows, came = begun
        if came is None:
            return rows
        first_bottom, second_top, first_top, second_bottom = came
        room = jnp.zeros_like(rows[0])
        parts = (*rows, first_top, first_bottom, second_top, second_bottom, room, room)
        return self(lambda *parts: jnp.concatenate(parts, axis=0), *parts)

    def complete(self, made, pieces):
        if not isinstance(pieces, list):
            return made
        rows = pieces[-1].shape[0]

        def put(before, first, second):
            before = lax.dynamic_update_slice_in_dim(before, first, 6 * rows, axis=0)
            return lax.dynamic_update_slice_in_dim(before, second, 7 * rows, axis=0)

        return self(put, made, *pieces[-2:])

    def pass_on(self, begun, *before):
        rows, came = begun
        if came is None:
            return rows
        first_bottom, second_top, first_top, second_bottom = came
        self.after(*came)
        if before:
            second_top, first_bottom = gate((second_top, first_bottom), *before)
        far = [swap(second_top, 1), swap(first_bottom, 2)]
        return [*rows, first_top, first_bottom, second_top, second_bottom, *far]

    def halves(self, product, rows):
        def cut(values):
            made = product(values)
            half = made.shape[0] // 2
            return made[:half], made[half:]

        return self(cut, rows)

    def add_far(self, made, far, direct, *before, at=None):
        wide = jnp.float32
        half = far[0].shape[0]
        start = made.shape[0] - 4 * half if at is None else at

        def add(made, top, bottom):
            at = start
            first = (made[at + half : at + 2 * half].astype(wide) + bottom.astype(wide)).astype(made.dtype)
            second = (made[at + 2 * half : at + 3 * half].astype(wide) + top.astype(wide)).astype(made.dtype)
            if direct is None:
                first = jnp.concatenate([made[at : at + half], first], axis=0)
                second = jnp.concatenate([second, made[at + 3 * half : at + 4 * half]], axis=0)
            return first, second

        first, second = self(add, made, *far)
        if before:
            first, second = gate((first, second), *before)
        first, second = swap(first, 1), swap(second, 2)
        return (first, second) if direct is None else (direct[0], first, second, direct[1])


def swap_far(halves):
    return swap(halves[0], 1), swap(halves[1], 2)


def swap_direct(made, half):
    at = made.shape[0] - 4 * half
    return swap(made[at : at + half], 1), swap(made[at + 3 * half :], 2)


def summed(own, came):
    wide = jnp.float32
    own = own.astype(wide)
    return sum((part.astype(wide) for part in came), own)


def whole(parts):
    return jnp.concatenate(parts, axis=0) if isinstance(parts, list) else parts


def total_stages():
    stages = []
    for axis in ("fsdp", "seq"):
        count, bit = lax.axis_size(axis), 1
        bits = count.bit_length() - 1
        while bit < count:
            stages.append((axis, [bit] if bits % 2 else [bit, 2 * bit, 3 * bit]))
            bit <<= 1 if bits % 2 else 2
            bits -= bits % 2
    return stages


def local(
    tokens,
    cotangent,
    w_qkv,
    qv_bias,
    w_out,
    out_bias,
    ln1_gain,
    ln1_shift,
    ln2_gain,
    ln2_shift,
    w_up,
    up_bias,
    w_down,
    down_bias,
):
    seq_count, local_len, model_width = tokens.shape
    groups, shards = lax.axis_size("seq"), lax.axis_size("fsdp")
    me = lax.axis_index("seq")
    square = groups == 4
    heads_here = HEADS // groups
    slab = heads_here * HEAD_DIM
    pairs = slab // PAIR
    hidden_width = w_up.shape[1]
    hidden_slab = hidden_width // groups
    rows_here = seq_count * local_len
    low, wide = jnp.bfloat16, jnp.float32
    mask = jnp.reshape(me if square else jnp.zeros_like(me), (1,)).astype(jnp.int32)
    head_index = me * heads_here + jnp.arange(1, heads_here + 1, dtype=jnp.int32)
    slopes = 2.0 ** (-8.0 * head_index.astype(wide) / HEADS)

    def head_columns(values):
        rows = values.shape[0]
        return pl.pallas_call(
            head_columns_kernel,
            grid_spec=pltpu.PrefetchScalarGridSpec(
                num_scalar_prefetch=1,
                grid=(3,),
                in_specs=[pl.BlockSpec((rows, slab), lambda t, at: (0, t * groups + at[0]))],
                out_specs=pl.BlockSpec((rows, 3 * slab), lambda t, at: (0, 0)),
            ),
            out_shape=jax.ShapeDtypeStruct((rows, 3 * slab), values.dtype),
            name="head_columns",
        )(jnp.reshape(me, (1,)).astype(jnp.int32), values)

    def own_slab(values, axis):
        width = values.shape[axis] // groups
        return lax.dynamic_slice_in_dim(values, me * width, width, axis=axis)

    order = Order()
    x_low = tokens.reshape(rows_here, model_width)
    x = x_low.astype(wide)
    dz_low = cotangent.reshape(rows_here, model_width)
    qkv_slab = lax.all_gather(head_columns(w_qkv), "fsdp", axis=0, tiled=True)
    qkv_bias = head_columns(jnp.concatenate([qv_bias[0], jnp.zeros_like(qv_bias[0]), qv_bias[1]])[None])
    up_bias_slab = own_slab(up_bias, 0)

    first_norm, *first_stats = layer_norm(x, ln1_gain, ln1_shift)
    half = rows_here // 2

    def halves_of(values):
        return values[:half].astype(low), values[half:].astype(low)

    normed = order.gather(order(halves_of, first_norm))
    normed = order.pass_on(normed)
    full_out = lax.all_gather(w_out, "fsdp", axis=0, tiled=True)
    up_slab = lax.all_gather(own_slab(gate(w_up, normed[0]) if square else w_up, 1), "fsdp", axis=0, tiled=True)
    down_slab = lax.all_gather(own_slab(gate(w_down, normed[0]) if square else w_down, 0), "fsdp", axis=1, tiled=True)
    normed = whole(normed)
    upstream = order.gather(halves_of(gate(dz_low, normed)))
    qkv = order(lambda rows: (contract(rows, qkv_slab) + qkv_bias).astype(low), normed)
    attended, log_totals = order(lambda rows: attend_forward(mask, slopes, rows, seq_count, local_len), qkv)
    if square:
        attended = gate(attended, *upstream[1])
    mixed_slots = exchange([attended[j * rows_here : (j + 1) * rows_here] for j in range(groups)])
    mixed_rows = jnp.concatenate(by_index(mixed_slots, me), axis=1)
    mixed_slots = jnp.concatenate(mixed_slots, axis=1)

    def pair_swap(values):
        return lax.ppermute(values, "fsdp", [(i, i ^ 1) for i in range(shards)])

    parity = lax.axis_index("fsdp") & 1
    out_rows = model_width // (groups * shards)

    def pair_halves(values):
        halves = values.reshape(rows_here, -1, 2, out_rows)
        return tuple(
            lax.dynamic_index_in_dim(halves, index, axis=2, keepdims=False).reshape(rows_here, -1)
            for index in (parity, 1 - parity)
        )

    middle = order(lambda rows: x + (contract(rows, full_out) + out_bias), mixed_rows)
    second_norm, *second_stats = layer_norm(middle, ln2_gain, ln2_shift)
    second = order.gather(order(halves_of, second_norm))
    mine, theirs = order(pair_halves, mixed_slots)
    upstream_made = order.fill(upstream)
    theirs = pair_swap(theirs)
    dz_sum = order(lambda values: jnp.sum(values.astype(wide), axis=0), dz_low)
    second = whole(order.pass_on(second))
    upstream = order.pass_on(upstream, second)
    active, slope = order(lambda rows: up_and_bend(rows, up_slab, up_bias_slab[None]), second)
    mixed_half = order(lambda *parts: jnp.concatenate(parts, axis=0), mine, theirs)
    upstream = order.complete(upstream_made, upstream)

    def slab_product(left, right, part_of=(0, 1)):
        return order(lambda rows, others: outer(rows, others, groups, shards, part_of), left, right)

    def slab_sum(made):
        return lax.psum_scatter(made, "fsdp", scatter_dimension=0, tiled=True)

    def slabs_of_rows(values):
        return lax.all_to_all(
            values.reshape(groups, -1, values.shape[1]), "seq", split_axis=0, concat_axis=0, tiled=True
        )

    down_sum = slab_sum(slab_product(upstream, active))
    count = rows_here

    def slots(product, start, stop):
        return lambda values: product(values[start * count : stop * count])

    def to_second(rows):
        return contract_last(rows, up_slab).astype(low)

    def to_result(rows):
        return contract(rows, down_slab).astype(low)

    def to_normed(rows):
        return contract_last(rows, qkv_slab).astype(low)

    def scatter(product, rows):
        return lax.psum_scatter(order(product, rows), "seq", scatter_dimension=0, tiled=True)

    hidden_grad, hidden_sum = order(lambda rows: hidden_gradient(rows, down_slab, slope, 0, groups * count), upstream)
    if square:
        far = swap_far(order.halves(slots(to_second, 3, 4), hidden_grad))
        rest = order(slots(to_second, 0, 3), hidden_grad)
        second_own = rest
        direct = swap_direct(rest, half)
        came = order.add_far(rest, far, direct)
        result_far = order.halves(slots(to_result, 3, 4), active)
        up_sum = slab_sum(gate(slab_product(second, hidden_grad), *came))
        result_far = swap_far(gate(result_far, *came))
    else:
        second_own, came = scatter(to_second, hidden_grad), ()
        up_sum = slab_sum(slab_product(second, hidden_grad))
    branch_grad, middle_grad, middle_sums = order(
        lambda own, *came: norm_back(own, middle, *second_stats, dz_low, ln2_gain, came), second_own, *came
    )

    def column_sum(values):
        return jnp.sum(values.astype(wide), axis=0)

    hidden_sum = lax.dynamic_update_slice_in_dim(
        jnp.zeros((hidden_width,), wide), hidden_sum[0], me * hidden_slab, axis=0
    )
    early = [middle_sums[2], middle_sums[0], middle_sums[1], hidden_sum, dz_sum]
    mixed_grad = order(lambda rows: mixed_gradient(rows, full_out, slab), branch_grad)
    mixed_grad = exchange(by_index([mixed_grad[:, j * slab : (j + 1) * slab] for j in range(groups)], me))
    if square:
        result_rest = order(lambda rows: product_of(rows, down_slab, 3 * count), active)
        order.after(*mixed_grad)
        result_came = order.add_far(result_rest, result_far, None)
    attention = (mask, slopes, qkv, log_totals, attended)
    order.after(down_sum)
    begun = order(
        lambda *grads: attend_backward(*attention, grads, seq_count, local_len, 0, pairs // 2), *mixed_grad
    )
    branch_other = pair_swap(branch_grad)
    branch_pair = jnp.concatenate([branch_grad, branch_other], axis=0)
    out_sum = order(lambda columns: outer(columns, branch_pair, groups, 1), mixed_half)
    if square:
        part = out_sum.shape[0] // 4
        out_far = out_sum[3 * part : 3 * part + part // 2], out_sum[3 * part + part // 2 :]
        out_far = swap_far(out_far)
    first_sum = slab_product(normed, begun, (0, 2))
    if square:
        first_sum = gate(first_sum, *result_came)
        order.after(*result_came)
    first_sum = slab_sum(first_sum)
    qkv_grad = order(
        lambda begun, *grads: attend_backward(
            *attention, grads, seq_count, local_len, pairs // 2, pairs, begun
        ),
        begun,
        *mixed_grad,
    )
    if square:
        out_came = order.add_far(out_sum, out_far, None, at=part)
    else:
        out_sum = lax.psum_scatter(out_sum, "seq", scatter_dimension=0, tiled=True)
    order.after(up_sum)
    if square:
        far = swap_far(order.halves(slots(to_normed, 3, 4), qkv_grad))
        order.after(first_sum)
        near = order(slots(to_normed, 1, 3), qkv_grad)
        direct = swap_direct(near, half)
        order.after(*out_came)
        out_sum = order(lambda own, *came: summed(own[:part], came).astype(low), out_sum, *out_came)
    out_sum = out_sum.reshape(-1, 1, out_rows, model_width)
    zero = jnp.zeros_like(out_sum)
    out_sum = jnp.concatenate(
        [jnp.where(parity == 0, out_sum, zero), jnp.where(parity == 1, out_sum, zero)], axis=1
    ).reshape(-1, model_width)
    if square:
        out_sum = gate(out_sum, *far)
    grad_w_out = lax.psum_scatter(out_sum, "fsdp", scatter_dimension=0, tiled=True).astype(wide)
    second_sum = slab_product(normed, qkv_grad, (1, 2))
    if square:
        second_sum = slab_sum(gate(second_sum, *far, *direct))
        came = order.add_far(near, far, direct)
        order.after(grad_w_out)
        normed_own = order(slots(to_normed, 0, 1), qkv_grad)
    else:
        second_sum = slab_sum(second_sum)
        normed_own, came = scatter(to_normed, qkv_grad), ()
    if square:
        result = order(
            lambda rest, *came: (middle + (summed(rest[:count], came) + down_bias)).astype(low),
            result_rest,
            *result_came,
        )
    else:
        result = (middle + (scatter(to_result, active).astype(wide) + down_bias)).astype(low)
    result = result.reshape(tokens.shape)
    qkv_column_sum = order(column_sum, qkv_grad)
    grad_tokens, _, input_sums = order(
        lambda own, *came: norm_back(own, x_low, *first_stats, middle_grad, ln1_gain, came), normed_own, *came
    )
    grad_tokens = grad_tokens.reshape(tokens.shape)
    three = jnp.concatenate([down_sum, up_sum, first_sum], axis=1)
    three = slabs_of_rows(gate(three, *came, normed_own))
    down_slabs, up_slabs, first_slabs = jnp.split(three, [hidden_slab, 2 * hidden_slab], axis=2)
    second_slabs = slabs_of_rows(second_sum)

    def rows_of(slabs):
        return jnp.swapaxes(slabs, 0, 1).astype(wide)

    grad_w_down = rows_of(down_slabs).reshape(-1, hidden_width).T
    grad_w_up = rows_of(up_slabs).reshape(-1, hidden_width)
    grad_w_qkv = [
        rows_of(part).reshape(-1, groups, pairs // 2, 3, PAIR) for part in (first_slabs, second_slabs)
    ]
    grad_w_qkv = jnp.concatenate(grad_w_qkv, axis=2)
    grad_w_qkv = jnp.transpose(grad_w_qkv, (0, 3, 1, 2, 4)).reshape(-1, 3 * model_width)

    head_sum = jnp.transpose(qkv_column_sum.reshape(pairs, 3, PAIR), (1, 0, 2)).reshape(3, slab)
    qv_sum = lax.dynamic_update_slice_in_dim(
        jnp.zeros((2, model_width), wide), head_sum[0::2], me * slab, axis=1
    )
    late = [qv_sum.reshape(-1), input_sums[0], input_sums[1]]
    sums = order(lambda *parts: jnp.concatenate(parts).reshape(-1, PAIR), *early, *late)
    stages = total_stages()
    for axis, masks in stages:
        others = range(lax.axis_size(axis))
        came = [lax.ppermute(sums, axis, [(i, i ^ mask) for i in others]) for mask in masks]
        if (axis, masks) == stages[-1]:
            order.after(three, second_slabs)
        sums = order(lambda *parts: sum(parts[1:], parts[0]), sums, *came)
    sums = sums.reshape(-1)

    def cut(at, count):
        return sums[at * model_width : (at + count) * model_width]

    ratio = hidden_width // model_width
    return (
        result,
        grad_tokens,
        grad_w_qkv,
        cut(4 + ratio, 2).reshape(2, model_width),
        grad_w_out,
        cut(0, 1),
        cut(6 + ratio, 1),
        cut(7 + ratio, 1),
        cut(1, 1),
        cut(2, 1),
        grad_w_up,
        cut(3, ratio),
        grad_w_down,
        cut(3 + ratio, 1),
    )


def solution(mesh):
    return jax.shard_map(
        local,
        mesh=mesh,
        in_specs=(
            P("fsdp", "seq", None),
            P("fsdp", "seq", None),
            P("fsdp", None),
            P(),
            P("fsdp", None),
            P(),
            P(),
            P(),
            P(),
            P(),
            P("fsdp", None),
            P(),
            P(None, "fsdp"),
            P(),
        ),
        out_specs=(
            P("fsdp", "seq", None),
            P("fsdp", "seq", None),
            P(("seq", "fsdp"), None),
            P(),
            P(("seq", "fsdp"), None),
            P(),
            P(),
            P(),
            P(),
            P(),
            P(("seq", "fsdp"), None),
            P(),
            P(None, ("seq", "fsdp")),
            P(),
        ),
        check_vma=False,
    )
```

```python
import math
from functools import partial

import jax
import jax.numpy as jnp
from jax import lax
from jax.experimental import pallas as pl
from jax.experimental.pallas import tpu as pltpu
from jax.sharding import PartitionSpec as P

HEADS = 32
HEAD_DIM = 64
BLOCK = 256
PAIR = 2 * HEAD_DIM
GRANT = 58 * 2**20


def estimate(flops, transcendentals=0):
    return pl.CostEstimate(flops=flops // 4, bytes_accessed=flops // 4096, transcendentals=transcendentals // 4)


def layer_norm(token_rows, gain_vec, shift_vec):
    average = jnp.mean(token_rows, axis=-1, keepdims=True)
    centred = token_rows - average
    spread = jnp.mean(centred * centred, axis=-1, keepdims=True)
    scale = lax.rsqrt(spread + 1e-05)
    return centred * scale * gain_vec + shift_vec, average, scale


def contract(left_side, right_side):
    return lax.dot_general(
        left_side, right_side, (((1,), (0,)), ((), ())), preferred_element_type=jnp.float32
    )


def contract_last(left_side, right_side):
    return lax.dot_general(
        left_side, right_side, (((1,), (1,)), ((), ())), preferred_element_type=jnp.float32
    )


def contract_first(left_side, right_side):
    return lax.dot_general(
        left_side, right_side, (((0,), (0,)), ((), ())), preferred_element_type=jnp.float32
    )


def row_pieces(mask, sequence, block, seqs, local):
    per = BLOCK // local
    return [
        pl.ds(pl.multiple_of((((block * per + r) ^ mask) * seqs + sequence) * local, local), local)
        for r in range(per)
    ]


def load_rows(ref, pieces, columns):
    parts = [ref[piece, columns] for piece in pieces]
    return parts[0] if len(parts) == 1 else jnp.concatenate(parts, axis=0)


def store_rows(ref, pieces, columns, values):
    local = values.shape[0] // len(pieces)
    for r, piece in enumerate(pieces):
        ref[piece, columns] = values[r * local : (r + 1) * local]


Q_COLUMNS, K_COLUMNS, V_COLUMNS = (slice(t * PAIR, (t + 1) * PAIR) for t in range(3))


def attend_forward_kernel(mask_ref, slope_ref, qkv_ref, mixed_ref, lse_ref, *, blocks, seqs, local):
    pair, sequence = pl.program_id(0), pl.program_id(1)
    mask = mask_ref[0]
    lane = lax.broadcasted_iota(jnp.int32, (BLOCK, PAIR), 1)
    row = lax.broadcasted_iota(jnp.int32, (BLOCK, BLOCK), 0)
    column = lax.broadcasted_iota(jnp.int32, (BLOCK, BLOCK), 1)
    gap = (row - column).astype(jnp.float32)
    pieces = [row_pieces(mask, sequence, block, seqs, local) for block in range(blocks)]

    for i in range(blocks):
        q_pair = load_rows(qkv_ref, pieces[i], Q_COLUMNS)
        outs, lses = [], []
        for head in range(2):
            slope = slope_ref[pair * 2 + head]
            mine = (lane >= head * HEAD_DIM) & (lane < (head + 1) * HEAD_DIM)
            q = jnp.where(mine, q_pair, jnp.zeros_like(q_pair)) * jnp.bfloat16(HEAD_DIM**-0.5)
            parts, highest = [], None
            for j in range(i + 1):
                scores = contract_last(q, load_rows(qkv_ref, pieces[j], K_COLUMNS))
                distance = jnp.abs(gap) if i == j else gap + float(BLOCK * (i - j))
                scores = scores - slope * distance
                parts.append(scores)
                top = jnp.max(scores, axis=-1, keepdims=True)
                highest = top if highest is None else jnp.maximum(highest, top)
            total, out = None, None
            for j in range(i + 1):
                weights = jnp.exp(parts[j] - highest)
                part = jnp.sum(weights, axis=-1, keepdims=True)
                mixed = contract(weights.astype(jnp.bfloat16), load_rows(qkv_ref, pieces[j], V_COLUMNS))
                total = part if total is None else total + part
                out = mixed if out is None else out + mixed
            outs.append(out / total)
            lses.append(highest + jnp.log(total))
        first = lane < HEAD_DIM
        everything = slice(0, PAIR)
        store_rows(
            mixed_ref, pieces[i], everything, jnp.where(first, outs[0], outs[1]).astype(mixed_ref.dtype)
        )
        store_rows(lse_ref, pieces[i], everything, jnp.where(first, lses[0], lses[1]))


def attend_backward_kernel(
    mask_ref, slope_ref, qkv_ref, lse_ref, mixed_ref, *rest, blocks, seqs, local, start, grads
):
    out_ref, dq_ref, dk_ref, dv_ref, grad_ref = rest[-5:]
    pair, sequence = pl.program_id(0) + start, pl.program_id(1)
    mask = mask_ref[0]
    lane = lax.broadcasted_iota(jnp.int32, (BLOCK, PAIR), 1)
    key = lax.broadcasted_iota(jnp.int32, (BLOCK, BLOCK), 0)
    query = lax.broadcasted_iota(jnp.int32, (BLOCK, BLOCK), 1)
    gap = (query - key).astype(jnp.float32)
    pieces = [row_pieces(mask, sequence, block, seqs, local) for block in range(blocks)]
    everything = slice(0, PAIR)

    @pl.when(sequence == 0)
    def _():
        at = 0
        for part in rest[:grads]:
            grad_ref[at : at + part.shape[0], :] = part[...]
            at += part.shape[0]

    for i in range(blocks):
        q_pair = load_rows(qkv_ref, pieces[i], Q_COLUMNS)
        up_pair = load_rows(grad_ref, pieces[i], everything)
        mixed_pair = load_rows(mixed_ref, pieces[i], everything)
        inner_all = (up_pair.astype(jnp.float32) * mixed_pair.astype(jnp.float32)).T
        lse_all = load_rows(lse_ref, pieces[i], everything).T
        dq = None
        for head in range(2):
            slope = slope_ref[pair * 2 + head]
            mine = (lane >= head * HEAD_DIM) & (lane < (head + 1) * HEAD_DIM)
            zero = jnp.zeros_like(q_pair)
            q = jnp.where(mine, q_pair, zero) * jnp.bfloat16(HEAD_DIM**-0.5)
            up = jnp.where(mine, up_pair, zero)
            inner = jnp.sum(inner_all[head * HEAD_DIM : (head + 1) * HEAD_DIM], axis=0, keepdims=True)
            lse = lse_all[head * HEAD_DIM : head * HEAD_DIM + 1]
            for j in range(i + 1):
                k_pair = load_rows(qkv_ref, pieces[j], K_COLUMNS)
                distance = jnp.abs(gap) if i == j else gap + float(BLOCK * (i - j))
                probs = jnp.exp(contract_last(k_pair, q) - slope * distance - lse)
                prob_grad = contract_last(load_rows(qkv_ref, pieces[j], V_COLUMNS), up)
                score_grad = (probs * (prob_grad - inner)).astype(jnp.bfloat16)
                dv = contract(probs.astype(jnp.bfloat16), up)
                dk = contract(score_grad, q)
                part = contract_first(score_grad, jnp.where(mine, k_pair, zero))
                dq = part if dq is None else dq + part
                if i == j and head == 0:
                    dv_ref[j] = dv
                    dk_ref[j] = dk
                else:
                    dv_ref[j] += dv
                    dk_ref[j] += dk
        dq_ref[i] = dq
    for i in range(blocks):
        store_rows(out_ref, pieces[i], Q_COLUMNS, (dq_ref[i] * HEAD_DIM**-0.5).astype(out_ref.dtype))
        store_rows(out_ref, pieces[i], K_COLUMNS, dk_ref[i].astype(out_ref.dtype))
        store_rows(out_ref, pieces[i], V_COLUMNS, dv_ref[i].astype(out_ref.dtype))


def attend_forward(mask, slopes, qkv, seqs, local):
    rows, width = qkv.shape
    pairs, blocks = width // (3 * PAIR), rows // seqs // BLOCK
    scored = pairs * seqs * blocks * (blocks + 1) * BLOCK * BLOCK
    return pl.pallas_call(
        partial(attend_forward_kernel, blocks=blocks, seqs=seqs, local=local),
        grid_spec=pltpu.PrefetchScalarGridSpec(
            num_scalar_prefetch=2,
            grid=(pairs, seqs),
            in_specs=[pl.BlockSpec((rows, 3 * PAIR), lambda p, *_: (0, p))],
            out_specs=[pl.BlockSpec((rows, PAIR), lambda p, *_: (0, p))] * 2,
        ),
        out_shape=[
            jax.ShapeDtypeStruct((rows, pairs * PAIR), jnp.bfloat16),
            jax.ShapeDtypeStruct((rows, pairs * PAIR), jnp.float32),
        ],
        compiler_params=pltpu.CompilerParams(vmem_limit_bytes=GRANT),
        cost_estimate=estimate(scored * 2 * 512, scored),
        name="attend_forward",
    )(mask, slopes, qkv)


def attend_backward(mask, slopes, qkv, lse, mixed, grads, seqs, local, start, stop, begun=None):
    rows, width = qkv.shape
    blocks = rows // seqs // BLOCK
    scored = (stop - start) * seqs * blocks * (blocks + 1) * BLOCK * BLOCK
    narrow = pl.BlockSpec((rows, PAIR), lambda p, *_: (0, p + start))
    wide = pl.BlockSpec((rows, 3 * PAIR), lambda p, *_: (0, p + start))
    earlier = [] if begun is None else [begun]
    return pl.pallas_call(
        partial(
            attend_backward_kernel, blocks=blocks, seqs=seqs, local=local, start=start, grads=len(grads)
        ),
        grid_spec=pltpu.PrefetchScalarGridSpec(
            num_scalar_prefetch=2,
            grid=(stop - start, seqs),
            in_specs=[wide, narrow, narrow]
            + [pl.BlockSpec((grad.shape[0], PAIR), lambda p, *_: (0, p + start)) for grad in grads]
            + [pl.BlockSpec(memory_space=pl.ANY)] * len(earlier),
            out_specs=wide,
            scratch_shapes=[pltpu.VMEM((blocks, BLOCK, PAIR), jnp.float32)] * 3
            + [pltpu.VMEM((rows, PAIR), jnp.bfloat16)],
        ),
        out_shape=jax.ShapeDtypeStruct((rows, width), jnp.bfloat16),
        input_output_aliases={5 + len(grads): 0} if earlier else {},
        compiler_params=pltpu.CompilerParams(vmem_limit_bytes=GRANT),
        cost_estimate=estimate(scored * 2 * 1280, scored),
        name="attend_backward",
    )(mask, slopes, qkv, lse, mixed, *grads, *earlier)


def head_columns_kernel(at_ref, in_ref, out_ref):
    for t in range(3):

        @pl.when(pl.program_id(0) == t)
        def _():
            for pair in range(in_ref.shape[1] // PAIR):
                at = (pair * 3 + t) * PAIR
                out_ref[:, at : at + PAIR] = in_ref[:, pair * PAIR : (pair + 1) * PAIR]


def up_kernel(rows_ref, weight_ref, bias_ref, active_ref, slope_ref, *, chunk):
    rows = rows_ref[...]
    for at in range(0, weight_ref.shape[1], chunk):
        columns = slice(at, at + chunk)
        hidden = contract(rows, weight_ref[:, columns]) + bias_ref[:, columns]
        below = 0.5 + 0.5 * lax.erf(hidden * 2**-0.5)
        active_ref[:, columns] = (hidden * below).astype(active_ref.dtype)
        slope_ref[:, columns] = below + hidden * ((2 * math.pi) ** -0.5 * jnp.exp(-0.5 * hidden * hidden))


def hidden_grad_kernel(rows_ref, weight_ref, slope_ref, grad_ref, sum_ref, *, chunk):
    rows = rows_ref[...]
    starting = pl.program_id(0) == 0
    for at in range(0, weight_ref.shape[0], chunk):
        columns = slice(at, at + chunk)
        grad = contract_last(rows, weight_ref[columns, :]) * slope_ref[:, columns]
        grad = grad.astype(grad_ref.dtype)
        grad_ref[:, columns] = grad
        part = jnp.sum(grad.astype(jnp.float32), axis=0, keepdims=True)
        sum_ref[:, columns] = jnp.where(starting, part, sum_ref[:, columns] + part)


TILE = 256


def up_and_bend(rows, weight, bias):
    count, depth = rows.shape
    width = weight.shape[1]
    tile = pl.BlockSpec((TILE, width), lambda i: (i, 0))
    return pl.pallas_call(
        partial(up_kernel, chunk=512),
        grid=(count // TILE,),
        in_specs=[
            pl.BlockSpec((TILE, depth), lambda i: (i, 0)),
            pl.BlockSpec((depth, width), lambda i: (0, 0), pipeline_mode=pl.Buffered(1)),
            pl.BlockSpec((1, width), lambda i: (0, 0)),
        ],
        out_specs=[tile, tile],
        out_shape=[
            jax.ShapeDtypeStruct((count, width), jnp.bfloat16),
            jax.ShapeDtypeStruct((count, width), jnp.float32),
        ],
        compiler_params=pltpu.CompilerParams(vmem_limit_bytes=GRANT),
        cost_estimate=estimate(count * depth * width * 4, 2 * count * width),
        name="up_and_bend",
    )(rows, weight, bias)


def hidden_gradient(rows, weight, slope, start, count):
    depth = rows.shape[1]
    width = weight.shape[0]
    first = start // TILE
    line = pl.BlockSpec((1, width), lambda i: (0, 0))
    return pl.pallas_call(
        partial(hidden_grad_kernel, chunk=512),
        grid=(count // TILE,),
        in_specs=[
            pl.BlockSpec((TILE, depth), lambda i: (i + first, 0)),
            pl.BlockSpec((width, depth), lambda i: (0, 0), pipeline_mode=pl.Buffered(1)),
            pl.BlockSpec((TILE, width), lambda i: (i + first, 0)),
        ],
        out_specs=[pl.BlockSpec((TILE, width), lambda i: (i, 0)), line],
        out_shape=[
            jax.ShapeDtypeStruct((count, width), jnp.bfloat16),
            jax.ShapeDtypeStruct((1, width), jnp.float32),
        ],
        compiler_params=pltpu.CompilerParams(vmem_limit_bytes=GRANT),
        cost_estimate=estimate(count * depth * width * 3, 0),
        name="hidden_gradient",
    )(rows, weight, slope)


def product_kernel(rows_ref, weight_ref, out_ref):
    out_ref[...] = contract(rows_ref[...], weight_ref[...]).astype(out_ref.dtype)


def product_of(rows, weight, count):
    depth, width = weight.shape
    return pl.pallas_call(
        product_kernel,
        grid=(count // TILE,),
        in_specs=[
            pl.BlockSpec((TILE, depth), lambda i: (i, 0)),
            pl.BlockSpec((depth, width), lambda i: (0, 0), pipeline_mode=pl.Buffered(1)),
        ],
        out_specs=pl.BlockSpec((TILE, width), lambda i: (i, 0)),
        out_shape=jax.ShapeDtypeStruct((count, width), jnp.bfloat16),
        compiler_params=pltpu.CompilerParams(vmem_limit_bytes=GRANT),
        cost_estimate=estimate(2 * count * depth * width, 0),
        name="product",
    )(rows, weight)


def mixed_grad_kernel(rows_ref, weight_ref, out_ref):
    out_ref[...] = contract_last(rows_ref[...], weight_ref[...]).astype(out_ref.dtype)


def mixed_gradient(rows, weight, slab):
    count, depth = rows.shape
    width = weight.shape[0]
    return pl.pallas_call(
        mixed_grad_kernel,
        grid=(width // slab,),
        in_specs=[
            pl.BlockSpec((count, depth), lambda i: (0, 0), pipeline_mode=pl.Buffered(1)),
            pl.BlockSpec((slab, depth), lambda i: (i, 0)),
        ],
        out_specs=pl.BlockSpec((count, slab), lambda i: (0, i)),
        out_shape=jax.ShapeDtypeStruct((count, width), jnp.bfloat16),
        compiler_params=pltpu.CompilerParams(vmem_limit_bytes=GRANT),
        cost_estimate=estimate(2 * count * depth * width, 0),
        name="mixed_gradient",
    )(rows, weight)


def norm_back_kernel(own_ref, values_ref, average_ref, scale_ref, base_ref, gain_ref, *refs, parts):
    came, (low_ref, wide_ref, sums_ref) = refs[:parts], refs[parts:]
    wide = jnp.float32
    step = pl.program_id(0)

    @pl.when(step == 0)
    def _():
        sums_ref[...] = jnp.zeros_like(sums_ref)

    def make(came):
        grad = own_ref[...].astype(wide)
        for part in came:
            grad = grad + part[...].astype(wide)
        scale = scale_ref[...]
        normal = (values_ref[...].astype(wide) - average_ref[...]) * scale
        gained = grad * gain_ref[...]
        along = jnp.mean(gained * normal, axis=-1, keepdims=True)
        across = jnp.mean(gained, axis=-1, keepdims=True)
        made = base_ref[...].astype(wide) + scale * (gained - across - normal * along)
        low = made.astype(low_ref.dtype)
        low_ref[...] = low
        wide_ref[...] = made
        for at, part in enumerate((grad * normal, grad, low.astype(wide))):
            sums_ref[8 * at : 8 * at + 8, :] += jnp.sum(part.reshape(-1, 8, part.shape[1]), axis=0)

    if not came:
        make(())
        return
    upper = step < pl.num_programs(0) // 2
    pl.when(upper)(lambda: make(came[0::2]))
    pl.when(jnp.logical_not(upper))(lambda: make(came[1::2]))


def norm_back(rest, values, average, scale, base, gain, came):
    rows, width = values.shape
    steps = 8
    half = steps // 2
    came = list(came or ())
    count = rows // steps
    tile = pl.BlockSpec((count, width), lambda i: (i, 0))
    thin = pl.BlockSpec((count, 1), lambda i: (i, 0))
    top = pl.BlockSpec((count, width), lambda i: (jnp.minimum(i, half - 1), 0))
    bottom = pl.BlockSpec((count, width), lambda i: (jnp.maximum(i - half, 0), 0))
    low, full, sums = pl.pallas_call(
        partial(norm_back_kernel, parts=len(came)),
        grid=(steps,),
        in_specs=[tile, tile, thin, thin, tile, pl.BlockSpec((1, width), lambda i: (0, 0))]
        + [top, bottom] * (len(came) // 2),
        out_specs=[tile, tile, pl.BlockSpec((24, width), lambda i: (0, 0))],
        out_shape=[
            jax.ShapeDtypeStruct((rows, width), jnp.bfloat16),
            jax.ShapeDtypeStruct((rows, width), jnp.float32),
            jax.ShapeDtypeStruct((24, width), jnp.float32),
        ],
        compiler_params=pltpu.CompilerParams(vmem_limit_bytes=GRANT),
        cost_estimate=estimate(30 * rows * width, rows),
        name="norm_back",
    )(rest, values, average, scale, base, gain[None], *came)
    return low, full, jnp.sum(sums.reshape(3, 8, width), axis=1)


def outer_kernel(left_ref, right_ref, out_ref, *, chunk):
    left = left_ref[...]
    shards = out_ref.shape[0]
    for at in range(0, out_ref.shape[3], chunk):
        columns = slice(at, at + chunk)
        made = contract_first(left, right_ref[:, columns]).astype(out_ref.dtype)
        out_ref[:, 0, :, columns] = made.reshape(shards, -1, made.shape[1])


def outer(left, right, groups, shards, part_of=(0, 1)):
    at, parts = part_of
    tokens, rows = left.shape
    width = right.shape[1] // parts
    part = rows // groups
    made = pl.pallas_call(
        partial(outer_kernel, chunk=next(c for c in (512, 384, 256, 128) if width % c == 0)),
        grid=(groups,),
        in_specs=[
            pl.BlockSpec((tokens, part), lambda i: (0, i)),
            pl.BlockSpec((tokens, width), lambda i: (0, at), pipeline_mode=pl.Buffered(1)),
        ],
        out_specs=pl.BlockSpec((shards, 1, part // shards, width), lambda i: (0, i, 0, 0)),
        out_shape=jax.ShapeDtypeStruct((shards, groups, part // shards, width), jnp.bfloat16),
        compiler_params=pltpu.CompilerParams(vmem_limit_bytes=GRANT),
        cost_estimate=estimate(2 * tokens * rows * width, 0),
        name="outer",
    )(left, right)
    return made.reshape(rows, width)


def swap(values, bit):
    return lax.ppermute(values, "seq", [(i, i ^ bit) for i in range(4)])


def by_index(parts, me):
    if len(parts) != 4:
        return parts
    odd, upper = (me & 1) == 1, (me & 2) == 2
    a, b, c, d = parts
    a, b, c, d = (
        jnp.where(odd, b, a),
        jnp.where(odd, a, b),
        jnp.where(odd, d, c),
        jnp.where(odd, c, d),
    )
    return [jnp.where(upper, c, a), jnp.where(upper, d, b), jnp.where(upper, a, c), jnp.where(upper, b, d)]


def exchange(slots):
    if lax.axis_size("seq") != 4:
        return list(lax.all_to_all(jnp.stack(slots), "seq", split_axis=0, concat_axis=0, tiled=True))
    return [slots[0]] + [swap(slots[j], j) for j in (1, 2, 3)]


def gate(values, *before):
    return lax.optimization_barrier((values, *before))[0]


class Order:
    def __init__(self):
        self.pending = []

    def after(self, *values):
        self.pending += values

    def __call__(self, operation, *operands):
        if self.pending:
            count = len(operands)
            operands = lax.optimization_barrier((*operands, *self.pending))[:count]
        made = operation(*operands)
        self.pending = jax.tree.leaves(made)
        return made

    def gather(self, rows):
        if lax.axis_size("seq") != 4:
            return lax.all_gather(jnp.concatenate(rows, axis=0), "seq", axis=0, tiled=True), None
        top, bottom = rows
        return rows, (swap(bottom, 1), swap(top, 2), swap(top, 1), swap(bottom, 2))

    def fill(self, begun):
        rows, came = begun
        if came is None:
            return rows
        first_bottom, second_top, first_top, second_bottom = came
        room = jnp.zeros_like(rows[0])
        parts = (*rows, first_top, first_bottom, second_top, second_bottom, room, room)
        return self(lambda *parts: jnp.concatenate(parts, axis=0), *parts)

    def complete(self, made, pieces):
        if not isinstance(pieces, list):
            return made
        rows = pieces[-1].shape[0]

        def put(before, first, second):
            before = lax.dynamic_update_slice_in_dim(before, first, 6 * rows, axis=0)
            return lax.dynamic_update_slice_in_dim(before, second, 7 * rows, axis=0)

        return self(put, made, *pieces[-2:])

    def pass_on(self, begun, *before):
        rows, came = begun
        if came is None:
            return rows
        first_bottom, second_top, first_top, second_bottom = came
        self.after(*came)
        if before:
            second_top, first_bottom = gate((second_top, first_bottom), *before)
        far = [swap(second_top, 1), swap(first_bottom, 2)]
        return [*rows, first_top, first_bottom, second_top, second_bottom, *far]

    def halves(self, product, rows):
        def cut(values):
            made = product(values)
            half = made.shape[0] // 2
            return made[:half], made[half:]

        return self(cut, rows)

    def add_far(self, made, far, direct, *before, at=None):
        wide = jnp.float32
        half = far[0].shape[0]
        start = made.shape[0] - 4 * half if at is None else at

        def add(made, top, bottom):
            at = start
            first = (made[at + half : at + 2 * half].astype(wide) + bottom.astype(wide)).astype(made.dtype)
            second = (made[at + 2 * half : at + 3 * half].astype(wide) + top.astype(wide)).astype(made.dtype)
            if direct is None:
                first = jnp.concatenate([made[at : at + half], first], axis=0)
                second = jnp.concatenate([second, made[at + 3 * half : at + 4 * half]], axis=0)
            return first, second

        first, second = self(add, made, *far)
        if before:
            first, second = gate((first, second), *before)
        first, second = swap(first, 1), swap(second, 2)
        return (first, second) if direct is None else (direct[0], first, second, direct[1])


def swap_far(halves):
    return swap(halves[0], 1), swap(halves[1], 2)


def swap_direct(made, half):
    at = made.shape[0] - 4 * half
    return swap(made[at : at + half], 1), swap(made[at + 3 * half :], 2)


def summed(own, came):
    wide = jnp.float32
    own = own.astype(wide)
    return sum((part.astype(wide) for part in came), own)


def whole(parts):
    return jnp.concatenate(parts, axis=0) if isinstance(parts, list) else parts


def total_stages():
    stages = []
    for axis in ("fsdp", "seq"):
        count, bit = lax.axis_size(axis), 1
        bits = count.bit_length() - 1
        while bit < count:
            stages.append((axis, [bit] if bits % 2 else [bit, 2 * bit, 3 * bit]))
            bit <<= 1 if bits % 2 else 2
            bits -= bits % 2
    return stages


def local(
    tokens,
    cotangent,
    w_qkv,
    qv_bias,
    w_out,
    out_bias,
    ln1_gain,
    ln1_shift,
    ln2_gain,
    ln2_shift,
    w_up,
    up_bias,
    w_down,
    down_bias,
):
    seq_count, local_len, model_width = tokens.shape
    groups, shards = lax.axis_size("seq"), lax.axis_size("fsdp")
    me = lax.axis_index("seq")
    square = groups == 4
    heads_here = HEADS // groups
    slab = heads_here * HEAD_DIM
    pairs = slab // PAIR
    hidden_width = w_up.shape[1]
    hidden_slab = hidden_width // groups
    rows_here = seq_count * local_len
    low, wide = jnp.bfloat16, jnp.float32
    mask = jnp.reshape(me if square else jnp.zeros_like(me), (1,)).astype(jnp.int32)
    head_index = me * heads_here + jnp.arange(1, heads_here + 1, dtype=jnp.int32)
    slopes = 2.0 ** (-8.0 * head_index.astype(wide) / HEADS)

    def head_columns(values):
        rows = values.shape[0]
        return pl.pallas_call(
            head_columns_kernel,
            grid_spec=pltpu.PrefetchScalarGridSpec(
                num_scalar_prefetch=1,
                grid=(3,),
                in_specs=[pl.BlockSpec((rows, slab), lambda t, at: (0, t * groups + at[0]))],
                out_specs=pl.BlockSpec((rows, 3 * slab), lambda t, at: (0, 0)),
            ),
            out_shape=jax.ShapeDtypeStruct((rows, 3 * slab), values.dtype),
            name="head_columns",
        )(jnp.reshape(me, (1,)).astype(jnp.int32), values)

    def own_slab(values, axis):
        width = values.shape[axis] // groups
        return lax.dynamic_slice_in_dim(values, me * width, width, axis=axis)

    order = Order()
    x_low = tokens.reshape(rows_here, model_width)
    x = x_low.astype(wide)
    dz_low = cotangent.reshape(rows_here, model_width)
    qkv_slab = lax.all_gather(head_columns(w_qkv), "fsdp", axis=0, tiled=True)
    qkv_bias = head_columns(jnp.concatenate([qv_bias[0], jnp.zeros_like(qv_bias[0]), qv_bias[1]])[None])
    up_bias_slab = own_slab(up_bias, 0)

    first_norm, *first_stats = layer_norm(x, ln1_gain, ln1_shift)
    half = rows_here // 2

    def halves_of(values):
        return values[:half].astype(low), values[half:].astype(low)

    normed = order.gather(order(halves_of, first_norm))
    normed = order.pass_on(normed)
    full_out = lax.all_gather(w_out, "fsdp", axis=0, tiled=True)
    up_slab = lax.all_gather(own_slab(gate(w_up, normed[0]) if square else w_up, 1), "fsdp", axis=0, tiled=True)
    down_slab = lax.all_gather(own_slab(gate(w_down, normed[0]) if square else w_down, 0), "fsdp", axis=1, tiled=True)
    normed = whole(normed)
    upstream = order.gather(halves_of(gate(dz_low, normed)))
    qkv = order(lambda rows: (contract(rows, qkv_slab) + qkv_bias).astype(low), normed)
    attended, log_totals = order(lambda rows: attend_forward(mask, slopes, rows, seq_count, local_len), qkv)
    if square:
        attended = gate(attended, *upstream[1])
    mixed_slots = exchange([attended[j * rows_here : (j + 1) * rows_here] for j in range(groups)])
    mixed_rows = jnp.concatenate(by_index(mixed_slots, me), axis=1)
    mixed_slots = jnp.concatenate(mixed_slots, axis=1)

    def pair_swap(values):
        return lax.ppermute(values, "fsdp", [(i, i ^ 1) for i in range(shards)])

    parity = lax.axis_index("fsdp") & 1
    out_rows = model_width // (groups * shards)

    def pair_halves(values):
        halves = values.reshape(rows_here, -1, 2, out_rows)
        return tuple(
            lax.dynamic_index_in_dim(halves, index, axis=2, keepdims=False).reshape(rows_here, -1)
            for index in (parity, 1 - parity)
        )

    middle = order(lambda rows: x + (contract(rows, full_out) + out_bias), mixed_rows)
    second_norm, *second_stats = layer_norm(middle, ln2_gain, ln2_shift)
    second = order.gather(order(halves_of, second_norm))
    mine, theirs = order(pair_halves, mixed_slots)
    upstream_made = order.fill(upstream)
    theirs = pair_swap(theirs)
    dz_sum = order(lambda values: jnp.sum(values.astype(wide), axis=0), dz_low)
    second = whole(order.pass_on(second))
    upstream = order.pass_on(upstream, second)
    active, slope = order(lambda rows: up_and_bend(rows, up_slab, up_bias_slab[None]), second)
    mixed_half = order(lambda *parts: jnp.concatenate(parts, axis=0), mine, theirs)
    upstream = order.complete(upstream_made, upstream)

    def slab_product(left, right, part_of=(0, 1)):
        return order(lambda rows, others: outer(rows, others, groups, shards, part_of), left, right)

    def slab_sum(made):
        return lax.psum_scatter(made, "fsdp", scatter_dimension=0, tiled=True)

    def slabs_of_rows(values):
        return lax.all_to_all(
            values.reshape(groups, -1, values.shape[1]), "seq", split_axis=0, concat_axis=0, tiled=True
        )

    down_sum = slab_sum(slab_product(upstream, active))
    count = rows_here

    def slots(product, start, stop):
        return lambda values: product(values[start * count : stop * count])

    def to_second(rows):
        return contract_last(rows, up_slab).astype(low)

    def to_result(rows):
        return contract(rows, down_slab).astype(low)

    def to_normed(rows):
        return contract_last(rows, qkv_slab).astype(low)

    def scatter(product, rows):
        return lax.psum_scatter(order(product, rows), "seq", scatter_dimension=0, tiled=True)

    hidden_grad, hidden_sum = order(lambda rows: hidden_gradient(rows, down_slab, slope, 0, groups * count), upstream)
    if square:
        far = swap_far(order.halves(slots(to_second, 3, 4), hidden_grad))
        rest = order(slots(to_second, 0, 3), hidden_grad)
        second_own = rest
        direct = swap_direct(rest, half)
        came = order.add_far(rest, far, direct)
        result_far = order.halves(slots(to_result, 3, 4), active)
        up_sum = slab_sum(gate(slab_product(second, hidden_grad), *came))
        result_far = swap_far(gate(result_far, *came))
    else:
        second_own, came = scatter(to_second, hidden_grad), ()
        up_sum = slab_sum(slab_product(second, hidden_grad))
    branch_grad, middle_grad, middle_sums = order(
        lambda own, *came: norm_back(own, middle, *second_stats, dz_low, ln2_gain, came), second_own, *came
    )

    def column_sum(values):
        return jnp.sum(values.astype(wide), axis=0)

    hidden_sum = lax.dynamic_update_slice_in_dim(
        jnp.zeros((hidden_width,), wide), hidden_sum[0], me * hidden_slab, axis=0
    )
    early = [middle_sums[2], middle_sums[0], middle_sums[1], hidden_sum, dz_sum]
    mixed_grad = order(lambda rows: mixed_gradient(rows, full_out, slab), branch_grad)
    mixed_grad = exchange(by_index([mixed_grad[:, j * slab : (j + 1) * slab] for j in range(groups)], me))
    if square:
        result_rest = order(lambda rows: product_of(rows, down_slab, 3 * count), active)
        order.after(*mixed_grad)
        result_came = order.add_far(result_rest, result_far, None)
    attention = (mask, slopes, qkv, log_totals, attended)
    order.after(down_sum)
    begun = order(
        lambda *grads: attend_backward(*attention, grads, seq_count, local_len, 0, pairs // 2), *mixed_grad
    )
    branch_other = pair_swap(branch_grad)
    branch_pair = jnp.concatenate([branch_grad, branch_other], axis=0)
    out_sum = order(lambda columns: outer(columns, branch_pair, groups, 1), mixed_half)
    if square:
        part = out_sum.shape[0] // 4
        out_far = out_sum[3 * part : 3 * part + part // 2], out_sum[3 * part + part // 2 :]
        out_far = swap_far(out_far)
    first_sum = slab_product(normed, begun, (0, 2))
    if square:
        first_sum = gate(first_sum, *result_came, *out_far)
        order.after(*result_came)
        out_came = order.add_far(out_sum, out_far, None, at=part)
    first_sum = slab_sum(first_sum)
    qkv_grad = order(
        lambda begun, *grads: attend_backward(
            *attention, grads, seq_count, local_len, pairs // 2, pairs, begun
        ),
        begun,
        *mixed_grad,
    )
    if not square:
        out_sum = lax.psum_scatter(out_sum, "seq", scatter_dimension=0, tiled=True)
    order.after(up_sum)
    if square:
        far = swap_far(order.halves(slots(to_normed, 3, 4), qkv_grad))
        order.after(first_sum)
        near = order(slots(to_normed, 1, 3), qkv_grad)
        direct = swap_direct(near, half)
        order.after(*out_came)
        out_sum = order(lambda own, *came: summed(own[:part], came).astype(low), out_sum, *out_came)
    out_sum = out_sum.reshape(-1, 1, out_rows, model_width)
    zero = jnp.zeros_like(out_sum)
    out_sum = jnp.concatenate(
        [jnp.where(parity == 0, out_sum, zero), jnp.where(parity == 1, out_sum, zero)], axis=1
    ).reshape(-1, model_width)
    if square:
        out_sum = gate(out_sum, *far)
    grad_w_out = lax.psum_scatter(out_sum, "fsdp", scatter_dimension=0, tiled=True).astype(wide)
    second_sum = slab_product(normed, qkv_grad, (1, 2))
    if square:
        second_sum = slab_sum(gate(second_sum, *far, *direct))
        came = order.add_far(near, far, direct)
        order.after(grad_w_out)
        normed_own = order(slots(to_normed, 0, 1), qkv_grad)
    else:
        second_sum = slab_sum(second_sum)
        normed_own, came = scatter(to_normed, qkv_grad), ()
    qkv_column_sum = order(column_sum, qkv_grad)
    grad_tokens, _, input_sums = order(
        lambda own, *came: norm_back(own, x_low, *first_stats, middle_grad, ln1_gain, came), normed_own, *came
    )
    grad_tokens = grad_tokens.reshape(tokens.shape)
    three = jnp.concatenate([down_sum, up_sum, first_sum], axis=1)
    three = slabs_of_rows(gate(three, *came, normed_own))
    down_slabs, up_slabs, first_slabs = jnp.split(three, [hidden_slab, 2 * hidden_slab], axis=2)
    second_slabs = slabs_of_rows(second_sum)

    def rows_of(slabs):
        return jnp.swapaxes(slabs, 0, 1).astype(wide)

    grad_w_down = rows_of(down_slabs).reshape(-1, hidden_width).T
    grad_w_up = rows_of(up_slabs).reshape(-1, hidden_width)
    grad_w_qkv = [
        rows_of(part).reshape(-1, groups, pairs // 2, 3, PAIR) for part in (first_slabs, second_slabs)
    ]
    grad_w_qkv = jnp.concatenate(grad_w_qkv, axis=2)
    grad_w_qkv = jnp.transpose(grad_w_qkv, (0, 3, 1, 2, 4)).reshape(-1, 3 * model_width)

    head_sum = jnp.transpose(qkv_column_sum.reshape(pairs, 3, PAIR), (1, 0, 2)).reshape(3, slab)
    qv_sum = lax.dynamic_update_slice_in_dim(
        jnp.zeros((2, model_width), wide), head_sum[0::2], me * slab, axis=1
    )
    late = [qv_sum.reshape(-1), input_sums[0], input_sums[1]]
    sums = order(lambda *parts: jnp.concatenate(parts).reshape(-1, PAIR), *early, *late)
    stages = total_stages()
    for axis, masks in stages:
        others = range(lax.axis_size(axis))
        came = [lax.ppermute(sums, axis, [(i, i ^ mask) for i in others]) for mask in masks]
        if (axis, masks) == stages[1]:
            order.after(three)
        if (axis, masks) == stages[-1]:
            order.after(second_slabs)
        sums = order(lambda *parts: sum(parts[1:], parts[0]), sums, *came)
        if (axis, masks) != stages[0]:
            continue
        if square:
            result = order(
                lambda rest, *came: (middle + (summed(rest[:count], came) + down_bias)).astype(low),
                result_rest,
                *result_came,
            )
        else:
            result = (middle + (scatter(to_result, active).astype(wide) + down_bias)).astype(low)
        result = result.reshape(tokens.shape)
    sums = sums.reshape(-1)

    def cut(at, count):
        return sums[at * model_width : (at + count) * model_width]

    ratio = hidden_width // model_width
    return (
        result,
        grad_tokens,
        grad_w_qkv,
        cut(4 + ratio, 2).reshape(2, model_width),
        grad_w_out,
        cut(0, 1),
        cut(6 + ratio, 1),
        cut(7 + ratio, 1),
        cut(1, 1),
        cut(2, 1),
        grad_w_up,
        cut(3, ratio),
        grad_w_down,
        cut(3 + ratio, 1),
    )


def solution(mesh):
    return jax.shard_map(
        local,
        mesh=mesh,
        in_specs=(
            P("fsdp", "seq", None),
            P("fsdp", "seq", None),
            P("fsdp", None),
            P(),
            P("fsdp", None),
            P(),
            P(),
            P(),
            P(),
            P(),
            P("fsdp", None),
            P(),
            P(None, "fsdp"),
            P(),
        ),
        out_specs=(
            P("fsdp", "seq", None),
            P("fsdp", "seq", None),
            P(("seq", "fsdp"), None),
            P(),
            P(("seq", "fsdp"), None),
            P(),
            P(),
            P(),
            P(),
            P(),
            P(("seq", "fsdp"), None),
            P(),
            P(None, ("seq", "fsdp")),
            P(),
        ),
        check_vma=False,
    )
```

```python
import math
from functools import partial

import jax
import jax.numpy as jnp
from jax import lax
from jax.experimental import pallas as pl
from jax.experimental.pallas import tpu as pltpu
from jax.sharding import PartitionSpec as P

HEADS = 32
HEAD_DIM = 64
BLOCK = 256
PAIR = 2 * HEAD_DIM
GRANT = 58 * 2**20


def estimate(flops, transcendentals=0):
    return pl.CostEstimate(flops=flops // 4, bytes_accessed=flops // 4096, transcendentals=transcendentals // 4)


def layer_norm(token_rows, gain_vec, shift_vec):
    average = jnp.mean(token_rows, axis=-1, keepdims=True)
    centred = token_rows - average
    spread = jnp.mean(centred * centred, axis=-1, keepdims=True)
    scale = lax.rsqrt(spread + 1e-05)
    return centred * scale * gain_vec + shift_vec, average, scale


def contract(left_side, right_side):
    return lax.dot_general(
        left_side, right_side, (((1,), (0,)), ((), ())), preferred_element_type=jnp.float32
    )


def contract_last(left_side, right_side):
    return lax.dot_general(
        left_side, right_side, (((1,), (1,)), ((), ())), preferred_element_type=jnp.float32
    )


def contract_first(left_side, right_side):
    return lax.dot_general(
        left_side, right_side, (((0,), (0,)), ((), ())), preferred_element_type=jnp.float32
    )


def row_pieces(mask, sequence, block, seqs, local):
    per = BLOCK // local
    return [
        pl.ds(pl.multiple_of((((block * per + r) ^ mask) * seqs + sequence) * local, local), local)
        for r in range(per)
    ]


def load_rows(ref, pieces, columns):
    parts = [ref[piece, columns] for piece in pieces]
    return parts[0] if len(parts) == 1 else jnp.concatenate(parts, axis=0)


def store_rows(ref, pieces, columns, values):
    local = values.shape[0] // len(pieces)
    for r, piece in enumerate(pieces):
        ref[piece, columns] = values[r * local : (r + 1) * local]


Q_COLUMNS, K_COLUMNS, V_COLUMNS = (slice(t * PAIR, (t + 1) * PAIR) for t in range(3))


def attend_forward_kernel(mask_ref, slope_ref, qkv_ref, mixed_ref, lse_ref, *, blocks, seqs, local):
    pair, sequence = pl.program_id(0), pl.program_id(1)
    mask = mask_ref[0]
    lane = lax.broadcasted_iota(jnp.int32, (BLOCK, PAIR), 1)
    row = lax.broadcasted_iota(jnp.int32, (BLOCK, BLOCK), 0)
    column = lax.broadcasted_iota(jnp.int32, (BLOCK, BLOCK), 1)
    gap = (row - column).astype(jnp.float32)
    pieces = [row_pieces(mask, sequence, block, seqs, local) for block in range(blocks)]

    for i in range(blocks):
        q_pair = load_rows(qkv_ref, pieces[i], Q_COLUMNS)
        outs, lses = [], []
        for head in range(2):
            slope = slope_ref[pair * 2 + head]
            mine = (lane >= head * HEAD_DIM) & (lane < (head + 1) * HEAD_DIM)
            q = jnp.where(mine, q_pair, jnp.zeros_like(q_pair)) * jnp.bfloat16(HEAD_DIM**-0.5)
            parts, highest = [], None
            for j in range(i + 1):
                scores = contract_last(q, load_rows(qkv_ref, pieces[j], K_COLUMNS))
                distance = jnp.abs(gap) if i == j else gap + float(BLOCK * (i - j))
                scores = scores - slope * distance
                parts.append(scores)
                top = jnp.max(scores, axis=-1, keepdims=True)
                highest = top if highest is None else jnp.maximum(highest, top)
            total, out = None, None
            for j in range(i + 1):
                weights = jnp.exp(parts[j] - highest)
                part = jnp.sum(weights, axis=-1, keepdims=True)
                mixed = contract(weights.astype(jnp.bfloat16), load_rows(qkv_ref, pieces[j], V_COLUMNS))
                total = part if total is None else total + part
                out = mixed if out is None else out + mixed
            outs.append(out / total)
            lses.append(highest + jnp.log(total))
        first = lane < HEAD_DIM
        everything = slice(0, PAIR)
        store_rows(
            mixed_ref, pieces[i], everything, jnp.where(first, outs[0], outs[1]).astype(mixed_ref.dtype)
        )
        store_rows(lse_ref, pieces[i], everything, jnp.where(first, lses[0], lses[1]))


def attend_backward_kernel(
    mask_ref, slope_ref, qkv_ref, lse_ref, mixed_ref, *rest, blocks, seqs, local, start, grads
):
    out_ref, dq_ref, dk_ref, dv_ref, grad_ref = rest[-5:]
    pair, sequence = pl.program_id(0) + start, pl.program_id(1)
    mask = mask_ref[0]
    lane = lax.broadcasted_iota(jnp.int32, (BLOCK, PAIR), 1)
    key = lax.broadcasted_iota(jnp.int32, (BLOCK, BLOCK), 0)
    query = lax.broadcasted_iota(jnp.int32, (BLOCK, BLOCK), 1)
    gap = (query - key).astype(jnp.float32)
    pieces = [row_pieces(mask, sequence, block, seqs, local) for block in range(blocks)]
    everything = slice(0, PAIR)

    @pl.when(sequence == 0)
    def _():
        at = 0
        for part in rest[:grads]:
            grad_ref[at : at + part.shape[0], :] = part[...]
            at += part.shape[0]

    for i in range(blocks):
        q_pair = load_rows(qkv_ref, pieces[i], Q_COLUMNS)
        up_pair = load_rows(grad_ref, pieces[i], everything)
        mixed_pair = load_rows(mixed_ref, pieces[i], everything)
        inner_all = (up_pair.astype(jnp.float32) * mixed_pair.astype(jnp.float32)).T
        lse_all = load_rows(lse_ref, pieces[i], everything).T
        dq = None
        for head in range(2):
            slope = slope_ref[pair * 2 + head]
            mine = (lane >= head * HEAD_DIM) & (lane < (head + 1) * HEAD_DIM)
            zero = jnp.zeros_like(q_pair)
            q = jnp.where(mine, q_pair, zero) * jnp.bfloat16(HEAD_DIM**-0.5)
            up = jnp.where(mine, up_pair, zero)
            inner = jnp.sum(inner_all[head * HEAD_DIM : (head + 1) * HEAD_DIM], axis=0, keepdims=True)
            lse = lse_all[head * HEAD_DIM : head * HEAD_DIM + 1]
            for j in range(i + 1):
                k_pair = load_rows(qkv_ref, pieces[j], K_COLUMNS)
                distance = jnp.abs(gap) if i == j else gap + float(BLOCK * (i - j))
                probs = jnp.exp(contract_last(k_pair, q) - slope * distance - lse)
                prob_grad = contract_last(load_rows(qkv_ref, pieces[j], V_COLUMNS), up)
                score_grad = (probs * (prob_grad - inner)).astype(jnp.bfloat16)
                dv = contract(probs.astype(jnp.bfloat16), up)
                dk = contract(score_grad, q)
                part = contract_first(score_grad, jnp.where(mine, k_pair, zero))
                dq = part if dq is None else dq + part
                if i == j and head == 0:
                    dv_ref[j] = dv
                    dk_ref[j] = dk
                else:
                    dv_ref[j] += dv
                    dk_ref[j] += dk
        dq_ref[i] = dq
    for i in range(blocks):
        store_rows(out_ref, pieces[i], Q_COLUMNS, (dq_ref[i] * HEAD_DIM**-0.5).astype(out_ref.dtype))
        store_rows(out_ref, pieces[i], K_COLUMNS, dk_ref[i].astype(out_ref.dtype))
        store_rows(out_ref, pieces[i], V_COLUMNS, dv_ref[i].astype(out_ref.dtype))


def attend_forward(mask, slopes, qkv, seqs, local):
    rows, width = qkv.shape
    pairs, blocks = width // (3 * PAIR), rows // seqs // BLOCK
    scored = pairs * seqs * blocks * (blocks + 1) * BLOCK * BLOCK
    return pl.pallas_call(
        partial(attend_forward_kernel, blocks=blocks, seqs=seqs, local=local),
        grid_spec=pltpu.PrefetchScalarGridSpec(
            num_scalar_prefetch=2,
            grid=(pairs, seqs),
            in_specs=[pl.BlockSpec((rows, 3 * PAIR), lambda p, *_: (0, p))],
            out_specs=[pl.BlockSpec((rows, PAIR), lambda p, *_: (0, p))] * 2,
        ),
        out_shape=[
            jax.ShapeDtypeStruct((rows, pairs * PAIR), jnp.bfloat16),
            jax.ShapeDtypeStruct((rows, pairs * PAIR), jnp.float32),
        ],
        compiler_params=pltpu.CompilerParams(vmem_limit_bytes=GRANT),
        cost_estimate=estimate(scored * 2 * 512, scored),
        name="attend_forward",
    )(mask, slopes, qkv)


def attend_backward(mask, slopes, qkv, lse, mixed, grads, seqs, local, start, stop, begun=None):
    rows, width = qkv.shape
    blocks = rows // seqs // BLOCK
    scored = (stop - start) * seqs * blocks * (blocks + 1) * BLOCK * BLOCK
    narrow = pl.BlockSpec((rows, PAIR), lambda p, *_: (0, p + start))
    wide = pl.BlockSpec((rows, 3 * PAIR), lambda p, *_: (0, p + start))
    earlier = [] if begun is None else [begun]
    return pl.pallas_call(
        partial(
            attend_backward_kernel, blocks=blocks, seqs=seqs, local=local, start=start, grads=len(grads)
        ),
        grid_spec=pltpu.PrefetchScalarGridSpec(
            num_scalar_prefetch=2,
            grid=(stop - start, seqs),
            in_specs=[wide, narrow, narrow]
            + [pl.BlockSpec((grad.shape[0], PAIR), lambda p, *_: (0, p + start)) for grad in grads]
            + [pl.BlockSpec(memory_space=pl.ANY)] * len(earlier),
            out_specs=wide,
            scratch_shapes=[pltpu.VMEM((blocks, BLOCK, PAIR), jnp.float32)] * 3
            + [pltpu.VMEM((rows, PAIR), jnp.bfloat16)],
        ),
        out_shape=jax.ShapeDtypeStruct((rows, width), jnp.bfloat16),
        input_output_aliases={5 + len(grads): 0} if earlier else {},
        compiler_params=pltpu.CompilerParams(vmem_limit_bytes=GRANT),
        cost_estimate=estimate(scored * 2 * 1280, scored),
        name="attend_backward",
    )(mask, slopes, qkv, lse, mixed, *grads, *earlier)


def head_columns_kernel(at_ref, in_ref, out_ref):
    for t in range(3):

        @pl.when(pl.program_id(0) == t)
        def _():
            for pair in range(in_ref.shape[1] // PAIR):
                at = (pair * 3 + t) * PAIR
                out_ref[:, at : at + PAIR] = in_ref[:, pair * PAIR : (pair + 1) * PAIR]


def up_kernel(rows_ref, weight_ref, bias_ref, active_ref, slope_ref, *, chunk):
    rows = rows_ref[...]
    for at in range(0, weight_ref.shape[1], chunk):
        columns = slice(at, at + chunk)
        hidden = contract(rows, weight_ref[:, columns]) + bias_ref[:, columns]
        below = 0.5 + 0.5 * lax.erf(hidden * 2**-0.5)
        active_ref[:, columns] = (hidden * below).astype(active_ref.dtype)
        slope_ref[:, columns] = below + hidden * ((2 * math.pi) ** -0.5 * jnp.exp(-0.5 * hidden * hidden))


def hidden_grad_kernel(rows_ref, weight_ref, slope_ref, grad_ref, sum_ref, *, chunk):
    rows = rows_ref[...]
    starting = pl.program_id(0) == 0
    for at in range(0, weight_ref.shape[0], chunk):
        columns = slice(at, at + chunk)
        grad = contract_last(rows, weight_ref[columns, :]) * slope_ref[:, columns]
        grad = grad.astype(grad_ref.dtype)
        grad_ref[:, columns] = grad
        part = jnp.sum(grad.astype(jnp.float32), axis=0, keepdims=True)
        sum_ref[:, columns] = jnp.where(starting, part, sum_ref[:, columns] + part)


TILE = 256


def up_and_bend(rows, weight, bias):
    count, depth = rows.shape
    width = weight.shape[1]
    tile = pl.BlockSpec((TILE, width), lambda i: (i, 0))
    return pl.pallas_call(
        partial(up_kernel, chunk=512),
        grid=(count // TILE,),
        in_specs=[
            pl.BlockSpec((TILE, depth), lambda i: (i, 0)),
            pl.BlockSpec((depth, width), lambda i: (0, 0), pipeline_mode=pl.Buffered(1)),
            pl.BlockSpec((1, width), lambda i: (0, 0)),
        ],
        out_specs=[tile, tile],
        out_shape=[
            jax.ShapeDtypeStruct((count, width), jnp.bfloat16),
            jax.ShapeDtypeStruct((count, width), jnp.float32),
        ],
        compiler_params=pltpu.CompilerParams(vmem_limit_bytes=GRANT),
        cost_estimate=estimate(count * depth * width * 4, 2 * count * width),
        name="up_and_bend",
    )(rows, weight, bias)


def hidden_gradient(rows, weight, slope, start, count):
    depth = rows.shape[1]
    width = weight.shape[0]
    first = start // TILE
    line = pl.BlockSpec((1, width), lambda i: (0, 0))
    return pl.pallas_call(
        partial(hidden_grad_kernel, chunk=512),
        grid=(count // TILE,),
        in_specs=[
            pl.BlockSpec((TILE, depth), lambda i: (i + first, 0)),
            pl.BlockSpec((width, depth), lambda i: (0, 0), pipeline_mode=pl.Buffered(1)),
            pl.BlockSpec((TILE, width), lambda i: (i + first, 0)),
        ],
        out_specs=[pl.BlockSpec((TILE, width), lambda i: (i, 0)), line],
        out_shape=[
            jax.ShapeDtypeStruct((count, width), jnp.bfloat16),
            jax.ShapeDtypeStruct((1, width), jnp.float32),
        ],
        compiler_params=pltpu.CompilerParams(vmem_limit_bytes=GRANT),
        cost_estimate=estimate(count * depth * width * 3, 0),
        name="hidden_gradient",
    )(rows, weight, slope)


def product_kernel(rows_ref, weight_ref, out_ref):
    out_ref[...] = contract(rows_ref[...], weight_ref[...]).astype(out_ref.dtype)


def product_of(rows, weight, count):
    depth, width = weight.shape
    return pl.pallas_call(
        product_kernel,
        grid=(count // TILE,),
        in_specs=[
            pl.BlockSpec((TILE, depth), lambda i: (i, 0)),
            pl.BlockSpec((depth, width), lambda i: (0, 0), pipeline_mode=pl.Buffered(1)),
        ],
        out_specs=pl.BlockSpec((TILE, width), lambda i: (i, 0)),
        out_shape=jax.ShapeDtypeStruct((count, width), jnp.bfloat16),
        compiler_params=pltpu.CompilerParams(vmem_limit_bytes=GRANT),
        cost_estimate=estimate(2 * count * depth * width, 0),
        name="product",
    )(rows, weight)


def mixed_grad_kernel(rows_ref, weight_ref, out_ref):
    out_ref[...] = contract_last(rows_ref[...], weight_ref[...]).astype(out_ref.dtype)


def mixed_gradient(rows, weight, slab):
    count, depth = rows.shape
    width = weight.shape[0]
    return pl.pallas_call(
        mixed_grad_kernel,
        grid=(width // slab,),
        in_specs=[
            pl.BlockSpec((count, depth), lambda i: (0, 0), pipeline_mode=pl.Buffered(1)),
            pl.BlockSpec((slab, depth), lambda i: (i, 0)),
        ],
        out_specs=pl.BlockSpec((count, slab), lambda i: (0, i)),
        out_shape=jax.ShapeDtypeStruct((count, width), jnp.bfloat16),
        compiler_params=pltpu.CompilerParams(vmem_limit_bytes=GRANT),
        cost_estimate=estimate(2 * count * depth * width, 0),
        name="mixed_gradient",
    )(rows, weight)


def norm_back_kernel(own_ref, values_ref, average_ref, scale_ref, base_ref, gain_ref, *refs, parts):
    came, (low_ref, wide_ref, sums_ref) = refs[:parts], refs[parts:]
    wide = jnp.float32
    step = pl.program_id(0)

    @pl.when(step == 0)
    def _():
        sums_ref[...] = jnp.zeros_like(sums_ref)

    def make(came):
        grad = own_ref[...].astype(wide)
        for part in came:
            grad = grad + part[...].astype(wide)
        scale = scale_ref[...]
        normal = (values_ref[...].astype(wide) - average_ref[...]) * scale
        gained = grad * gain_ref[...]
        along = jnp.mean(gained * normal, axis=-1, keepdims=True)
        across = jnp.mean(gained, axis=-1, keepdims=True)
        made = base_ref[...].astype(wide) + scale * (gained - across - normal * along)
        low = made.astype(low_ref.dtype)
        low_ref[...] = low
        wide_ref[...] = made
        for at, part in enumerate((grad * normal, grad, low.astype(wide))):
            sums_ref[8 * at : 8 * at + 8, :] += jnp.sum(part.reshape(-1, 8, part.shape[1]), axis=0)

    if not came:
        make(())
        return
    upper = step < pl.num_programs(0) // 2
    pl.when(upper)(lambda: make(came[0::2]))
    pl.when(jnp.logical_not(upper))(lambda: make(came[1::2]))


def norm_back(rest, values, average, scale, base, gain, came):
    rows, width = values.shape
    steps = 8
    half = steps // 2
    came = list(came or ())
    count = rows // steps
    tile = pl.BlockSpec((count, width), lambda i: (i, 0))
    thin = pl.BlockSpec((count, 1), lambda i: (i, 0))
    top = pl.BlockSpec((count, width), lambda i: (jnp.minimum(i, half - 1), 0))
    bottom = pl.BlockSpec((count, width), lambda i: (jnp.maximum(i - half, 0), 0))
    low, full, sums = pl.pallas_call(
        partial(norm_back_kernel, parts=len(came)),
        grid=(steps,),
        in_specs=[tile, tile, thin, thin, tile, pl.BlockSpec((1, width), lambda i: (0, 0))]
        + [top, bottom] * (len(came) // 2),
        out_specs=[tile, tile, pl.BlockSpec((24, width), lambda i: (0, 0))],
        out_shape=[
            jax.ShapeDtypeStruct((rows, width), jnp.bfloat16),
            jax.ShapeDtypeStruct((rows, width), jnp.float32),
            jax.ShapeDtypeStruct((24, width), jnp.float32),
        ],
        compiler_params=pltpu.CompilerParams(vmem_limit_bytes=GRANT),
        cost_estimate=estimate(30 * rows * width, rows),
        name="norm_back",
    )(rest, values, average, scale, base, gain[None], *came)
    return low, full, jnp.sum(sums.reshape(3, 8, width), axis=1)


def outer_kernel(left_ref, right_ref, out_ref, *, chunk):
    left = left_ref[...]
    shards = out_ref.shape[0]
    for at in range(0, out_ref.shape[3], chunk):
        columns = slice(at, at + chunk)
        made = contract_first(left, right_ref[:, columns]).astype(out_ref.dtype)
        out_ref[:, 0, :, columns] = made.reshape(shards, -1, made.shape[1])


def outer(left, right, groups, shards, part_of=(0, 1)):
    at, parts = part_of
    tokens, rows = left.shape
    width = right.shape[1] // parts
    part = rows // groups
    made = pl.pallas_call(
        partial(outer_kernel, chunk=next(c for c in (512, 384, 256, 128) if width % c == 0)),
        grid=(groups,),
        in_specs=[
            pl.BlockSpec((tokens, part), lambda i: (0, i)),
            pl.BlockSpec((tokens, width), lambda i: (0, at), pipeline_mode=pl.Buffered(1)),
        ],
        out_specs=pl.BlockSpec((shards, 1, part // shards, width), lambda i: (0, i, 0, 0)),
        out_shape=jax.ShapeDtypeStruct((shards, groups, part // shards, width), jnp.bfloat16),
        compiler_params=pltpu.CompilerParams(vmem_limit_bytes=GRANT),
        cost_estimate=estimate(2 * tokens * rows * width, 0),
        name="outer",
    )(left, right)
    return made.reshape(rows, width)


def swap(values, bit):
    return lax.ppermute(values, "seq", [(i, i ^ bit) for i in range(4)])


def by_index(parts, me):
    if len(parts) != 4:
        return parts
    odd, upper = (me & 1) == 1, (me & 2) == 2
    a, b, c, d = parts
    a, b, c, d = (
        jnp.where(odd, b, a),
        jnp.where(odd, a, b),
        jnp.where(odd, d, c),
        jnp.where(odd, c, d),
    )
    return [jnp.where(upper, c, a), jnp.where(upper, d, b), jnp.where(upper, a, c), jnp.where(upper, b, d)]


def exchange(slots):
    if lax.axis_size("seq") != 4:
        return list(lax.all_to_all(jnp.stack(slots), "seq", split_axis=0, concat_axis=0, tiled=True))
    return [slots[0]] + [swap(slots[j], j) for j in (1, 2, 3)]


def gate(values, *before):
    return lax.optimization_barrier((values, *before))[0]


class Order:
    def __init__(self):
        self.pending = []

    def after(self, *values):
        self.pending += values

    def __call__(self, operation, *operands):
        if self.pending:
            count = len(operands)
            operands = lax.optimization_barrier((*operands, *self.pending))[:count]
        made = operation(*operands)
        self.pending = jax.tree.leaves(made)
        return made

    def gather(self, rows):
        if lax.axis_size("seq") != 4:
            return lax.all_gather(jnp.concatenate(rows, axis=0), "seq", axis=0, tiled=True), None
        top, bottom = rows
        return rows, (swap(bottom, 1), swap(top, 2), swap(top, 1), swap(bottom, 2))

    def fill(self, begun):
        rows, came = begun
        if came is None:
            return rows
        first_bottom, second_top, first_top, second_bottom = came
        room = jnp.zeros_like(rows[0])
        parts = (*rows, first_top, first_bottom, second_top, second_bottom, room, room)
        return self(lambda *parts: jnp.concatenate(parts, axis=0), *parts)

    def complete(self, made, pieces):
        if not isinstance(pieces, list):
            return made
        rows = pieces[-1].shape[0]

        def put(before, first, second):
            before = lax.dynamic_update_slice_in_dim(before, first, 6 * rows, axis=0)
            return lax.dynamic_update_slice_in_dim(before, second, 7 * rows, axis=0)

        return self(put, made, *pieces[-2:])

    def pass_on(self, begun, *before):
        rows, came = begun
        if came is None:
            return rows
        first_bottom, second_top, first_top, second_bottom = came
        self.after(*came)
        if before:
            second_top, first_bottom = gate((second_top, first_bottom), *before)
        far = [swap(second_top, 1), swap(first_bottom, 2)]
        return [*rows, first_top, first_bottom, second_top, second_bottom, *far]

    def halves(self, product, rows):
        def cut(values):
            made = product(values)
            half = made.shape[0] // 2
            return made[:half], made[half:]

        return self(cut, rows)

    def add_far(self, made, far, direct, *before, at=None):
        wide = jnp.float32
        half = far[0].shape[0]
        start = made.shape[0] - 4 * half if at is None else at

        def add(made, top, bottom):
            at = start
            first = (made[at + half : at + 2 * half].astype(wide) + bottom.astype(wide)).astype(made.dtype)
            second = (made[at + 2 * half : at + 3 * half].astype(wide) + top.astype(wide)).astype(made.dtype)
            if direct is None:
                first = jnp.concatenate([made[at : at + half], first], axis=0)
                second = jnp.concatenate([second, made[at + 3 * half : at + 4 * half]], axis=0)
            return first, second

        first, second = self(add, made, *far)
        if before:
            first, second = gate((first, second), *before)
        first, second = swap(first, 1), swap(second, 2)
        return (first, second) if direct is None else (direct[0], first, second, direct[1])


def swap_far(halves):
    return swap(halves[0], 1), swap(halves[1], 2)


def swap_direct(made, half):
    at = made.shape[0] - 4 * half
    return swap(made[at : at + half], 1), swap(made[at + 3 * half :], 2)


def summed(own, came):
    wide = jnp.float32
    own = own.astype(wide)
    return sum((part.astype(wide) for part in came), own)


def whole(parts):
    return jnp.concatenate(parts, axis=0) if isinstance(parts, list) else parts


def total_stages():
    stages = []
    for axis in ("fsdp", "seq"):
        count, bit = lax.axis_size(axis), 1
        bits = count.bit_length() - 1
        while bit < count:
            stages.append((axis, [bit] if bits % 2 else [bit, 2 * bit, 3 * bit]))
            bit <<= 1 if bits % 2 else 2
            bits -= bits % 2
    return stages


def local(
    tokens,
    cotangent,
    w_qkv,
    qv_bias,
    w_out,
    out_bias,
    ln1_gain,
    ln1_shift,
    ln2_gain,
    ln2_shift,
    w_up,
    up_bias,
    w_down,
    down_bias,
):
    seq_count, local_len, model_width = tokens.shape
    groups, shards = lax.axis_size("seq"), lax.axis_size("fsdp")
    me = lax.axis_index("seq")
    square = groups == 4
    heads_here = HEADS // groups
    slab = heads_here * HEAD_DIM
    pairs = slab // PAIR
    hidden_width = w_up.shape[1]
    hidden_slab = hidden_width // groups
    rows_here = seq_count * local_len
    low, wide = jnp.bfloat16, jnp.float32
    mask = jnp.reshape(me if square else jnp.zeros_like(me), (1,)).astype(jnp.int32)
    head_index = me * heads_here + jnp.arange(1, heads_here + 1, dtype=jnp.int32)
    slopes = 2.0 ** (-8.0 * head_index.astype(wide) / HEADS)

    def head_columns(values):
        rows = values.shape[0]
        return pl.pallas_call(
            head_columns_kernel,
            grid_spec=pltpu.PrefetchScalarGridSpec(
                num_scalar_prefetch=1,
                grid=(3,),
                in_specs=[pl.BlockSpec((rows, slab), lambda t, at: (0, t * groups + at[0]))],
                out_specs=pl.BlockSpec((rows, 3 * slab), lambda t, at: (0, 0)),
            ),
            out_shape=jax.ShapeDtypeStruct((rows, 3 * slab), values.dtype),
            name="head_columns",
        )(jnp.reshape(me, (1,)).astype(jnp.int32), values)

    def own_slab(values, axis):
        width = values.shape[axis] // groups
        return lax.dynamic_slice_in_dim(values, me * width, width, axis=axis)

    order = Order()
    x_low = tokens.reshape(rows_here, model_width)
    x = x_low.astype(wide)
    dz_low = cotangent.reshape(rows_here, model_width)
    qkv_slab = lax.all_gather(head_columns(w_qkv), "fsdp", axis=0, tiled=True)
    qkv_bias = head_columns(jnp.concatenate([qv_bias[0], jnp.zeros_like(qv_bias[0]), qv_bias[1]])[None])
    up_bias_slab = own_slab(up_bias, 0)

    first_norm, *first_stats = layer_norm(x, ln1_gain, ln1_shift)
    half = rows_here // 2

    def halves_of(values):
        return values[:half].astype(low), values[half:].astype(low)

    normed = order.gather(order(halves_of, first_norm))
    normed = order.pass_on(normed)
    full_out = lax.all_gather(w_out, "fsdp", axis=0, tiled=True)
    up_slab = lax.all_gather(own_slab(gate(w_up, normed[0]) if square else w_up, 1), "fsdp", axis=0, tiled=True)
    down_slab = lax.all_gather(own_slab(gate(w_down, normed[0]) if square else w_down, 0), "fsdp", axis=1, tiled=True)
    normed = whole(normed)
    upstream = order.gather(halves_of(gate(dz_low, normed)))
    qkv = order(lambda rows: (contract(rows, qkv_slab) + qkv_bias).astype(low), normed)
    attended, log_totals = order(lambda rows: attend_forward(mask, slopes, rows, seq_count, local_len), qkv)
    if square:
        attended = gate(attended, *upstream[1])
    mixed_slots = exchange([attended[j * rows_here : (j + 1) * rows_here] for j in range(groups)])
    mixed_rows = jnp.concatenate(by_index(mixed_slots, me), axis=1)
    mixed_slots = jnp.concatenate(mixed_slots, axis=1)

    def pair_swap(values):
        return lax.ppermute(values, "fsdp", [(i, i ^ 1) for i in range(shards)])

    parity = lax.axis_index("fsdp") & 1
    out_rows = model_width // (groups * shards)

    def pair_halves(values):
        halves = values.reshape(rows_here, -1, 2, out_rows)
        return tuple(
            lax.dynamic_index_in_dim(halves, index, axis=2, keepdims=False).reshape(rows_here, -1)
            for index in (parity, 1 - parity)
        )

    middle = order(lambda rows: x + (contract(rows, full_out) + out_bias), mixed_rows)
    second_norm, *second_stats = layer_norm(middle, ln2_gain, ln2_shift)
    second = order.gather(order(halves_of, second_norm))
    mine, theirs = order(pair_halves, mixed_slots)
    upstream_made = order.fill(upstream)
    theirs = pair_swap(theirs)
    dz_sum = order(lambda values: jnp.sum(values.astype(wide), axis=0), dz_low)
    second = whole(order.pass_on(second))
    upstream = order.pass_on(upstream, second)
    active, slope = order(lambda rows: up_and_bend(rows, up_slab, up_bias_slab[None]), second)
    mixed_half = order(lambda *parts: jnp.concatenate(parts, axis=0), mine, theirs)
    upstream = order.complete(upstream_made, upstream)

    def slab_product(left, right, part_of=(0, 1)):
        return order(lambda rows, others: outer(rows, others, groups, shards, part_of), left, right)

    def slab_sum(made):
        return lax.psum_scatter(made, "fsdp", scatter_dimension=0, tiled=True)

    def slabs_of_rows(values):
        return lax.all_to_all(
            values.reshape(groups, -1, values.shape[1]), "seq", split_axis=0, concat_axis=0, tiled=True
        )

    down_sum = slab_sum(slab_product(upstream, active))
    count = rows_here

    def slots(product, start, stop):
        return lambda values: product(values[start * count : stop * count])

    def to_second(rows):
        return contract_last(rows, up_slab).astype(low)

    def to_result(rows):
        return contract(rows, down_slab).astype(low)

    def to_normed(rows):
        return contract_last(rows, qkv_slab).astype(low)

    def scatter(product, rows):
        return lax.psum_scatter(order(product, rows), "seq", scatter_dimension=0, tiled=True)

    hidden_grad, hidden_sum = order(lambda rows: hidden_gradient(rows, down_slab, slope, 0, groups * count), upstream)
    if square:
        far = swap_far(order.halves(slots(to_second, 3, 4), hidden_grad))
        rest = order(slots(to_second, 0, 3), hidden_grad)
        second_own = rest
        direct = swap_direct(rest, half)
        came = order.add_far(rest, far, direct)
        result_far = order.halves(slots(to_result, 3, 4), active)
        up_sum = slab_sum(gate(slab_product(second, hidden_grad), *came))
        result_far = swap_far(gate(result_far, *came))
    else:
        second_own, came = scatter(to_second, hidden_grad), ()
        up_sum = slab_sum(slab_product(second, hidden_grad))
    branch_grad, middle_grad, middle_sums = order(
        lambda own, *came: norm_back(own, middle, *second_stats, dz_low, ln2_gain, came), second_own, *came
    )

    def column_sum(values):
        return jnp.sum(values.astype(wide), axis=0)

    hidden_sum = lax.dynamic_update_slice_in_dim(
        jnp.zeros((hidden_width,), wide), hidden_sum[0], me * hidden_slab, axis=0
    )
    early = [middle_sums[2], middle_sums[0], middle_sums[1], hidden_sum, dz_sum]
    mixed_grad = order(lambda rows: mixed_gradient(rows, full_out, slab), branch_grad)
    mixed_grad = exchange(by_index([mixed_grad[:, j * slab : (j + 1) * slab] for j in range(groups)], me))
    if square:
        result_rest = order(lambda rows: product_of(rows, down_slab, 3 * count), active)
        order.after(*mixed_grad)
        result_came = order.add_far(result_rest, result_far, None)
    attention = (mask, slopes, qkv, log_totals, attended)
    order.after(down_sum)
    begun = order(
        lambda *grads: attend_backward(*attention, grads, seq_count, local_len, 0, pairs // 2), *mixed_grad
    )
    branch_other = pair_swap(gate(branch_grad, result_rest) if square else branch_grad)
    branch_pair = jnp.concatenate([branch_grad, branch_other], axis=0)
    out_sum = order(lambda columns: outer(columns, branch_pair, groups, 1), mixed_half)
    if square:
        part = out_sum.shape[0] // 4
        out_far = out_sum[3 * part : 3 * part + part // 2], out_sum[3 * part + part // 2 :]
        out_far = swap_far(out_far)
    first_sum = slab_product(normed, begun, (0, 2))
    if square:
        first_sum = gate(first_sum, *result_came, *out_far)
        order.after(*result_came)
        out_came = order.add_far(out_sum, out_far, None, at=part)
    first_sum = slab_sum(first_sum)
    qkv_grad = order(
        lambda begun, *grads: attend_backward(
            *attention, grads, seq_count, local_len, pairs // 2, pairs, begun
        ),
        begun,
        *mixed_grad,
    )
    if not square:
        out_sum = lax.psum_scatter(out_sum, "seq", scatter_dimension=0, tiled=True)
    order.after(up_sum)
    if square:
        far = swap_far(order.halves(slots(to_normed, 3, 4), qkv_grad))
        order.after(first_sum)
        near = order(slots(to_normed, 1, 3), qkv_grad)
        direct = swap_direct(near, half)
        order.after(*out_came)
        out_sum = order(lambda own, *came: summed(own[:part], came).astype(low), out_sum, *out_came)
    out_sum = out_sum.reshape(-1, 1, out_rows, model_width)
    zero = jnp.zeros_like(out_sum)
    out_sum = jnp.concatenate(
        [jnp.where(parity == 0, out_sum, zero), jnp.where(parity == 1, out_sum, zero)], axis=1
    ).reshape(-1, model_width)
    if square:
        out_sum = gate(out_sum, *far)
    grad_w_out = lax.psum_scatter(out_sum, "fsdp", scatter_dimension=0, tiled=True).astype(wide)
    second_sum = slab_product(normed, qkv_grad, (1, 2))
    qkv_column_sum = order(column_sum, qkv_grad)
    if square:
        second_sum = slab_sum(gate(second_sum, *far, *direct))
        came = order.add_far(near, far, direct)
        order.after(grad_w_out)
        normed_own = order(slots(to_normed, 0, 1), qkv_grad)
    else:
        second_sum = slab_sum(second_sum)
        normed_own, came = scatter(to_normed, qkv_grad), ()
    grad_tokens, _, input_sums = order(
        lambda own, *came: norm_back(own, x_low, *first_stats, middle_grad, ln1_gain, came), normed_own, *came
    )
    grad_tokens = grad_tokens.reshape(tokens.shape)
    three = jnp.concatenate([down_sum, up_sum, first_sum], axis=1)
    three = slabs_of_rows(gate(three, *came, normed_own))
    down_slabs, up_slabs, first_slabs = jnp.split(three, [hidden_slab, 2 * hidden_slab], axis=2)
    second_slabs = slabs_of_rows(second_sum)

    def rows_of(slabs):
        return jnp.swapaxes(slabs, 0, 1).astype(wide)

    grad_w_down = rows_of(down_slabs).reshape(-1, hidden_width).T
    grad_w_up = rows_of(up_slabs).reshape(-1, hidden_width)
    grad_w_qkv = [
        rows_of(part).reshape(-1, groups, pairs // 2, 3, PAIR) for part in (first_slabs, second_slabs)
    ]
    grad_w_qkv = jnp.concatenate(grad_w_qkv, axis=2)
    grad_w_qkv = jnp.transpose(grad_w_qkv, (0, 3, 1, 2, 4)).reshape(-1, 3 * model_width)

    head_sum = jnp.transpose(qkv_column_sum.reshape(pairs, 3, PAIR), (1, 0, 2)).reshape(3, slab)
    qv_sum = lax.dynamic_update_slice_in_dim(
        jnp.zeros((2, model_width), wide), head_sum[0::2], me * slab, axis=1
    )
    late = [qv_sum.reshape(-1), input_sums[0], input_sums[1]]
    sums = order(lambda *parts: jnp.concatenate(parts).reshape(-1, PAIR), *early, *late)
    stages = total_stages()
    for axis, masks in stages:
        others = range(lax.axis_size(axis))
        came = [lax.ppermute(sums, axis, [(i, i ^ mask) for i in others]) for mask in masks]
        if (axis, masks) == stages[1]:
            order.after(three)
        if (axis, masks) == stages[-1]:
            order.after(second_slabs)
        sums = order(lambda *parts: sum(parts[1:], parts[0]), sums, *came)
        if (axis, masks) != stages[0]:
            continue
        if square:
            result = order(
                lambda rest, *came: (middle + (summed(rest[:count], came) + down_bias)).astype(low),
                result_rest,
                *result_came,
            )
        else:
            result = (middle + (scatter(to_result, active).astype(wide) + down_bias)).astype(low)
        result = result.reshape(tokens.shape)
    sums = sums.reshape(-1)

    def cut(at, count):
        return sums[at * model_width : (at + count) * model_width]

    ratio = hidden_width // model_width
    return (
        result,
        grad_tokens,
        grad_w_qkv,
        cut(4 + ratio, 2).reshape(2, model_width),
        grad_w_out,
        cut(0, 1),
        cut(6 + ratio, 1),
        cut(7 + ratio, 1),
        cut(1, 1),
        cut(2, 1),
        grad_w_up,
        cut(3, ratio),
        grad_w_down,
        cut(3 + ratio, 1),
    )


def solution(mesh):
    return jax.shard_map(
        local,
        mesh=mesh,
        in_specs=(
            P("fsdp", "seq", None),
            P("fsdp", "seq", None),
            P("fsdp", None),
            P(),
            P("fsdp", None),
            P(),
            P(),
            P(),
            P(),
            P(),
            P("fsdp", None),
            P(),
            P(None, "fsdp"),
            P(),
        ),
        out_specs=(
            P("fsdp", "seq", None),
            P("fsdp", "seq", None),
            P(("seq", "fsdp"), None),
            P(),
            P(("seq", "fsdp"), None),
            P(),
            P(),
            P(),
            P(),
            P(),
            P(("seq", "fsdp"), None),
            P(),
            P(None, ("seq", "fsdp")),
            P(),
        ),
        check_vma=False,
    )
```

```python
import math
from functools import partial

import jax
import jax.numpy as jnp
from jax import lax
from jax.experimental import pallas as pl
from jax.experimental.pallas import tpu as pltpu
from jax.sharding import PartitionSpec as P

HEADS = 32
HEAD_DIM = 64
BLOCK = 256
PAIR = 2 * HEAD_DIM
GRANT = 58 * 2**20


def estimate(flops, transcendentals=0):
    return pl.CostEstimate(flops=flops // 4, bytes_accessed=flops // 4096, transcendentals=transcendentals // 4)


def layer_norm(token_rows, gain_vec, shift_vec):
    average = jnp.mean(token_rows, axis=-1, keepdims=True)
    centred = token_rows - average
    spread = jnp.mean(centred * centred, axis=-1, keepdims=True)
    scale = lax.rsqrt(spread + 1e-05)
    return centred * scale * gain_vec + shift_vec, average, scale


def contract(left_side, right_side):
    return lax.dot_general(
        left_side, right_side, (((1,), (0,)), ((), ())), preferred_element_type=jnp.float32
    )


def contract_last(left_side, right_side):
    return lax.dot_general(
        left_side, right_side, (((1,), (1,)), ((), ())), preferred_element_type=jnp.float32
    )


def contract_first(left_side, right_side):
    return lax.dot_general(
        left_side, right_side, (((0,), (0,)), ((), ())), preferred_element_type=jnp.float32
    )


def row_pieces(mask, sequence, block, seqs, local):
    per = BLOCK // local
    return [
        pl.ds(pl.multiple_of((((block * per + r) ^ mask) * seqs + sequence) * local, local), local)
        for r in range(per)
    ]


def load_rows(ref, pieces, columns):
    parts = [ref[piece, columns] for piece in pieces]
    return parts[0] if len(parts) == 1 else jnp.concatenate(parts, axis=0)


def store_rows(ref, pieces, columns, values):
    local = values.shape[0] // len(pieces)
    for r, piece in enumerate(pieces):
        ref[piece, columns] = values[r * local : (r + 1) * local]


Q_COLUMNS, K_COLUMNS, V_COLUMNS = (slice(t * PAIR, (t + 1) * PAIR) for t in range(3))


def attend_forward_kernel(mask_ref, slope_ref, qkv_ref, mixed_ref, lse_ref, *, blocks, seqs, local):
    pair, sequence = pl.program_id(0), pl.program_id(1)
    mask = mask_ref[0]
    lane = lax.broadcasted_iota(jnp.int32, (BLOCK, PAIR), 1)
    row = lax.broadcasted_iota(jnp.int32, (BLOCK, BLOCK), 0)
    column = lax.broadcasted_iota(jnp.int32, (BLOCK, BLOCK), 1)
    gap = (row - column).astype(jnp.float32)
    pieces = [row_pieces(mask, sequence, block, seqs, local) for block in range(blocks)]

    for i in range(blocks):
        q_pair = load_rows(qkv_ref, pieces[i], Q_COLUMNS)
        outs, lses = [], []
        for head in range(2):
            slope = slope_ref[pair * 2 + head]
            mine = (lane >= head * HEAD_DIM) & (lane < (head + 1) * HEAD_DIM)
            q = jnp.where(mine, q_pair, jnp.zeros_like(q_pair)) * jnp.bfloat16(HEAD_DIM**-0.5)
            parts, highest = [], None
            for j in range(i + 1):
                scores = contract_last(q, load_rows(qkv_ref, pieces[j], K_COLUMNS))
                distance = jnp.abs(gap) if i == j else gap + float(BLOCK * (i - j))
                scores = scores - slope * distance
                parts.append(scores)
                top = jnp.max(scores, axis=-1, keepdims=True)
                highest = top if highest is None else jnp.maximum(highest, top)
            total, out = None, None
            for j in range(i + 1):
                weights = jnp.exp(parts[j] - highest)
                part = jnp.sum(weights, axis=-1, keepdims=True)
                mixed = contract(weights.astype(jnp.bfloat16), load_rows(qkv_ref, pieces[j], V_COLUMNS))
                total = part if total is None else total + part
                out = mixed if out is None else out + mixed
            outs.append(out / total)
            lses.append(highest + jnp.log(total))
        first = lane < HEAD_DIM
        everything = slice(0, PAIR)
        store_rows(
            mixed_ref, pieces[i], everything, jnp.where(first, outs[0], outs[1]).astype(mixed_ref.dtype)
        )
        store_rows(lse_ref, pieces[i], everything, jnp.where(first, lses[0], lses[1]))


def attend_backward_kernel(
    mask_ref, slope_ref, qkv_ref, lse_ref, mixed_ref, *rest, blocks, seqs, local, start, grads
):
    out_ref, dq_ref, dk_ref, dv_ref, grad_ref = rest[-5:]
    pair, sequence = pl.program_id(0) + start, pl.program_id(1)
    mask = mask_ref[0]
    lane = lax.broadcasted_iota(jnp.int32, (BLOCK, PAIR), 1)
    key = lax.broadcasted_iota(jnp.int32, (BLOCK, BLOCK), 0)
    query = lax.broadcasted_iota(jnp.int32, (BLOCK, BLOCK), 1)
    gap = (query - key).astype(jnp.float32)
    pieces = [row_pieces(mask, sequence, block, seqs, local) for block in range(blocks)]
    everything = slice(0, PAIR)

    @pl.when(sequence == 0)
    def _():
        at = 0
        for part in rest[:grads]:
            grad_ref[at : at + part.shape[0], :] = part[...]
            at += part.shape[0]

    for i in range(blocks):
        q_pair = load_rows(qkv_ref, pieces[i], Q_COLUMNS)
        up_pair = load_rows(grad_ref, pieces[i], everything)
        mixed_pair = load_rows(mixed_ref, pieces[i], everything)
        inner_all = (up_pair.astype(jnp.float32) * mixed_pair.astype(jnp.float32)).T
        lse_all = load_rows(lse_ref, pieces[i], everything).T
        dq = None
        for head in range(2):
            slope = slope_ref[pair * 2 + head]
            mine = (lane >= head * HEAD_DIM) & (lane < (head + 1) * HEAD_DIM)
            zero = jnp.zeros_like(q_pair)
            q = jnp.where(mine, q_pair, zero) * jnp.bfloat16(HEAD_DIM**-0.5)
            up = jnp.where(mine, up_pair, zero)
            inner = jnp.sum(inner_all[head * HEAD_DIM : (head + 1) * HEAD_DIM], axis=0, keepdims=True)
            lse = lse_all[head * HEAD_DIM : head * HEAD_DIM + 1]
            for j in range(i + 1):
                k_pair = load_rows(qkv_ref, pieces[j], K_COLUMNS)
                distance = jnp.abs(gap) if i == j else gap + float(BLOCK * (i - j))
                probs = jnp.exp(contract_last(k_pair, q) - slope * distance - lse)
                prob_grad = contract_last(load_rows(qkv_ref, pieces[j], V_COLUMNS), up)
                score_grad = (probs * (prob_grad - inner)).astype(jnp.bfloat16)
                dv = contract(probs.astype(jnp.bfloat16), up)
                dk = contract(score_grad, q)
                part = contract_first(score_grad, jnp.where(mine, k_pair, zero))
                dq = part if dq is None else dq + part
                if i == j and head == 0:
                    dv_ref[j] = dv
                    dk_ref[j] = dk
                else:
                    dv_ref[j] += dv
                    dk_ref[j] += dk
        dq_ref[i] = dq
    for i in range(blocks):
        store_rows(out_ref, pieces[i], Q_COLUMNS, (dq_ref[i] * HEAD_DIM**-0.5).astype(out_ref.dtype))
        store_rows(out_ref, pieces[i], K_COLUMNS, dk_ref[i].astype(out_ref.dtype))
        store_rows(out_ref, pieces[i], V_COLUMNS, dv_ref[i].astype(out_ref.dtype))


def attend_forward(mask, slopes, qkv, seqs, local):
    rows, width = qkv.shape
    pairs, blocks = width // (3 * PAIR), rows // seqs // BLOCK
    scored = pairs * seqs * blocks * (blocks + 1) * BLOCK * BLOCK
    return pl.pallas_call(
        partial(attend_forward_kernel, blocks=blocks, seqs=seqs, local=local),
        grid_spec=pltpu.PrefetchScalarGridSpec(
            num_scalar_prefetch=2,
            grid=(pairs, seqs),
            in_specs=[pl.BlockSpec((rows, 3 * PAIR), lambda p, *_: (0, p))],
            out_specs=[pl.BlockSpec((rows, PAIR), lambda p, *_: (0, p))] * 2,
        ),
        out_shape=[
            jax.ShapeDtypeStruct((rows, pairs * PAIR), jnp.bfloat16),
            jax.ShapeDtypeStruct((rows, pairs * PAIR), jnp.float32),
        ],
        compiler_params=pltpu.CompilerParams(vmem_limit_bytes=GRANT),
        cost_estimate=estimate(scored * 2 * 512, scored),
        name="attend_forward",
    )(mask, slopes, qkv)


def attend_backward(mask, slopes, qkv, lse, mixed, grads, seqs, local, start, stop, begun=None):
    rows, width = qkv.shape
    blocks = rows // seqs // BLOCK
    scored = (stop - start) * seqs * blocks * (blocks + 1) * BLOCK * BLOCK
    narrow = pl.BlockSpec((rows, PAIR), lambda p, *_: (0, p + start))
    wide = pl.BlockSpec((rows, 3 * PAIR), lambda p, *_: (0, p + start))
    earlier = [] if begun is None else [begun]
    return pl.pallas_call(
        partial(
            attend_backward_kernel, blocks=blocks, seqs=seqs, local=local, start=start, grads=len(grads)
        ),
        grid_spec=pltpu.PrefetchScalarGridSpec(
            num_scalar_prefetch=2,
            grid=(stop - start, seqs),
            in_specs=[wide, narrow, narrow]
            + [pl.BlockSpec((grad.shape[0], PAIR), lambda p, *_: (0, p + start)) for grad in grads]
            + [pl.BlockSpec(memory_space=pl.ANY)] * len(earlier),
            out_specs=wide,
            scratch_shapes=[pltpu.VMEM((blocks, BLOCK, PAIR), jnp.float32)] * 3
            + [pltpu.VMEM((rows, PAIR), jnp.bfloat16)],
        ),
        out_shape=jax.ShapeDtypeStruct((rows, width), jnp.bfloat16),
        input_output_aliases={5 + len(grads): 0} if earlier else {},
        compiler_params=pltpu.CompilerParams(vmem_limit_bytes=GRANT),
        cost_estimate=estimate(scored * 2 * 1280, scored),
        name="attend_backward",
    )(mask, slopes, qkv, lse, mixed, *grads, *earlier)


def head_columns_kernel(at_ref, in_ref, out_ref):
    for t in range(3):

        @pl.when(pl.program_id(0) == t)
        def _():
            for pair in range(in_ref.shape[1] // PAIR):
                at = (pair * 3 + t) * PAIR
                out_ref[:, at : at + PAIR] = in_ref[:, pair * PAIR : (pair + 1) * PAIR]


def up_kernel(rows_ref, weight_ref, bias_ref, active_ref, slope_ref, *, chunk):
    rows = rows_ref[...]
    for at in range(0, weight_ref.shape[1], chunk):
        columns = slice(at, at + chunk)
        hidden = contract(rows, weight_ref[:, columns]) + bias_ref[:, columns]
        below = 0.5 + 0.5 * lax.erf(hidden * 2**-0.5)
        active_ref[:, columns] = (hidden * below).astype(active_ref.dtype)
        slope_ref[:, columns] = below + hidden * ((2 * math.pi) ** -0.5 * jnp.exp(-0.5 * hidden * hidden))


def hidden_grad_kernel(rows_ref, weight_ref, slope_ref, grad_ref, sum_ref, *, chunk):
    rows = rows_ref[...]
    starting = pl.program_id(0) == 0
    for at in range(0, weight_ref.shape[0], chunk):
        columns = slice(at, at + chunk)
        grad = contract_last(rows, weight_ref[columns, :]) * slope_ref[:, columns]
        grad = grad.astype(grad_ref.dtype)
        grad_ref[:, columns] = grad
        part = jnp.sum(grad.astype(jnp.float32), axis=0, keepdims=True)
        sum_ref[:, columns] = jnp.where(starting, part, sum_ref[:, columns] + part)


TILE = 256


def up_and_bend(rows, weight, bias):
    count, depth = rows.shape
    width = weight.shape[1]
    tile = pl.BlockSpec((TILE, width), lambda i: (i, 0))
    return pl.pallas_call(
        partial(up_kernel, chunk=512),
        grid=(count // TILE,),
        in_specs=[
            pl.BlockSpec((TILE, depth), lambda i: (i, 0)),
            pl.BlockSpec((depth, width), lambda i: (0, 0), pipeline_mode=pl.Buffered(1)),
            pl.BlockSpec((1, width), lambda i: (0, 0)),
        ],
        out_specs=[tile, tile],
        out_shape=[
            jax.ShapeDtypeStruct((count, width), jnp.bfloat16),
            jax.ShapeDtypeStruct((count, width), jnp.float32),
        ],
        compiler_params=pltpu.CompilerParams(vmem_limit_bytes=GRANT),
        cost_estimate=estimate(count * depth * width * 4, 2 * count * width),
        name="up_and_bend",
    )(rows, weight, bias)


def hidden_gradient(rows, weight, slope, start, count):
    depth = rows.shape[1]
    width = weight.shape[0]
    first = start // TILE
    line = pl.BlockSpec((1, width), lambda i: (0, 0))
    return pl.pallas_call(
        partial(hidden_grad_kernel, chunk=512),
        grid=(count // TILE,),
        in_specs=[
            pl.BlockSpec((TILE, depth), lambda i: (i + first, 0)),
            pl.BlockSpec((width, depth), lambda i: (0, 0), pipeline_mode=pl.Buffered(1)),
            pl.BlockSpec((TILE, width), lambda i: (i + first, 0)),
        ],
        out_specs=[pl.BlockSpec((TILE, width), lambda i: (i, 0)), line],
        out_shape=[
            jax.ShapeDtypeStruct((count, width), jnp.bfloat16),
            jax.ShapeDtypeStruct((1, width), jnp.float32),
        ],
        compiler_params=pltpu.CompilerParams(vmem_limit_bytes=GRANT),
        cost_estimate=estimate(count * depth * width * 3, 0),
        name="hidden_gradient",
    )(rows, weight, slope)


def product_kernel(rows_ref, weight_ref, out_ref):
    out_ref[...] = contract(rows_ref[...], weight_ref[...]).astype(out_ref.dtype)


def product_of(rows, weight, count):
    depth, width = weight.shape
    return pl.pallas_call(
        product_kernel,
        grid=(count // TILE,),
        in_specs=[
            pl.BlockSpec((TILE, depth), lambda i: (i, 0)),
            pl.BlockSpec((depth, width), lambda i: (0, 0), pipeline_mode=pl.Buffered(1)),
        ],
        out_specs=pl.BlockSpec((TILE, width), lambda i: (i, 0)),
        out_shape=jax.ShapeDtypeStruct((count, width), jnp.bfloat16),
        compiler_params=pltpu.CompilerParams(vmem_limit_bytes=GRANT),
        cost_estimate=estimate(2 * count * depth * width, 0),
        name="product",
    )(rows, weight)


def mixed_grad_kernel(rows_ref, weight_ref, out_ref):
    out_ref[...] = contract_last(rows_ref[...], weight_ref[...]).astype(out_ref.dtype)


def mixed_gradient(rows, weight, slab):
    count, depth = rows.shape
    width = weight.shape[0]
    return pl.pallas_call(
        mixed_grad_kernel,
        grid=(width // slab,),
        in_specs=[
            pl.BlockSpec((count, depth), lambda i: (0, 0), pipeline_mode=pl.Buffered(1)),
            pl.BlockSpec((slab, depth), lambda i: (i, 0)),
        ],
        out_specs=pl.BlockSpec((count, slab), lambda i: (0, i)),
        out_shape=jax.ShapeDtypeStruct((count, width), jnp.bfloat16),
        compiler_params=pltpu.CompilerParams(vmem_limit_bytes=GRANT),
        cost_estimate=estimate(2 * count * depth * width, 0),
        name="mixed_gradient",
    )(rows, weight)


def norm_back_kernel(own_ref, values_ref, average_ref, scale_ref, base_ref, gain_ref, *refs, parts):
    came, (low_ref, wide_ref, sums_ref) = refs[:parts], refs[parts:]
    wide = jnp.float32
    step = pl.program_id(0)

    @pl.when(step == 0)
    def _():
        sums_ref[...] = jnp.zeros_like(sums_ref)

    def make(came):
        grad = own_ref[...].astype(wide)
        for part in came:
            grad = grad + part[...].astype(wide)
        scale = scale_ref[...]
        normal = (values_ref[...].astype(wide) - average_ref[...]) * scale
        gained = grad * gain_ref[...]
        along = jnp.mean(gained * normal, axis=-1, keepdims=True)
        across = jnp.mean(gained, axis=-1, keepdims=True)
        made = base_ref[...].astype(wide) + scale * (gained - across - normal * along)
        low = made.astype(low_ref.dtype)
        low_ref[...] = low
        wide_ref[...] = made
        for at, part in enumerate((grad * normal, grad, low.astype(wide))):
            sums_ref[8 * at : 8 * at + 8, :] += jnp.sum(part.reshape(-1, 8, part.shape[1]), axis=0)

    if not came:
        make(())
        return
    upper = step < pl.num_programs(0) // 2
    pl.when(upper)(lambda: make(came[0::2]))
    pl.when(jnp.logical_not(upper))(lambda: make(came[1::2]))


def norm_back(rest, values, average, scale, base, gain, came):
    rows, width = values.shape
    steps = 8
    half = steps // 2
    came = list(came or ())
    count = rows // steps
    tile = pl.BlockSpec((count, width), lambda i: (i, 0))
    thin = pl.BlockSpec((count, 1), lambda i: (i, 0))
    top = pl.BlockSpec((count, width), lambda i: (jnp.minimum(i, half - 1), 0))
    bottom = pl.BlockSpec((count, width), lambda i: (jnp.maximum(i - half, 0), 0))
    low, full, sums = pl.pallas_call(
        partial(norm_back_kernel, parts=len(came)),
        grid=(steps,),
        in_specs=[tile, tile, thin, thin, tile, pl.BlockSpec((1, width), lambda i: (0, 0))]
        + [top, bottom] * (len(came) // 2),
        out_specs=[tile, tile, pl.BlockSpec((24, width), lambda i: (0, 0))],
        out_shape=[
            jax.ShapeDtypeStruct((rows, width), jnp.bfloat16),
            jax.ShapeDtypeStruct((rows, width), jnp.float32),
            jax.ShapeDtypeStruct((24, width), jnp.float32),
        ],
        compiler_params=pltpu.CompilerParams(vmem_limit_bytes=GRANT),
        cost_estimate=estimate(30 * rows * width, rows),
        name="norm_back",
    )(rest, values, average, scale, base, gain[None], *came)
    return low, full, jnp.sum(sums.reshape(3, 8, width), axis=1)


def outer_kernel(left_ref, right_ref, out_ref, *, chunk):
    left = left_ref[...]
    shards = out_ref.shape[0]
    for at in range(0, out_ref.shape[3], chunk):
        columns = slice(at, at + chunk)
        made = contract_first(left, right_ref[:, columns]).astype(out_ref.dtype)
        out_ref[:, 0, :, columns] = made.reshape(shards, -1, made.shape[1])


def outer(left, right, groups, shards, part_of=(0, 1)):
    at, parts = part_of
    tokens, rows = left.shape
    width = right.shape[1] // parts
    part = rows // groups
    made = pl.pallas_call(
        partial(outer_kernel, chunk=next(c for c in (512, 384, 256, 128) if width % c == 0)),
        grid=(groups,),
        in_specs=[
            pl.BlockSpec((tokens, part), lambda i: (0, i)),
            pl.BlockSpec((tokens, width), lambda i: (0, at), pipeline_mode=pl.Buffered(1)),
        ],
        out_specs=pl.BlockSpec((shards, 1, part // shards, width), lambda i: (0, i, 0, 0)),
        out_shape=jax.ShapeDtypeStruct((shards, groups, part // shards, width), jnp.bfloat16),
        compiler_params=pltpu.CompilerParams(vmem_limit_bytes=GRANT),
        cost_estimate=estimate(2 * tokens * rows * width, 0),
        name="outer",
    )(left, right)
    return made.reshape(rows, width)


def swap(values, bit):
    return lax.ppermute(values, "seq", [(i, i ^ bit) for i in range(4)])


def by_index(parts, me):
    if len(parts) != 4:
        return parts
    odd, upper = (me & 1) == 1, (me & 2) == 2
    a, b, c, d = parts
    a, b, c, d = (
        jnp.where(odd, b, a),
        jnp.where(odd, a, b),
        jnp.where(odd, d, c),
        jnp.where(odd, c, d),
    )
    return [jnp.where(upper, c, a), jnp.where(upper, d, b), jnp.where(upper, a, c), jnp.where(upper, b, d)]


def exchange(slots):
    if lax.axis_size("seq") != 4:
        return list(lax.all_to_all(jnp.stack(slots), "seq", split_axis=0, concat_axis=0, tiled=True))
    return [slots[0]] + [swap(slots[j], j) for j in (1, 2, 3)]


def gate(values, *before):
    return lax.optimization_barrier((values, *before))[0]


class Order:
    def __init__(self):
        self.pending = []

    def after(self, *values):
        self.pending += values

    def __call__(self, operation, *operands):
        if self.pending:
            count = len(operands)
            operands = lax.optimization_barrier((*operands, *self.pending))[:count]
        made = operation(*operands)
        self.pending = jax.tree.leaves(made)
        return made

    def gather(self, rows):
        if lax.axis_size("seq") != 4:
            return lax.all_gather(jnp.concatenate(rows, axis=0), "seq", axis=0, tiled=True), None
        top, bottom = rows
        return rows, (swap(bottom, 1), swap(top, 2), swap(top, 1), swap(bottom, 2))

    def fill(self, begun):
        rows, came = begun
        if came is None:
            return rows
        first_bottom, second_top, first_top, second_bottom = came
        room = jnp.zeros_like(rows[0])
        parts = (*rows, first_top, first_bottom, second_top, second_bottom, room, room)
        return self(lambda *parts: jnp.concatenate(parts, axis=0), *parts)

    def complete(self, made, pieces):
        if not isinstance(pieces, list):
            return made
        rows = pieces[-1].shape[0]

        def put(before, first, second):
            before = lax.dynamic_update_slice_in_dim(before, first, 6 * rows, axis=0)
            return lax.dynamic_update_slice_in_dim(before, second, 7 * rows, axis=0)

        return self(put, made, *pieces[-2:])

    def pass_on(self, begun, *before):
        rows, came = begun
        if came is None:
            return rows
        first_bottom, second_top, first_top, second_bottom = came
        self.after(*came)
        if before:
            second_top, first_bottom = gate((second_top, first_bottom), *before)
        far = [swap(second_top, 1), swap(first_bottom, 2)]
        return [*rows, first_top, first_bottom, second_top, second_bottom, *far]

    def halves(self, product, rows):
        def cut(values):
            made = product(values)
            half = made.shape[0] // 2
            return made[:half], made[half:]

        return self(cut, rows)

    def add_far(self, made, far, direct, *before, at=None):
        wide = jnp.float32
        half = far[0].shape[0]
        start = made.shape[0] - 4 * half if at is None else at

        def add(made, top, bottom):
            at = start
            first = (made[at + half : at + 2 * half].astype(wide) + bottom.astype(wide)).astype(made.dtype)
            second = (made[at + 2 * half : at + 3 * half].astype(wide) + top.astype(wide)).astype(made.dtype)
            if direct is None:
                first = jnp.concatenate([made[at : at + half], first], axis=0)
                second = jnp.concatenate([second, made[at + 3 * half : at + 4 * half]], axis=0)
            return first, second

        first, second = self(add, made, *far)
        if before:
            first, second = gate((first, second), *before)
        first, second = swap(first, 1), swap(second, 2)
        return (first, second) if direct is None else (direct[0], first, second, direct[1])


def swap_far(halves):
    return swap(halves[0], 1), swap(halves[1], 2)


def swap_direct(made, half):
    at = made.shape[0] - 4 * half
    return swap(made[at : at + half], 1), swap(made[at + 3 * half :], 2)


def summed(own, came):
    wide = jnp.float32
    own = own.astype(wide)
    return sum((part.astype(wide) for part in came), own)


def whole(parts):
    return jnp.concatenate(parts, axis=0) if isinstance(parts, list) else parts


def total_stages():
    stages = []
    for axis in ("fsdp", "seq"):
        count, bit = lax.axis_size(axis), 1
        bits = count.bit_length() - 1
        while bit < count:
            stages.append((axis, [bit] if bits % 2 else [bit, 2 * bit, 3 * bit]))
            bit <<= 1 if bits % 2 else 2
            bits -= bits % 2
    return stages


def local(
    tokens,
    cotangent,
    w_qkv,
    qv_bias,
    w_out,
    out_bias,
    ln1_gain,
    ln1_shift,
    ln2_gain,
    ln2_shift,
    w_up,
    up_bias,
    w_down,
    down_bias,
):
    seq_count, local_len, model_width = tokens.shape
    groups, shards = lax.axis_size("seq"), lax.axis_size("fsdp")
    me = lax.axis_index("seq")
    square = groups == 4
    heads_here = HEADS // groups
    slab = heads_here * HEAD_DIM
    pairs = slab // PAIR
    hidden_width = w_up.shape[1]
    hidden_slab = hidden_width // groups
    rows_here = seq_count * local_len
    low, wide = jnp.bfloat16, jnp.float32
    mask = jnp.reshape(me if square else jnp.zeros_like(me), (1,)).astype(jnp.int32)
    head_index = me * heads_here + jnp.arange(1, heads_here + 1, dtype=jnp.int32)
    slopes = 2.0 ** (-8.0 * head_index.astype(wide) / HEADS)

    def head_columns(values):
        rows = values.shape[0]
        return pl.pallas_call(
            head_columns_kernel,
            grid_spec=pltpu.PrefetchScalarGridSpec(
                num_scalar_prefetch=1,
                grid=(3,),
                in_specs=[pl.BlockSpec((rows, slab), lambda t, at: (0, t * groups + at[0]))],
                out_specs=pl.BlockSpec((rows, 3 * slab), lambda t, at: (0, 0)),
            ),
            out_shape=jax.ShapeDtypeStruct((rows, 3 * slab), values.dtype),
            name="head_columns",
        )(jnp.reshape(me, (1,)).astype(jnp.int32), values)

    def own_slab(values, axis):
        width = values.shape[axis] // groups
        return lax.dynamic_slice_in_dim(values, me * width, width, axis=axis)

    order = Order()
    x_low = tokens.reshape(rows_here, model_width)
    x = x_low.astype(wide)
    dz_low = cotangent.reshape(rows_here, model_width)
    qkv_slab = lax.all_gather(head_columns(w_qkv), "fsdp", axis=0, tiled=True)
    qkv_bias = head_columns(jnp.concatenate([qv_bias[0], jnp.zeros_like(qv_bias[0]), qv_bias[1]])[None])
    up_bias_slab = own_slab(up_bias, 0)

    first_norm, *first_stats = layer_norm(x, ln1_gain, ln1_shift)
    half = rows_here // 2

    def halves_of(values):
        return values[:half].astype(low), values[half:].astype(low)

    normed = order.gather(order(halves_of, first_norm))
    normed = order.pass_on(normed)
    full_out = lax.all_gather(w_out, "fsdp", axis=0, tiled=True)
    up_slab = lax.all_gather(own_slab(gate(w_up, normed[0]) if square else w_up, 1), "fsdp", axis=0, tiled=True)
    down_slab = lax.all_gather(own_slab(gate(w_down, normed[0]) if square else w_down, 0), "fsdp", axis=1, tiled=True)
    normed = whole(normed)
    upstream = order.gather(halves_of(gate(dz_low, normed)))
    qkv = order(lambda rows: (contract(rows, qkv_slab) + qkv_bias).astype(low), normed)
    attended, log_totals = order(lambda rows: attend_forward(mask, slopes, rows, seq_count, local_len), qkv)
    if square:
        attended = gate(attended, *upstream[1])
    mixed_slots = exchange([attended[j * rows_here : (j + 1) * rows_here] for j in range(groups)])
    mixed_rows = jnp.concatenate(by_index(mixed_slots, me), axis=1)
    mixed_slots = jnp.concatenate(mixed_slots, axis=1)

    def pair_swap(values):
        return lax.ppermute(values, "fsdp", [(i, i ^ 1) for i in range(shards)])

    parity = lax.axis_index("fsdp") & 1
    out_rows = model_width // (groups * shards)

    def pair_halves(values):
        halves = values.reshape(rows_here, -1, 2, out_rows)
        return tuple(
            lax.dynamic_index_in_dim(halves, index, axis=2, keepdims=False).reshape(rows_here, -1)
            for index in (parity, 1 - parity)
        )

    middle = order(lambda rows: x + (contract(rows, full_out) + out_bias), mixed_rows)
    second_norm, *second_stats = layer_norm(middle, ln2_gain, ln2_shift)
    second = order.gather(order(halves_of, second_norm))
    mine, theirs = order(pair_halves, mixed_slots)
    upstream_made = order.fill(upstream)
    theirs = pair_swap(theirs)
    dz_sum = order(lambda values: jnp.sum(values.astype(wide), axis=0), dz_low)
    mixed_half = order(lambda *parts: jnp.concatenate(parts, axis=0), mine, theirs)
    second = whole(order.pass_on(second, mixed_half))
    upstream = order.pass_on(upstream, second)
    active, slope = order(lambda rows: up_and_bend(rows, up_slab, up_bias_slab[None]), second)
    upstream = order.complete(upstream_made, upstream)

    def slab_product(left, right, part_of=(0, 1)):
        return order(lambda rows, others: outer(rows, others, groups, shards, part_of), left, right)

    def slab_sum(made):
        return lax.psum_scatter(made, "fsdp", scatter_dimension=0, tiled=True)

    def slabs_of_rows(values):
        return lax.all_to_all(
            values.reshape(groups, -1, values.shape[1]), "seq", split_axis=0, concat_axis=0, tiled=True
        )

    down_sum = slab_sum(slab_product(upstream, active))
    count = rows_here

    def slots(product, start, stop):
        return lambda values: product(values[start * count : stop * count])

    def to_second(rows):
        return contract_last(rows, up_slab).astype(low)

    def to_result(rows):
        return contract(rows, down_slab).astype(low)

    def to_normed(rows):
        return contract_last(rows, qkv_slab).astype(low)

    def scatter(product, rows):
        return lax.psum_scatter(order(product, rows), "seq", scatter_dimension=0, tiled=True)

    hidden_grad, hidden_sum = order(lambda rows: hidden_gradient(rows, down_slab, slope, 0, groups * count), upstream)
    if square:
        far = swap_far(order.halves(slots(to_second, 3, 4), hidden_grad))
        rest = order(slots(to_second, 0, 3), hidden_grad)
        second_own = rest
        direct = swap_direct(rest, half)
        came = order.add_far(rest, far, direct)
        result_far = order.halves(slots(to_result, 3, 4), active)
        up_sum = slab_sum(gate(slab_product(second, hidden_grad), *came))
        result_far = swap_far(gate(result_far, *came))
    else:
        second_own, came = scatter(to_second, hidden_grad), ()
        up_sum = slab_sum(slab_product(second, hidden_grad))
    branch_grad, middle_grad, middle_sums = order(
        lambda own, *came: norm_back(own, middle, *second_stats, dz_low, ln2_gain, came), second_own, *came
    )

    def column_sum(values):
        return jnp.sum(values.astype(wide), axis=0)

    hidden_sum = lax.dynamic_update_slice_in_dim(
        jnp.zeros((hidden_width,), wide), hidden_sum[0], me * hidden_slab, axis=0
    )
    early = [middle_sums[2], middle_sums[0], middle_sums[1], hidden_sum, dz_sum]
    mixed_grad = order(lambda rows: mixed_gradient(rows, full_out, slab), branch_grad)
    mixed_grad = exchange(by_index([mixed_grad[:, j * slab : (j + 1) * slab] for j in range(groups)], me))
    if square:
        result_rest = order(lambda rows: product_of(rows, down_slab, 3 * count), active)
        order.after(*mixed_grad)
        result_came = order.add_far(result_rest, result_far, None)
    attention = (mask, slopes, qkv, log_totals, attended)
    order.after(down_sum)
    begun = order(
        lambda *grads: attend_backward(*attention, grads, seq_count, local_len, 0, pairs // 2), *mixed_grad
    )
    branch_other = pair_swap(gate(branch_grad, result_rest) if square else branch_grad)
    branch_pair = jnp.concatenate([branch_grad, branch_other], axis=0)
    out_sum = order(lambda columns: outer(columns, branch_pair, groups, 1), mixed_half)
    if square:
        part = out_sum.shape[0] // 4
        out_far = out_sum[3 * part : 3 * part + part // 2], out_sum[3 * part + part // 2 :]
        out_far = swap_far(out_far)
    first_sum = slab_product(normed, begun, (0, 2))
    if square:
        first_sum = gate(first_sum, *result_came, *out_far)
        order.after(*result_came)
        out_came = order.add_far(out_sum, out_far, None, at=part)
    first_sum = slab_sum(first_sum)
    qkv_grad = order(
        lambda begun, *grads: attend_backward(
            *attention, grads, seq_count, local_len, pairs // 2, pairs, begun
        ),
        begun,
        *mixed_grad,
    )
    if not square:
        out_sum = lax.psum_scatter(out_sum, "seq", scatter_dimension=0, tiled=True)
    order.after(up_sum)
    if square:
        far = swap_far(order.halves(slots(to_normed, 3, 4), qkv_grad))
        order.after(first_sum)
        near = order(slots(to_normed, 1, 3), qkv_grad)
        direct = swap_direct(near, half)
        qkv_column_sum = order(column_sum, qkv_grad)
        order.after(*out_came)
        out_sum = order(lambda own, *came: summed(own[:part], came).astype(low), out_sum, *out_came)
    out_sum = out_sum.reshape(-1, 1, out_rows, model_width)
    zero = jnp.zeros_like(out_sum)
    out_sum = jnp.concatenate(
        [jnp.where(parity == 0, out_sum, zero), jnp.where(parity == 1, out_sum, zero)], axis=1
    ).reshape(-1, model_width)
    if square:
        out_sum = gate(out_sum, *far)
    grad_w_out = lax.psum_scatter(out_sum, "fsdp", scatter_dimension=0, tiled=True).astype(wide)
    second_sum = slab_product(normed, qkv_grad, (1, 2))
    if square:
        second_sum = slab_sum(gate(second_sum, *far, *direct))
        came = order.add_far(near, far, direct)
        order.after(grad_w_out)
        normed_own = order(slots(to_normed, 0, 1), qkv_grad)
    else:
        second_sum = slab_sum(second_sum)
        qkv_column_sum = order(column_sum, qkv_grad)
        normed_own, came = scatter(to_normed, qkv_grad), ()
    grad_tokens, _, input_sums = order(
        lambda own, *came: norm_back(own, x_low, *first_stats, middle_grad, ln1_gain, came), normed_own, *came
    )
    grad_tokens = grad_tokens.reshape(tokens.shape)
    three = jnp.concatenate([down_sum, up_sum, first_sum], axis=1)
    three = slabs_of_rows(gate(three, *came, normed_own))
    down_slabs, up_slabs, first_slabs = jnp.split(three, [hidden_slab, 2 * hidden_slab], axis=2)
    second_slabs = slabs_of_rows(second_sum)

    def rows_of(slabs):
        return jnp.swapaxes(slabs, 0, 1).astype(wide)

    grad_w_down = rows_of(down_slabs).reshape(-1, hidden_width).T
    grad_w_up = rows_of(up_slabs).reshape(-1, hidden_width)
    grad_w_qkv = [
        rows_of(part).reshape(-1, groups, pairs // 2, 3, PAIR) for part in (first_slabs, second_slabs)
    ]
    grad_w_qkv = jnp.concatenate(grad_w_qkv, axis=2)
    grad_w_qkv = jnp.transpose(grad_w_qkv, (0, 3, 1, 2, 4)).reshape(-1, 3 * model_width)

    head_sum = jnp.transpose(qkv_column_sum.reshape(pairs, 3, PAIR), (1, 0, 2)).reshape(3, slab)
    qv_sum = lax.dynamic_update_slice_in_dim(
        jnp.zeros((2, model_width), wide), head_sum[0::2], me * slab, axis=1
    )
    late = [qv_sum.reshape(-1), input_sums[0], input_sums[1]]
    sums = order(lambda *parts: jnp.concatenate(parts).reshape(-1, PAIR), *early, *late)
    stages = total_stages()
    for axis, masks in stages:
        others = range(lax.axis_size(axis))
        came = [lax.ppermute(sums, axis, [(i, i ^ mask) for i in others]) for mask in masks]
        if (axis, masks) == stages[1]:
            order.after(three)
        if (axis, masks) == stages[-1]:
            order.after(second_slabs)
        sums = order(lambda *parts: sum(parts[1:], parts[0]), sums, *came)
        if (axis, masks) != stages[0]:
            continue
        if square:
            result = order(
                lambda rest, *came: (middle + (summed(rest[:count], came) + down_bias)).astype(low),
                result_rest,
                *result_came,
            )
        else:
            result = (middle + (scatter(to_result, active).astype(wide) + down_bias)).astype(low)
        result = result.reshape(tokens.shape)
    sums = sums.reshape(-1)

    def cut(at, count):
        return sums[at * model_width : (at + count) * model_width]

    ratio = hidden_width // model_width
    return (
        result,
        grad_tokens,
        grad_w_qkv,
        cut(4 + ratio, 2).reshape(2, model_width),
        grad_w_out,
        cut(0, 1),
        cut(6 + ratio, 1),
        cut(7 + ratio, 1),
        cut(1, 1),
        cut(2, 1),
        grad_w_up,
        cut(3, ratio),
        grad_w_down,
        cut(3 + ratio, 1),
    )


def solution(mesh):
    return jax.shard_map(
        local,
        mesh=mesh,
        in_specs=(
            P("fsdp", "seq", None),
            P("fsdp", "seq", None),
            P("fsdp", None),
            P(),
            P("fsdp", None),
            P(),
            P(),
            P(),
            P(),
            P(),
            P("fsdp", None),
            P(),
            P(None, "fsdp"),
            P(),
        ),
        out_specs=(
            P("fsdp", "seq", None),
            P("fsdp", "seq", None),
            P(("seq", "fsdp"), None),
            P(),
            P(("seq", "fsdp"), None),
            P(),
            P(),
            P(),
            P(),
            P(),
            P(("seq", "fsdp"), None),
            P(),
            P(None, ("seq", "fsdp")),
            P(),
        ),
        check_vma=False,
    )
```

```python
import math
from functools import partial

import jax
import jax.numpy as jnp
from jax import lax
from jax.experimental import pallas as pl
from jax.experimental.pallas import tpu as pltpu
from jax.sharding import PartitionSpec as P

HEADS = 32
HEAD_DIM = 64
BLOCK = 256
PAIR = 2 * HEAD_DIM
GRANT = 58 * 2**20


def estimate(flops, transcendentals=0):
    return pl.CostEstimate(flops=flops // 4, bytes_accessed=flops // 4096, transcendentals=transcendentals // 4)


def layer_norm(token_rows, gain_vec, shift_vec):
    average = jnp.mean(token_rows, axis=-1, keepdims=True)
    centred = token_rows - average
    spread = jnp.mean(centred * centred, axis=-1, keepdims=True)
    scale = lax.rsqrt(spread + 1e-05)
    return centred * scale * gain_vec + shift_vec, average, scale


def contract(left_side, right_side):
    return lax.dot_general(
        left_side, right_side, (((1,), (0,)), ((), ())), preferred_element_type=jnp.float32
    )


def contract_last(left_side, right_side):
    return lax.dot_general(
        left_side, right_side, (((1,), (1,)), ((), ())), preferred_element_type=jnp.float32
    )


def contract_first(left_side, right_side):
    return lax.dot_general(
        left_side, right_side, (((0,), (0,)), ((), ())), preferred_element_type=jnp.float32
    )


def row_pieces(mask, sequence, block, seqs, local):
    per = BLOCK // local
    return [
        pl.ds(pl.multiple_of((((block * per + r) ^ mask) * seqs + sequence) * local, local), local)
        for r in range(per)
    ]


def load_rows(ref, pieces, columns):
    parts = [ref[piece, columns] for piece in pieces]
    return parts[0] if len(parts) == 1 else jnp.concatenate(parts, axis=0)


def store_rows(ref, pieces, columns, values):
    local = values.shape[0] // len(pieces)
    for r, piece in enumerate(pieces):
        ref[piece, columns] = values[r * local : (r + 1) * local]


Q_COLUMNS, K_COLUMNS, V_COLUMNS = (slice(t * PAIR, (t + 1) * PAIR) for t in range(3))


def attend_forward_kernel(mask_ref, slope_ref, qkv_ref, mixed_ref, lse_ref, *, blocks, seqs, local):
    pair, sequence = pl.program_id(0), pl.program_id(1)
    mask = mask_ref[0]
    lane = lax.broadcasted_iota(jnp.int32, (BLOCK, PAIR), 1)
    row = lax.broadcasted_iota(jnp.int32, (BLOCK, BLOCK), 0)
    column = lax.broadcasted_iota(jnp.int32, (BLOCK, BLOCK), 1)
    gap = (row - column).astype(jnp.float32)
    pieces = [row_pieces(mask, sequence, block, seqs, local) for block in range(blocks)]

    for i in range(blocks):
        q_pair = load_rows(qkv_ref, pieces[i], Q_COLUMNS)
        outs, lses = [], []
        for head in range(2):
            slope = slope_ref[pair * 2 + head]
            mine = (lane >= head * HEAD_DIM) & (lane < (head + 1) * HEAD_DIM)
            q = jnp.where(mine, q_pair, jnp.zeros_like(q_pair)) * jnp.bfloat16(HEAD_DIM**-0.5)
            parts, highest = [], None
            for j in range(i + 1):
                scores = contract_last(q, load_rows(qkv_ref, pieces[j], K_COLUMNS))
                distance = jnp.abs(gap) if i == j else gap + float(BLOCK * (i - j))
                scores = scores - slope * distance
                parts.append(scores)
                top = jnp.max(scores, axis=-1, keepdims=True)
                highest = top if highest is None else jnp.maximum(highest, top)
            total, out = None, None
            for j in range(i + 1):
                weights = jnp.exp(parts[j] - highest)
                part = jnp.sum(weights, axis=-1, keepdims=True)
                mixed = contract(weights.astype(jnp.bfloat16), load_rows(qkv_ref, pieces[j], V_COLUMNS))
                total = part if total is None else total + part
                out = mixed if out is None else out + mixed
            outs.append(out / total)
            lses.append(highest + jnp.log(total))
        first = lane < HEAD_DIM
        everything = slice(0, PAIR)
        store_rows(
            mixed_ref, pieces[i], everything, jnp.where(first, outs[0], outs[1]).astype(mixed_ref.dtype)
        )
        store_rows(lse_ref, pieces[i], everything, jnp.where(first, lses[0], lses[1]))


def attend_backward_kernel(
    mask_ref, slope_ref, qkv_ref, lse_ref, mixed_ref, *rest, blocks, seqs, local, start, grads
):
    out_ref, dq_ref, dk_ref, dv_ref, grad_ref = rest[-5:]
    pair, sequence = pl.program_id(0) + start, pl.program_id(1)
    mask = mask_ref[0]
    lane = lax.broadcasted_iota(jnp.int32, (BLOCK, PAIR), 1)
    key = lax.broadcasted_iota(jnp.int32, (BLOCK, BLOCK), 0)
    query = lax.broadcasted_iota(jnp.int32, (BLOCK, BLOCK), 1)
    gap = (query - key).astype(jnp.float32)
    pieces = [row_pieces(mask, sequence, block, seqs, local) for block in range(blocks)]
    everything = slice(0, PAIR)

    @pl.when(sequence == 0)
    def _():
        at = 0
        for part in rest[:grads]:
            grad_ref[at : at + part.shape[0], :] = part[...]
            at += part.shape[0]

    for i in range(blocks):
        q_pair = load_rows(qkv_ref, pieces[i], Q_COLUMNS)
        up_pair = load_rows(grad_ref, pieces[i], everything)
        mixed_pair = load_rows(mixed_ref, pieces[i], everything)
        inner_all = (up_pair.astype(jnp.float32) * mixed_pair.astype(jnp.float32)).T
        lse_all = load_rows(lse_ref, pieces[i], everything).T
        dq = None
        for head in range(2):
            slope = slope_ref[pair * 2 + head]
            mine = (lane >= head * HEAD_DIM) & (lane < (head + 1) * HEAD_DIM)
            zero = jnp.zeros_like(q_pair)
            q = jnp.where(mine, q_pair, zero) * jnp.bfloat16(HEAD_DIM**-0.5)
            up = jnp.where(mine, up_pair, zero)
            inner = jnp.sum(inner_all[head * HEAD_DIM : (head + 1) * HEAD_DIM], axis=0, keepdims=True)
            lse = lse_all[head * HEAD_DIM : head * HEAD_DIM + 1]
            for j in range(i + 1):
                k_pair = load_rows(qkv_ref, pieces[j], K_COLUMNS)
                distance = jnp.abs(gap) if i == j else gap + float(BLOCK * (i - j))
                probs = jnp.exp(contract_last(k_pair, q) - slope * distance - lse)
                prob_grad = contract_last(load_rows(qkv_ref, pieces[j], V_COLUMNS), up)
                score_grad = (probs * (prob_grad - inner)).astype(jnp.bfloat16)
                dv = contract(probs.astype(jnp.bfloat16), up)
                dk = contract(score_grad, q)
                part = contract_first(score_grad, jnp.where(mine, k_pair, zero))
                dq = part if dq is None else dq + part
                if i == j and head == 0:
                    dv_ref[j] = dv
                    dk_ref[j] = dk
                else:
                    dv_ref[j] += dv
                    dk_ref[j] += dk
        dq_ref[i] = dq
    for i in range(blocks):
        store_rows(out_ref, pieces[i], Q_COLUMNS, (dq_ref[i] * HEAD_DIM**-0.5).astype(out_ref.dtype))
        store_rows(out_ref, pieces[i], K_COLUMNS, dk_ref[i].astype(out_ref.dtype))
        store_rows(out_ref, pieces[i], V_COLUMNS, dv_ref[i].astype(out_ref.dtype))


def attend_forward(mask, slopes, qkv, seqs, local):
    rows, width = qkv.shape
    pairs, blocks = width // (3 * PAIR), rows // seqs // BLOCK
    scored = pairs * seqs * blocks * (blocks + 1) * BLOCK * BLOCK
    return pl.pallas_call(
        partial(attend_forward_kernel, blocks=blocks, seqs=seqs, local=local),
        grid_spec=pltpu.PrefetchScalarGridSpec(
            num_scalar_prefetch=2,
            grid=(pairs, seqs),
            in_specs=[pl.BlockSpec((rows, 3 * PAIR), lambda p, *_: (0, p))],
            out_specs=[pl.BlockSpec((rows, PAIR), lambda p, *_: (0, p))] * 2,
        ),
        out_shape=[
            jax.ShapeDtypeStruct((rows, pairs * PAIR), jnp.bfloat16),
            jax.ShapeDtypeStruct((rows, pairs * PAIR), jnp.float32),
        ],
        compiler_params=pltpu.CompilerParams(vmem_limit_bytes=GRANT),
        cost_estimate=estimate(scored * 2 * 512, scored),
        name="attend_forward",
    )(mask, slopes, qkv)


def attend_backward(mask, slopes, qkv, lse, mixed, grads, seqs, local, start, stop, begun=None):
    rows, width = qkv.shape
    blocks = rows // seqs // BLOCK
    scored = (stop - start) * seqs * blocks * (blocks + 1) * BLOCK * BLOCK
    narrow = pl.BlockSpec((rows, PAIR), lambda p, *_: (0, p + start))
    wide = pl.BlockSpec((rows, 3 * PAIR), lambda p, *_: (0, p + start))
    earlier = [] if begun is None else [begun]
    return pl.pallas_call(
        partial(
            attend_backward_kernel, blocks=blocks, seqs=seqs, local=local, start=start, grads=len(grads)
        ),
        grid_spec=pltpu.PrefetchScalarGridSpec(
            num_scalar_prefetch=2,
            grid=(stop - start, seqs),
            in_specs=[wide, narrow, narrow]
            + [pl.BlockSpec((grad.shape[0], PAIR), lambda p, *_: (0, p + start)) for grad in grads]
            + [pl.BlockSpec(memory_space=pl.ANY)] * len(earlier),
            out_specs=wide,
            scratch_shapes=[pltpu.VMEM((blocks, BLOCK, PAIR), jnp.float32)] * 3
            + [pltpu.VMEM((rows, PAIR), jnp.bfloat16)],
        ),
        out_shape=jax.ShapeDtypeStruct((rows, width), jnp.bfloat16),
        input_output_aliases={5 + len(grads): 0} if earlier else {},
        compiler_params=pltpu.CompilerParams(vmem_limit_bytes=GRANT),
        cost_estimate=estimate(scored * 2 * 1280, scored),
        name="attend_backward",
    )(mask, slopes, qkv, lse, mixed, *grads, *earlier)


def head_columns_kernel(at_ref, in_ref, out_ref):
    for t in range(3):

        @pl.when(pl.program_id(0) == t)
        def _():
            for pair in range(in_ref.shape[1] // PAIR):
                at = (pair * 3 + t) * PAIR
                out_ref[:, at : at + PAIR] = in_ref[:, pair * PAIR : (pair + 1) * PAIR]


def up_kernel(rows_ref, weight_ref, bias_ref, active_ref, slope_ref, *, chunk):
    rows = rows_ref[...]
    for at in range(0, weight_ref.shape[1], chunk):
        columns = slice(at, at + chunk)
        hidden = contract(rows, weight_ref[:, columns]) + bias_ref[:, columns]
        below = 0.5 + 0.5 * lax.erf(hidden * 2**-0.5)
        active_ref[:, columns] = (hidden * below).astype(active_ref.dtype)
        slope_ref[:, columns] = below + hidden * ((2 * math.pi) ** -0.5 * jnp.exp(-0.5 * hidden * hidden))


def hidden_grad_kernel(rows_ref, weight_ref, slope_ref, grad_ref, sum_ref, *, chunk):
    rows = rows_ref[...]
    starting = pl.program_id(0) == 0
    for at in range(0, weight_ref.shape[0], chunk):
        columns = slice(at, at + chunk)
        grad = contract_last(rows, weight_ref[columns, :]) * slope_ref[:, columns]
        grad = grad.astype(grad_ref.dtype)
        grad_ref[:, columns] = grad
        part = jnp.sum(grad.astype(jnp.float32), axis=0, keepdims=True)
        sum_ref[:, columns] = jnp.where(starting, part, sum_ref[:, columns] + part)


TILE = 256


def up_and_bend(rows, weight, bias):
    count, depth = rows.shape
    width = weight.shape[1]
    tile = pl.BlockSpec((TILE, width), lambda i: (i, 0))
    return pl.pallas_call(
        partial(up_kernel, chunk=512),
        grid=(count // TILE,),
        in_specs=[
            pl.BlockSpec((TILE, depth), lambda i: (i, 0)),
            pl.BlockSpec((depth, width), lambda i: (0, 0), pipeline_mode=pl.Buffered(1)),
            pl.BlockSpec((1, width), lambda i: (0, 0)),
        ],
        out_specs=[tile, tile],
        out_shape=[
            jax.ShapeDtypeStruct((count, width), jnp.bfloat16),
            jax.ShapeDtypeStruct((count, width), jnp.float32),
        ],
        compiler_params=pltpu.CompilerParams(vmem_limit_bytes=GRANT),
        cost_estimate=estimate(count * depth * width * 4, 2 * count * width),
        name="up_and_bend",
    )(rows, weight, bias)


def hidden_gradient(rows, weight, slope, start, count):
    depth = rows.shape[1]
    width = weight.shape[0]
    first = start // TILE
    line = pl.BlockSpec((1, width), lambda i: (0, 0))
    return pl.pallas_call(
        partial(hidden_grad_kernel, chunk=512),
        grid=(count // TILE,),
        in_specs=[
            pl.BlockSpec((TILE, depth), lambda i: (i + first, 0)),
            pl.BlockSpec((width, depth), lambda i: (0, 0), pipeline_mode=pl.Buffered(1)),
            pl.BlockSpec((TILE, width), lambda i: (i + first, 0)),
        ],
        out_specs=[pl.BlockSpec((TILE, width), lambda i: (i, 0)), line],
        out_shape=[
            jax.ShapeDtypeStruct((count, width), jnp.bfloat16),
            jax.ShapeDtypeStruct((1, width), jnp.float32),
        ],
        compiler_params=pltpu.CompilerParams(vmem_limit_bytes=GRANT),
        cost_estimate=estimate(count * depth * width * 3, 0),
        name="hidden_gradient",
    )(rows, weight, slope)


def product_kernel(rows_ref, weight_ref, out_ref):
    out_ref[...] = contract(rows_ref[...], weight_ref[...]).astype(out_ref.dtype)


def product_of(rows, weight, count):
    depth, width = weight.shape
    return pl.pallas_call(
        product_kernel,
        grid=(count // TILE,),
        in_specs=[
            pl.BlockSpec((TILE, depth), lambda i: (i, 0)),
            pl.BlockSpec((depth, width), lambda i: (0, 0), pipeline_mode=pl.Buffered(1)),
        ],
        out_specs=pl.BlockSpec((TILE, width), lambda i: (i, 0)),
        out_shape=jax.ShapeDtypeStruct((count, width), jnp.bfloat16),
        compiler_params=pltpu.CompilerParams(vmem_limit_bytes=GRANT),
        cost_estimate=estimate(2 * count * depth * width, 0),
        name="product",
    )(rows, weight)


def mixed_grad_kernel(rows_ref, weight_ref, out_ref):
    out_ref[...] = contract_last(rows_ref[...], weight_ref[...]).astype(out_ref.dtype)


def mixed_gradient(rows, weight, slab):
    count, depth = rows.shape
    width = weight.shape[0]
    return pl.pallas_call(
        mixed_grad_kernel,
        grid=(width // slab,),
        in_specs=[
            pl.BlockSpec((count, depth), lambda i: (0, 0), pipeline_mode=pl.Buffered(1)),
            pl.BlockSpec((slab, depth), lambda i: (i, 0)),
        ],
        out_specs=pl.BlockSpec((count, slab), lambda i: (0, i)),
        out_shape=jax.ShapeDtypeStruct((count, width), jnp.bfloat16),
        compiler_params=pltpu.CompilerParams(vmem_limit_bytes=GRANT),
        cost_estimate=estimate(2 * count * depth * width, 0),
        name="mixed_gradient",
    )(rows, weight)


def norm_back_kernel(own_ref, values_ref, average_ref, scale_ref, base_ref, gain_ref, *refs, parts):
    came, (low_ref, wide_ref, sums_ref) = refs[:parts], refs[parts:]
    wide = jnp.float32
    step = pl.program_id(0)

    @pl.when(step == 0)
    def _():
        sums_ref[...] = jnp.zeros_like(sums_ref)

    def make(came):
        grad = own_ref[...].astype(wide)
        for part in came:
            grad = grad + part[...].astype(wide)
        scale = scale_ref[...]
        normal = (values_ref[...].astype(wide) - average_ref[...]) * scale
        gained = grad * gain_ref[...]
        along = jnp.mean(gained * normal, axis=-1, keepdims=True)
        across = jnp.mean(gained, axis=-1, keepdims=True)
        made = base_ref[...].astype(wide) + scale * (gained - across - normal * along)
        low = made.astype(low_ref.dtype)
        low_ref[...] = low
        wide_ref[...] = made
        for at, part in enumerate((grad * normal, grad, low.astype(wide))):
            sums_ref[8 * at : 8 * at + 8, :] += jnp.sum(part.reshape(-1, 8, part.shape[1]), axis=0)

    if not came:
        make(())
        return
    upper = step < pl.num_programs(0) // 2
    pl.when(upper)(lambda: make(came[0::2]))
    pl.when(jnp.logical_not(upper))(lambda: make(came[1::2]))


def norm_back(rest, values, average, scale, base, gain, came):
    rows, width = values.shape
    steps = 8
    half = steps // 2
    came = list(came or ())
    count = rows // steps
    tile = pl.BlockSpec((count, width), lambda i: (i, 0))
    thin = pl.BlockSpec((count, 1), lambda i: (i, 0))
    top = pl.BlockSpec((count, width), lambda i: (jnp.minimum(i, half - 1), 0))
    bottom = pl.BlockSpec((count, width), lambda i: (jnp.maximum(i - half, 0), 0))
    low, full, sums = pl.pallas_call(
        partial(norm_back_kernel, parts=len(came)),
        grid=(steps,),
        in_specs=[tile, tile, thin, thin, tile, pl.BlockSpec((1, width), lambda i: (0, 0))]
        + [top, bottom] * (len(came) // 2),
        out_specs=[tile, tile, pl.BlockSpec((24, width), lambda i: (0, 0))],
        out_shape=[
            jax.ShapeDtypeStruct((rows, width), jnp.bfloat16),
            jax.ShapeDtypeStruct((rows, width), jnp.float32),
            jax.ShapeDtypeStruct((24, width), jnp.float32),
        ],
        compiler_params=pltpu.CompilerParams(vmem_limit_bytes=GRANT),
        cost_estimate=estimate(30 * rows * width, rows),
        name="norm_back",
    )(rest, values, average, scale, base, gain[None], *came)
    return low, full, jnp.sum(sums.reshape(3, 8, width), axis=1)


def outer_kernel(left_ref, right_ref, out_ref, *, chunk):
    left = left_ref[...]
    shards = out_ref.shape[0]
    for at in range(0, out_ref.shape[3], chunk):
        columns = slice(at, at + chunk)
        made = contract_first(left, right_ref[:, columns]).astype(out_ref.dtype)
        out_ref[:, 0, :, columns] = made.reshape(shards, -1, made.shape[1])


def outer(left, right, groups, shards, part_of=(0, 1)):
    at, parts = part_of
    tokens, rows = left.shape
    width = right.shape[1] // parts
    part = rows // groups
    made = pl.pallas_call(
        partial(outer_kernel, chunk=next(c for c in (512, 384, 256, 128) if width % c == 0)),
        grid=(groups,),
        in_specs=[
            pl.BlockSpec((tokens, part), lambda i: (0, i)),
            pl.BlockSpec((tokens, width), lambda i: (0, at), pipeline_mode=pl.Buffered(1)),
        ],
        out_specs=pl.BlockSpec((shards, 1, part // shards, width), lambda i: (0, i, 0, 0)),
        out_shape=jax.ShapeDtypeStruct((shards, groups, part // shards, width), jnp.bfloat16),
        compiler_params=pltpu.CompilerParams(vmem_limit_bytes=GRANT),
        cost_estimate=estimate(2 * tokens * rows * width, 0),
        name="outer",
    )(left, right)
    return made.reshape(rows, width)


def swap(values, bit):
    return lax.ppermute(values, "seq", [(i, i ^ bit) for i in range(4)])


def by_index(parts, me):
    if len(parts) != 4:
        return parts
    odd, upper = (me & 1) == 1, (me & 2) == 2
    a, b, c, d = parts
    a, b, c, d = (
        jnp.where(odd, b, a),
        jnp.where(odd, a, b),
        jnp.where(odd, d, c),
        jnp.where(odd, c, d),
    )
    return [jnp.where(upper, c, a), jnp.where(upper, d, b), jnp.where(upper, a, c), jnp.where(upper, b, d)]


def exchange(slots):
    if lax.axis_size("seq") != 4:
        return list(lax.all_to_all(jnp.stack(slots), "seq", split_axis=0, concat_axis=0, tiled=True))
    return [slots[0]] + [swap(slots[j], j) for j in (1, 2, 3)]


def gate(values, *before):
    return lax.optimization_barrier((values, *before))[0]


class Order:
    def __init__(self):
        self.pending = []

    def after(self, *values):
        self.pending += values

    def __call__(self, operation, *operands):
        if self.pending:
            count = len(operands)
            operands = lax.optimization_barrier((*operands, *self.pending))[:count]
        made = operation(*operands)
        self.pending = jax.tree.leaves(made)
        return made

    def gather(self, rows):
        if lax.axis_size("seq") != 4:
            return lax.all_gather(jnp.concatenate(rows, axis=0), "seq", axis=0, tiled=True), None
        top, bottom = rows
        return rows, (swap(bottom, 1), swap(top, 2), swap(top, 1), swap(bottom, 2))

    def fill(self, begun):
        rows, came = begun
        if came is None:
            return rows
        first_bottom, second_top, first_top, second_bottom = came
        room = jnp.zeros_like(rows[0])
        parts = (*rows, first_top, first_bottom, second_top, second_bottom, room, room)
        return self(lambda *parts: jnp.concatenate(parts, axis=0), *parts)

    def complete(self, made, pieces):
        if not isinstance(pieces, list):
            return made
        rows = pieces[-1].shape[0]

        def put(before, first, second):
            before = lax.dynamic_update_slice_in_dim(before, first, 6 * rows, axis=0)
            return lax.dynamic_update_slice_in_dim(before, second, 7 * rows, axis=0)

        return self(put, made, *pieces[-2:])

    def pass_on(self, begun, *before):
        rows, came = begun
        if came is None:
            return rows
        first_bottom, second_top, first_top, second_bottom = came
        self.after(*came)
        if before:
            second_top, first_bottom = gate((second_top, first_bottom), *before)
        far = [swap(second_top, 1), swap(first_bottom, 2)]
        return [*rows, first_top, first_bottom, second_top, second_bottom, *far]

    def halves(self, product, rows):
        def cut(values):
            made = product(values)
            half = made.shape[0] // 2
            return made[:half], made[half:]

        return self(cut, rows)

    def add_far(self, made, far, direct, *before, at=None):
        wide = jnp.float32
        half = far[0].shape[0]
        start = made.shape[0] - 4 * half if at is None else at

        def add(made, top, bottom):
            at = start
            first = (made[at + half : at + 2 * half].astype(wide) + bottom.astype(wide)).astype(made.dtype)
            second = (made[at + 2 * half : at + 3 * half].astype(wide) + top.astype(wide)).astype(made.dtype)
            if direct is None:
                first = jnp.concatenate([made[at : at + half], first], axis=0)
                second = jnp.concatenate([second, made[at + 3 * half : at + 4 * half]], axis=0)
            return first, second

        first, second = self(add, made, *far)
        if before:
            first, second = gate((first, second), *before)
        first, second = swap(first, 1), swap(second, 2)
        return (first, second) if direct is None else (direct[0], first, second, direct[1])


def swap_far(halves):
    return swap(halves[0], 1), swap(halves[1], 2)


def swap_direct(made, half):
    at = made.shape[0] - 4 * half
    return swap(made[at : at + half], 1), swap(made[at + 3 * half :], 2)


def summed(own, came):
    wide = jnp.float32
    own = own.astype(wide)
    return sum((part.astype(wide) for part in came), own)


def whole(parts):
    return jnp.concatenate(parts, axis=0) if isinstance(parts, list) else parts


def total_stages():
    stages = []
    for axis in ("fsdp", "seq"):
        count, bit = lax.axis_size(axis), 1
        bits = count.bit_length() - 1
        while bit < count:
            stages.append((axis, [bit] if bits % 2 else [bit, 2 * bit, 3 * bit]))
            bit <<= 1 if bits % 2 else 2
            bits -= bits % 2
    return stages


def local(
    tokens,
    cotangent,
    w_qkv,
    qv_bias,
    w_out,
    out_bias,
    ln1_gain,
    ln1_shift,
    ln2_gain,
    ln2_shift,
    w_up,
    up_bias,
    w_down,
    down_bias,
):
    seq_count, local_len, model_width = tokens.shape
    groups, shards = lax.axis_size("seq"), lax.axis_size("fsdp")
    me = lax.axis_index("seq")
    square = groups == 4
    heads_here = HEADS // groups
    slab = heads_here * HEAD_DIM
    pairs = slab // PAIR
    hidden_width = w_up.shape[1]
    hidden_slab = hidden_width // groups
    rows_here = seq_count * local_len
    low, wide = jnp.bfloat16, jnp.float32
    mask = jnp.reshape(me if square else jnp.zeros_like(me), (1,)).astype(jnp.int32)
    head_index = me * heads_here + jnp.arange(1, heads_here + 1, dtype=jnp.int32)
    slopes = 2.0 ** (-8.0 * head_index.astype(wide) / HEADS)

    def head_columns(values):
        rows = values.shape[0]
        return pl.pallas_call(
            head_columns_kernel,
            grid_spec=pltpu.PrefetchScalarGridSpec(
                num_scalar_prefetch=1,
                grid=(3,),
                in_specs=[pl.BlockSpec((rows, slab), lambda t, at: (0, t * groups + at[0]))],
                out_specs=pl.BlockSpec((rows, 3 * slab), lambda t, at: (0, 0)),
            ),
            out_shape=jax.ShapeDtypeStruct((rows, 3 * slab), values.dtype),
            name="head_columns",
        )(jnp.reshape(me, (1,)).astype(jnp.int32), values)

    def own_slab(values, axis):
        width = values.shape[axis] // groups
        return lax.dynamic_slice_in_dim(values, me * width, width, axis=axis)

    order = Order()
    x_low = tokens.reshape(rows_here, model_width)
    x = x_low.astype(wide)
    dz_low = cotangent.reshape(rows_here, model_width)
    qkv_slab = lax.all_gather(head_columns(w_qkv), "fsdp", axis=0, tiled=True)
    qkv_bias = head_columns(jnp.concatenate([qv_bias[0], jnp.zeros_like(qv_bias[0]), qv_bias[1]])[None])
    up_bias_slab = own_slab(up_bias, 0)

    first_norm, *first_stats = layer_norm(x, ln1_gain, ln1_shift)
    half = rows_here // 2

    def halves_of(values):
        return values[:half].astype(low), values[half:].astype(low)

    normed = order.gather(order(halves_of, first_norm))
    normed = order.pass_on(normed)
    full_out = lax.all_gather(w_out, "fsdp", axis=0, tiled=True)
    up_slab = lax.all_gather(own_slab(gate(w_up, normed[0]) if square else w_up, 1), "fsdp", axis=0, tiled=True)
    down_slab = lax.all_gather(own_slab(gate(w_down, normed[0]) if square else w_down, 0), "fsdp", axis=1, tiled=True)
    normed = whole(normed)
    upstream = order.gather(halves_of(gate(dz_low, normed)))
    qkv = order(lambda rows: (contract(rows, qkv_slab) + qkv_bias).astype(low), normed)
    attended, log_totals = order(lambda rows: attend_forward(mask, slopes, rows, seq_count, local_len), qkv)
    if square:
        attended = gate(attended, *upstream[1])
    mixed_slots = exchange([attended[j * rows_here : (j + 1) * rows_here] for j in range(groups)])
    mixed_rows = jnp.concatenate(by_index(mixed_slots, me), axis=1)
    mixed_slots = jnp.concatenate(mixed_slots, axis=1)

    def pair_swap(values):
        return lax.ppermute(values, "fsdp", [(i, i ^ 1) for i in range(shards)])

    parity = lax.axis_index("fsdp") & 1
    out_rows = model_width // (groups * shards)

    def pair_halves(values):
        halves = values.reshape(rows_here, -1, 2, out_rows)
        return tuple(
            lax.dynamic_index_in_dim(halves, index, axis=2, keepdims=False).reshape(rows_here, -1)
            for index in (parity, 1 - parity)
        )

    middle = order(lambda rows: x + (contract(rows, full_out) + out_bias), mixed_rows)
    second_norm, *second_stats = layer_norm(middle, ln2_gain, ln2_shift)
    second = order.gather(order(halves_of, second_norm))
    mine, theirs = order(pair_halves, mixed_slots)
    upstream_made = order.fill(upstream)
    theirs = pair_swap(theirs)
    dz_sum = order(lambda values: jnp.sum(values.astype(wide), axis=0), dz_low)
    mixed_half = order(lambda *parts: jnp.concatenate(parts, axis=0), mine, theirs)
    second = whole(order.pass_on(second, mixed_half))
    upstream = order.pass_on(upstream, second)
    active, slope = order(lambda rows: up_and_bend(rows, up_slab, up_bias_slab[None]), second)
    upstream = order.complete(upstream_made, upstream)

    def slab_product(left, right, part_of=(0, 1)):
        return order(lambda rows, others: outer(rows, others, groups, shards, part_of), left, right)

    def slab_sum(made):
        return lax.psum_scatter(made, "fsdp", scatter_dimension=0, tiled=True)

    def slabs_of_rows(values):
        return lax.all_to_all(
            values.reshape(groups, -1, values.shape[1]), "seq", split_axis=0, concat_axis=0, tiled=True
        )

    down_sum = slab_sum(slab_product(upstream, active))
    count = rows_here

    def slots(product, start, stop):
        return lambda values: product(values[start * count : stop * count])

    def to_second(rows):
        return contract_last(rows, up_slab).astype(low)

    def to_result(rows):
        return contract(rows, down_slab).astype(low)

    def to_normed(rows):
        return contract_last(rows, qkv_slab).astype(low)

    def scatter(product, rows):
        return lax.psum_scatter(order(product, rows), "seq", scatter_dimension=0, tiled=True)

    hidden_grad, hidden_sum = order(lambda rows: hidden_gradient(rows, down_slab, slope, 0, groups * count), upstream)
    if square:
        far = swap_far(order.halves(slots(to_second, 3, 4), hidden_grad))
        rest = order(slots(to_second, 0, 3), hidden_grad)
        second_own = rest
        direct = swap_direct(rest, half)
        came = order.add_far(rest, far, direct)
        result_far = order.halves(slots(to_result, 3, 4), active)
        up_sum = slab_sum(gate(slab_product(second, hidden_grad), *came))
        result_far = swap_far(gate(result_far, *came))
    else:
        second_own, came = scatter(to_second, hidden_grad), ()
        up_sum = slab_sum(slab_product(second, hidden_grad))
    branch_grad, middle_grad, middle_sums = order(
        lambda own, *came: norm_back(own, middle, *second_stats, dz_low, ln2_gain, came), second_own, *came
    )

    def column_sum(values):
        return jnp.sum(values.astype(wide), axis=0)

    hidden_sum = lax.dynamic_update_slice_in_dim(
        jnp.zeros((hidden_width,), wide), hidden_sum[0], me * hidden_slab, axis=0
    )
    early = [middle_sums[2], middle_sums[0], middle_sums[1], hidden_sum, dz_sum]
    mixed_grad = order(lambda rows: mixed_gradient(rows, full_out, slab), branch_grad)
    mixed_grad = exchange(by_index([mixed_grad[:, j * slab : (j + 1) * slab] for j in range(groups)], me))
    if square:
        result_rest = order(lambda rows: product_of(rows, down_slab, 3 * count), active)
        order.after(*mixed_grad)
        result_came = order.add_far(result_rest, result_far, None)
    attention = (mask, slopes, qkv, log_totals, attended)
    order.after(down_sum)
    begun = order(
        lambda *grads: attend_backward(*attention, grads, seq_count, local_len, 0, pairs // 2), *mixed_grad
    )
    branch_other = pair_swap(gate(branch_grad, result_rest) if square else branch_grad)
    branch_pair = jnp.concatenate([branch_grad, branch_other], axis=0)
    out_sum = order(lambda columns: outer(columns, branch_pair, groups, 1), mixed_half)
    if square:
        part = out_sum.shape[0] // 4
        out_far = out_sum[3 * part : 3 * part + part // 2], out_sum[3 * part + part // 2 :]
        out_far = swap_far(out_far)
    first_sum = slab_product(normed, begun, (0, 2))
    if square:
        first_sum = gate(first_sum, *result_came, *out_far)
        order.after(*result_came)
        out_came = order.add_far(out_sum, out_far, None, at=part)
    first_sum = slab_sum(first_sum)
    qkv_grad = order(
        lambda begun, *grads: attend_backward(
            *attention, grads, seq_count, local_len, pairs // 2, pairs, begun
        ),
        begun,
        *mixed_grad,
    )
    if not square:
        out_sum = lax.psum_scatter(out_sum, "seq", scatter_dimension=0, tiled=True)
    order.after(up_sum)
    if square:
        far = swap_far(order.halves(slots(to_normed, 3, 4), qkv_grad))
        order.after(first_sum)
        near = order(slots(to_normed, 1, 3), qkv_grad)
        direct = swap_direct(near, half)
        qkv_column_sum = order(column_sum, qkv_grad)
        order.after(*out_came)
        out_sum = order(lambda own, *came: summed(own[:part], came).astype(low), out_sum, *out_came)
    out_sum = out_sum.reshape(-1, 1, out_rows, model_width)
    zero = jnp.zeros_like(out_sum)
    out_sum = jnp.concatenate(
        [jnp.where(parity == 0, out_sum, zero), jnp.where(parity == 1, out_sum, zero)], axis=1
    ).reshape(-1, model_width)
    if square:
        out_sum = gate(out_sum, *far)
    grad_w_out = lax.psum_scatter(out_sum, "fsdp", scatter_dimension=0, tiled=True).astype(wide)
    if square:
        came = order.add_far(near, far, direct)
    second_sum = slab_product(normed, qkv_grad, (1, 2))
    if square:
        second_sum = slab_sum(gate(second_sum, *far, *direct))
        order.after(grad_w_out)
        normed_own = order(slots(to_normed, 0, 1), qkv_grad)
    else:
        second_sum = slab_sum(second_sum)
        qkv_column_sum = order(column_sum, qkv_grad)
        normed_own, came = scatter(to_normed, qkv_grad), ()
    grad_tokens, _, input_sums = order(
        lambda own, *came: norm_back(own, x_low, *first_stats, middle_grad, ln1_gain, came), normed_own, *came
    )
    grad_tokens = grad_tokens.reshape(tokens.shape)
    three = jnp.concatenate([down_sum, up_sum, first_sum], axis=1)
    three = slabs_of_rows(gate(three, *came, normed_own))
    down_slabs, up_slabs, first_slabs = jnp.split(three, [hidden_slab, 2 * hidden_slab], axis=2)
    second_slabs = slabs_of_rows(second_sum)

    def rows_of(slabs):
        return jnp.swapaxes(slabs, 0, 1).astype(wide)

    grad_w_down = rows_of(down_slabs).reshape(-1, hidden_width).T
    grad_w_up = rows_of(up_slabs).reshape(-1, hidden_width)
    grad_w_qkv = [
        rows_of(part).reshape(-1, groups, pairs // 2, 3, PAIR) for part in (first_slabs, second_slabs)
    ]
    grad_w_qkv = jnp.concatenate(grad_w_qkv, axis=2)
    grad_w_qkv = jnp.transpose(grad_w_qkv, (0, 3, 1, 2, 4)).reshape(-1, 3 * model_width)

    head_sum = jnp.transpose(qkv_column_sum.reshape(pairs, 3, PAIR), (1, 0, 2)).reshape(3, slab)
    qv_sum = lax.dynamic_update_slice_in_dim(
        jnp.zeros((2, model_width), wide), head_sum[0::2], me * slab, axis=1
    )
    late = [qv_sum.reshape(-1), input_sums[0], input_sums[1]]
    sums = order(lambda *parts: jnp.concatenate(parts).reshape(-1, PAIR), *early, *late)
    stages = total_stages()
    for axis, masks in stages:
        others = range(lax.axis_size(axis))
        came = [lax.ppermute(sums, axis, [(i, i ^ mask) for i in others]) for mask in masks]
        if (axis, masks) == stages[1]:
            order.after(three)
        if (axis, masks) == stages[-1]:
            order.after(second_slabs)
        sums = order(lambda *parts: sum(parts[1:], parts[0]), sums, *came)
        if (axis, masks) != stages[0]:
            continue
        if square:
            result = order(
                lambda rest, *came: (middle + (summed(rest[:count], came) + down_bias)).astype(low),
                result_rest,
                *result_came,
            )
        else:
            result = (middle + (scatter(to_result, active).astype(wide) + down_bias)).astype(low)
        result = result.reshape(tokens.shape)
    sums = sums.reshape(-1)

    def cut(at, count):
        return sums[at * model_width : (at + count) * model_width]

    ratio = hidden_width // model_width
    return (
        result,
        grad_tokens,
        grad_w_qkv,
        cut(4 + ratio, 2).reshape(2, model_width),
        grad_w_out,
        cut(0, 1),
        cut(6 + ratio, 1),
        cut(7 + ratio, 1),
        cut(1, 1),
        cut(2, 1),
        grad_w_up,
        cut(3, ratio),
        grad_w_down,
        cut(3 + ratio, 1),
    )


def solution(mesh):
    return jax.shard_map(
        local,
        mesh=mesh,
        in_specs=(
            P("fsdp", "seq", None),
            P("fsdp", "seq", None),
            P("fsdp", None),
            P(),
            P("fsdp", None),
            P(),
            P(),
            P(),
            P(),
            P(),
            P("fsdp", None),
            P(),
            P(None, "fsdp"),
            P(),
        ),
        out_specs=(
            P("fsdp", "seq", None),
            P("fsdp", "seq", None),
            P(("seq", "fsdp"), None),
            P(),
            P(("seq", "fsdp"), None),
            P(),
            P(),
            P(),
            P(),
            P(),
            P(("seq", "fsdp"), None),
            P(),
            P(None, ("seq", "fsdp")),
            P(),
        ),
        check_vma=False,
    )
```
